32 devices in a mesh: ctx: 8 (over z, y), head: 4 (over x, core).
Axes of the slice: x: 2, y: 2, z: 4, core: 2. Of those that a mesh axis runs over, the one named last changes fastest.
Arguments:
- tokens: bfloat16 [4096, 1024], P(('ctx', 'head')), may hold values from -6 to 6
- conv_kernel: float32 [7, 1024], replicated, may hold values from -2.5 to 2.5
- w_qkv: bfloat16 [1024, 3072], replicated, may hold values from -0.1875 to 0.1875
- w_out: bfloat16 [1024, 1024], replicated, may hold values from -0.1875 to 0.1875
- lengths: int32 [4], replicated, may hold values from 1 to 2048, 4096 in all
- cotangent: bfloat16 [4096, 1024], P(('ctx', 'head')), may hold values from -6 to 6
Outputs:
- attended: bfloat16 [4096, 1024], P(('ctx', 'head'))
- input_grad: bfloat16 [4096, 1024], P(('ctx', 'head'))
The draws below stay inside these ranges and needn't reach their ends.
Inputs may be any that keep to these rules, and one draw needn't show every extreme that they name: `lengths`: they sum to 4096; the longest recording has exactly 2048 tokens.
All inputs are finite; a program needn't handle non-finite values.
Results may differ from the reference program's by a relative error of at most 0.017.
The reference program's roundings to bfloat16 on the way count: a program that leaves them out, or rounds other values in their place, can miss the bound.
Values may be sent and summed in bfloat16 or wider, within the bound.
No kernel may reach another device: no remote copies, remote signals or barrier semaphores. Data moves between devices by JAX's collectives and lax.ppermute only.
A program may use at most 128 MiB of HBM per device.

```python
import math
import jax
import jax.numpy as jnp
import numpy as np
from jax import lax

D = 1024
HEADS = 16
HD = 64
KS = 7
MAXLEN = 2048
T_CTX = 512
TOKENS = 4096
NREC = 4


def shard_levels(rng, dims, split, smallest, top_value):
    factor_of, own = 1.0, jax.random.fold_in(rng, 6)
    for axis_at, parts in split:
        draws = jnp.exp(jax.random.uniform(jax.random.fold_in(own, axis_at), (parts,), jnp.float32, smallest / len(split), top_value / len(split)))
        factor_of = factor_of * jnp.repeat(draws, dims[axis_at] // parts).reshape([-1 if axis == axis_at else 1 for axis in range(len(dims))])
    return factor_of


def profile(amount, total, reach, slope):
    weights = [(1 << 20) // math.isqrt(rank ** slope) + 1 for rank in range(2, amount + 1)]
    surplus, counts = total - reach - (amount - 1), [1] * (amount - 1)
    while surplus > 0:
        movable = [i for i in range(amount - 1) if counts[i] < reach]
        whole, remaining = sum([weights[i] for i in movable]), surplus
        for i in movable:
            addition = min(reach - counts[i], max(1, remaining * weights[i] // whole), surplus)
            counts[i] = counts[i] + addition
            surplus = surplus - addition
    return np.array([reach] + counts)


def uneven_parts(stream_key, amount, total, limit, lean):
    if amount == 2:
        one = jax.random.randint(stream_key, (), max(1, total - limit), min(limit, total - 1) + 1)
        return jnp.stack([one, total - one])
    tallies = jnp.asarray(profile(amount, total, limit, lean), jnp.int32)
    couples = (amount - 1) // 2
    donor, taker = tallies[1:1 + 2 * couples:2], tallies[2:2 + 2 * couples:2]
    room = jnp.minimum(donor - 1, limit - taker)
    passed = jax.random.randint(jax.random.fold_in(stream_key, 1), (couples,), 0, 1 << 20) % (room + 1)
    tallies = tallies.at[1:1 + 2 * couples:2].set(donor - passed).at[2:2 + 2 * couples:2].set(taker + passed)
    return tallies[jax.random.permutation(jax.random.fold_in(stream_key, 2), amount)]


def centred(rng, extent, width, most, shards=(), kind=jnp.bfloat16):
    array = jax.random.normal(rng, extent, jnp.float32) * width
    if len(shards) > 0:
        array = shard_levels(rng, extent, shards, -0.22, 0.18) * array
    return jnp.clip(array, min=-most, max=most).astype(kind)


def setup_inputs(seed: int = 0) -> dict:
    arg_keys = jax.random.split(jax.random.key(seed), 7)
    tokens = centred(arg_keys[0], (TOKENS, D), 1.0, 6.0, ((0, 32),))
    conv_kernel = centred(arg_keys[1], (KS, D), 0.3, 2.5, (), jnp.float32)
    w_qkv = centred(arg_keys[2], (D, 3 * D), D ** -0.5, 0.1875)
    w_out = centred(arg_keys[3], (D, D), D ** -0.5, 0.1875)
    lengths = uneven_parts(arg_keys[4], NREC, TOKENS, MAXLEN, 1).astype(jnp.int32)
    cotangent = centred(arg_keys[5], (TOKENS, D), 1.0, 6.0, ((0, 32),))
    return {"tokens": tokens, "conv_kernel": conv_kernel, "w_qkv": w_qkv, "w_out": w_out, "lengths": lengths, "cotangent": cotangent}


def segment_of(positions, lengths):
    record_ends = jnp.cumsum(lengths).astype(jnp.int32)
    return jnp.sum((record_ends[None, :] <= positions[:, None]).astype(jnp.int32), axis=1).astype(jnp.int32)


def convolve(values, kernel, segments):
    count = values.shape[0]
    half_width = KS // 2
    padded = jnp.pad(values.astype(jnp.float32), ((half_width, half_width), (0, 0)))
    seg_padded = jnp.pad(segments, (half_width, half_width), constant_values=-1)
    summed = values.astype(jnp.float32)
    for tap_index in range(KS):
        same_seg = (seg_padded[tap_index:tap_index + count] == segments).astype(jnp.float32)
        summed = summed + kernel[tap_index][None, :] * padded[tap_index:tap_index + count] * same_seg[:, None]
    return summed.astype(jnp.bfloat16)


def rounded(values):
    return lax.optimization_barrier(values.astype(jnp.bfloat16)).astype(jnp.float32)


def reference(tokens, conv_kernel, w_qkv, w_out, lengths, cotangent):
    positions = jnp.arange(TOKENS, dtype=jnp.int32)
    segments = segment_of(positions, lengths)
    mixed = convolve(tokens, conv_kernel, segments)
    projected = jnp.dot(mixed, w_qkv, preferred_element_type=jnp.float32).astype(jnp.bfloat16)
    queries = projected[:, :D].reshape(TOKENS, HEADS, HD)
    key_all = projected[:, D:2 * D].reshape(TOKENS, HEADS, HD)
    value_all = projected[:, 2 * D:].reshape(TOKENS, HEADS, HD)
    score_scale = HD ** -0.5
    blocks = TOKENS // T_CTX
    window = MAXLEN + T_CTX
    key_pad = jnp.pad(key_all, ((MAXLEN, 0), (0, 0), (0, 0)))
    value_pad = jnp.pad(value_all, ((MAXLEN, 0), (0, 0), (0, 0)))
    seg_keys = jnp.pad(segments, (MAXLEN, 0), constant_values=-1)

    def weights_of(block_index):
        first_row = (block_index * T_CTX).astype(jnp.int32)
        query_block = lax.dynamic_slice_in_dim(queries, first_row, T_CTX, 0).astype(jnp.float32)
        key_window = lax.dynamic_slice_in_dim(key_pad, first_row, window, 0).astype(jnp.float32)
        value_window = lax.dynamic_slice_in_dim(value_pad, first_row, window, 0).astype(jnp.float32)
        query_pos = first_row + jnp.arange(T_CTX, dtype=jnp.int32)
        key_pos = first_row - MAXLEN + jnp.arange(window, dtype=jnp.int32)
        seg_query = lax.dynamic_slice_in_dim(segments, first_row, T_CTX, 0)
        seg_key = lax.dynamic_slice_in_dim(seg_keys, first_row, window, 0)
        allowed = (seg_query[:, None] == seg_key[None, :]) & (key_pos[None, :] <= query_pos[:, None])
        scores = jnp.einsum("qhd,khd->hqk", query_block, key_window) * score_scale
        weights = jnp.where(allowed[None], jnp.exp(scores), 0.0)
        return weights, query_block, key_window, value_window, first_row

    def forward_block(block_index):
        weights, query_block, key_window, value_window, first_row = weights_of(block_index)
        totals = jnp.sum(weights, axis=2)
        weighted = jnp.einsum("hqk,khd->qhd", rounded(weights), value_window)
        context = (weighted / totals.T[:, :, None]).astype(jnp.bfloat16)
        return context, totals

    contexts, totals_all = lax.map(forward_block, jnp.arange(blocks, dtype=jnp.int32))
    context_flat = contexts.reshape(TOKENS, D)
    attended = jnp.dot(context_flat, w_out, preferred_element_type=jnp.float32).astype(jnp.bfloat16)
    d_context = jnp.dot(cotangent, w_out.T, preferred_element_type=jnp.float32).astype(jnp.bfloat16)
    d_heads = d_context.reshape(TOKENS, HEADS, HD)
    row_delta = jnp.sum(d_heads.astype(jnp.float32) * contexts.reshape(TOKENS, HEADS, HD).astype(jnp.float32), axis=2)

    def backward_block(carry, block_index):
        d_key_pad, d_value_pad = carry
        weights, query_block, key_window, value_window, first_row = weights_of(block_index)
        totals = totals_all[block_index]
        prob_full = weights / totals[:, :, None]
        d_block = lax.dynamic_slice_in_dim(d_heads, first_row, T_CTX, 0).astype(jnp.float32)
        delta_block = lax.dynamic_slice_in_dim(row_delta, first_row, T_CTX, 0)
        d_values = jnp.einsum("hqk,qhd->khd", rounded(prob_full), d_block)
        d_probs = jnp.einsum("qhd,khd->hqk", d_block, value_window)
        d_scores = rounded(prob_full * (d_probs - delta_block.T[:, :, None]))
        d_query = jnp.einsum("hqk,khd->qhd", d_scores, key_window) * score_scale
        d_keys = jnp.einsum("hqk,qhd->khd", d_scores, query_block) * score_scale
        old_keys = lax.dynamic_slice_in_dim(d_key_pad, first_row, window, 0)
        old_values = lax.dynamic_slice_in_dim(d_value_pad, first_row, window, 0)
        d_key_pad = lax.dynamic_update_slice_in_dim(d_key_pad, old_keys + d_keys, first_row, 0)
        d_value_pad = lax.dynamic_update_slice_in_dim(d_value_pad, old_values + d_values, first_row, 0)
        return (d_key_pad, d_value_pad), d_query

    zeros_pad = jnp.zeros((MAXLEN + TOKENS, HEADS, HD), jnp.float32)
    (d_key_pad, d_value_pad), d_queries = lax.scan(backward_block, (zeros_pad, zeros_pad), jnp.arange(blocks, dtype=jnp.int32))
    grad_q = d_queries.reshape(TOKENS, D).astype(jnp.bfloat16)
    grad_k = d_key_pad[MAXLEN:].reshape(TOKENS, D).astype(jnp.bfloat16)
    grad_v = d_value_pad[MAXLEN:].reshape(TOKENS, D).astype(jnp.bfloat16)
    grad_qkv = jnp.concatenate([grad_q, grad_k, grad_v], axis=1)
    grad_mixed = jnp.dot(grad_qkv, w_qkv.T, preferred_element_type=jnp.float32).astype(jnp.bfloat16)
    input_grad = convolve(grad_mixed, conv_kernel[::-1], segments)
    return attended, input_grad
```

```python
import functools
import math

import jax
import jax.numpy as jnp
from jax import lax
from jax.experimental import pallas as pl
from jax.experimental.pallas import tpu as pltpu
from jax.sharding import PartitionSpec as P

HD = 64
KS = 7
HALF = KS // 2
MAXLEN = 2048
AXES = ("ctx", "head")
LANES = 128
EDGE = 16
VMEM_LIMIT = 48 * 1024 * 1024
F32 = jnp.float32
BF16 = jnp.bfloat16


def params():
    return pltpu.CompilerParams(vmem_limit_bytes=VMEM_LIMIT)


def record_span(positions, lengths_ref):
    start = jnp.zeros_like(positions)
    stop = jnp.full_like(positions, jnp.iinfo(jnp.int32).max)
    end = jnp.int32(0)
    for i in range(lengths_ref.shape[0]):
        end = end + lengths_ref[i]
        past = end <= positions
        start = jnp.where(past, end, start)
        stop = jnp.where(past, stop, jnp.minimum(stop, end))
    return start, stop


def low_lanes(shape):
    return lax.broadcasted_iota(jnp.int32, shape, len(shape) - 1) % LANES < HD


def swap_halves(x):
    return pltpu.roll(x, HD, x.ndim - 1)


def zip_low(x, y):
    return jnp.where(low_lanes(x.shape), x, swap_halves(y))


def zip_high(x, y):
    return jnp.where(low_lanes(x.shape), swap_halves(x), y)


def conv_rows(padded_ref, cols, kernel_ref, lengths_ref, first_row, rows, flip):
    pos = first_row + lax.broadcasted_iota(jnp.int32, (rows, LANES), 0)
    start, stop = record_span(pos, lengths_ref)
    masks = []
    for t in range(KS):
        at = pos + (t - HALF)
        masks.append((at >= start) & (at < stop))
    pieces = []
    for c in cols:
        lanes = pl.ds(c * LANES, LANES)
        total = padded_ref[pl.ds(8, rows), lanes]
        for t in range(KS):
            tap = kernel_ref[KS - 1 - t if flip else t, lanes]
            shifted = padded_ref[pl.ds(8 - HALF + t, rows), lanes]
            total = total + jnp.where(masks[t], shifted, 0.0) * tap[None, :]
        pieces.append(total)
    return jnp.concatenate(pieces, axis=1)


def d_rows_kernel(cot_ref, w_ref, out_ref):
    out_ref[...] = lax.dot_general(
        cot_ref[...], w_ref[...], (((1,), (1,)), ((), ())), preferred_element_type=F32
    ).astype(BF16)


def d_rows_call(cotangent, w_out):
    rows, width = cotangent.shape
    blk = 256
    return pl.pallas_call(
        d_rows_kernel,
        grid=(width // blk,),
        in_specs=[
            pl.BlockSpec((rows, width), lambda i: (0, 0)),
            pl.BlockSpec((blk, width), lambda i: (i, 0)),
        ],
        out_specs=pl.BlockSpec((rows, blk), lambda i: (0, i)),
        out_shape=jax.ShapeDtypeStruct((rows, width), BF16),
        compiler_params=params(),
        cost_estimate=pl.CostEstimate(
            flops=2 * rows * width * width, bytes_accessed=2 * width * width, transcendentals=0
        ),
        name="d_rows",
    )(cotangent, w_out)


def qkv_kernel(
    lengths_ref, where_ref, before_ref, x_ref, after_ref, taps_ref, wq_ref, wk_ref, wv_ref, d_ref,
    kv_ref, qd_ref, padded, mixed,
):
    rows, width = x_ref.shape

    @pl.when(pl.program_id(0) == 0)
    def _():
        padded[pl.ds(0, 8), :] = before_ref[...].astype(F32)[EDGE - 8 :]
        padded[pl.ds(8, rows), :] = x_ref[...].astype(F32)
        padded[pl.ds(8 + rows, 8), :] = after_ref[...].astype(F32)[:8]
        mixed[...] = conv_rows(
            padded, range(width // LANES), taps_ref, lengths_ref, where_ref[0], rows, False
        ).astype(BF16)

    m = mixed[...]
    q = jnp.dot(m, wq_ref[...], preferred_element_type=F32)
    k = jnp.dot(m, wk_ref[...], preferred_element_type=F32)
    v = jnp.dot(m, wv_ref[...], preferred_element_type=F32)
    d = d_ref[...].astype(F32)
    for pair in range(q.shape[1] // LANES):
        cols = slice(pair * LANES, (pair + 1) * LANES)
        kv_ref[2 * pair] = zip_low(k[:, cols], v[:, cols]).astype(BF16)
        kv_ref[2 * pair + 1] = zip_high(k[:, cols], v[:, cols]).astype(BF16)
        qd_ref[2 * pair] = zip_low(q[:, cols], d[:, cols]).astype(BF16)
        qd_ref[2 * pair + 1] = zip_high(q[:, cols], d[:, cols]).astype(BF16)


def qkv_call(lengths, where, before, x, after, taps, w_qkv, d_rows):
    rows, width = x.shape
    heads = width // HD
    blk = 256
    steps = width // blk
    per = blk // HD
    smem = pl.BlockSpec(memory_space=pltpu.SMEM)
    whole = lambda a: pl.BlockSpec(a.shape, lambda i: (0, 0))
    packed = pl.BlockSpec((per, rows, LANES), lambda i: (i, 0, 0))
    shape = jax.ShapeDtypeStruct((heads, rows, LANES), BF16)
    return pl.pallas_call(
        qkv_kernel,
        grid=(steps,),
        in_specs=[
            smem, smem, whole(before), whole(x), whole(after), whole(taps),
            pl.BlockSpec((width, blk), lambda i: (0, i)),
            pl.BlockSpec((width, blk), lambda i: (0, steps + i)),
            pl.BlockSpec((width, blk), lambda i: (0, 2 * steps + i)),
            pl.BlockSpec((rows, blk), lambda i: (0, i)),
        ],
        out_specs=[packed, packed],
        out_shape=[shape, shape],
        scratch_shapes=[pltpu.VMEM((rows + 16, width), F32), pltpu.VMEM((rows, width), BF16)],
        compiler_params=params(),
        cost_estimate=pl.CostEstimate(
            flops=6 * rows * width * width, bytes_accessed=6 * width * width, transcendentals=0
        ),
        name="qkv",
    )(lengths, where, before, x, after, taps, w_qkv, w_qkv, w_qkv, d_rows)


def attention_kernel(
    pre, lengths_ref, where_ref, kv_mine, kv_other, qd_ref,
    cq_ref, dkv_mine, dkv_other, kvt_mine, kvt_other, e_ref, acc_mine, acc_other,
):
    slots, rows, _ = qd_ref.shape
    key_slots = kv_mine.shape[0]
    tile = 2 * rows
    base, parity = where_ref[1], where_ref[2]
    unit = HD**-0.5
    to_exp2 = unit * math.log2(math.e)
    for source, turned in ((kv_mine, kvt_mine), (kv_other, kvt_other)):
        for t in range(key_slots // 2):
            block = source[pl.ds(2 * t, 2)].reshape(tile, LANES)
            turned[t] = block.T
    acc_mine[...] = jnp.zeros_like(acc_mine)
    acc_other[...] = jnp.zeros_like(acc_other)
    halves = ((kv_mine, kvt_mine, acc_mine, parity), (kv_other, kvt_other, acc_other, 1 - parity))

    lane = lax.broadcasted_iota(jnp.int32, (1, tile), 1)
    lane_pos = (lane // rows) * (2 * rows) + lane % rows
    sub = lax.broadcasted_iota(jnp.int32, (tile, 1), 0)
    sub_pos = (sub // rows) * (2 * rows) + sub % rows

    def queries(u, carry):
        first = base + u * (4 * rows) + parity * rows
        q_pos = first + lane_pos
        q_start, _ = record_span(q_pos, lengths_ref)
        end = jnp.int32(0)
        begin = jnp.int32(0)
        for i in range(lengths_ref.shape[0]):
            end = end + lengths_ref[i]
            begin = jnp.where(end <= first, end, begin)
        origin = base - pre * (2 * rows)
        t_first = jnp.maximum(begin - origin, 0) // (4 * rows)
        t_stop = u + pre // 2 + 1

        qd = qd_ref[pl.ds(2 * u, 2)].reshape(tile, LANES).astype(F32)
        low = low_lanes(qd.shape)
        q_pad = jnp.where(low, qd, 0.0).astype(BF16)
        d_pad = jnp.where(low, 0.0, qd).astype(BF16)
        qd_cat = jnp.concatenate([q_pad, d_pad], axis=0)
        d_turned = qd.T[HD:]

        def forward(t, carry):
            total, context = carry
            for half, (kv, turned, _, side) in enumerate(halves):
                keys = kv[pl.ds(2 * t, 2)].reshape(tile, LANES)
                scores = lax.dot_general(
                    keys, q_pad, (((1,), (1,)), ((), ())), preferred_element_type=F32
                )
                k_pos = origin + t * (4 * rows) + side * rows + sub_pos
                allowed = (k_pos <= q_pos) & (k_pos >= q_start)
                e = jnp.where(allowed, jnp.exp2(scores * to_exp2), 0.0)
                e_ref[t - t_first, half] = e
                total = total + jnp.sum(e.reshape(tile // 8, 8, tile), axis=0)
                context = context + jnp.dot(
                    turned[t, HD:], e.astype(BF16), preferred_element_type=F32
                )
            return total, context

        total, context = lax.fori_loop(
            t_first, t_stop, forward, (jnp.zeros((8, tile), F32), jnp.zeros((HD, tile), F32))
        )
        inverse = 1.0 / jnp.sum(total, axis=0, keepdims=True)
        context = (context * inverse).astype(BF16).astype(F32)
        delta = jnp.sum(d_turned * context, axis=0, keepdims=True)

        def backward(t, d_queries):
            for half, (kv, turned, acc, _) in enumerate(halves):
                keys = kv[pl.ds(2 * t, 2)].reshape(tile, LANES)
                probs = e_ref[t - t_first, half] * inverse
                d_probs = lax.dot_general(
                    keys, d_pad, (((1,), (1,)), ((), ())), preferred_element_type=F32
                )
                d_scores = (probs * (d_probs - delta)).astype(BF16)
                both = jnp.concatenate([d_scores, probs.astype(BF16)], axis=1)
                acc[t] += jnp.dot(both, qd_cat, preferred_element_type=F32)
                d_queries = d_queries + jnp.dot(
                    turned[t, :HD], d_scores, preferred_element_type=F32
                )
            return d_queries

        d_queries = lax.fori_loop(t_first, t_stop, backward, jnp.zeros((HD, tile), F32))
        packed = jnp.concatenate([context, d_queries * unit], axis=0).T
        cq_ref[pl.ds(2 * u, 2)] = packed.astype(BF16).reshape(2, rows, LANES)
        return carry

    lax.fori_loop(0, slots // 2, queries, 0)
    scale = jnp.where(low_lanes((1, LANES)), unit, 1.0)
    for t in range(key_slots // 2):
        dkv_mine[pl.ds(2 * t, 2)] = (acc_mine[t] * scale).reshape(2, rows, LANES)
        dkv_other[pl.ds(2 * t, 2)] = (acc_other[t] * scale).astype(BF16).reshape(2, rows, LANES)


def attention_call(lengths, where, kv_mine, kv_other, qd, pre):
    slots, rows, _ = qd.shape
    key_slots = kv_mine.shape[0]
    tile = 2 * rows
    tiles = key_slots // 2
    reach = MAXLEN // (4 * rows) + 1
    smem = pl.BlockSpec(memory_space=pltpu.SMEM)
    vmem = pl.BlockSpec(memory_space=pltpu.VMEM)
    return pl.pallas_call(
        functools.partial(attention_kernel, pre),
        in_specs=[smem, smem, vmem, vmem, vmem],
        out_specs=[vmem, vmem, vmem],
        out_shape=[
            jax.ShapeDtypeStruct(qd.shape, BF16),
            jax.ShapeDtypeStruct(kv_mine.shape, F32),
            jax.ShapeDtypeStruct(kv_mine.shape, BF16),
        ],
        scratch_shapes=[
            pltpu.VMEM((tiles, LANES, tile), BF16),
            pltpu.VMEM((tiles, LANES, tile), BF16),
            pltpu.VMEM((reach, 2, tile, tile), F32),
            pltpu.VMEM((tiles, tile, LANES), F32),
            pltpu.VMEM((tiles, tile, LANES), F32),
        ],
        compiler_params=params(),
        cost_estimate=pl.CostEstimate(
            flops=10 * slots * rows * MAXLEN * LANES,
            bytes_accessed=20 * slots * rows * LANES,
            transcendentals=slots * rows * MAXLEN,
        ),
        name="attention",
    )(lengths, where, kv_mine, kv_other, qd)


def attended_kernel(cq_ref, w_ref, out_ref, context):
    heads = cq_ref.shape[0]

    @pl.when(pl.program_id(0) == 0)
    def _():
        for pair in range(heads // 2):
            x, y = (cq_ref[2 * pair + i].astype(F32) for i in range(2))
            context[:, pl.ds(pair * LANES, LANES)] = zip_low(x, y).astype(BF16)

    out_ref[...] = jnp.dot(context[...], w_ref[...], preferred_element_type=F32).astype(BF16)


def attended_call(cq, w_out):
    heads, rows, _ = cq.shape
    width = heads * HD
    blk = 256
    return pl.pallas_call(
        attended_kernel,
        grid=(width // blk,),
        in_specs=[
            pl.BlockSpec(cq.shape, lambda i: (0, 0, 0)),
            pl.BlockSpec((width, blk), lambda i: (0, i)),
        ],
        out_specs=pl.BlockSpec((rows, blk), lambda i: (0, i)),
        out_shape=jax.ShapeDtypeStruct((rows, width), BF16),
        scratch_shapes=[pltpu.VMEM((rows, width), BF16)],
        compiler_params=params(),
        cost_estimate=pl.CostEstimate(
            flops=2 * rows * width * width, bytes_accessed=2 * width * width, transcendentals=0
        ),
        name="attended",
    )(cq, w_out)


def grad_mixed_kernel(cq_ref, dkv_ref, w_ref, out_ref, grads):
    heads = cq_ref.shape[0]
    width = heads * HD

    @pl.when(pl.program_id(0) == 0)
    def _():
        for pair in range(heads // 2):
            x, y = (cq_ref[2 * pair + i].astype(F32) for i in range(2))
            grads[:, pl.ds(pair * LANES, LANES)] = zip_high(x, y).astype(BF16)
            x, y = (dkv_ref[2 * pair + i].astype(F32) for i in range(2))
            grads[:, pl.ds(width + pair * LANES, LANES)] = zip_low(x, y).astype(BF16)
            grads[:, pl.ds(2 * width + pair * LANES, LANES)] = zip_high(x, y).astype(BF16)

    out_ref[...] = lax.dot_general(
        grads[...], w_ref[...], (((1,), (1,)), ((), ())), preferred_element_type=F32
    ).astype(BF16)


def grad_mixed_call(cq, dkv, w_qkv):
    heads, rows, _ = cq.shape
    width = heads * HD
    blk = 256
    return pl.pallas_call(
        grad_mixed_kernel,
        grid=(width // blk,),
        in_specs=[
            pl.BlockSpec(cq.shape, lambda i: (0, 0, 0)),
            pl.BlockSpec(dkv.shape, lambda i: (0, 0, 0)),
            pl.BlockSpec((blk, 3 * width), lambda i: (i, 0)),
        ],
        out_specs=pl.BlockSpec((rows, blk), lambda i: (0, i)),
        out_shape=jax.ShapeDtypeStruct((rows, width), BF16),
        scratch_shapes=[pltpu.VMEM((rows, 3 * width), BF16)],
        compiler_params=params(),
        cost_estimate=pl.CostEstimate(
            flops=6 * rows * width * width, bytes_accessed=6 * width * width, transcendentals=0
        ),
        name="grad_mixed",
    )(cq, dkv, w_qkv)


def conv_kernel_body(
    lengths_ref, where_ref, before_ref, x_ref, after_ref, taps_ref, out_ref, padded
):
    rows, width = x_ref.shape
    padded[pl.ds(0, 8), :] = before_ref[...].astype(F32)[EDGE - 8 :]
    padded[pl.ds(8, rows), :] = x_ref[...].astype(F32)
    padded[pl.ds(8 + rows, 8), :] = after_ref[...].astype(F32)[:8]
    out_ref[...] = conv_rows(
        padded, range(width // LANES), taps_ref, lengths_ref, where_ref[0], rows, True
    ).astype(BF16)


def conv_call(lengths, where, before, x, after, taps):
    rows, width = x.shape
    smem = pl.BlockSpec(memory_space=pltpu.SMEM)
    vmem = pl.BlockSpec(memory_space=pltpu.VMEM)
    return pl.pallas_call(
        conv_kernel_body,
        in_specs=[smem, smem, vmem, vmem, vmem, vmem],
        out_specs=vmem,
        out_shape=jax.ShapeDtypeStruct((rows, width), BF16),
        scratch_shapes=[pltpu.VMEM((rows + 16, width), F32)],
        compiler_params=params(),
        name="input_grad",
    )(lengths, where, before, x, after, taps)


def on_device(tokens, conv_kernel, w_qkv, w_out, lengths, cotangent):
    rows, width = tokens.shape
    heads = width // HD
    devices = lax.axis_size(AXES)
    window = 2 * heads
    windows = devices // window
    pre = MAXLEN // (2 * rows) if windows > 1 else 0
    me = lax.axis_index(AXES)
    where = jnp.stack([me * rows, me // window * (window * rows), me % 2]).astype(jnp.int32)
    same_side = [
        [w * window + 2 * c + side for c in range(heads)]
        for w in range(windows)
        for side in range(2)
    ]
    swapped = [(i, i ^ 1) for i in range(devices)]
    up = [(i, i + 1) for i in range(devices - 1)]
    down = [(i + 1, i) for i in range(devices - 1)]

    def exchange(x):
        return lax.all_to_all(
            x, AXES, split_axis=0, concat_axis=0, axis_index_groups=same_side, tiled=True
        )

    before = lax.ppermute(tokens[rows - EDGE :], AXES, up)
    after = lax.ppermute(tokens[:EDGE], AXES, down)
    d_rows = d_rows_call(cotangent, w_out)
    kv, qd = qkv_call(lengths, where, before, tokens, after, conv_kernel, w_qkv, d_rows)
    kv_mine = exchange(kv)
    qd = exchange(qd)
    if pre:
        shift = [(i, i + window) for i in range(devices - window)]
        kv_mine = jnp.concatenate([lax.ppermute(kv_mine[heads - pre :], AXES, shift), kv_mine])
    kv_other = lax.ppermute(kv_mine, AXES, swapped)
    cq, dkv_mine, dkv_other = attention_call(lengths, where, kv_mine, kv_other, qd, pre)
    dkv = dkv_mine + lax.ppermute(dkv_other, AXES, swapped).astype(F32)
    if pre:
        back = [(i + window, i) for i in range(devices - window)]
        earlier = lax.ppermute(dkv[:pre].astype(BF16), AXES, back).astype(F32)
        dkv = dkv[pre:].at[heads - pre :].add(earlier)
    cq = exchange(cq)
    dkv = exchange(dkv.astype(BF16))
    attended = attended_call(cq, w_out)
    grad_mixed = grad_mixed_call(cq, dkv, w_qkv)
    before = lax.ppermute(grad_mixed[rows - EDGE :], AXES, up)
    after = lax.ppermute(grad_mixed[:EDGE], AXES, down)
    input_grad = conv_call(lengths, where, before, grad_mixed, after, conv_kernel)
    return attended, input_grad


def solution(mesh):
    placed = (P(AXES, None), P(), P(), P(), P(), P(AXES, None))
    return jax.shard_map(
        on_device,
        mesh=mesh,
        in_specs=placed,
        out_specs=(P(AXES, None), P(AXES, None)),
        check_vma=False,
    )
```

```python
import functools
import math

import jax
import jax.numpy as jnp
from jax import lax
from jax.experimental import pallas as pl
from jax.experimental.pallas import tpu as pltpu
from jax.sharding import PartitionSpec as P

HD = 64
KS = 7
HALF = KS // 2
MAXLEN = 2048
AXES = ("ctx", "head")
LANES = 128
EDGE = 16
VMEM_ALL = 60 * 1024 * 1024
VMEM_SOME = 24 * 1024 * 1024
VMEM_FEW = 16 * 1024 * 1024
F32 = jnp.float32
BF16 = jnp.bfloat16


def params(limit):
    return pltpu.CompilerParams(vmem_limit_bytes=limit)


def record_span(positions, lengths_ref):
    start = jnp.zeros_like(positions)
    stop = jnp.full_like(positions, jnp.iinfo(jnp.int32).max)
    end = jnp.int32(0)
    for i in range(lengths_ref.shape[0]):
        end = end + lengths_ref[i]
        past = end <= positions
        start = jnp.where(past, end, start)
        stop = jnp.where(past, stop, jnp.minimum(stop, end))
    return start, stop


def low_lanes(shape):
    return lax.broadcasted_iota(jnp.int32, shape, len(shape) - 1) % LANES < HD


def swap_halves(x):
    return pltpu.roll(x, HD, x.ndim - 1)


def zip_low(x, y):
    return jnp.where(low_lanes(x.shape), x, swap_halves(y))


def zip_high(x, y):
    return jnp.where(low_lanes(x.shape), swap_halves(x), y)


def conv_rows(padded_ref, cols, kernel_ref, lengths_ref, first_row, rows, flip):
    pos = first_row + lax.broadcasted_iota(jnp.int32, (rows, LANES), 0)
    start, stop = record_span(pos, lengths_ref)
    masks = []
    for t in range(KS):
        at = pos + (t - HALF)
        masks.append((at >= start) & (at < stop))
    pieces = []
    for c in cols:
        lanes = pl.ds(c * LANES, LANES)
        total = padded_ref[pl.ds(8, rows), lanes]
        for t in range(KS):
            tap = kernel_ref[KS - 1 - t if flip else t, lanes]
            shifted = padded_ref[pl.ds(8 - HALF + t, rows), lanes]
            total = total + jnp.where(masks[t], shifted, 0.0) * tap[None, :]
        pieces.append(total)
    return jnp.concatenate(pieces, axis=1)


def front_kernel(
    lengths_ref, where_ref, before_ref, x_ref, after_ref, taps_ref, w_ref, cot_ref, wo_ref,
    out_ref, padded, projected, d_rows,
):
    rows, blk = x_ref.shape
    step = pl.program_id(0)
    steps = pl.num_programs(0)
    padded[pl.ds(0, 8), :] = before_ref[...].astype(F32)[EDGE - 8 :]
    padded[pl.ds(8, rows), :] = x_ref[...].astype(F32)
    padded[pl.ds(8 + rows, 8), :] = after_ref[...].astype(F32)[:8]
    mixed = conv_rows(
        padded, range(blk // LANES), taps_ref, lengths_ref, where_ref[0], rows, False
    ).astype(BF16)
    d_rows[step] = lax.dot_general(
        cot_ref[...], wo_ref[...], (((1,), (1,)), ((), ())), preferred_element_type=F32
    )
    part = jnp.dot(mixed, w_ref[...], preferred_element_type=F32)

    @pl.when(step == 0)
    def _():
        projected[...] = part

    @pl.when(step > 0)
    def _():
        projected[...] += part

    @pl.when(step == steps - 1)
    def _():
        width = projected.shape[1] // 3
        per = blk // LANES
        for pair in range(width // LANES):
            q, k, v = (projected[:, pl.ds(i * width + pair * LANES, LANES)] for i in range(3))
            d = d_rows[pair // per, :, pl.ds(pair % per * LANES, LANES)]
            out_ref[2 * pair] = jnp.concatenate([zip_low(k, v), zip_low(q, d)]).astype(BF16)
            out_ref[2 * pair + 1] = jnp.concatenate([zip_high(k, v), zip_high(q, d)]).astype(BF16)


def front_call(lengths, where, before, x, after, taps, w_qkv, cotangent, w_out):
    rows, width = x.shape
    heads = width // HD
    blk = 256
    smem = pl.BlockSpec(memory_space=pltpu.SMEM)
    columns = lambda a: pl.BlockSpec((a.shape[0], blk), lambda i: (0, i))
    return pl.pallas_call(
        front_kernel,
        grid=(width // blk,),
        in_specs=[
            smem, smem, columns(before), columns(x), columns(after), columns(taps),
            pl.BlockSpec((blk, 3 * width), lambda i: (i, 0)),
            pl.BlockSpec((rows, width), lambda i: (0, 0)),
            pl.BlockSpec((blk, width), lambda i: (i, 0)),
        ],
        out_specs=pl.BlockSpec((heads, 2 * rows, LANES), lambda i: (0, 0, 0)),
        out_shape=jax.ShapeDtypeStruct((heads, 2 * rows, LANES), BF16),
        scratch_shapes=[
            pltpu.VMEM((rows + 16, blk), F32),
            pltpu.VMEM((rows, 3 * width), F32),
            pltpu.VMEM((width // blk, rows, blk), F32),
        ],
        compiler_params=params(VMEM_ALL),
        cost_estimate=pl.CostEstimate(
            flops=8 * rows * width * width, bytes_accessed=8 * width * width, transcendentals=0
        ),
        name="front",
    )(lengths, where, before, x, after, taps, w_qkv, cotangent, w_out)


def attention_kernel(
    pre, lengths_ref, where_ref, kv_mine, kv_other, qd_ref,
    cq_ref, dkv_mine, edge_mine, send_ref, kvt_mine, kvt_other, e_ref, acc_other, cq_full,
):
    slots = qd_ref.shape[0]
    key_slots, rows, _ = kv_mine.shape
    acc_mine = dkv_mine
    tile = 2 * rows
    base, parity = where_ref[1], where_ref[2]
    unit = HD**-0.5
    to_exp2 = unit * math.log2(math.e)
    for source, turned in ((kv_mine, kvt_mine), (kv_other, kvt_other)):
        for t in range(key_slots // 2):
            block = source[pl.ds(2 * t, 2)].reshape(tile, LANES)
            turned[t] = block.T
    acc_mine[...] = jnp.zeros_like(acc_mine)
    acc_other[...] = jnp.zeros_like(acc_other)
    halves = ((kv_mine, kvt_mine, acc_mine, parity), (kv_other, kvt_other, acc_other, 1 - parity))

    lane = lax.broadcasted_iota(jnp.int32, (1, tile), 1)
    lane_pos = (lane // rows) * (2 * rows) + lane % rows
    sub = lax.broadcasted_iota(jnp.int32, (tile, 1), 0)
    sub_pos = (sub // rows) * (2 * rows) + sub % rows

    def queries(u, carry):
        first = base + u * (4 * rows) + parity * rows
        q_pos = first + lane_pos
        q_start, _ = record_span(q_pos, lengths_ref)
        end = jnp.int32(0)
        begin = jnp.int32(0)
        for i in range(lengths_ref.shape[0]):
            end = end + lengths_ref[i]
            begin = jnp.where(end <= first, end, begin)
        origin = base - pre * (2 * rows)
        t_first = jnp.maximum(begin - origin, 0) // (4 * rows)
        t_stop = u + pre // 2 + 1

        qd = qd_ref[pl.ds(2 * u, 2), pl.ds(rows, rows)].reshape(tile, LANES).astype(F32)
        low = low_lanes(qd.shape)
        q_pad = jnp.where(low, qd, 0.0).astype(BF16)
        d_pad = jnp.where(low, 0.0, qd).astype(BF16)
        qd_cat = jnp.concatenate([q_pad, d_pad], axis=0)
        d_turned = qd.T[HD:]

        def forward(t, carry):
            total, context = carry
            for half, (kv, turned, _, side) in enumerate(halves):
                keys = kv[pl.ds(2 * t, 2)].reshape(tile, LANES)
                scores = lax.dot_general(
                    keys, q_pad, (((1,), (1,)), ((), ())), preferred_element_type=F32
                )
                k_pos = origin + t * (4 * rows) + side * rows + sub_pos
                allowed = (k_pos <= q_pos) & (k_pos >= q_start)
                e = jnp.where(allowed, jnp.exp2(scores * to_exp2), 0.0)
                e_ref[t - t_first, half] = e
                total = total + jnp.sum(e.reshape(tile // 8, 8, tile), axis=0)
                context = context + jnp.dot(
                    turned[t, HD:], e.astype(BF16), preferred_element_type=F32
                )
            return total, context

        total, context = lax.fori_loop(
            t_first, t_stop, forward, (jnp.zeros((8, tile), F32), jnp.zeros((HD, tile), F32))
        )
        inverse = 1.0 / jnp.sum(total, axis=0, keepdims=True)
        context = (context * inverse).astype(BF16).astype(F32)
        delta = jnp.sum(d_turned * context, axis=0, keepdims=True)

        def backward(t, d_queries):
            for half, (kv, turned, acc, _) in enumerate(halves):
                keys = kv[pl.ds(2 * t, 2)].reshape(tile, LANES)
                probs = e_ref[t - t_first, half] * inverse
                d_probs = lax.dot_general(
                    keys, d_pad, (((1,), (1,)), ((), ())), preferred_element_type=F32
                )
                d_scores = (probs * (d_probs - delta)).astype(BF16)
                both = jnp.concatenate([d_scores, probs.astype(BF16)], axis=1)
                acc[pl.ds(2 * t, 2)] += jnp.dot(both, qd_cat, preferred_element_type=F32).reshape(
                    2, rows, LANES
                )
                d_queries = d_queries + jnp.dot(
                    turned[t, :HD], d_scores, preferred_element_type=F32
                )
            return d_queries

        d_queries = lax.fori_loop(t_first, t_stop, backward, jnp.zeros((HD, tile), F32))
        packed = jnp.concatenate([context, d_queries * unit], axis=0).T.reshape(2, rows, LANES)
        cq_full[pl.ds(2 * u, 2)] = packed
        cq_ref[pl.ds(2 * u, 2)] = packed.astype(BF16)
        return carry

    lax.fori_loop(0, slots // 2, queries, 0)
    scale = jnp.where(low_lanes((1, LANES)), unit, 1.0)
    head = lax.broadcasted_iota(jnp.int32, (8, LANES), 0) < 4

    def edge(ref, offset, before, after):
        before = offset + jnp.clip(before, 0, slots - 1)
        after = offset + jnp.clip(after, 0, slots - 1)
        return jnp.where(head, ref[after, pl.ds(0, 8)], ref[before, pl.ds(rows - 8, 8)])

    for s in range(key_slots):
        dkv_mine[s] = acc_mine[s] * scale
        acc_other[s] = acc_other[s] * scale
        send_ref[s, pl.ds(0, rows)] = acc_other[s].astype(BF16)
        if s < pre:
            send_ref[s, pl.ds(rows, 16)] = jnp.zeros((16, LANES), BF16)
    for s in range(slots):
        edge_mine[s] = edge(acc_other, pre, s - 1 + parity, s + parity)
        sent = [edge(r, o, s - parity, s + 1 - parity) for r, o in ((dkv_mine, pre), (cq_full, 0))]
        send_ref[pre + s, pl.ds(rows, 16)] = jnp.concatenate(sent).astype(BF16)


def attention_call(lengths, where, kv_mine, kv_other, qd, pre):
    slots = qd.shape[0]
    key_slots, rows, _ = kv_mine.shape
    tile = 2 * rows
    tiles = key_slots // 2
    reach = MAXLEN // (4 * rows) + 1
    smem = pl.BlockSpec(memory_space=pltpu.SMEM)
    vmem = pl.BlockSpec(memory_space=pltpu.VMEM)
    return pl.pallas_call(
        functools.partial(attention_kernel, pre),
        in_specs=[smem, smem, vmem, vmem, vmem],
        out_specs=[vmem, vmem, vmem, vmem],
        out_shape=[
            jax.ShapeDtypeStruct((slots, rows, LANES), BF16),
            jax.ShapeDtypeStruct((key_slots, rows, LANES), F32),
            jax.ShapeDtypeStruct((slots, 8, LANES), F32),
            jax.ShapeDtypeStruct((key_slots, rows + 16, LANES), BF16),
        ],
        scratch_shapes=[
            pltpu.VMEM((tiles, LANES, tile), BF16),
            pltpu.VMEM((tiles, LANES, tile), BF16),
            pltpu.VMEM((reach, 2, tile, tile), F32),
            pltpu.VMEM((key_slots, rows, LANES), F32),
            pltpu.VMEM((slots, rows, LANES), F32),
        ],
        compiler_params=params(VMEM_SOME),
        cost_estimate=pl.CostEstimate(
            flops=10 * slots * rows * MAXLEN * LANES,
            bytes_accessed=20 * slots * rows * LANES,
            transcendentals=slots * rows * MAXLEN,
        ),
        name="attention",
    )(lengths, where, kv_mine, kv_other, qd)


def combine_kernel(cq_ref, mine_ref, edge_ref, got_ref, out_ref):
    slots, rows, _ = cq_ref.shape
    for s in range(slots):
        out_ref[s, pl.ds(0, rows)] = cq_ref[s]
        got = got_ref[s].astype(F32)
        out_ref[s, pl.ds(rows, rows)] = (mine_ref[s] + got[:rows]).astype(BF16)
        edges = [edge_ref[s] + got[rows : rows + 8], got[rows + 8 :]]
        out_ref[s, pl.ds(2 * rows, 16)] = jnp.concatenate(edges).astype(BF16)


def combine_call(cq, mine, edge, got):
    slots, rows, _ = cq.shape
    vmem = pl.BlockSpec(memory_space=pltpu.VMEM)
    return pl.pallas_call(
        combine_kernel,
        in_specs=[vmem] * 4,
        out_specs=vmem,
        out_shape=jax.ShapeDtypeStruct((slots, 2 * rows + 16, LANES), BF16),
        compiler_params=params(VMEM_SOME),
        name="combine",
    )(cq, mine, edge, got)


def combine_windows(cq, mine, got, pre, side, window, devices):
    slots, rows, _ = cq.shape
    dkv = mine + got[:, :rows].astype(F32)
    back = [(i + window, i) for i in range(devices - window)]
    earlier = lax.ppermute(dkv[:pre].astype(BF16), AXES, back).astype(F32)
    dkv = dkv[pre:].at[slots - pre :].add(earlier).astype(BF16)
    both = jnp.concatenate([cq, dkv], axis=2)
    tails, heads = both[:, rows - 8 :], both[:, :8]
    swapped = [(i, i ^ 1) for i in range(devices)]
    tails_other = lax.ppermute(tails, AXES, swapped)
    heads_other = lax.ppermute(heads, AXES, swapped)
    last = [(i, i + window - 1) for i in range(1, devices - window, 2)]
    tail_past = lax.ppermute(tails[-1:], AXES, last)
    head_next = lax.ppermute(heads[:1], AXES, [(j, i) for i, j in last])
    before = jnp.where(
        side == 0, jnp.concatenate([tail_past, tails_other[:-1]]), tails_other
    )
    after = jnp.where(side == 0, heads_other, jnp.concatenate([heads_other[1:], head_next]))
    edge = jnp.where(jnp.arange(8)[None, :, None] < 4, after, before)
    return jnp.concatenate([cq, dkv, edge[..., LANES:], edge[..., :LANES]], axis=1)


def back_kernel(
    lengths_ref, where_ref, r_ref, taps_ref, w_ref, wo_ref,
    attended_ref, grad_ref, context, grads, padded,
):
    heads = r_ref.shape[0]
    rows = context.shape[0]
    width = heads * HD
    blk = grad_ref.shape[1]

    @pl.when(pl.program_id(0) == 0)
    def _():
        for pair in range(heads // 2):
            lanes = pl.ds(pair * LANES, LANES)
            x, y = (r_ref[2 * pair + i].astype(F32) for i in range(2))
            main, dkv, edge_dkv, edge_cq = (
                (slice(0, rows)), slice(rows, 2 * rows),
                slice(2 * rows, 2 * rows + 8), slice(2 * rows + 8, 2 * rows + 16),
            )
            context[:, lanes] = zip_low(x[main], y[main]).astype(BF16)
            pad = jnp.zeros((8, LANES), F32)

            def gather(mix, part, edge):
                return jnp.concatenate(
                    [mix(x[part], y[part]), mix(x[edge], y[edge]), pad]
                ).astype(BF16)

            grads[:, lanes] = gather(zip_high, main, edge_cq)
            grads[:, pl.ds(width + pair * LANES, LANES)] = gather(zip_low, dkv, edge_dkv)
            grads[:, pl.ds(2 * width + pair * LANES, LANES)] = gather(zip_high, dkv, edge_dkv)

    attended_ref[...] = jnp.dot(context[...], wo_ref[...], preferred_element_type=F32).astype(BF16)
    mixed = lax.dot_general(
        grads[...], w_ref[...], (((1,), (1,)), ((), ())), preferred_element_type=F32
    ).astype(BF16).astype(F32)
    edge = mixed[rows : rows + 8]
    padded[pl.ds(0, 8), :] = edge
    padded[pl.ds(8, rows), :] = mixed[:rows]
    padded[pl.ds(8 + rows, 8), :] = edge
    grad_ref[...] = conv_rows(
        padded, range(blk // LANES), taps_ref, lengths_ref, where_ref[0], rows, True
    ).astype(BF16)


def back_call(lengths, where, r, taps, w_qkv, w_out):
    heads = r.shape[0]
    rows = (r.shape[1] - 16) // 2
    width = heads * HD
    blk = 256
    smem = pl.BlockSpec(memory_space=pltpu.SMEM)
    out = pl.BlockSpec((rows, blk), lambda i: (0, i))
    shape = jax.ShapeDtypeStruct((rows, width), BF16)
    return pl.pallas_call(
        back_kernel,
        grid=(width // blk,),
        in_specs=[
            smem, smem,
            pl.BlockSpec(r.shape, lambda i: (0, 0, 0)),
            pl.BlockSpec((KS, blk), lambda i: (0, i)),
            pl.BlockSpec((blk, 3 * width), lambda i: (i, 0)),
            pl.BlockSpec((width, blk), lambda i: (0, i)),
        ],
        out_specs=[out, out],
        out_shape=[shape, shape],
        scratch_shapes=[
            pltpu.VMEM((rows, width), BF16),
            pltpu.VMEM((rows + 16, 3 * width), BF16),
            pltpu.VMEM((rows + 16, blk), F32),
        ],
        compiler_params=params(VMEM_FEW),
        cost_estimate=pl.CostEstimate(
            flops=8 * rows * width * width, bytes_accessed=8 * width * width, transcendentals=0
        ),
        name="back",
    )(lengths, where, r, taps, w_qkv, w_out)


def on_device(tokens, conv_kernel, w_qkv, w_out, lengths, cotangent):
    rows, width = tokens.shape
    heads = width // HD
    devices = lax.axis_size(AXES)
    window = 2 * heads
    windows = devices // window
    pre = MAXLEN // (2 * rows) if windows > 1 else 0
    me = lax.axis_index(AXES)
    where = jnp.stack([me * rows, me // window * (window * rows), me % 2]).astype(jnp.int32)
    same_side = [
        [w * window + 2 * c + side for c in range(heads)]
        for w in range(windows)
        for side in range(2)
    ]
    swapped = [(i, i ^ 1) for i in range(devices)]
    up = [(i, i + 1) for i in range(devices - 1)]
    down = [(i + 1, i) for i in range(devices - 1)]

    def exchange(x):
        return lax.all_to_all(
            x, AXES, split_axis=0, concat_axis=0, axis_index_groups=same_side, tiled=True
        )

    before = lax.ppermute(tokens[rows - EDGE :], AXES, up)
    after = lax.ppermute(tokens[:EDGE], AXES, down)
    sent = front_call(lengths, where, before, tokens, after, conv_kernel, w_qkv, cotangent, w_out)
    qd = exchange(sent)
    kv_mine = qd[:, :rows]
    if pre:
        shift = [(i, i + window) for i in range(devices - window)]
        kv_mine = jnp.concatenate([lax.ppermute(kv_mine[heads - pre :], AXES, shift), kv_mine])
    kv_other = lax.ppermute(kv_mine, AXES, swapped)
    cq, mine, edge, send = attention_call(lengths, where, kv_mine, kv_other, qd, pre)
    got = lax.ppermute(send, AXES, swapped)
    if pre:
        grads = combine_windows(cq, mine, got, pre, me % 2, window, devices)
    else:
        grads = combine_call(cq, mine, edge, got)
    return back_call(lengths, where, exchange(grads), conv_kernel, w_qkv, w_out)


def solution(mesh):
    placed = (P(AXES, None), P(), P(), P(), P(), P(AXES, None))
    return jax.shard_map(
        on_device,
        mesh=mesh,
        in_specs=placed,
        out_specs=(P(AXES, None), P(AXES, None)),
        check_vma=False,
    )
```

```python
import functools
import math

import jax
import jax.numpy as jnp
from jax import lax
from jax.experimental import pallas as pl
from jax.experimental.pallas import tpu as pltpu
from jax.sharding import PartitionSpec as P

HD = 64
KS = 7
HALF = KS // 2
MAXLEN = 2048
AXES = ("ctx", "head")
LANES = 128
EDGE = 16
PER_STEP = 2
VMEM_ALL = 60 * 1024 * 1024
VMEM_MOST = 44 * 1024 * 1024
VMEM_SOME = 24 * 1024 * 1024
VMEM_FEW = 16 * 1024 * 1024
F32 = jnp.float32
BF16 = jnp.bfloat16


def params(limit):
    return pltpu.CompilerParams(vmem_limit_bytes=limit)


def record_span(positions, lengths_ref):
    start = jnp.zeros_like(positions)
    stop = jnp.full_like(positions, jnp.iinfo(jnp.int32).max)
    end = jnp.int32(0)
    for i in range(lengths_ref.shape[0]):
        end = end + lengths_ref[i]
        past = end <= positions
        start = jnp.where(past, end, start)
        stop = jnp.where(past, stop, jnp.minimum(stop, end))
    return start, stop


def low_lanes(shape):
    return lax.broadcasted_iota(jnp.int32, shape, len(shape) - 1) % LANES < HD


def swap_halves(x):
    return pltpu.roll(x, HD, x.ndim - 1)


def zip_low(x, y):
    return jnp.where(low_lanes(x.shape), x, swap_halves(y))


def zip_high(x, y):
    return jnp.where(low_lanes(x.shape), swap_halves(x), y)


def conv_rows(padded_ref, cols, kernel_ref, lengths_ref, first_row, rows, flip):
    pos = first_row + lax.broadcasted_iota(jnp.int32, (rows, LANES), 0)
    start, stop = record_span(pos, lengths_ref)
    masks = []
    for t in range(KS):
        at = pos + (t - HALF)
        masks.append((at >= start) & (at < stop))
    pieces = []
    for c in cols:
        lanes = pl.ds(c * LANES, LANES)
        total = padded_ref[pl.ds(8, rows), lanes]
        for t in range(KS):
            tap = kernel_ref[KS - 1 - t if flip else t, lanes]
            shifted = padded_ref[pl.ds(8 - HALF + t, rows), lanes]
            total = total + jnp.where(masks[t], shifted, 0.0) * tap[None, :]
        pieces.append(total)
    return jnp.concatenate(pieces, axis=1)


def front_kernel(
    lengths_ref, where_ref, before_ref, x_ref, after_ref, taps_ref, w_ref, cot_ref, wo_ref,
    out_ref, padded, projected, d_rows,
):
    rows, blk = x_ref.shape
    step = pl.program_id(0)
    steps = pl.num_programs(0)
    padded[pl.ds(0, 8), :] = before_ref[...].astype(F32)[EDGE - 8 :]
    padded[pl.ds(8, rows), :] = x_ref[...].astype(F32)
    padded[pl.ds(8 + rows, 8), :] = after_ref[...].astype(F32)[:8]
    mixed = conv_rows(
        padded, range(blk // LANES), taps_ref, lengths_ref, where_ref[0], rows, False
    ).astype(BF16)
    d_rows[step] = lax.dot_general(
        cot_ref[...], wo_ref[...], (((1,), (1,)), ((), ())), preferred_element_type=F32
    )
    part = jnp.dot(mixed, w_ref[...], preferred_element_type=F32)

    @pl.when(step == 0)
    def _():
        projected[...] = part

    @pl.when(step > 0)
    def _():
        projected[...] += part

    @pl.when(step == steps - 1)
    def _():
        width = projected.shape[1] // 3
        per = blk // LANES
        for pair in range(width // LANES):
            q, k, v = (projected[:, pl.ds(i * width + pair * LANES, LANES)] for i in range(3))
            d = d_rows[pair // per, :, pl.ds(pair % per * LANES, LANES)]
            out_ref[2 * pair] = jnp.concatenate([zip_low(k, v), zip_low(q, d)]).astype(BF16)
            out_ref[2 * pair + 1] = jnp.concatenate([zip_high(k, v), zip_high(q, d)]).astype(BF16)


def front_call(lengths, where, before, x, after, taps, w_qkv, cotangent, w_out):
    rows, width = x.shape
    heads = width // HD
    blk = 256
    smem = pl.BlockSpec(memory_space=pltpu.SMEM)
    columns = lambda a: pl.BlockSpec((a.shape[0], blk), lambda i: (0, i))
    return pl.pallas_call(
        front_kernel,
        grid=(width // blk,),
        in_specs=[
            smem, smem, columns(before), columns(x), columns(after), columns(taps),
            pl.BlockSpec((blk, 3 * width), lambda i: (i, 0)),
            pl.BlockSpec((rows, width), lambda i: (0, 0)),
            pl.BlockSpec((blk, width), lambda i: (i, 0)),
        ],
        out_specs=pl.BlockSpec((heads, 2 * rows, LANES), lambda i: (0, 0, 0)),
        out_shape=jax.ShapeDtypeStruct((heads, 2 * rows, LANES), BF16),
        scratch_shapes=[
            pltpu.VMEM((rows + 16, blk), F32),
            pltpu.VMEM((rows, 3 * width), F32),
            pltpu.VMEM((width // blk, rows, blk), F32),
        ],
        compiler_params=params(VMEM_ALL),
        cost_estimate=pl.CostEstimate(
            flops=8 * rows * width * width, bytes_accessed=8 * width * width, transcendentals=0
        ),
        name="front",
    )(lengths, where, before, x, after, taps, w_qkv, cotangent, w_out)


def attention_kernel(
    pre, place, lengths_ref, where_ref, kv_mine, kv_other, qd_ref,
    cq_ref, dkv_mine, edge_mine, send_ref,
    visit_q, visit_k, keys_ref, turned_ref, qd_cat_ref, d_turned_ref, span_ref, e_ref,
    total_ref, context_ref, row_ref, d_query_ref, acc_ref, cq_full,
):
    slots = qd_ref.shape[0]
    key_slots, rows, _ = kv_mine.shape
    tile = 2 * rows
    tiles, groups = key_slots // 2, slots // 2
    base, parity = where_ref[1], where_ref[2]
    origin = base - pre * tile
    unit = HD**-0.5
    to_exp2 = unit * math.log2(math.e)

    lane = lax.broadcasted_iota(jnp.int32, (1, tile), 1)
    lane_pos = (lane // rows) * tile + lane % rows
    sub = lax.broadcasted_iota(jnp.int32, (2 * tile, 1), 0)
    side = jnp.where(sub < tile, parity, 1 - parity)
    sub_pos = (sub // rows % 2) * tile + sub % rows + side * rows

    count = jnp.int32(0)
    for u in range(groups):
        first = base + u * (2 * tile) + parity * rows
        begin, end = jnp.int32(0), jnp.int32(0)
        for i in range(lengths_ref.shape[0]):
            end = end + lengths_ref[i]
            begin = jnp.where(end <= first, end, begin)
        t_first = jnp.maximum(begin - origin, 0) // (2 * tile)

        def note(t, count, u=u):
            visit_q[count] = u
            visit_k[count] = t
            return count + 1

        count = lax.fori_loop(t_first, u + pre // 2 + 1, note, count)
    visit_q[count] = groups
    visit_k[count] = tiles

    for t in range(tiles):
        for half, source in enumerate((kv_mine, kv_other)):
            block = jnp.concatenate([source[place(2 * t + i)] for i in range(2)])
            keys_ref[t, pl.ds(half * tile, tile)] = block
            turned_ref[t, :, pl.ds(half * tile, tile)] = block.T
    keys_ref[tiles] = jnp.zeros_like(keys_ref[tiles])
    turned_ref[tiles] = jnp.zeros_like(turned_ref[tiles])
    acc_ref[...] = jnp.zeros_like(acc_ref)
    total_ref[...] = jnp.zeros_like(total_ref)
    context_ref[...] = jnp.zeros_like(context_ref)
    d_query_ref[...] = jnp.zeros_like(d_query_ref)
    for u in range(groups):
        qd = jnp.concatenate(
            [qd_ref[place(2 * u + i), pl.ds(rows, rows)] for i in range(2)]
        ).astype(F32)
        low = low_lanes(qd.shape)
        qd_cat_ref[u, pl.ds(0, tile)] = jnp.where(low, qd, 0.0).astype(BF16)
        qd_cat_ref[u, pl.ds(tile, tile)] = jnp.where(low, 0.0, qd).astype(BF16)
        d_turned_ref[u] = qd.T[HD:]
        q_pos = base + u * (2 * tile) + parity * rows + lane_pos
        q_start, _ = record_span(q_pos, lengths_ref)
        span_ref[u, pl.ds(0, 1)] = q_start
        span_ref[u, pl.ds(1, 1)] = q_pos
    qd_cat_ref[groups] = jnp.zeros_like(qd_cat_ref[groups])
    span_ref[groups] = jnp.zeros_like(span_ref[groups])
    row_ref[groups] = jnp.zeros_like(row_ref[groups])

    def forward(i):
        u, t = visit_q[i], visit_k[i]
        scores = lax.dot_general(
            keys_ref[t], qd_cat_ref[u, pl.ds(0, tile)], (((1,), (1,)), ((), ())),
            preferred_element_type=F32,
        )
        k_pos = origin + t * (2 * tile) + sub_pos
        span = span_ref[u]
        allowed = (k_pos >= span[0:1]) & (k_pos <= span[1:2])
        e = jnp.where(allowed, jnp.exp2(scores * to_exp2), 0.0)
        e_ref[i] = e
        context = jnp.dot(turned_ref[t, HD:], e.astype(BF16), preferred_element_type=F32)
        return u, jnp.sum(e.reshape(2 * tile // 8, 8, tile), axis=0), context

    def forward_some(j, carry):
        for u, total, context in [forward(PER_STEP * j + i) for i in range(PER_STEP)]:
            total_ref[u] += total
            context_ref[u] += context
        return carry

    steps = (count + PER_STEP - 1) // PER_STEP
    lax.fori_loop(0, steps, forward_some, 0)
    for u in range(groups):
        inverse = 1.0 / jnp.sum(total_ref[u], axis=0, keepdims=True)
        context = (context_ref[u] * inverse).astype(BF16).astype(F32)
        context_ref[u] = context
        row_ref[u, pl.ds(0, 1)] = inverse
        row_ref[u, pl.ds(1, 1)] = jnp.sum(d_turned_ref[u] * context, axis=0, keepdims=True)

    def backward(i):
        u, t = visit_q[i], visit_k[i]
        row = row_ref[u]
        probs = e_ref[i] * row[0:1]
        d_probs = lax.dot_general(
            keys_ref[t], qd_cat_ref[u, pl.ds(tile, tile)], (((1,), (1,)), ((), ())),
            preferred_element_type=F32,
        )
        d_scores = (probs * (d_probs - row[1:2])).astype(BF16)
        both = jnp.concatenate([d_scores, probs.astype(BF16)], axis=1)
        d_keys = jnp.dot(both, qd_cat_ref[u], preferred_element_type=F32)
        d_queries = jnp.dot(turned_ref[t, :HD], d_scores, preferred_element_type=F32)
        return u, t, d_keys, d_queries

    def backward_some(j, carry):
        for u, t, d_keys, d_queries in [backward(PER_STEP * j + i) for i in range(PER_STEP)]:
            acc_ref[t] += d_keys
            d_query_ref[u] += d_queries
        return carry

    lax.fori_loop(0, steps, backward_some, 0)
    for u in range(groups):
        packed = jnp.concatenate([context_ref[u], d_query_ref[u] * unit], axis=0).T
        for i in range(2):
            part = packed[i * rows : (i + 1) * rows]
            cq_full[2 * u + i] = part
            cq_ref[2 * u + i] = part.astype(BF16)
    scale = jnp.where(low_lanes((1, LANES)), unit, 1.0)
    head = lax.broadcasted_iota(jnp.int32, (8, LANES), 0) < 4

    def end_rows(half, slot, first):
        slot = pre + jnp.clip(slot, 0, slots - 1)
        at = half * tile + slot % 2 * rows + first
        return acc_ref[slot // 2, pl.ds(pl.multiple_of(at, 8), 8)] * scale

    for s in range(key_slots):
        part = pl.ds(s % 2 * rows, rows)
        dkv_mine[s] = acc_ref[s // 2, part] * scale
        part = pl.ds(tile + s % 2 * rows, rows)
        send_ref[s, pl.ds(0, rows)] = (acc_ref[s // 2, part] * scale).astype(BF16)
        if s < pre:
            send_ref[s, pl.ds(rows, 16)] = jnp.zeros((16, LANES), BF16)
    for s in range(slots):
        edge_mine[s] = jnp.where(
            head, end_rows(1, s + parity, 0), end_rows(1, s - 1 + parity, rows - 8)
        )
        past, later = s - parity, s + 1 - parity
        d_edge = jnp.where(head, end_rows(0, later, 0), end_rows(0, past, rows - 8))
        q_edge = jnp.where(
            head,
            cq_full[jnp.clip(later, 0, slots - 1), pl.ds(0, 8)],
            cq_full[jnp.clip(past, 0, slots - 1), pl.ds(rows - 8, 8)],
        )
        send_ref[pre + s, pl.ds(rows, 16)] = jnp.concatenate([d_edge, q_edge]).astype(BF16)


def attention_call(lengths, where, kv_mine, kv_other, qd, pre):
    slots = qd.shape[0]
    key_slots, rows, _ = kv_mine.shape
    tile = 2 * rows
    tiles, groups = key_slots // 2, slots // 2
    reach = MAXLEN // (2 * tile) + 1
    visits = sum(min(u + pre // 2 + 1, reach) for u in range(groups)) + PER_STEP - 1
    smem = pl.BlockSpec(memory_space=pltpu.SMEM)
    vmem = pl.BlockSpec(memory_space=pltpu.VMEM)
    return pl.pallas_call(
        functools.partial(attention_kernel, pre, lambda s: s),
        in_specs=[smem, smem, vmem, vmem, vmem],
        out_specs=[vmem, vmem, vmem, vmem],
        out_shape=[
            jax.ShapeDtypeStruct((slots, rows, LANES), BF16),
            jax.ShapeDtypeStruct((key_slots, rows, LANES), F32),
            jax.ShapeDtypeStruct((slots, 8, LANES), F32),
            jax.ShapeDtypeStruct((key_slots, rows + 16, LANES), BF16),
        ],
        scratch_shapes=[
            pltpu.SMEM((visits + 1,), jnp.int32),
            pltpu.SMEM((visits + 1,), jnp.int32),
            pltpu.VMEM((tiles + 1, 2 * tile, LANES), BF16),
            pltpu.VMEM((tiles + 1, LANES, 2 * tile), BF16),
            pltpu.VMEM((groups + 1, 2 * tile, LANES), BF16),
            pltpu.VMEM((groups, HD, tile), F32),
            pltpu.VMEM((groups + 1, 8, tile), jnp.int32),
            pltpu.VMEM((visits, 2 * tile, tile), F32),
            pltpu.VMEM((groups + 1, 8, tile), F32),
            pltpu.VMEM((groups + 1, HD, tile), F32),
            pltpu.VMEM((groups + 1, 8, tile), F32),
            pltpu.VMEM((groups + 1, HD, tile), F32),
            pltpu.VMEM((tiles + 1, 2 * tile, LANES), F32),
            pltpu.VMEM((slots, rows, LANES), F32),
        ],
        compiler_params=params(VMEM_MOST),
        cost_estimate=pl.CostEstimate(
            flops=10 * slots * rows * MAXLEN * LANES,
            bytes_accessed=20 * slots * rows * LANES,
            transcendentals=slots * rows * MAXLEN,
        ),
        name="attention",
    )(lengths, where, kv_mine, kv_other, qd)


def combine_kernel(cq_ref, mine_ref, edge_ref, got_ref, out_ref):
    slots, rows, _ = cq_ref.shape
    for s in range(slots):
        out_ref[s, pl.ds(0, rows)] = cq_ref[s]
        got = got_ref[s].astype(F32)
        out_ref[s, pl.ds(rows, rows)] = (mine_ref[s] + got[:rows]).astype(BF16)
        edges = [edge_ref[s] + got[rows : rows + 8], got[rows + 8 :]]
        out_ref[s, pl.ds(2 * rows, 16)] = jnp.concatenate(edges).astype(BF16)


def combine_call(cq, mine, edge, got):
    slots, rows, _ = cq.shape
    vmem = pl.BlockSpec(memory_space=pltpu.VMEM)
    return pl.pallas_call(
        combine_kernel,
        in_specs=[vmem] * 4,
        out_specs=vmem,
        out_shape=jax.ShapeDtypeStruct((slots, 2 * rows + 16, LANES), BF16),
        compiler_params=params(VMEM_SOME),
        name="combine",
    )(cq, mine, edge, got)


def combine_windows(cq, mine, got, pre, side, window, devices):
    slots, rows, _ = cq.shape
    dkv = mine + got[:, :rows].astype(F32)
    back = [(i + window, i) for i in range(devices - window)]
    earlier = lax.ppermute(dkv[:pre].astype(BF16), AXES, back).astype(F32)
    dkv = dkv[pre:].at[slots - pre :].add(earlier).astype(BF16)
    both = jnp.concatenate([cq, dkv], axis=2)
    tails, heads = both[:, rows - 8 :], both[:, :8]
    swapped = [(i, i ^ 1) for i in range(devices)]
    tails_other = lax.ppermute(tails, AXES, swapped)
    heads_other = lax.ppermute(heads, AXES, swapped)
    last = [(i, i + window - 1) for i in range(1, devices - window, 2)]
    tail_past = lax.ppermute(tails[-1:], AXES, last)
    head_next = lax.ppermute(heads[:1], AXES, [(j, i) for i, j in last])
    before = jnp.where(
        side == 0, jnp.concatenate([tail_past, tails_other[:-1]]), tails_other
    )
    after = jnp.where(side == 0, heads_other, jnp.concatenate([heads_other[1:], head_next]))
    edge = jnp.where(jnp.arange(8)[None, :, None] < 4, after, before)
    return jnp.concatenate([cq, dkv, edge[..., LANES:], edge[..., :LANES]], axis=1)


def back_kernel(
    lengths_ref, where_ref, r_ref, taps_ref, w_ref, wo_ref,
    attended_ref, grad_ref, context, grads, padded,
):
    heads = r_ref.shape[0]
    rows = context.shape[0]
    width = heads * HD
    blk = grad_ref.shape[1]

    @pl.when(pl.program_id(0) == 0)
    def _():
        for pair in range(heads // 2):
            lanes = pl.ds(pair * LANES, LANES)
            x, y = (r_ref[2 * pair + i].astype(F32) for i in range(2))
            main, dkv, edge_dkv, edge_cq = (
                (slice(0, rows)), slice(rows, 2 * rows),
                slice(2 * rows, 2 * rows + 8), slice(2 * rows + 8, 2 * rows + 16),
            )
            context[:, lanes] = zip_low(x[main], y[main]).astype(BF16)
            pad = jnp.zeros((8, LANES), F32)

            def gather(mix, part, edge):
                return jnp.concatenate(
                    [mix(x[part], y[part]), mix(x[edge], y[edge]), pad]
                ).astype(BF16)

            grads[:, lanes] = gather(zip_high, main, edge_cq)
            grads[:, pl.ds(width + pair * LANES, LANES)] = gather(zip_low, dkv, edge_dkv)
            grads[:, pl.ds(2 * width + pair * LANES, LANES)] = gather(zip_high, dkv, edge_dkv)

    attended_ref[...] = jnp.dot(context[...], wo_ref[...], preferred_element_type=F32).astype(BF16)
    mixed = lax.dot_general(
        grads[...], w_ref[...], (((1,), (1,)), ((), ())), preferred_element_type=F32
    ).astype(BF16).astype(F32)
    edge = mixed[rows : rows + 8]
    padded[pl.ds(0, 8), :] = edge
    padded[pl.ds(8, rows), :] = mixed[:rows]
    padded[pl.ds(8 + rows, 8), :] = edge
    grad_ref[...] = conv_rows(
        padded, range(blk // LANES), taps_ref, lengths_ref, where_ref[0], rows, True
    ).astype(BF16)


def back_call(lengths, where, r, taps, w_qkv, w_out):
    heads = r.shape[0]
    rows = (r.shape[1] - 16) // 2
    width = heads * HD
    blk = 256
    smem = pl.BlockSpec(memory_space=pltpu.SMEM)
    out = pl.BlockSpec((rows, blk), lambda i: (0, i))
    shape = jax.ShapeDtypeStruct((rows, width), BF16)
    return pl.pallas_call(
        back_kernel,
        grid=(width // blk,),
        in_specs=[
            smem, smem,
            pl.BlockSpec(r.shape, lambda i: (0, 0, 0)),
            pl.BlockSpec((KS, blk), lambda i: (0, i)),
            pl.BlockSpec((blk, 3 * width), lambda i: (i, 0)),
            pl.BlockSpec((width, blk), lambda i: (0, i)),
        ],
        out_specs=[out, out],
        out_shape=[shape, shape],
        scratch_shapes=[
            pltpu.VMEM((rows, width), BF16),
            pltpu.VMEM((rows + 16, 3 * width), BF16),
            pltpu.VMEM((rows + 16, blk), F32),
        ],
        compiler_params=params(VMEM_FEW),
        cost_estimate=pl.CostEstimate(
            flops=8 * rows * width * width, bytes_accessed=8 * width * width, transcendentals=0
        ),
        name="back",
    )(lengths, where, r, taps, w_qkv, w_out)


def on_device(tokens, conv_kernel, w_qkv, w_out, lengths, cotangent):
    rows, width = tokens.shape
    heads = width // HD
    devices = lax.axis_size(AXES)
    window = 2 * heads
    windows = devices // window
    pre = MAXLEN // (2 * rows) if windows > 1 else 0
    me = lax.axis_index(AXES)
    where = jnp.stack([me * rows, me // window * (window * rows), me % 2]).astype(jnp.int32)
    same_side = [
        [w * window + 2 * c + side for c in range(heads)]
        for w in range(windows)
        for side in range(2)
    ]
    swapped = [(i, i ^ 1) for i in range(devices)]
    up = [(i, i + 1) for i in range(devices - 1)]
    down = [(i + 1, i) for i in range(devices - 1)]

    def exchange(x):
        return lax.all_to_all(
            x, AXES, split_axis=0, concat_axis=0, axis_index_groups=same_side, tiled=True
        )

    before = lax.ppermute(tokens[rows - EDGE :], AXES, up)
    after = lax.ppermute(tokens[:EDGE], AXES, down)
    sent = front_call(lengths, where, before, tokens, after, conv_kernel, w_qkv, cotangent, w_out)
    qd = exchange(sent)
    kv_mine = qd[:, :rows]
    if pre:
        shift = [(i, i + window) for i in range(devices - window)]
        kv_mine = jnp.concatenate([lax.ppermute(kv_mine[heads - pre :], AXES, shift), kv_mine])
    kv_other = lax.ppermute(kv_mine, AXES, swapped)
    cq, mine, edge, send = attention_call(lengths, where, kv_mine, kv_other, qd, pre)
    got = lax.ppermute(send, AXES, swapped)
    if pre:
        grads = combine_windows(cq, mine, got, pre, me % 2, window, devices)
    else:
        grads = combine_call(cq, mine, edge, got)
    return back_call(lengths, where, exchange(grads), conv_kernel, w_qkv, w_out)


def solution(mesh):
    placed = (P(AXES, None), P(), P(), P(), P(), P(AXES, None))
    return jax.shard_map(
        on_device,
        mesh=mesh,
        in_specs=placed,
        out_specs=(P(AXES, None), P(AXES, None)),
        check_vma=False,
    )
```

```python
import functools
import math

import jax
import jax.numpy as jnp
from jax import lax
from jax.experimental import pallas as pl
from jax.experimental.pallas import tpu as pltpu
from jax.sharding import PartitionSpec as P

HD = 64
KS = 7
HALF = KS // 2
MAXLEN = 2048
AXES = ("ctx", "head")
LANES = 128
EDGE = 16
PER_STEP = 2
VMEM_ALL = 60 * 1024 * 1024
VMEM_MOST = 44 * 1024 * 1024
VMEM_SOME = 24 * 1024 * 1024
VMEM_FEW = 16 * 1024 * 1024
F32 = jnp.float32
BF16 = jnp.bfloat16


def params(limit):
    return pltpu.CompilerParams(vmem_limit_bytes=limit)


def record_span(positions, lengths_ref):
    start = jnp.zeros_like(positions)
    stop = jnp.full_like(positions, jnp.iinfo(jnp.int32).max)
    end = jnp.int32(0)
    for i in range(lengths_ref.shape[0]):
        end = end + lengths_ref[i]
        past = end <= positions
        start = jnp.where(past, end, start)
        stop = jnp.where(past, stop, jnp.minimum(stop, end))
    return start, stop


def low_lanes(shape):
    return lax.broadcasted_iota(jnp.int32, shape, len(shape) - 1) % LANES < HD


def swap_halves(x):
    return pltpu.roll(x, HD, x.ndim - 1)


def zip_low(x, y):
    return jnp.where(low_lanes(x.shape), x, swap_halves(y))


def zip_high(x, y):
    return jnp.where(low_lanes(x.shape), swap_halves(x), y)


def conv_rows(padded_ref, cols, kernel_ref, lengths_ref, first_row, rows, flip):
    pos = first_row + lax.broadcasted_iota(jnp.int32, (rows, LANES), 0)
    start, stop = record_span(pos, lengths_ref)
    masks = []
    for t in range(KS):
        at = pos + (t - HALF)
        masks.append((at >= start) & (at < stop))
    pieces = []
    for c in cols:
        lanes = pl.ds(c * LANES, LANES)
        total = padded_ref[pl.ds(8, rows), lanes]
        for t in range(KS):
            tap = kernel_ref[KS - 1 - t if flip else t, lanes]
            shifted = padded_ref[pl.ds(8 - HALF + t, rows), lanes]
            total = total + jnp.where(masks[t], shifted, 0.0) * tap[None, :]
        pieces.append(total)
    return jnp.concatenate(pieces, axis=1)


def front_kernel(
    lengths_ref, where_ref, before_ref, x_ref, after_ref, taps_ref, w_ref, cot_ref, wo_ref,
    out_ref, padded, projected, d_rows,
):
    rows, blk = x_ref.shape
    step = pl.program_id(0)
    steps = pl.num_programs(0)
    padded[pl.ds(0, 8), :] = before_ref[...].astype(F32)[EDGE - 8 :]
    padded[pl.ds(8, rows), :] = x_ref[...].astype(F32)
    padded[pl.ds(8 + rows, 8), :] = after_ref[...].astype(F32)[:8]
    mixed = conv_rows(
        padded, range(blk // LANES), taps_ref, lengths_ref, where_ref[0], rows, False
    ).astype(BF16)
    d_rows[step] = lax.dot_general(
        cot_ref[...], wo_ref[...], (((1,), (1,)), ((), ())), preferred_element_type=F32
    )
    part = jnp.dot(mixed, w_ref[...], preferred_element_type=F32)

    @pl.when(step == 0)
    def _():
        projected[...] = part

    @pl.when(step > 0)
    def _():
        projected[...] += part

    @pl.when(step == steps - 1)
    def _():
        width = projected.shape[1] // 3
        per = blk // LANES
        for pair in range(width // LANES):
            q, k, v = (projected[:, pl.ds(i * width + pair * LANES, LANES)] for i in range(3))
            d = d_rows[pair // per, :, pl.ds(pair % per * LANES, LANES)]
            out_ref[2 * pair] = jnp.concatenate([zip_low(k, v), zip_low(q, d)]).astype(BF16)
            out_ref[2 * pair + 1] = jnp.concatenate([zip_high(k, v), zip_high(q, d)]).astype(BF16)


def front_call(lengths, where, before, x, after, taps, w_qkv, cotangent, w_out):
    rows, width = x.shape
    heads = width // HD
    blk = 256
    smem = pl.BlockSpec(memory_space=pltpu.SMEM)
    columns = lambda a: pl.BlockSpec((a.shape[0], blk), lambda i: (0, i))
    return pl.pallas_call(
        front_kernel,
        grid=(width // blk,),
        in_specs=[
            smem, smem, columns(before), columns(x), columns(after), columns(taps),
            pl.BlockSpec((blk, 3 * width), lambda i: (i, 0)),
            pl.BlockSpec((rows, width), lambda i: (0, 0)),
            pl.BlockSpec((blk, width), lambda i: (i, 0)),
        ],
        out_specs=pl.BlockSpec((heads, 2 * rows, LANES), lambda i: (0, 0, 0)),
        out_shape=jax.ShapeDtypeStruct((heads, 2 * rows, LANES), BF16),
        scratch_shapes=[
            pltpu.VMEM((rows + 16, blk), F32),
            pltpu.VMEM((rows, 3 * width), F32),
            pltpu.VMEM((width // blk, rows, blk), F32),
        ],
        compiler_params=params(VMEM_ALL),
        cost_estimate=pl.CostEstimate(
            flops=8 * rows * width * width, bytes_accessed=8 * width * width, transcendentals=0
        ),
        name="front",
    )(lengths, where, before, x, after, taps, w_qkv, cotangent, w_out)


def attention_kernel(
    pre, place, lengths_ref, where_ref, kv_mine, kv_other, qd_ref,
    cq_ref, dkv_mine, edge_mine, send_ref,
    visit_q, visit_k, keys_ref, turned_ref, qd_cat_ref, d_turned_ref, span_ref, e_ref,
    total_ref, context_ref, row_ref, d_query_ref, acc_ref, cq_full,
):
    slots = qd_ref.shape[0]
    key_slots, rows, _ = kv_mine.shape
    tile = 2 * rows
    tiles, groups = key_slots // 2, slots // 2
    base, parity = where_ref[1], where_ref[2]
    origin = base - pre * tile
    unit = HD**-0.5
    to_exp2 = unit * math.log2(math.e)

    lane = lax.broadcasted_iota(jnp.int32, (1, tile), 1)
    lane_pos = (lane // rows) * tile + lane % rows
    sub = lax.broadcasted_iota(jnp.int32, (2 * tile, 1), 0)
    side = jnp.where(sub < tile, parity, 1 - parity)
    sub_pos = (sub // rows % 2) * tile + sub % rows + side * rows

    count = jnp.int32(0)
    for u in range(groups):
        first = base + u * (2 * tile) + parity * rows
        begin, end = jnp.int32(0), jnp.int32(0)
        for i in range(lengths_ref.shape[0]):
            end = end + lengths_ref[i]
            begin = jnp.where(end <= first, end, begin)
        t_first = jnp.maximum(begin - origin, 0) // (2 * tile)

        def note(t, count, u=u):
            visit_q[count] = u
            visit_k[count] = t
            return count + 1

        count = lax.fori_loop(t_first, u + pre // 2 + 1, note, count)
    visit_q[count] = groups
    visit_k[count] = tiles

    for t in range(tiles):
        for half, source in enumerate((kv_mine, kv_other)):
            block = jnp.concatenate([source[place(2 * t + i, pre)] for i in range(2)])
            keys_ref[t, pl.ds(half * tile, tile)] = block
            turned_ref[t, :, pl.ds(half * tile, tile)] = block.T
    keys_ref[tiles] = jnp.zeros_like(keys_ref[tiles])
    turned_ref[tiles] = jnp.zeros_like(turned_ref[tiles])
    acc_ref[...] = jnp.zeros_like(acc_ref)
    total_ref[...] = jnp.zeros_like(total_ref)
    context_ref[...] = jnp.zeros_like(context_ref)
    d_query_ref[...] = jnp.zeros_like(d_query_ref)
    for u in range(groups):
        qd = jnp.concatenate(
            [qd_ref[place(2 * u + i, 0), pl.ds(rows, rows)] for i in range(2)]
        ).astype(F32)
        low = low_lanes(qd.shape)
        qd_cat_ref[u, pl.ds(0, tile)] = jnp.where(low, qd, 0.0).astype(BF16)
        qd_cat_ref[u, pl.ds(tile, tile)] = jnp.where(low, 0.0, qd).astype(BF16)
        d_turned_ref[u] = qd.T[HD:]
        q_pos = base + u * (2 * tile) + parity * rows + lane_pos
        q_start, _ = record_span(q_pos, lengths_ref)
        span_ref[u, pl.ds(0, 1)] = q_start
        span_ref[u, pl.ds(1, 1)] = q_pos
    qd_cat_ref[groups] = jnp.zeros_like(qd_cat_ref[groups])
    span_ref[groups] = jnp.zeros_like(span_ref[groups])
    row_ref[groups] = jnp.zeros_like(row_ref[groups])

    def forward(i):
        u, t = visit_q[i], visit_k[i]
        scores = lax.dot_general(
            keys_ref[t], qd_cat_ref[u, pl.ds(0, tile)], (((1,), (1,)), ((), ())),
            preferred_element_type=F32,
        )
        k_pos = origin + t * (2 * tile) + sub_pos
        span = span_ref[u]
        allowed = (k_pos >= span[0:1]) & (k_pos <= span[1:2])
        e = jnp.where(allowed, jnp.exp2(scores * to_exp2), 0.0)
        e_ref[i] = e
        context = jnp.dot(turned_ref[t, HD:], e.astype(BF16), preferred_element_type=F32)
        return u, jnp.sum(e.reshape(2 * tile // 8, 8, tile), axis=0), context

    def forward_some(j, carry):
        for u, total, context in [forward(PER_STEP * j + i) for i in range(PER_STEP)]:
            total_ref[u] += total
            context_ref[u] += context
        return carry

    steps = (count + PER_STEP - 1) // PER_STEP
    lax.fori_loop(0, steps, forward_some, 0)
    for u in range(groups):
        inverse = 1.0 / jnp.sum(total_ref[u], axis=0, keepdims=True)
        context = (context_ref[u] * inverse).astype(BF16).astype(F32)
        context_ref[u] = context
        row_ref[u, pl.ds(0, 1)] = inverse
        row_ref[u, pl.ds(1, 1)] = jnp.sum(d_turned_ref[u] * context, axis=0, keepdims=True)

    def backward(i):
        u, t = visit_q[i], visit_k[i]
        row = row_ref[u]
        probs = e_ref[i] * row[0:1]
        d_probs = lax.dot_general(
            keys_ref[t], qd_cat_ref[u, pl.ds(tile, tile)], (((1,), (1,)), ((), ())),
            preferred_element_type=F32,
        )
        d_scores = (probs * (d_probs - row[1:2])).astype(BF16)
        both = jnp.concatenate([d_scores, probs.astype(BF16)], axis=1)
        d_keys = jnp.dot(both, qd_cat_ref[u], preferred_element_type=F32)
        d_queries = jnp.dot(turned_ref[t, :HD], d_scores, preferred_element_type=F32)
        return u, t, d_keys, d_queries

    def backward_some(j, carry):
        for u, t, d_keys, d_queries in [backward(PER_STEP * j + i) for i in range(PER_STEP)]:
            acc_ref[t] += d_keys
            d_query_ref[u] += d_queries
        return carry

    lax.fori_loop(0, steps, backward_some, 0)
    for u in range(groups):
        packed = jnp.concatenate([context_ref[u], d_query_ref[u] * unit], axis=0).T
        for i in range(2):
            part = packed[i * rows : (i + 1) * rows]
            cq_full[2 * u + i] = part
            cq_ref[2 * u + i] = part.astype(BF16)
    scale = jnp.where(low_lanes((1, LANES)), unit, 1.0)
    head = lax.broadcasted_iota(jnp.int32, (8, LANES), 0) < 4

    def end_rows(half, slot, first):
        slot = pre + jnp.clip(slot, 0, slots - 1)
        at = half * tile + slot % 2 * rows + first
        return acc_ref[slot // 2, pl.ds(pl.multiple_of(at, 8), 8)] * scale

    for s in range(key_slots):
        part = pl.ds(s % 2 * rows, rows)
        dkv_mine[s] = acc_ref[s // 2, part] * scale
        part = pl.ds(tile + s % 2 * rows, rows)
        send_ref[s, pl.ds(0, rows)] = (acc_ref[s // 2, part] * scale).astype(BF16)
        if s < pre:
            send_ref[s, pl.ds(rows, 16)] = jnp.zeros((16, LANES), BF16)
    for s in range(slots):
        edge_mine[s] = jnp.where(
            head, end_rows(1, s + parity, 0), end_rows(1, s - 1 + parity, rows - 8)
        )
        past, later = s - parity, s + 1 - parity
        d_edge = jnp.where(head, end_rows(0, later, 0), end_rows(0, past, rows - 8))
        q_edge = jnp.where(
            head,
            cq_full[jnp.clip(later, 0, slots - 1), pl.ds(0, 8)],
            cq_full[jnp.clip(past, 0, slots - 1), pl.ds(rows - 8, 8)],
        )
        send_ref[pre + s, pl.ds(rows, 16)] = jnp.concatenate([d_edge, q_edge]).astype(BF16)


def attention_call(lengths, where, kv_mine, kv_other, qd, pre):
    slots = qd.shape[0]
    key_slots, rows, _ = kv_mine.shape
    tile = 2 * rows
    tiles, groups = key_slots // 2, slots // 2
    reach = MAXLEN // (2 * tile) + 1
    place = lambda s, ordered: s if ordered else bit_reversed(s, slots)
    visits = sum(min(u + pre // 2 + 1, reach) for u in range(groups)) + PER_STEP - 1
    smem = pl.BlockSpec(memory_space=pltpu.SMEM)
    vmem = pl.BlockSpec(memory_space=pltpu.VMEM)
    return pl.pallas_call(
        functools.partial(attention_kernel, pre, place),
        in_specs=[smem, smem, vmem, vmem, vmem],
        out_specs=[vmem, vmem, vmem, vmem],
        out_shape=[
            jax.ShapeDtypeStruct((slots, rows, LANES), BF16),
            jax.ShapeDtypeStruct((key_slots, rows, LANES), F32),
            jax.ShapeDtypeStruct((slots, 8, LANES), F32),
            jax.ShapeDtypeStruct((key_slots, rows + 16, LANES), BF16),
        ],
        scratch_shapes=[
            pltpu.SMEM((visits + 1,), jnp.int32),
            pltpu.SMEM((visits + 1,), jnp.int32),
            pltpu.VMEM((tiles + 1, 2 * tile, LANES), BF16),
            pltpu.VMEM((tiles + 1, LANES, 2 * tile), BF16),
            pltpu.VMEM((groups + 1, 2 * tile, LANES), BF16),
            pltpu.VMEM((groups, HD, tile), F32),
            pltpu.VMEM((groups + 1, 8, tile), jnp.int32),
            pltpu.VMEM((visits, 2 * tile, tile), F32),
            pltpu.VMEM((groups + 1, 8, tile), F32),
            pltpu.VMEM((groups + 1, HD, tile), F32),
            pltpu.VMEM((groups + 1, 8, tile), F32),
            pltpu.VMEM((groups + 1, HD, tile), F32),
            pltpu.VMEM((tiles + 1, 2 * tile, LANES), F32),
            pltpu.VMEM((slots, rows, LANES), F32),
        ],
        compiler_params=params(VMEM_MOST),
        cost_estimate=pl.CostEstimate(
            flops=10 * slots * rows * MAXLEN * LANES,
            bytes_accessed=20 * slots * rows * LANES,
            transcendentals=slots * rows * MAXLEN,
        ),
        name="attention",
    )(lengths, where, kv_mine, kv_other, qd)


def combine_kernel(cq_ref, mine_ref, edge_ref, got_ref, out_ref):
    slots, rows, _ = cq_ref.shape
    for s in range(slots):
        at = bit_reversed(s, slots)
        out_ref[at, pl.ds(0, rows)] = cq_ref[s]
        got = got_ref[s].astype(F32)
        out_ref[at, pl.ds(rows, rows)] = (mine_ref[s] + got[:rows]).astype(BF16)
        edges = [edge_ref[s] + got[rows : rows + 8], got[rows + 8 :]]
        out_ref[at, pl.ds(2 * rows, 16)] = jnp.concatenate(edges).astype(BF16)


def combine_call(cq, mine, edge, got):
    slots, rows, _ = cq.shape
    vmem = pl.BlockSpec(memory_space=pltpu.VMEM)
    return pl.pallas_call(
        combine_kernel,
        in_specs=[vmem] * 4,
        out_specs=vmem,
        out_shape=jax.ShapeDtypeStruct((slots, 2 * rows + 16, LANES), BF16),
        compiler_params=params(VMEM_SOME),
        name="combine",
    )(cq, mine, edge, got)


def combine_windows(cq, mine, got, pre, side, window, devices):
    slots, rows, _ = cq.shape
    dkv = mine + got[:, :rows].astype(F32)
    back = [(i + window, i) for i in range(devices - window)]
    earlier = lax.ppermute(dkv[:pre].astype(BF16), AXES, back).astype(F32)
    dkv = dkv[pre:].at[slots - pre :].add(earlier).astype(BF16)
    both = jnp.concatenate([cq, dkv], axis=2)
    tails, heads = both[:, rows - 8 :], both[:, :8]
    swapped = [(i, i ^ 1) for i in range(devices)]
    tails_other = lax.ppermute(tails, AXES, swapped)
    heads_other = lax.ppermute(heads, AXES, swapped)
    last = [(i, i + window - 1) for i in range(1, devices - window, 2)]
    tail_past = lax.ppermute(tails[-1:], AXES, last)
    head_next = lax.ppermute(heads[:1], AXES, [(j, i) for i, j in last])
    before = jnp.where(
        side == 0, jnp.concatenate([tail_past, tails_other[:-1]]), tails_other
    )
    after = jnp.where(side == 0, heads_other, jnp.concatenate([heads_other[1:], head_next]))
    edge = jnp.where(jnp.arange(8)[None, :, None] < 4, after, before)
    grads = jnp.concatenate([cq, dkv, edge[..., LANES:], edge[..., :LANES]], axis=1)
    return jnp.stack([grads[bit_reversed(s, slots)] for s in range(slots)])


def back_kernel(
    lengths_ref, where_ref, r_ref, taps_ref, w_ref, wo_ref,
    attended_ref, grad_ref, context, grads, padded,
):
    heads = r_ref.shape[0]
    rows = context.shape[0]
    width = heads * HD
    blk = grad_ref.shape[1]

    @pl.when(pl.program_id(0) == 0)
    def _():
        for pair in range(heads // 2):
            lanes = pl.ds(pair * LANES, LANES)
            x, y = (r_ref[2 * pair + i].astype(F32) for i in range(2))
            main, dkv, edge_dkv, edge_cq = (
                (slice(0, rows)), slice(rows, 2 * rows),
                slice(2 * rows, 2 * rows + 8), slice(2 * rows + 8, 2 * rows + 16),
            )
            context[:, lanes] = zip_low(x[main], y[main]).astype(BF16)
            pad = jnp.zeros((8, LANES), F32)

            def gather(mix, part, edge):
                return jnp.concatenate(
                    [mix(x[part], y[part]), mix(x[edge], y[edge]), pad]
                ).astype(BF16)

            grads[:, lanes] = gather(zip_high, main, edge_cq)
            grads[:, pl.ds(width + pair * LANES, LANES)] = gather(zip_low, dkv, edge_dkv)
            grads[:, pl.ds(2 * width + pair * LANES, LANES)] = gather(zip_high, dkv, edge_dkv)

    attended_ref[...] = jnp.dot(context[...], wo_ref[...], preferred_element_type=F32).astype(BF16)
    mixed = lax.dot_general(
        grads[...], w_ref[...], (((1,), (1,)), ((), ())), preferred_element_type=F32
    ).astype(BF16).astype(F32)
    edge = mixed[rows : rows + 8]
    padded[pl.ds(0, 8), :] = edge
    padded[pl.ds(8, rows), :] = mixed[:rows]
    padded[pl.ds(8 + rows, 8), :] = edge
    grad_ref[...] = conv_rows(
        padded, range(blk // LANES), taps_ref, lengths_ref, where_ref[0], rows, True
    ).astype(BF16)


def back_call(lengths, where, r, taps, w_qkv, w_out):
    heads = r.shape[0]
    rows = (r.shape[1] - 16) // 2
    width = heads * HD
    blk = 256
    smem = pl.BlockSpec(memory_space=pltpu.SMEM)
    out = pl.BlockSpec((rows, blk), lambda i: (0, i))
    shape = jax.ShapeDtypeStruct((rows, width), BF16)
    return pl.pallas_call(
        back_kernel,
        grid=(width // blk,),
        in_specs=[
            smem, smem,
            pl.BlockSpec(r.shape, lambda i: (0, 0, 0)),
            pl.BlockSpec((KS, blk), lambda i: (0, i)),
            pl.BlockSpec((blk, 3 * width), lambda i: (i, 0)),
            pl.BlockSpec((width, blk), lambda i: (0, i)),
        ],
        out_specs=[out, out],
        out_shape=[shape, shape],
        scratch_shapes=[
            pltpu.VMEM((rows, width), BF16),
            pltpu.VMEM((rows + 16, 3 * width), BF16),
            pltpu.VMEM((rows + 16, blk), F32),
        ],
        compiler_params=params(VMEM_FEW),
        cost_estimate=pl.CostEstimate(
            flops=8 * rows * width * width, bytes_accessed=8 * width * width, transcendentals=0
        ),
        name="back",
    )(lengths, where, r, taps, w_qkv, w_out)


def bit_reversed(i, count):
    bits = count.bit_length() - 1
    if count != 1 << bits:
        return i
    return sum((i >> b & 1) << (bits - 1 - b) for b in range(bits))


def on_device(tokens, conv_kernel, w_qkv, w_out, lengths, cotangent):
    rows, width = tokens.shape
    heads = width // HD
    devices = lax.axis_size(AXES)
    window = 2 * heads
    windows = devices // window
    pre = MAXLEN // (2 * rows) if windows > 1 else 0
    me = lax.axis_index(AXES)
    where = jnp.stack([me * rows, me // window * (window * rows), me % 2]).astype(jnp.int32)
    same_side = [
        [w * window + 2 * bit_reversed(c, heads) + side for c in range(heads)]
        for w in range(windows)
        for side in range(2)
    ]
    swapped = [(i, i ^ 1) for i in range(devices)]
    up = [(i, i + 1) for i in range(devices - 1)]
    down = [(i + 1, i) for i in range(devices - 1)]

    def exchange(x):
        return lax.all_to_all(
            x, AXES, split_axis=0, concat_axis=0, axis_index_groups=same_side, tiled=True
        )

    before = lax.ppermute(tokens[rows - EDGE :], AXES, up)
    after = lax.ppermute(tokens[:EDGE], AXES, down)
    sent = front_call(lengths, where, before, tokens, after, conv_kernel, w_qkv, cotangent, w_out)
    qd = exchange(sent)
    kv_mine = qd[:, :rows]
    if pre:
        shift = [(i, i + window) for i in range(devices - window)]
        kv_mine = jnp.stack([kv_mine[bit_reversed(s, heads)] for s in range(heads)])
        kv_mine = jnp.concatenate([lax.ppermute(kv_mine[heads - pre :], AXES, shift), kv_mine])
    kv_other = lax.ppermute(kv_mine, AXES, swapped)
    cq, mine, edge, send = attention_call(lengths, where, kv_mine, kv_other, qd, pre)
    got = lax.ppermute(send, AXES, swapped)
    if pre:
        grads = combine_windows(cq, mine, got, pre, me % 2, window, devices)
    else:
        grads = combine_call(cq, mine, edge, got)
    return back_call(lengths, where, exchange(grads), conv_kernel, w_qkv, w_out)


def solution(mesh):
    placed = (P(AXES, None), P(), P(), P(), P(), P(AXES, None))
    return jax.shard_map(
        on_device,
        mesh=mesh,
        in_specs=placed,
        out_specs=(P(AXES, None), P(AXES, None)),
        check_vma=False,
    )
```

```python
import functools
import math

import jax
import jax.numpy as jnp
from jax import lax
from jax.experimental import pallas as pl
from jax.experimental.pallas import tpu as pltpu
from jax.sharding import PartitionSpec as P

HD = 64
KS = 7
HALF = KS // 2
MAXLEN = 2048
AXES = ("ctx", "head")
LANES = 128
EDGE = 16
PER_STEP = 4
VMEM_ALL = 60 * 1024 * 1024
VMEM_MOST = 44 * 1024 * 1024
VMEM_SOME = 24 * 1024 * 1024
VMEM_FEW = 16 * 1024 * 1024
F32 = jnp.float32
BF16 = jnp.bfloat16


def params(limit):
    return pltpu.CompilerParams(vmem_limit_bytes=limit)


def record_span(positions, lengths_ref):
    start = jnp.zeros_like(positions)
    stop = jnp.full_like(positions, jnp.iinfo(jnp.int32).max)
    end = jnp.int32(0)
    for i in range(lengths_ref.shape[0]):
        end = end + lengths_ref[i]
        past = end <= positions
        start = jnp.where(past, end, start)
        stop = jnp.where(past, stop, jnp.minimum(stop, end))
    return start, stop


def device_index():
    return lax.axis_index("ctx") * lax.axis_size("head") + lax.axis_index("head")


def low_lanes(shape):
    return lax.broadcasted_iota(jnp.int32, shape, len(shape) - 1) % LANES < HD


def swap_halves(x):
    return pltpu.roll(x, HD, x.ndim - 1)


def zip_low(x, y):
    return jnp.where(low_lanes(x.shape), x, swap_halves(y))


def zip_high(x, y):
    return jnp.where(low_lanes(x.shape), swap_halves(x), y)


def conv_rows(padded_ref, cols, kernel_ref, lengths_ref, first_row, rows, flip):
    pos = first_row + lax.broadcasted_iota(jnp.int32, (rows, LANES), 0)
    start, stop = record_span(pos, lengths_ref)
    masks = []
    for t in range(KS):
        at = pos + (t - HALF)
        masks.append((at >= start) & (at < stop))
    pieces = []
    for c in cols:
        lanes = pl.ds(c * LANES, LANES)
        total = padded_ref[pl.ds(8, rows), lanes]
        for t in range(KS):
            tap = kernel_ref[KS - 1 - t if flip else t, lanes]
            shifted = padded_ref[pl.ds(8 - HALF + t, rows), lanes]
            total = total + jnp.where(masks[t], shifted, 0.0) * tap[None, :]
        pieces.append(total)
    return jnp.concatenate(pieces, axis=1)


def front_kernel(
    lengths_ref, before_ref, x_ref, after_ref, taps_ref, w_ref, cot_ref, wo_ref,
    out_ref, padded, projected, d_rows,
):
    rows, blk = x_ref.shape
    step = pl.program_id(0)
    steps = pl.num_programs(0)
    padded[pl.ds(0, 8), :] = before_ref[...].astype(F32)[EDGE - 8 :]
    padded[pl.ds(8, rows), :] = x_ref[...].astype(F32)
    padded[pl.ds(8 + rows, 8), :] = after_ref[...].astype(F32)[:8]
    mixed = conv_rows(
        padded, range(blk // LANES), taps_ref, lengths_ref, device_index() * rows, rows, False
    ).astype(BF16)
    d_rows[step] = lax.dot_general(
        cot_ref[...], wo_ref[...], (((1,), (1,)), ((), ())), preferred_element_type=F32
    )
    part = jnp.dot(mixed, w_ref[...], preferred_element_type=F32)

    @pl.when(step == 0)
    def _():
        projected[...] = part

    @pl.when(step > 0)
    def _():
        projected[...] += part

    @pl.when(step == steps - 1)
    def _():
        width = projected.shape[1] // 3
        per = blk // LANES
        for pair in range(width // LANES):
            q, k, v = (projected[:, pl.ds(i * width + pair * LANES, LANES)] for i in range(3))
            d = d_rows[pair // per, :, pl.ds(pair % per * LANES, LANES)]
            out_ref[2 * pair] = jnp.concatenate([zip_low(k, v), zip_low(q, d)]).astype(BF16)
            out_ref[2 * pair + 1] = jnp.concatenate([zip_high(k, v), zip_high(q, d)]).astype(BF16)


def front_call(lengths, before, x, after, taps, w_qkv, cotangent, w_out):
    rows, width = x.shape
    heads = width // HD
    blk = 256
    smem = pl.BlockSpec(memory_space=pltpu.SMEM)
    columns = lambda a: pl.BlockSpec((a.shape[0], blk), lambda i: (0, i))
    return pl.pallas_call(
        front_kernel,
        grid=(width // blk,),
        in_specs=[
            smem, columns(before), columns(x), columns(after), columns(taps),
            pl.BlockSpec((blk, 3 * width), lambda i: (i, 0)),
            pl.BlockSpec((rows, width), lambda i: (0, 0)),
            pl.BlockSpec((blk, width), lambda i: (i, 0)),
        ],
        out_specs=pl.BlockSpec((heads, 2 * rows, LANES), lambda i: (0, 0, 0)),
        out_shape=jax.ShapeDtypeStruct((heads, 2 * rows, LANES), BF16),
        scratch_shapes=[
            pltpu.VMEM((rows + 16, blk), F32),
            pltpu.VMEM((rows, 3 * width), F32),
            pltpu.VMEM((width // blk, rows, blk), F32),
        ],
        compiler_params=params(VMEM_ALL),
        cost_estimate=pl.CostEstimate(
            flops=8 * rows * width * width, bytes_accessed=8 * width * width, transcendentals=0
        ),
        name="front",
    )(lengths, before, x, after, taps, w_qkv, cotangent, w_out)


def attention_kernel(
    pre, place, lengths_ref, kv_mine, kv_other, qd_ref,
    cq_ref, dkv_mine, edge_mine, send_ref,
    visit_q, visit_k, keys_ref, turned_ref, qd_cat_ref, d_turned_ref, span_ref, e_ref,
    total_ref, context_ref, row_ref, d_query_ref, acc_ref, cq_full,
):
    slots = qd_ref.shape[0]
    key_slots, rows, _ = kv_mine.shape
    tile = 2 * rows
    tiles, groups = key_slots // 2, slots // 2
    me = device_index()
    window = 2 * slots
    base, parity = me // window * (window * rows), me % 2
    origin = base - pre * tile
    unit = HD**-0.5
    to_exp2 = unit * math.log2(math.e)

    lane = lax.broadcasted_iota(jnp.int32, (1, tile), 1)
    lane_pos = (lane // rows) * tile + lane % rows
    sub = lax.broadcasted_iota(jnp.int32, (2 * tile, 1), 0)
    side = jnp.where(sub < tile, parity, 1 - parity)
    sub_pos = (sub // rows % 2) * tile + sub % rows + side * rows

    count = jnp.int32(0)
    for u in range(groups):
        first = base + u * (2 * tile) + parity * rows
        begin, end = jnp.int32(0), jnp.int32(0)
        for i in range(lengths_ref.shape[0]):
            end = end + lengths_ref[i]
            begin = jnp.where(end <= first, end, begin)
        t_first = jnp.maximum(begin - origin, 0) // (2 * tile)

        def note(t, count, u=u):
            visit_q[count] = u
            visit_k[count] = t
            return count + 1

        count = lax.fori_loop(t_first, u + pre // 2 + 1, note, count)
    for i in range(PER_STEP - 1):
        visit_q[count + i] = groups
        visit_k[count + i] = tiles

    for t in range(tiles):
        for half, source in enumerate((kv_mine, kv_other)):
            block = jnp.concatenate([source[place(2 * t + i, pre)] for i in range(2)])
            keys_ref[t, pl.ds(half * tile, tile)] = block
            turned_ref[t, :, pl.ds(half * tile, tile)] = block.T
    keys_ref[tiles] = jnp.zeros_like(keys_ref[tiles])
    turned_ref[tiles] = jnp.zeros_like(turned_ref[tiles])
    acc_ref[...] = jnp.zeros_like(acc_ref)
    total_ref[...] = jnp.zeros_like(total_ref)
    context_ref[...] = jnp.zeros_like(context_ref)
    d_query_ref[...] = jnp.zeros_like(d_query_ref)
    for u in range(groups):
        qd = jnp.concatenate(
            [qd_ref[place(2 * u + i, 0), pl.ds(rows, rows)] for i in range(2)]
        )
        d_turned_ref[u] = qd.T[HD:].astype(F32)
        qd = qd.astype(F32)
        low = low_lanes(qd.shape)
        qd_cat_ref[u, pl.ds(0, tile)] = jnp.where(low, qd, 0.0).astype(BF16)
        qd_cat_ref[u, pl.ds(tile, tile)] = jnp.where(low, 0.0, qd).astype(BF16)
        q_pos = base + u * (2 * tile) + parity * rows + lane_pos
        q_start, _ = record_span(q_pos, lengths_ref)
        span_ref[u, pl.ds(0, 1)] = q_start
        span_ref[u, pl.ds(1, 1)] = q_pos
    qd_cat_ref[groups] = jnp.zeros_like(qd_cat_ref[groups])
    span_ref[groups] = jnp.zeros_like(span_ref[groups])
    row_ref[groups] = jnp.zeros_like(row_ref[groups])

    def forward(i):
        u, t = visit_q[i], visit_k[i]
        scores = lax.dot_general(
            keys_ref[t], qd_cat_ref[u, pl.ds(0, tile)], (((1,), (1,)), ((), ())),
            preferred_element_type=F32,
        )
        k_pos = origin + t * (2 * tile) + sub_pos
        span = span_ref[u]
        allowed = (k_pos >= span[0:1]) & (k_pos <= span[1:2])
        e = jnp.where(allowed, jnp.exp2(scores * to_exp2), 0.0)
        e_ref[i] = e
        context = jnp.dot(turned_ref[t, HD:], e.astype(BF16), preferred_element_type=F32)
        return u, jnp.sum(e.reshape(2 * tile // 8, 8, tile), axis=0), context

    def forward_some(j, carry):
        for u, total, context in [forward(PER_STEP * j + i) for i in range(PER_STEP)]:
            total_ref[u] += total
            context_ref[u] += context
        return carry

    steps = (count + PER_STEP - 1) // PER_STEP
    lax.fori_loop(0, steps, forward_some, 0)
    for u in range(groups):
        inverse = 1.0 / jnp.sum(total_ref[u], axis=0, keepdims=True)
        context = (context_ref[u] * inverse).astype(BF16).astype(F32)
        context_ref[u] = context
        row_ref[u, pl.ds(0, 1)] = inverse
        row_ref[u, pl.ds(1, 1)] = jnp.sum(d_turned_ref[u] * context, axis=0, keepdims=True)

    def backward(i):
        u, t = visit_q[i], visit_k[i]
        row = row_ref[u]
        probs = e_ref[i] * row[0:1]
        d_probs = lax.dot_general(
            keys_ref[t], qd_cat_ref[u, pl.ds(tile, tile)], (((1,), (1,)), ((), ())),
            preferred_element_type=F32,
        )
        d_scores = (probs * (d_probs - row[1:2])).astype(BF16)
        both = jnp.concatenate([d_scores, probs.astype(BF16)], axis=1)
        d_keys = jnp.dot(both, qd_cat_ref[u], preferred_element_type=F32)
        d_queries = jnp.dot(turned_ref[t, :HD], d_scores, preferred_element_type=F32)
        return u, t, d_keys, d_queries

    def backward_some(j, carry):
        for u, t, d_keys, d_queries in [backward(PER_STEP * j + i) for i in range(PER_STEP)]:
            acc_ref[t] += d_keys
            d_query_ref[u] += d_queries
        return carry

    lax.fori_loop(0, steps, backward_some, 0)
    for u in range(groups):
        packed = jnp.concatenate([context_ref[u], d_query_ref[u] * unit], axis=0).T
        for i in range(2):
            part = packed[i * rows : (i + 1) * rows]
            cq_full[2 * u + i] = part
            cq_ref[2 * u + i] = part.astype(BF16)
    scale = jnp.where(low_lanes((1, LANES)), unit, 1.0)
    head = lax.broadcasted_iota(jnp.int32, (8, LANES), 0) < 4

    def end_rows(half, slot, first):
        slot = pre + jnp.clip(slot, 0, slots - 1)
        at = half * tile + slot % 2 * rows + first
        return acc_ref[slot // 2, pl.ds(pl.multiple_of(at, 8), 8)] * scale

    for s in range(key_slots):
        part = pl.ds(s % 2 * rows, rows)
        dkv_mine[s] = acc_ref[s // 2, part] * scale
        part = pl.ds(tile + s % 2 * rows, rows)
        send_ref[s, pl.ds(0, rows)] = (acc_ref[s // 2, part] * scale).astype(BF16)
        if s < pre:
            send_ref[s, pl.ds(rows, 16)] = jnp.zeros((16, LANES), BF16)
    for s in range(slots):
        edge_mine[s] = jnp.where(
            head, end_rows(1, s + parity, 0), end_rows(1, s - 1 + parity, rows - 8)
        )
        past, later = s - parity, s + 1 - parity
        d_edge = jnp.where(head, end_rows(0, later, 0), end_rows(0, past, rows - 8))
        q_edge = jnp.where(
            head,
            cq_full[jnp.clip(later, 0, slots - 1), pl.ds(0, 8)],
            cq_full[jnp.clip(past, 0, slots - 1), pl.ds(rows - 8, 8)],
        )
        send_ref[pre + s, pl.ds(rows, 16)] = jnp.concatenate([d_edge, q_edge]).astype(BF16)


def attention_call(lengths, kv_mine, kv_other, qd, pre):
    slots = qd.shape[0]
    key_slots, rows, _ = kv_mine.shape
    tile = 2 * rows
    tiles, groups = key_slots // 2, slots // 2
    reach = MAXLEN // (2 * tile) + 1
    place = lambda s, ordered: s if ordered else bit_reversed(s, slots)
    visits = sum(min(u + pre // 2 + 1, reach) for u in range(groups)) + PER_STEP - 1
    smem = pl.BlockSpec(memory_space=pltpu.SMEM)
    vmem = pl.BlockSpec(memory_space=pltpu.VMEM)
    return pl.pallas_call(
        functools.partial(attention_kernel, pre, place),
        in_specs=[smem, vmem, vmem, vmem],
        out_specs=[vmem, vmem, vmem, vmem],
        out_shape=[
            jax.ShapeDtypeStruct((slots, rows, LANES), BF16),
            jax.ShapeDtypeStruct((key_slots, rows, LANES), F32),
            jax.ShapeDtypeStruct((slots, 8, LANES), F32),
            jax.ShapeDtypeStruct((key_slots, rows + 16, LANES), BF16),
        ],
        scratch_shapes=[
            pltpu.SMEM((visits,), jnp.int32),
            pltpu.SMEM((visits,), jnp.int32),
            pltpu.VMEM((tiles + 1, 2 * tile, LANES), BF16),
            pltpu.VMEM((tiles + 1, LANES, 2 * tile), BF16),
            pltpu.VMEM((groups + 1, 2 * tile, LANES), BF16),
            pltpu.VMEM((groups, HD, tile), F32),
            pltpu.VMEM((groups + 1, 8, tile), jnp.int32),
            pltpu.VMEM((visits, 2 * tile, tile), F32),
            pltpu.VMEM((groups + 1, 8, tile), F32),
            pltpu.VMEM((groups + 1, HD, tile), F32),
            pltpu.VMEM((groups + 1, 8, tile), F32),
            pltpu.VMEM((groups + 1, HD, tile), F32),
            pltpu.VMEM((tiles + 1, 2 * tile, LANES), F32),
            pltpu.VMEM((slots, rows, LANES), F32),
        ],
        compiler_params=params(VMEM_MOST),
        cost_estimate=pl.CostEstimate(
            flops=10 * slots * rows * MAXLEN * LANES,
            bytes_accessed=20 * slots * rows * LANES,
            transcendentals=slots * rows * MAXLEN,
        ),
        name="attention",
    )(lengths, kv_mine, kv_other, qd)


def combine_kernel(cq_ref, mine_ref, edge_ref, got_ref, out_ref):
    slots, rows, _ = cq_ref.shape
    for s in range(slots):
        at = bit_reversed(s, slots)
        out_ref[at, pl.ds(0, rows)] = cq_ref[s]
        got = got_ref[s].astype(F32)
        out_ref[at, pl.ds(rows, rows)] = (mine_ref[s] + got[:rows]).astype(BF16)
        edges = [edge_ref[s] + got[rows : rows + 8], got[rows + 8 :]]
        out_ref[at, pl.ds(2 * rows, 16)] = jnp.concatenate(edges).astype(BF16)


def combine_call(cq, mine, edge, got):
    slots, rows, _ = cq.shape
    vmem = pl.BlockSpec(memory_space=pltpu.VMEM)
    return pl.pallas_call(
        combine_kernel,
        in_specs=[vmem] * 4,
        out_specs=vmem,
        out_shape=jax.ShapeDtypeStruct((slots, 2 * rows + 16, LANES), BF16),
        compiler_params=params(VMEM_SOME),
        name="combine",
    )(cq, mine, edge, got)


def combine_windows(cq, mine, got, pre, side, window, devices):
    slots, rows, _ = cq.shape
    dkv = mine + got[:, :rows].astype(F32)
    back = [(i + window, i) for i in range(devices - window)]
    earlier = lax.ppermute(dkv[:pre].astype(BF16), AXES, back).astype(F32)
    dkv = dkv[pre:].at[slots - pre :].add(earlier).astype(BF16)
    both = jnp.concatenate([cq, dkv], axis=2)
    tails, heads = both[:, rows - 8 :], both[:, :8]
    swapped = [(i, i ^ 1) for i in range(devices)]
    tails_other = lax.ppermute(tails, AXES, swapped)
    heads_other = lax.ppermute(heads, AXES, swapped)
    last = [(i, i + window - 1) for i in range(1, devices - window, 2)]
    tail_past = lax.ppermute(tails[-1:], AXES, last)
    head_next = lax.ppermute(heads[:1], AXES, [(j, i) for i, j in last])
    before = jnp.where(
        side == 0, jnp.concatenate([tail_past, tails_other[:-1]]), tails_other
    )
    after = jnp.where(side == 0, heads_other, jnp.concatenate([heads_other[1:], head_next]))
    edge = jnp.where(jnp.arange(8)[None, :, None] < 4, after, before)
    grads = jnp.concatenate([cq, dkv, edge[..., LANES:], edge[..., :LANES]], axis=1)
    return jnp.stack([grads[bit_reversed(s, slots)] for s in range(slots)])


def back_kernel(
    lengths_ref, r_ref, taps_ref, w_ref, wo_ref,
    attended_ref, grad_ref, context, grads, padded,
):
    heads = r_ref.shape[0]
    rows = context.shape[0]
    width = heads * HD
    blk = grad_ref.shape[1]

    @pl.when(pl.program_id(0) == 0)
    def _():
        for pair in range(heads // 2):
            lanes = pl.ds(pair * LANES, LANES)
            x, y = (r_ref[2 * pair + i].astype(F32) for i in range(2))
            main, dkv, edge_dkv, edge_cq = (
                (slice(0, rows)), slice(rows, 2 * rows),
                slice(2 * rows, 2 * rows + 8), slice(2 * rows + 8, 2 * rows + 16),
            )
            context[:, lanes] = zip_low(x[main], y[main]).astype(BF16)
            pad = jnp.zeros((8, LANES), F32)

            def gather(mix, part, edge):
                return jnp.concatenate(
                    [mix(x[part], y[part]), mix(x[edge], y[edge]), pad]
                ).astype(BF16)

            grads[:, lanes] = gather(zip_high, main, edge_cq)
            grads[:, pl.ds(width + pair * LANES, LANES)] = gather(zip_low, dkv, edge_dkv)
            grads[:, pl.ds(2 * width + pair * LANES, LANES)] = gather(zip_high, dkv, edge_dkv)

    attended_ref[...] = jnp.dot(context[...], wo_ref[...], preferred_element_type=F32).astype(BF16)
    mixed = lax.dot_general(
        grads[...], w_ref[...], (((1,), (1,)), ((), ())), preferred_element_type=F32
    ).astype(BF16).astype(F32)
    edge = mixed[rows : rows + 8]
    padded[pl.ds(0, 8), :] = edge
    padded[pl.ds(8, rows), :] = mixed[:rows]
    padded[pl.ds(8 + rows, 8), :] = edge
    grad_ref[...] = conv_rows(
        padded, range(blk // LANES), taps_ref, lengths_ref, device_index() * rows, rows, True
    ).astype(BF16)


def back_call(lengths, r, taps, w_qkv, w_out):
    heads = r.shape[0]
    rows = (r.shape[1] - 16) // 2
    width = heads * HD
    blk = 256
    smem = pl.BlockSpec(memory_space=pltpu.SMEM)
    out = pl.BlockSpec((rows, blk), lambda i: (0, i))
    shape = jax.ShapeDtypeStruct((rows, width), BF16)
    return pl.pallas_call(
        back_kernel,
        grid=(width // blk,),
        in_specs=[
            smem,
            pl.BlockSpec(r.shape, lambda i: (0, 0, 0)),
            pl.BlockSpec((KS, blk), lambda i: (0, i)),
            pl.BlockSpec((blk, 3 * width), lambda i: (i, 0)),
            pl.BlockSpec((width, blk), lambda i: (0, i)),
        ],
        out_specs=[out, out],
        out_shape=[shape, shape],
        scratch_shapes=[
            pltpu.VMEM((rows, width), BF16),
            pltpu.VMEM((rows + 16, 3 * width), BF16),
            pltpu.VMEM((rows + 16, blk), F32),
        ],
        compiler_params=params(VMEM_FEW),
        cost_estimate=pl.CostEstimate(
            flops=8 * rows * width * width, bytes_accessed=8 * width * width, transcendentals=0
        ),
        name="back",
    )(lengths, r, taps, w_qkv, w_out)


def bit_reversed(i, count):
    bits = count.bit_length() - 1
    if count != 1 << bits:
        return i
    return sum((i >> b & 1) << (bits - 1 - b) for b in range(bits))


def on_device(tokens, conv_kernel, w_qkv, w_out, lengths, cotangent):
    rows, width = tokens.shape
    heads = width // HD
    devices = lax.axis_size(AXES)
    window = 2 * heads
    windows = devices // window
    pre = MAXLEN // (2 * rows) if windows > 1 else 0
    me = lax.axis_index(AXES)
    same_side = [
        [w * window + 2 * bit_reversed(c, heads) + side for c in range(heads)]
        for w in range(windows)
        for side in range(2)
    ]
    swapped = [(i, i ^ 1) for i in range(devices)]
    up = [(i, i + 1) for i in range(devices - 1)]
    down = [(i + 1, i) for i in range(devices - 1)]

    def exchange(x):
        return lax.all_to_all(
            x, AXES, split_axis=0, concat_axis=0, axis_index_groups=same_side, tiled=True
        )

    before = lax.ppermute(tokens[rows - EDGE :], AXES, up)
    after = lax.ppermute(tokens[:EDGE], AXES, down)
    sent = front_call(lengths, before, tokens, after, conv_kernel, w_qkv, cotangent, w_out)
    qd = exchange(sent)
    kv_mine = qd[:, :rows]
    if pre:
        shift = [(i, i + window) for i in range(devices - window)]
        kv_mine = jnp.stack([kv_mine[bit_reversed(s, heads)] for s in range(heads)])
        kv_mine = jnp.concatenate([lax.ppermute(kv_mine[heads - pre :], AXES, shift), kv_mine])
    kv_other = lax.ppermute(kv_mine, AXES, swapped)
    cq, mine, edge, send = attention_call(lengths, kv_mine, kv_other, qd, pre)
    got = lax.ppermute(send, AXES, swapped)
    if pre:
        grads = combine_windows(cq, mine, got, pre, me % 2, window, devices)
    else:
        grads = combine_call(cq, mine, edge, got)
    return back_call(lengths, exchange(grads), conv_kernel, w_qkv, w_out)


def solution(mesh):
    placed = (P(AXES, None), P(), P(), P(), P(), P(AXES, None))
    return jax.shard_map(
        on_device,
        mesh=mesh,
        in_specs=placed,
        out_specs=(P(AXES, None), P(AXES, None)),
        check_vma=False,
    )
```

```python
import functools
import math

import jax
import jax.numpy as jnp
from jax import lax
from jax.experimental import pallas as pl
from jax.experimental.pallas import tpu as pltpu
from jax.sharding import PartitionSpec as P

HD = 64
KS = 7
HALF = KS // 2
MAXLEN = 2048
AXES = ("ctx", "head")
LANES = 128
EDGE = 16
PER_STEP = 4
FRONT_STEPS = 4
BACK_STEPS = 4
VMEM_ALL = 60 * 1024 * 1024
VMEM_MOST = 44 * 1024 * 1024
VMEM_SOME = 24 * 1024 * 1024
F32 = jnp.float32
BF16 = jnp.bfloat16


def params(limit):
    return pltpu.CompilerParams(vmem_limit_bytes=limit)


def record_span(positions, lengths_ref):
    start = jnp.zeros_like(positions)
    stop = jnp.full_like(positions, jnp.iinfo(jnp.int32).max)
    end = jnp.int32(0)
    for i in range(lengths_ref.shape[0]):
        end = end + lengths_ref[i]
        past = end <= positions
        start = jnp.where(past, end, start)
        stop = jnp.where(past, stop, jnp.minimum(stop, end))
    return start, stop


def device_index():
    return lax.axis_index("ctx") * lax.axis_size("head") + lax.axis_index("head")


def low_lanes(shape):
    return lax.broadcasted_iota(jnp.int32, shape, len(shape) - 1) % LANES < HD


def swap_halves(x):
    return pltpu.roll(x, HD, x.ndim - 1)


def zip_low(x, y):
    return jnp.where(low_lanes(x.shape), x, swap_halves(y))


def zip_high(x, y):
    return jnp.where(low_lanes(x.shape), swap_halves(x), y)


def conv_rows(padded_ref, cols, kernel_ref, lengths_ref, first_row, rows, flip):
    pos = first_row + lax.broadcasted_iota(jnp.int32, (rows, LANES), 0)
    start, stop = record_span(pos, lengths_ref)
    masks = []
    for t in range(KS):
        at = pos + (t - HALF)
        masks.append((at >= start) & (at < stop))
    pieces = []
    for c in cols:
        lanes = pl.ds(c * LANES, LANES)
        total = padded_ref[pl.ds(8, rows), lanes]
        for t in range(KS):
            tap = kernel_ref[KS - 1 - t if flip else t, lanes]
            shifted = padded_ref[pl.ds(8 - HALF + t, rows), lanes]
            total = total + jnp.where(masks[t], shifted, 0.0) * tap[None, :]
        pieces.append(total)
    return jnp.concatenate(pieces, axis=1)


def front_kernel(
    lengths_ref, before_ref, after_ref, x_hbm, taps_hbm, w_hbm, cot_hbm, wo_hbm,
    out_ref, x_ref, taps_ref, w_ref, cot_ref, wo_ref, padded, projected, d_rows, sems,
):
    rows, width = x_ref.shape
    blk = width // FRONT_STEPS

    def copy(source, target, i):
        return pltpu.make_async_copy(source, target, sems.at[i])

    whole = [
        copy(source, target, i)
        for i, (source, target) in enumerate(
            ((x_hbm, x_ref), (taps_hbm, taps_ref), (cot_hbm, cot_ref))
        )
    ]
    parts = []
    for step in range(FRONT_STEPS):
        part = pl.ds(step * blk, blk)
        at = 3 + 2 * step
        parts.append(
            (
                copy(w_hbm.at[part], w_ref.at[part], at),
                copy(wo_hbm.at[part], wo_ref.at[part], at + 1),
            )
        )
    for c in whole:
        c.start()
    for pair in parts:
        for c in pair:
            c.start()
    padded[pl.ds(0, 8), :] = before_ref[...].astype(F32)[EDGE - 8 :]
    padded[pl.ds(8 + rows, 8), :] = after_ref[...].astype(F32)[:8]
    for c in whole:
        c.wait()
    padded[pl.ds(8, rows), :] = x_ref[...].astype(F32)
    first_row = device_index() * rows
    per = blk // LANES
    for step in range(FRONT_STEPS):
        mixed = conv_rows(
            padded, range(step * per, (step + 1) * per), taps_ref, lengths_ref, first_row, rows,
            False,
        ).astype(BF16)
        parts[step][0].wait()
        part = jnp.dot(mixed, w_ref[pl.ds(step * blk, blk), :], preferred_element_type=F32)
        if step == 0:
            projected[...] = part
        else:
            projected[...] += part
        parts[step][1].wait()
        d_rows[:, pl.ds(step * blk, blk)] = lax.dot_general(
            cot_ref[...], wo_ref[pl.ds(step * blk, blk), :], (((1,), (1,)), ((), ())),
            preferred_element_type=F32,
        )
    for pair in range(width // LANES):
        lanes = pl.ds(pair * LANES, LANES)
        q, k, v = (projected[:, pl.ds(i * width + pair * LANES, LANES)] for i in range(3))
        d = d_rows[:, lanes]
        out_ref[2 * pair] = jnp.concatenate([zip_low(k, v), zip_low(q, d)]).astype(BF16)
        out_ref[2 * pair + 1] = jnp.concatenate([zip_high(k, v), zip_high(q, d)]).astype(BF16)


def front_call(lengths, before, x, after, taps, w_qkv, cotangent, w_out):
    rows, width = x.shape
    heads = width // HD
    smem = pl.BlockSpec(memory_space=pltpu.SMEM)
    vmem = pl.BlockSpec(memory_space=pltpu.VMEM)
    anywhere = pl.BlockSpec(memory_space=pl.ANY)
    return pl.pallas_call(
        front_kernel,
        in_specs=[smem, vmem, vmem] + [anywhere] * 5,
        out_specs=vmem,
        out_shape=jax.ShapeDtypeStruct((heads, 2 * rows, LANES), BF16),
        scratch_shapes=[
            pltpu.VMEM(x.shape, x.dtype),
            pltpu.VMEM(taps.shape, taps.dtype),
            pltpu.VMEM(w_qkv.shape, w_qkv.dtype),
            pltpu.VMEM(cotangent.shape, cotangent.dtype),
            pltpu.VMEM(w_out.shape, w_out.dtype),
            pltpu.VMEM((rows + 16, width), F32),
            pltpu.VMEM((rows, 3 * width), F32),
            pltpu.VMEM((rows, width), F32),
            pltpu.SemaphoreType.DMA((3 + 2 * FRONT_STEPS,)),
        ],
        compiler_params=params(VMEM_ALL),
        cost_estimate=pl.CostEstimate(
            flops=8 * rows * width * width, bytes_accessed=8 * width * width, transcendentals=0
        ),
        name="front",
    )(lengths, before, after, x, taps, w_qkv, cotangent, w_out)


def attention_kernel(
    pre, place, lengths_ref, kv_mine, kv_other, qd_ref,
    cq_ref, dkv_mine, edge_mine, send_ref,
    visit_q, visit_k, keys_ref, turned_ref, qd_cat_ref, d_turned_ref, span_ref, e_ref,
    total_ref, context_ref, row_ref, d_query_ref, acc_ref, cq_full,
):
    slots = qd_ref.shape[0]
    key_slots, rows, _ = kv_mine.shape
    tile = 2 * rows
    tiles, groups = key_slots // 2, slots // 2
    me = device_index()
    window = 2 * slots
    base, parity = me // window * (window * rows), me % 2
    origin = base - pre * tile
    unit = HD**-0.5
    to_exp2 = unit * math.log2(math.e)

    lane = lax.broadcasted_iota(jnp.int32, (1, tile), 1)
    lane_pos = (lane // rows) * tile + lane % rows
    sub = lax.broadcasted_iota(jnp.int32, (2 * tile, 1), 0)
    side = jnp.where(sub < tile, parity, 1 - parity)
    sub_pos = (sub // rows % 2) * tile + sub % rows + side * rows

    count = jnp.int32(0)
    for u in range(groups):
        first = base + u * (2 * tile) + parity * rows
        begin, end = jnp.int32(0), jnp.int32(0)
        for i in range(lengths_ref.shape[0]):
            end = end + lengths_ref[i]
            begin = jnp.where(end <= first, end, begin)
        t_first = jnp.maximum(begin - origin, 0) // (2 * tile)

        def note(t, count, u=u):
            visit_q[count] = u
            visit_k[count] = t
            return count + 1

        count = lax.fori_loop(t_first, u + pre // 2 + 1, note, count)
    for i in range(PER_STEP - 1):
        visit_q[count + i] = groups
        visit_k[count + i] = tiles

    for t in range(tiles):
        for half, source in enumerate((kv_mine, kv_other)):
            block = jnp.concatenate([source[place(2 * t + i, pre)] for i in range(2)])
            keys_ref[t, pl.ds(half * tile, tile)] = block
            turned_ref[t, :, pl.ds(half * tile, tile)] = block.T
    keys_ref[tiles] = jnp.zeros_like(keys_ref[tiles])
    turned_ref[tiles] = jnp.zeros_like(turned_ref[tiles])
    acc_ref[...] = jnp.zeros_like(acc_ref)
    total_ref[...] = jnp.zeros_like(total_ref)
    context_ref[...] = jnp.zeros_like(context_ref)
    d_query_ref[...] = jnp.zeros_like(d_query_ref)
    for u in range(groups):
        qd = jnp.concatenate(
            [qd_ref[place(2 * u + i, 0), pl.ds(rows, rows)] for i in range(2)]
        )
        d_turned_ref[u] = qd.T[HD:].astype(F32)
        qd = qd.astype(F32)
        low = low_lanes(qd.shape)
        qd_cat_ref[u, pl.ds(0, tile)] = jnp.where(low, qd, 0.0).astype(BF16)
        qd_cat_ref[u, pl.ds(tile, tile)] = jnp.where(low, 0.0, qd).astype(BF16)
        q_pos = base + u * (2 * tile) + parity * rows + lane_pos
        q_start, _ = record_span(q_pos, lengths_ref)
        span_ref[u, pl.ds(0, 1)] = q_start
        span_ref[u, pl.ds(1, 1)] = q_pos
    qd_cat_ref[groups] = jnp.zeros_like(qd_cat_ref[groups])
    span_ref[groups] = jnp.zeros_like(span_ref[groups])
    row_ref[groups] = jnp.zeros_like(row_ref[groups])

    def forward(i):
        u, t = visit_q[i], visit_k[i]
        scores = lax.dot_general(
            keys_ref[t], qd_cat_ref[u, pl.ds(0, tile)], (((1,), (1,)), ((), ())),
            preferred_element_type=F32,
        )
        k_pos = origin + t * (2 * tile) + sub_pos
        span = span_ref[u]
        allowed = (k_pos >= span[0:1]) & (k_pos <= span[1:2])
        e = jnp.where(allowed, jnp.exp2(scores * to_exp2), 0.0)
        e_ref[i] = e
        context = jnp.dot(turned_ref[t, HD:], e.astype(BF16), preferred_element_type=F32)
        return u, jnp.sum(e.reshape(2 * tile // 8, 8, tile), axis=0), context

    def forward_some(j, carry):
        for u, total, context in [forward(PER_STEP * j + i) for i in range(PER_STEP)]:
            total_ref[u] += total
            context_ref[u] += context
        return carry

    steps = (count + PER_STEP - 1) // PER_STEP
    lax.fori_loop(0, steps, forward_some, 0)
    for u in range(groups):
        inverse = 1.0 / jnp.sum(total_ref[u], axis=0, keepdims=True)
        context = (context_ref[u] * inverse).astype(BF16).astype(F32)
        context_ref[u] = context
        row_ref[u, pl.ds(0, 1)] = inverse
        row_ref[u, pl.ds(1, 1)] = jnp.sum(d_turned_ref[u] * context, axis=0, keepdims=True)

    def backward(i):
        u, t = visit_q[i], visit_k[i]
        row = row_ref[u]
        probs = e_ref[i] * row[0:1]
        d_probs = lax.dot_general(
            keys_ref[t], qd_cat_ref[u, pl.ds(tile, tile)], (((1,), (1,)), ((), ())),
            preferred_element_type=F32,
        )
        d_scores = (probs * (d_probs - row[1:2])).astype(BF16)
        both = jnp.concatenate([d_scores, probs.astype(BF16)], axis=1)
        d_keys = jnp.dot(both, qd_cat_ref[u], preferred_element_type=F32)
        d_queries = jnp.dot(turned_ref[t, :HD], d_scores, preferred_element_type=F32)
        return u, t, d_keys, d_queries

    def backward_some(j, carry):
        for u, t, d_keys, d_queries in [backward(PER_STEP * j + i) for i in range(PER_STEP)]:
            acc_ref[t] += d_keys
            d_query_ref[u] += d_queries
        return carry

    lax.fori_loop(0, steps, backward_some, 0)
    for u in range(groups):
        packed = jnp.concatenate([context_ref[u], d_query_ref[u] * unit], axis=0).T
        for i in range(2):
            part = packed[i * rows : (i + 1) * rows]
            cq_full[2 * u + i] = part
            cq_ref[2 * u + i] = part.astype(BF16)
    scale = jnp.where(low_lanes((1, LANES)), unit, 1.0)
    head = lax.broadcasted_iota(jnp.int32, (8, LANES), 0) < 4

    def end_rows(half, slot, first):
        slot = pre + jnp.clip(slot, 0, slots - 1)
        at = half * tile + slot % 2 * rows + first
        return acc_ref[slot // 2, pl.ds(pl.multiple_of(at, 8), 8)] * scale

    for s in range(key_slots):
        part = pl.ds(s % 2 * rows, rows)
        dkv_mine[s] = acc_ref[s // 2, part] * scale
        part = pl.ds(tile + s % 2 * rows, rows)
        send_ref[s, pl.ds(0, rows)] = (acc_ref[s // 2, part] * scale).astype(BF16)
        if s < pre:
            send_ref[s, pl.ds(rows, 16)] = jnp.zeros((16, LANES), BF16)
    for s in range(slots):
        edge_mine[s] = jnp.where(
            head, end_rows(1, s + parity, 0), end_rows(1, s - 1 + parity, rows - 8)
        )
        past, later = s - parity, s + 1 - parity
        d_edge = jnp.where(head, end_rows(0, later, 0), end_rows(0, past, rows - 8))
        q_edge = jnp.where(
            head,
            cq_full[jnp.clip(later, 0, slots - 1), pl.ds(0, 8)],
            cq_full[jnp.clip(past, 0, slots - 1), pl.ds(rows - 8, 8)],
        )
        send_ref[pre + s, pl.ds(rows, 16)] = jnp.concatenate([d_edge, q_edge]).astype(BF16)


def attention_call(lengths, kv_mine, kv_other, qd, pre):
    slots = qd.shape[0]
    key_slots, rows, _ = kv_mine.shape
    tile = 2 * rows
    tiles, groups = key_slots // 2, slots // 2
    reach = MAXLEN // (2 * tile) + 1
    place = lambda s, ordered: s if ordered else bit_reversed(s, slots)
    visits = sum(min(u + pre // 2 + 1, reach) for u in range(groups)) + PER_STEP - 1
    smem = pl.BlockSpec(memory_space=pltpu.SMEM)
    vmem = pl.BlockSpec(memory_space=pltpu.VMEM)
    return pl.pallas_call(
        functools.partial(attention_kernel, pre, place),
        in_specs=[smem, vmem, vmem, vmem],
        out_specs=[vmem, vmem, vmem, vmem],
        out_shape=[
            jax.ShapeDtypeStruct((slots, rows, LANES), BF16),
            jax.ShapeDtypeStruct((key_slots, rows, LANES), F32),
            jax.ShapeDtypeStruct((slots, 8, LANES), F32),
            jax.ShapeDtypeStruct((key_slots, rows + 16, LANES), BF16),
        ],
        scratch_shapes=[
            pltpu.SMEM((visits,), jnp.int32),
            pltpu.SMEM((visits,), jnp.int32),
            pltpu.VMEM((tiles + 1, 2 * tile, LANES), BF16),
            pltpu.VMEM((tiles + 1, LANES, 2 * tile), BF16),
            pltpu.VMEM((groups + 1, 2 * tile, LANES), BF16),
            pltpu.VMEM((groups, HD, tile), F32),
            pltpu.VMEM((groups + 1, 8, tile), jnp.int32),
            pltpu.VMEM((visits, 2 * tile, tile), F32),
            pltpu.VMEM((groups + 1, 8, tile), F32),
            pltpu.VMEM((groups + 1, HD, tile), F32),
            pltpu.VMEM((groups + 1, 8, tile), F32),
            pltpu.VMEM((groups + 1, HD, tile), F32),
            pltpu.VMEM((tiles + 1, 2 * tile, LANES), F32),
            pltpu.VMEM((slots, rows, LANES), F32),
        ],
        compiler_params=params(VMEM_MOST),
        cost_estimate=pl.CostEstimate(
            flops=10 * slots * rows * MAXLEN * LANES,
            bytes_accessed=20 * slots * rows * LANES,
            transcendentals=slots * rows * MAXLEN,
        ),
        name="attention",
    )(lengths, kv_mine, kv_other, qd)


def combine_kernel(cq_ref, mine_ref, edge_ref, got_ref, out_ref):
    slots, rows, _ = cq_ref.shape
    for s in range(slots):
        at = bit_reversed(s, slots)
        out_ref[at, pl.ds(0, rows)] = cq_ref[s]
        got = got_ref[s].astype(F32)
        out_ref[at, pl.ds(rows, rows)] = (mine_ref[s] + got[:rows]).astype(BF16)
        edges = [edge_ref[s] + got[rows : rows + 8], got[rows + 8 :]]
        out_ref[at, pl.ds(2 * rows, 16)] = jnp.concatenate(edges).astype(BF16)


def combine_call(cq, mine, edge, got):
    slots, rows, _ = cq.shape
    vmem = pl.BlockSpec(memory_space=pltpu.VMEM)
    return pl.pallas_call(
        combine_kernel,
        in_specs=[vmem] * 4,
        out_specs=vmem,
        out_shape=jax.ShapeDtypeStruct((slots, 2 * rows + 16, LANES), BF16),
        compiler_params=params(VMEM_SOME),
        name="combine",
    )(cq, mine, edge, got)


def combine_windows(cq, mine, got, pre, side, window, devices):
    slots, rows, _ = cq.shape
    dkv = mine + got[:, :rows].astype(F32)
    back = [(i + window, i) for i in range(devices - window)]
    earlier = lax.ppermute(dkv[:pre].astype(BF16), AXES, back).astype(F32)
    dkv = dkv[pre:].at[slots - pre :].add(earlier).astype(BF16)
    both = jnp.concatenate([cq, dkv], axis=2)
    tails, heads = both[:, rows - 8 :], both[:, :8]
    swapped = [(i, i ^ 1) for i in range(devices)]
    tails_other = lax.ppermute(tails, AXES, swapped)
    heads_other = lax.ppermute(heads, AXES, swapped)
    last = [(i, i + window - 1) for i in range(1, devices - window, 2)]
    tail_past = lax.ppermute(tails[-1:], AXES, last)
    head_next = lax.ppermute(heads[:1], AXES, [(j, i) for i, j in last])
    before = jnp.where(
        side == 0, jnp.concatenate([tail_past, tails_other[:-1]]), tails_other
    )
    after = jnp.where(side == 0, heads_other, jnp.concatenate([heads_other[1:], head_next]))
    edge = jnp.where(jnp.arange(8)[None, :, None] < 4, after, before)
    grads = jnp.concatenate([cq, dkv, edge[..., LANES:], edge[..., :LANES]], axis=1)
    return jnp.stack([grads[bit_reversed(s, slots)] for s in range(slots)])


def back_kernel(
    lengths_ref, r_ref, taps_ref, w_ref, wo_ref, attended_ref, grad_ref, context, grads, padded
):
    heads = r_ref.shape[0]
    rows, width = context.shape
    blk = width // BACK_STEPS
    main, dkv = slice(0, rows), slice(rows, 2 * rows)
    edge_dkv, edge_cq = slice(2 * rows, 2 * rows + 8), slice(2 * rows + 8, 2 * rows + 16)
    pad = jnp.zeros((8, LANES), F32)
    for pair in range(heads // 2):
        lanes = pl.ds(pair * LANES, LANES)
        x, y = (r_ref[2 * pair + i].astype(F32) for i in range(2))
        context[:, lanes] = zip_low(x[main], y[main]).astype(BF16)

        def gather(mix, part, edge):
            return jnp.concatenate([mix(x[part], y[part]), mix(x[edge], y[edge]), pad]).astype(BF16)

        grads[:, lanes] = gather(zip_high, main, edge_cq)
        grads[:, pl.ds(width + pair * LANES, LANES)] = gather(zip_low, dkv, edge_dkv)
        grads[:, pl.ds(2 * width + pair * LANES, LANES)] = gather(zip_high, dkv, edge_dkv)
    first_row = device_index() * rows
    per = blk // LANES
    for step in range(BACK_STEPS):
        part = pl.ds(step * blk, blk)
        mixed = lax.dot_general(
            grads[...], w_ref[part, :], (((1,), (1,)), ((), ())), preferred_element_type=F32
        ).astype(BF16).astype(F32)
        edge = mixed[rows : rows + 8]
        padded[pl.ds(0, 8), part] = edge
        padded[pl.ds(8, rows), part] = mixed[:rows]
        padded[pl.ds(8 + rows, 8), part] = edge
        attended_ref[:, part] = jnp.dot(
            context[...], wo_ref[:, part], preferred_element_type=F32
        ).astype(BF16)
        grad_ref[:, part] = conv_rows(
            padded, range(step * per, (step + 1) * per), taps_ref, lengths_ref, first_row, rows,
            True,
        ).astype(BF16)


def back_call(lengths, r, taps, w_qkv, w_out):
    heads = r.shape[0]
    rows = (r.shape[1] - 16) // 2
    width = heads * HD
    smem = pl.BlockSpec(memory_space=pltpu.SMEM)
    vmem = pl.BlockSpec(memory_space=pltpu.VMEM)
    shape = jax.ShapeDtypeStruct((rows, width), BF16)
    return pl.pallas_call(
        back_kernel,
        in_specs=[smem, vmem, vmem, vmem, vmem],
        out_specs=[vmem, vmem],
        out_shape=[shape, shape],
        scratch_shapes=[
            pltpu.VMEM((rows, width), BF16),
            pltpu.VMEM((rows + 16, 3 * width), BF16),
            pltpu.VMEM((rows + 16, width), F32),
        ],
        compiler_params=params(VMEM_SOME),
        cost_estimate=pl.CostEstimate(
            flops=8 * rows * width * width, bytes_accessed=8 * width * width, transcendentals=0
        ),
        name="back",
    )(lengths, r, taps, w_qkv, w_out)


def bit_reversed(i, count):
    bits = count.bit_length() - 1
    if count != 1 << bits:
        return i
    return sum((i >> b & 1) << (bits - 1 - b) for b in range(bits))


def on_device(tokens, conv_kernel, w_qkv, w_out, lengths, cotangent):
    rows, width = tokens.shape
    heads = width // HD
    devices = lax.axis_size(AXES)
    window = 2 * heads
    windows = devices // window
    pre = MAXLEN // (2 * rows) if windows > 1 else 0
    me = lax.axis_index(AXES)
    same_side = [
        [w * window + 2 * bit_reversed(c, heads) + side for c in range(heads)]
        for w in range(windows)
        for side in range(2)
    ]
    swapped = [(i, i ^ 1) for i in range(devices)]
    up = [(i, i + 1) for i in range(devices - 1)]
    down = [(i + 1, i) for i in range(devices - 1)]

    def exchange(x):
        return lax.all_to_all(
            x, AXES, split_axis=0, concat_axis=0, axis_index_groups=same_side, tiled=True
        )

    before = lax.ppermute(tokens[rows - EDGE :], AXES, up)
    after = lax.ppermute(tokens[:EDGE], AXES, down)
    sent = front_call(lengths, before, tokens, after, conv_kernel, w_qkv, cotangent, w_out)
    qd = exchange(sent)
    kv_mine = qd[:, :rows]
    if pre:
        shift = [(i, i + window) for i in range(devices - window)]
        kv_mine = jnp.stack([kv_mine[bit_reversed(s, heads)] for s in range(heads)])
        kv_mine = jnp.concatenate([lax.ppermute(kv_mine[heads - pre :], AXES, shift), kv_mine])
    kv_other = lax.ppermute(kv_mine, AXES, swapped)
    cq, mine, edge, send = attention_call(lengths, kv_mine, kv_other, qd, pre)
    got = lax.ppermute(send, AXES, swapped)
    if pre:
        grads = combine_windows(cq, mine, got, pre, me % 2, window, devices)
    else:
        grads = combine_call(cq, mine, edge, got)
    return back_call(lengths, exchange(grads), conv_kernel, w_qkv, w_out)


def solution(mesh):
    placed = (P(AXES, None), P(), P(), P(), P(), P(AXES, None))
    return jax.shard_map(
        on_device,
        mesh=mesh,
        in_specs=placed,
        out_specs=(P(AXES, None), P(AXES, None)),
        check_vma=False,
    )
```

```python
import functools
import math

import jax
import jax.numpy as jnp
from jax import lax
from jax.experimental import pallas as pl
from jax.experimental.pallas import tpu as pltpu
from jax.sharding import PartitionSpec as P

HD = 64
KS = 7
HALF = KS // 2
MAXLEN = 2048
AXES = ("ctx", "head")
LANES = 128
EDGE = 16
PER_STEP = 2
FAR = -1e30
FRONT_STEPS = 4
BACK_STEPS = 4
VMEM_ALL = 60 * 1024 * 1024
VMEM_MOST = 44 * 1024 * 1024
VMEM_SOME = 24 * 1024 * 1024
F32 = jnp.float32
BF16 = jnp.bfloat16


def params(limit):
    return pltpu.CompilerParams(vmem_limit_bytes=limit)


def record_span(positions, lengths_ref):
    start = jnp.zeros_like(positions)
    stop = jnp.full_like(positions, jnp.iinfo(jnp.int32).max)
    end = jnp.int32(0)
    for i in range(lengths_ref.shape[0]):
        end = end + lengths_ref[i]
        past = end <= positions
        start = jnp.where(past, end, start)
        stop = jnp.where(past, stop, jnp.minimum(stop, end))
    return start, stop


def device_index():
    return lax.axis_index("ctx") * lax.axis_size("head") + lax.axis_index("head")


def low_lanes(shape):
    return lax.broadcasted_iota(jnp.int32, shape, len(shape) - 1) % LANES < HD


def swap_halves(x):
    return pltpu.roll(x, HD, x.ndim - 1)


def zip_low(x, y):
    return jnp.where(low_lanes(x.shape), x, swap_halves(y))


def zip_high(x, y):
    return jnp.where(low_lanes(x.shape), swap_halves(x), y)


def conv_rows(padded_ref, cols, kernel_ref, lengths_ref, first_row, rows, flip):
    pos = first_row + lax.broadcasted_iota(jnp.int32, (rows, LANES), 0)
    start, stop = record_span(pos, lengths_ref)
    masks = []
    for t in range(KS):
        at = pos + (t - HALF)
        masks.append((at >= start) & (at < stop))
    pieces = []
    for c in cols:
        lanes = pl.ds(c * LANES, LANES)
        total = padded_ref[pl.ds(8, rows), lanes]
        for t in range(KS):
            tap = kernel_ref[KS - 1 - t if flip else t, lanes]
            shifted = padded_ref[pl.ds(8 - HALF + t, rows), lanes]
            total = total + jnp.where(masks[t], shifted, 0.0) * tap[None, :]
        pieces.append(total)
    return jnp.concatenate(pieces, axis=1)


def front_kernel(
    lengths_ref, before_ref, after_ref, x_hbm, taps_hbm, w_hbm, cot_hbm, wo_hbm,
    out_ref, x_ref, taps_ref, w_ref, cot_ref, wo_ref, padded, projected, d_rows, sems,
):
    rows, width = x_ref.shape
    blk = width // FRONT_STEPS

    def copy(source, target, i):
        return pltpu.make_async_copy(source, target, sems.at[i])

    whole = [
        copy(source, target, i)
        for i, (source, target) in enumerate(
            ((x_hbm, x_ref), (taps_hbm, taps_ref), (cot_hbm, cot_ref))
        )
    ]
    parts = []
    for step in range(FRONT_STEPS):
        part = pl.ds(step * blk, blk)
        at = 3 + 2 * step
        parts.append(
            (
                copy(w_hbm.at[part], w_ref.at[part], at),
                copy(wo_hbm.at[part], wo_ref.at[part], at + 1),
            )
        )
    for c in whole:
        c.start()
    for pair in parts:
        for c in pair:
            c.start()
    padded[pl.ds(0, 8), :] = before_ref[...].astype(F32)[EDGE - 8 :]
    padded[pl.ds(8 + rows, 8), :] = after_ref[...].astype(F32)[:8]
    for c in whole:
        c.wait()
    padded[pl.ds(8, rows), :] = x_ref[...].astype(F32)
    first_row = device_index() * rows
    per = blk // LANES
    for step in range(FRONT_STEPS):
        mixed = conv_rows(
            padded, range(step * per, (step + 1) * per), taps_ref, lengths_ref, first_row, rows,
            False,
        ).astype(BF16)
        parts[step][0].wait()
        part = jnp.dot(mixed, w_ref[pl.ds(step * blk, blk), :], preferred_element_type=F32)
        if step == 0:
            projected[...] = part
        else:
            projected[...] += part
        parts[step][1].wait()
        d_rows[:, pl.ds(step * blk, blk)] = lax.dot_general(
            cot_ref[...], wo_ref[pl.ds(step * blk, blk), :], (((1,), (1,)), ((), ())),
            preferred_element_type=F32,
        )
    for pair in range(width // LANES):
        lanes = pl.ds(pair * LANES, LANES)
        q, k, v = (projected[:, pl.ds(i * width + pair * LANES, LANES)] for i in range(3))
        d = d_rows[:, lanes]
        out_ref[2 * pair] = jnp.concatenate([zip_low(k, v), zip_low(q, d)]).astype(BF16)
        out_ref[2 * pair + 1] = jnp.concatenate([zip_high(k, v), zip_high(q, d)]).astype(BF16)


def front_call(lengths, before, x, after, taps, w_qkv, cotangent, w_out):
    rows, width = x.shape
    heads = width // HD
    smem = pl.BlockSpec(memory_space=pltpu.SMEM)
    vmem = pl.BlockSpec(memory_space=pltpu.VMEM)
    anywhere = pl.BlockSpec(memory_space=pl.ANY)
    return pl.pallas_call(
        front_kernel,
        in_specs=[smem, vmem, vmem] + [anywhere] * 5,
        out_specs=vmem,
        out_shape=jax.ShapeDtypeStruct((heads, 2 * rows, LANES), BF16),
        scratch_shapes=[
            pltpu.VMEM(x.shape, x.dtype),
            pltpu.VMEM(taps.shape, taps.dtype),
            pltpu.VMEM(w_qkv.shape, w_qkv.dtype),
            pltpu.VMEM(cotangent.shape, cotangent.dtype),
            pltpu.VMEM(w_out.shape, w_out.dtype),
            pltpu.VMEM((rows + 16, width), F32),
            pltpu.VMEM((rows, 3 * width), F32),
            pltpu.VMEM((rows, width), F32),
            pltpu.SemaphoreType.DMA((3 + 2 * FRONT_STEPS,)),
        ],
        compiler_params=params(VMEM_ALL),
        cost_estimate=pl.CostEstimate(
            flops=8 * rows * width * width, bytes_accessed=8 * width * width, transcendentals=0
        ),
        name="front",
    )(lengths, before, after, x, taps, w_qkv, cotangent, w_out)


def attention_kernel(
    pre, place, lengths_ref, kv_mine, kv_other, qd_ref,
    cq_ref, dkv_mine, edge_mine, send_ref,
    visit_q, visit_k, keys_ref, marked_ref, turned_ref, query_ref, qd_cat_ref, d_turned_ref, e_ref,
    total_ref, context_ref, row_ref, d_query_ref, acc_ref, cq_full,
):
    slots = qd_ref.shape[0]
    key_slots, rows, _ = kv_mine.shape
    tile = 2 * rows
    tiles, groups = key_slots // 2, slots // 2
    me = device_index()
    window = 2 * slots
    base, parity = me // window * (window * rows), me % 2
    origin = base - pre * tile
    unit = HD**-0.5
    to_exp2 = unit * math.log2(math.e)

    def row_at(slot, side):
        return slot * tile + side * rows + lax.broadcasted_iota(jnp.int32, (rows, 1), 0)

    lane = lax.broadcasted_iota(jnp.int32, (1, LANES), 1)
    starts = jnp.zeros((1, LANES), jnp.int32)
    stops = jnp.zeros((1, LANES), jnp.int32)
    end = jnp.int32(0)
    for i in range(lengths_ref.shape[0]):
        starts = jnp.where(lane == HD + i, end, starts)
        end = end + lengths_ref[i]
        stops = jnp.where(lane == HD + i, end, stops)

    count = jnp.int32(groups)
    for u in range(groups):
        visit_q[u] = u
        visit_k[u] = u + pre // 2
        first = base + u * (2 * tile) + parity * rows
        begin, end = jnp.int32(0), jnp.int32(0)
        for i in range(lengths_ref.shape[0]):
            end = end + lengths_ref[i]
            begin = jnp.where(end <= first, end, begin)
        t_first = jnp.maximum(begin - origin, 0) // (2 * tile)

        def note(t, count, u=u):
            visit_q[count] = u
            visit_k[count] = t
            return count + 1

        count = lax.fori_loop(t_first, u + pre // 2, note, count)
    for i in range(PER_STEP - 1):
        visit_q[count + i] = groups
        visit_k[count + i] = tiles

    low = low_lanes((rows, LANES))
    for t in range(tiles):
        for half, source in enumerate((kv_mine, kv_other)):
            side = parity if half == 0 else 1 - parity
            for i in range(2):
                block = source[place(2 * t + i, pre)]
                at = pl.ds(half * tile + i * rows, rows)
                keys_ref[t, at] = block
                turned_ref[t, :, at] = block.T
                pos = origin + row_at(2 * t + i, side)
                mark = jnp.where((pos >= starts) & (pos < stops), 0.0, FAR)
                marked_ref[t, at] = jnp.where(low, block.astype(F32), mark).astype(BF16)
    for ref in (keys_ref, marked_ref, turned_ref):
        ref[tiles] = jnp.zeros_like(ref[tiles])
    for ref in (query_ref, qd_cat_ref, row_ref):
        ref[groups] = jnp.zeros_like(ref[groups])
    for ref in (acc_ref, total_ref, context_ref, d_query_ref):
        ref[...] = jnp.zeros_like(ref)
    for u in range(groups):
        for i in range(2):
            qd = qd_ref[place(2 * u + i, 0), pl.ds(rows, rows)]
            at = pl.ds(i * rows, rows)
            d_turned_ref[u, :, at] = qd.T[HD:].astype(F32)
            qd = qd.astype(F32)
            pos = base + row_at(2 * u + i, parity)
            mark = jnp.where((pos >= starts) & (pos < stops), 1.0, 0.0)
            query_ref[u, at] = jnp.where(low, qd, mark).astype(BF16)
            qd_cat_ref[u, at] = jnp.where(low, qd, 0.0).astype(BF16)
            qd_cat_ref[u, pl.ds(tile + i * rows, rows)] = jnp.where(low, 0.0, qd).astype(BF16)

    nt = (((1,), (1,)), ((), ()))
    chunks = [pl.ds(c * rows, rows) for c in range(4)]
    q_lane = lax.broadcasted_iota(jnp.int32, (rows, tile), 1)
    q_row = q_lane // rows * tile + q_lane % rows + parity * rows
    k_sub = lax.broadcasted_iota(jnp.int32, (rows, tile), 0)

    def forward(i, diagonal):
        u, t = visit_q[i], visit_k[i]
        total = jnp.zeros((8, tile), F32)
        halves = []
        for c, at in enumerate(chunks):
            scores = lax.dot_general(
                marked_ref[t, at], query_ref[u], nt, preferred_element_type=F32
            )
            e = jnp.exp2(scores * to_exp2)
            if diagonal:
                side = parity if c < 2 else 1 - parity
                e = jnp.where(k_sub + (c % 2 * tile + side * rows) <= q_row, e, 0.0)
            e_ref[i, at] = e
            total = total + jnp.sum(e.reshape(rows // 8, 8, tile), axis=0)
            halves.append(e.astype(BF16))
        context = jnp.dot(
            turned_ref[t, HD:], jnp.concatenate(halves), preferred_element_type=F32
        )
        return u, total, context

    def forward_some(diagonal):
        def run(j, carry):
            for u, total, context in [
                forward(PER_STEP * j + i, diagonal) for i in range(PER_STEP)
            ]:
                total_ref[u] += total
                context_ref[u] += context
            return carry

        return run

    steps = (count + PER_STEP - 1) // PER_STEP
    lax.fori_loop(0, groups // PER_STEP, forward_some(True), 0)
    lax.fori_loop(groups // PER_STEP, steps, forward_some(False), 0)
    for u in range(groups):
        inverse = 1.0 / jnp.sum(total_ref[u], axis=0, keepdims=True)
        context = (context_ref[u] * inverse).astype(BF16).astype(F32)
        context_ref[u] = context
        row_ref[u, pl.ds(0, 1)] = inverse
        row_ref[u, pl.ds(1, 1)] = jnp.sum(d_turned_ref[u] * context, axis=0, keepdims=True)

    def backward(i):
        u, t = visit_q[i], visit_k[i]
        row = row_ref[u]
        halves, d_keys = [], []
        for at in chunks:
            probs = e_ref[i, at] * row[0:1]
            d_probs = lax.dot_general(
                keys_ref[t, at], qd_cat_ref[u, pl.ds(tile, tile)], nt, preferred_element_type=F32
            )
            d_scores = (probs * (d_probs - row[1:2])).astype(BF16)
            both = jnp.concatenate([d_scores, probs.astype(BF16)], axis=1)
            d_keys.append(jnp.dot(both, qd_cat_ref[u], preferred_element_type=F32))
            halves.append(d_scores)
        d_queries = jnp.dot(
            turned_ref[t, :HD], jnp.concatenate(halves), preferred_element_type=F32
        )
        return u, t, d_keys, d_queries

    def backward_some(j, carry):
        for u, t, d_keys, d_queries in [backward(PER_STEP * j + i) for i in range(PER_STEP)]:
            for at, part in zip(chunks, d_keys):
                acc_ref[t, at] += part
            d_query_ref[u] += d_queries
        return carry

    lax.fori_loop(0, steps, backward_some, 0)
    for u in range(groups):
        packed = jnp.concatenate([context_ref[u], d_query_ref[u] * unit], axis=0).T
        for i in range(2):
            part = packed[i * rows : (i + 1) * rows]
            cq_full[2 * u + i] = part
            cq_ref[2 * u + i] = part.astype(BF16)
    scale = jnp.where(low_lanes((1, LANES)), unit, 1.0)
    head = lax.broadcasted_iota(jnp.int32, (8, LANES), 0) < 4

    def end_rows(half, slot, first):
        slot = pre + jnp.clip(slot, 0, slots - 1)
        at = half * tile + slot % 2 * rows + first
        return acc_ref[slot // 2, pl.ds(pl.multiple_of(at, 8), 8)] * scale

    for s in range(key_slots):
        part = pl.ds(s % 2 * rows, rows)
        dkv_mine[s] = acc_ref[s // 2, part] * scale
        part = pl.ds(tile + s % 2 * rows, rows)
        send_ref[s, pl.ds(0, rows)] = (acc_ref[s // 2, part] * scale).astype(BF16)
        if s < pre:
            send_ref[s, pl.ds(rows, 16)] = jnp.zeros((16, LANES), BF16)
    for s in range(slots):
        edge_mine[s] = jnp.where(
            head, end_rows(1, s + parity, 0), end_rows(1, s - 1 + parity, rows - 8)
        )
        past, later = s - parity, s + 1 - parity
        d_edge = jnp.where(head, end_rows(0, later, 0), end_rows(0, past, rows - 8))
        q_edge = jnp.where(
            head,
            cq_full[jnp.clip(later, 0, slots - 1), pl.ds(0, 8)],
            cq_full[jnp.clip(past, 0, slots - 1), pl.ds(rows - 8, 8)],
        )
        send_ref[pre + s, pl.ds(rows, 16)] = jnp.concatenate([d_edge, q_edge]).astype(BF16)


def attention_call(lengths, kv_mine, kv_other, qd, pre):
    slots = qd.shape[0]
    key_slots, rows, _ = kv_mine.shape
    tile = 2 * rows
    tiles, groups = key_slots // 2, slots // 2
    reach = MAXLEN // (2 * tile) + 1
    place = lambda s, ordered: s if ordered else bit_reversed(s, slots)
    visits = sum(min(u + pre // 2 + 1, reach) for u in range(groups)) + PER_STEP - 1
    smem = pl.BlockSpec(memory_space=pltpu.SMEM)
    vmem = pl.BlockSpec(memory_space=pltpu.VMEM)
    return pl.pallas_call(
        functools.partial(attention_kernel, pre, place),
        in_specs=[smem, vmem, vmem, vmem],
        out_specs=[vmem, vmem, vmem, vmem],
        out_shape=[
            jax.ShapeDtypeStruct((slots, rows, LANES), BF16),
            jax.ShapeDtypeStruct((key_slots, rows, LANES), F32),
            jax.ShapeDtypeStruct((slots, 8, LANES), F32),
            jax.ShapeDtypeStruct((key_slots, rows + 16, LANES), BF16),
        ],
        scratch_shapes=[
            pltpu.SMEM((visits,), jnp.int32),
            pltpu.SMEM((visits,), jnp.int32),
            pltpu.VMEM((tiles + 1, 2 * tile, LANES), BF16),
            pltpu.VMEM((tiles + 1, 2 * tile, LANES), BF16),
            pltpu.VMEM((tiles + 1, LANES, 2 * tile), BF16),
            pltpu.VMEM((groups + 1, tile, LANES), BF16),
            pltpu.VMEM((groups + 1, 2 * tile, LANES), BF16),
            pltpu.VMEM((groups, HD, tile), F32),
            pltpu.VMEM((visits, 2 * tile, tile), F32),
            pltpu.VMEM((groups + 1, 8, tile), F32),
            pltpu.VMEM((groups + 1, HD, tile), F32),
            pltpu.VMEM((groups + 1, 8, tile), F32),
            pltpu.VMEM((groups + 1, HD, tile), F32),
            pltpu.VMEM((tiles + 1, 2 * tile, LANES), F32),
            pltpu.VMEM((slots, rows, LANES), F32),
        ],
        compiler_params=params(VMEM_MOST),
        cost_estimate=pl.CostEstimate(
            flops=10 * slots * rows * MAXLEN * LANES,
            bytes_accessed=20 * slots * rows * LANES,
            transcendentals=slots * rows * MAXLEN,
        ),
        name="attention",
    )(lengths, kv_mine, kv_other, qd)


def combine_kernel(cq_ref, mine_ref, edge_ref, got_ref, out_ref):
    slots, rows, _ = cq_ref.shape
    for s in range(slots):
        at = bit_reversed(s, slots)
        out_ref[at, pl.ds(0, rows)] = cq_ref[s]
        got = got_ref[s].astype(F32)
        out_ref[at, pl.ds(rows, rows)] = (mine_ref[s] + got[:rows]).astype(BF16)
        edges = [edge_ref[s] + got[rows : rows + 8], got[rows + 8 :]]
        out_ref[at, pl.ds(2 * rows, 16)] = jnp.concatenate(edges).astype(BF16)


def combine_call(cq, mine, edge, got):
    slots, rows, _ = cq.shape
    vmem = pl.BlockSpec(memory_space=pltpu.VMEM)
    return pl.pallas_call(
        combine_kernel,
        in_specs=[vmem] * 4,
        out_specs=vmem,
        out_shape=jax.ShapeDtypeStruct((slots, 2 * rows + 16, LANES), BF16),
        compiler_params=params(VMEM_SOME),
        name="combine",
    )(cq, mine, edge, got)


def combine_windows(cq, mine, got, pre, side, window, devices):
    slots, rows, _ = cq.shape
    dkv = mine + got[:, :rows].astype(F32)
    back = [(i + window, i) for i in range(devices - window)]
    earlier = lax.ppermute(dkv[:pre].astype(BF16), AXES, back).astype(F32)
    dkv = dkv[pre:].at[slots - pre :].add(earlier).astype(BF16)
    both = jnp.concatenate([cq, dkv], axis=2)
    tails, heads = both[:, rows - 8 :], both[:, :8]
    swapped = [(i, i ^ 1) for i in range(devices)]
    tails_other = lax.ppermute(tails, AXES, swapped)
    heads_other = lax.ppermute(heads, AXES, swapped)
    last = [(i, i + window - 1) for i in range(1, devices - window, 2)]
    tail_past = lax.ppermute(tails[-1:], AXES, last)
    head_next = lax.ppermute(heads[:1], AXES, [(j, i) for i, j in last])
    before = jnp.where(
        side == 0, jnp.concatenate([tail_past, tails_other[:-1]]), tails_other
    )
    after = jnp.where(side == 0, heads_other, jnp.concatenate([heads_other[1:], head_next]))
    edge = jnp.where(jnp.arange(8)[None, :, None] < 4, after, before)
    grads = jnp.concatenate([cq, dkv, edge[..., LANES:], edge[..., :LANES]], axis=1)
    return jnp.stack([grads[bit_reversed(s, slots)] for s in range(slots)])


def back_kernel(
    lengths_ref, r_ref, taps_ref, w_ref, wo_ref, attended_ref, grad_ref, context, grads, padded
):
    heads = r_ref.shape[0]
    rows, width = context.shape
    blk = width // BACK_STEPS
    main, dkv = slice(0, rows), slice(rows, 2 * rows)
    edge_dkv, edge_cq = slice(2 * rows, 2 * rows + 8), slice(2 * rows + 8, 2 * rows + 16)
    pad = jnp.zeros((8, LANES), F32)
    for pair in range(heads // 2):
        lanes = pl.ds(pair * LANES, LANES)
        x, y = (r_ref[2 * pair + i].astype(F32) for i in range(2))
        context[:, lanes] = zip_low(x[main], y[main]).astype(BF16)

        def gather(mix, part, edge):
            return jnp.concatenate([mix(x[part], y[part]), mix(x[edge], y[edge]), pad]).astype(BF16)

        grads[:, lanes] = gather(zip_high, main, edge_cq)
        grads[:, pl.ds(width + pair * LANES, LANES)] = gather(zip_low, dkv, edge_dkv)
        grads[:, pl.ds(2 * width + pair * LANES, LANES)] = gather(zip_high, dkv, edge_dkv)
    first_row = device_index() * rows
    per = blk // LANES
    for step in range(BACK_STEPS):
        part = pl.ds(step * blk, blk)
        mixed = lax.dot_general(
            grads[...], w_ref[part, :], (((1,), (1,)), ((), ())), preferred_element_type=F32
        ).astype(BF16).astype(F32)
        edge = mixed[rows : rows + 8]
        padded[pl.ds(0, 8), part] = edge
        padded[pl.ds(8, rows), part] = mixed[:rows]
        padded[pl.ds(8 + rows, 8), part] = edge
        attended_ref[:, part] = jnp.dot(
            context[...], wo_ref[:, part], preferred_element_type=F32
        ).astype(BF16)
        grad_ref[:, part] = conv_rows(
            padded, range(step * per, (step + 1) * per), taps_ref, lengths_ref, first_row, rows,
            True,
        ).astype(BF16)


def back_call(lengths, r, taps, w_qkv, w_out):
    heads = r.shape[0]
    rows = (r.shape[1] - 16) // 2
    width = heads * HD
    smem = pl.BlockSpec(memory_space=pltpu.SMEM)
    vmem = pl.BlockSpec(memory_space=pltpu.VMEM)
    shape = jax.ShapeDtypeStruct((rows, width), BF16)
    return pl.pallas_call(
        back_kernel,
        in_specs=[smem, vmem, vmem, vmem, vmem],
        out_specs=[vmem, vmem],
        out_shape=[shape, shape],
        scratch_shapes=[
            pltpu.VMEM((rows, width), BF16),
            pltpu.VMEM((rows + 16, 3 * width), BF16),
            pltpu.VMEM((rows + 16, width), F32),
        ],
        compiler_params=params(VMEM_SOME),
        cost_estimate=pl.CostEstimate(
            flops=8 * rows * width * width, bytes_accessed=8 * width * width, transcendentals=0
        ),
        name="back",
    )(lengths, r, taps, w_qkv, w_out)


def bit_reversed(i, count):
    bits = count.bit_length() - 1
    if count != 1 << bits:
        return i
    return sum((i >> b & 1) << (bits - 1 - b) for b in range(bits))


def on_device(tokens, conv_kernel, w_qkv, w_out, lengths, cotangent):
    rows, width = tokens.shape
    heads = width // HD
    devices = lax.axis_size(AXES)
    window = 2 * heads
    windows = devices // window
    pre = MAXLEN // (2 * rows) if windows > 1 else 0
    me = lax.axis_index(AXES)
    same_side = [
        [w * window + 2 * bit_reversed(c, heads) + side for c in range(heads)]
        for w in range(windows)
        for side in range(2)
    ]
    swapped = [(i, i ^ 1) for i in range(devices)]
    up = [(i, i + 1) for i in range(devices - 1)]
    down = [(i + 1, i) for i in range(devices - 1)]

    def exchange(x):
        return lax.all_to_all(
            x, AXES, split_axis=0, concat_axis=0, axis_index_groups=same_side, tiled=True
        )

    before = lax.ppermute(tokens[rows - EDGE :], AXES, up)
    after = lax.ppermute(tokens[:EDGE], AXES, down)
    sent = front_call(lengths, before, tokens, after, conv_kernel, w_qkv, cotangent, w_out)
    qd = exchange(sent)
    kv_mine = qd[:, :rows]
    if pre:
        shift = [(i, i + window) for i in range(devices - window)]
        kv_mine = jnp.stack([kv_mine[bit_reversed(s, heads)] for s in range(heads)])
        kv_mine = jnp.concatenate([lax.ppermute(kv_mine[heads - pre :], AXES, shift), kv_mine])
    kv_other = lax.ppermute(kv_mine, AXES, swapped)
    cq, mine, edge, send = attention_call(lengths, kv_mine, kv_other, qd, pre)
    got = lax.ppermute(send, AXES, swapped)
    if pre:
        grads = combine_windows(cq, mine, got, pre, me % 2, window, devices)
    else:
        grads = combine_call(cq, mine, edge, got)
    return back_call(lengths, exchange(grads), conv_kernel, w_qkv, w_out)


def solution(mesh):
    placed = (P(AXES, None), P(), P(), P(), P(), P(AXES, None))
    return jax.shard_map(
        on_device,
        mesh=mesh,
        in_specs=placed,
        out_specs=(P(AXES, None), P(AXES, None)),
        check_vma=False,
    )
```

```python
import functools
import math

import jax
import jax.numpy as jnp
from jax import lax
from jax.experimental import pallas as pl
from jax.experimental.pallas import tpu as pltpu
from jax.sharding import PartitionSpec as P

HD = 64
KS = 7
HALF = KS // 2
MAXLEN = 2048
AXES = ("ctx", "head")
LANES = 128
EDGE = 16
PER_STEP = 4
FAR = -1e30
FRONT_STEPS = 4
BACK_STEPS = 4
VMEM_ALL = 60 * 1024 * 1024
VMEM_MOST = 44 * 1024 * 1024
VMEM_SOME = 24 * 1024 * 1024
F32 = jnp.float32
BF16 = jnp.bfloat16


def params(limit):
    return pltpu.CompilerParams(vmem_limit_bytes=limit)


def record_span(positions, lengths_ref):
    start = jnp.zeros_like(positions)
    stop = jnp.full_like(positions, jnp.iinfo(jnp.int32).max)
    end = jnp.int32(0)
    for i in range(lengths_ref.shape[0]):
        end = end + lengths_ref[i]
        past = end <= positions
        start = jnp.where(past, end, start)
        stop = jnp.where(past, stop, jnp.minimum(stop, end))
    return start, stop


def device_index():
    return lax.axis_index("ctx") * lax.axis_size("head") + lax.axis_index("head")


def low_lanes(shape):
    return lax.broadcasted_iota(jnp.int32, shape, len(shape) - 1) % LANES < HD


def swap_halves(x):
    return pltpu.roll(x, HD, x.ndim - 1)


def zip_low(x, y):
    return jnp.where(low_lanes(x.shape), x, swap_halves(y))


def zip_high(x, y):
    return jnp.where(low_lanes(x.shape), swap_halves(x), y)


def conv_rows(padded_ref, cols, kernel_ref, lengths_ref, first_row, rows, flip):
    pos = first_row + lax.broadcasted_iota(jnp.int32, (rows, LANES), 0)
    start, stop = record_span(pos, lengths_ref)
    masks = []
    for t in range(KS):
        at = pos + (t - HALF)
        masks.append((at >= start) & (at < stop))
    pieces = []
    for c in cols:
        lanes = pl.ds(c * LANES, LANES)
        total = padded_ref[pl.ds(8, rows), lanes]
        for t in range(KS):
            tap = kernel_ref[KS - 1 - t if flip else t, lanes]
            shifted = padded_ref[pl.ds(8 - HALF + t, rows), lanes]
            total = total + jnp.where(masks[t], shifted, 0.0) * tap[None, :]
        pieces.append(total)
    return jnp.concatenate(pieces, axis=1)


def front_kernel(
    lengths_ref, before_ref, after_ref, x_hbm, taps_hbm, w_hbm, cot_hbm, wo_hbm,
    out_ref, x_ref, taps_ref, w_ref, cot_ref, wo_ref, padded, projected, d_rows, sems,
):
    rows, width = x_ref.shape
    blk = width // FRONT_STEPS

    def copy(source, target, i):
        return pltpu.make_async_copy(source, target, sems.at[i])

    whole = [
        copy(source, target, i)
        for i, (source, target) in enumerate(
            ((x_hbm, x_ref), (taps_hbm, taps_ref), (cot_hbm, cot_ref))
        )
    ]
    parts = []
    for step in range(FRONT_STEPS):
        part = pl.ds(step * blk, blk)
        at = 3 + 2 * step
        parts.append(
            (
                copy(w_hbm.at[part], w_ref.at[part], at),
                copy(wo_hbm.at[part], wo_ref.at[part], at + 1),
            )
        )
    for c in whole:
        c.start()
    for pair in parts:
        for c in pair:
            c.start()
    padded[pl.ds(0, 8), :] = before_ref[...].astype(F32)[EDGE - 8 :]
    padded[pl.ds(8 + rows, 8), :] = after_ref[...].astype(F32)[:8]
    for c in whole:
        c.wait()
    padded[pl.ds(8, rows), :] = x_ref[...].astype(F32)
    first_row = device_index() * rows
    per = blk // LANES
    for step in range(FRONT_STEPS):
        mixed = conv_rows(
            padded, range(step * per, (step + 1) * per), taps_ref, lengths_ref, first_row, rows,
            False,
        ).astype(BF16)
        parts[step][0].wait()
        part = jnp.dot(mixed, w_ref[pl.ds(step * blk, blk), :], preferred_element_type=F32)
        if step == 0:
            projected[...] = part
        else:
            projected[...] += part
        parts[step][1].wait()
        d_rows[:, pl.ds(step * blk, blk)] = lax.dot_general(
            cot_ref[...], wo_ref[pl.ds(step * blk, blk), :], (((1,), (1,)), ((), ())),
            preferred_element_type=F32,
        )
    for pair in range(width // LANES):
        lanes = pl.ds(pair * LANES, LANES)
        q, k, v = (projected[:, pl.ds(i * width + pair * LANES, LANES)] for i in range(3))
        d = d_rows[:, lanes]
        out_ref[2 * pair] = jnp.concatenate([zip_low(k, v), zip_low(q, d)]).astype(BF16)
        out_ref[2 * pair + 1] = jnp.concatenate([zip_high(k, v), zip_high(q, d)]).astype(BF16)


def front_call(lengths, before, x, after, taps, w_qkv, cotangent, w_out):
    rows, width = x.shape
    heads = width // HD
    smem = pl.BlockSpec(memory_space=pltpu.SMEM)
    vmem = pl.BlockSpec(memory_space=pltpu.VMEM)
    anywhere = pl.BlockSpec(memory_space=pl.ANY)
    return pl.pallas_call(
        front_kernel,
        in_specs=[smem, vmem, vmem] + [anywhere] * 5,
        out_specs=vmem,
        out_shape=jax.ShapeDtypeStruct((heads, 2 * rows, LANES), BF16),
        scratch_shapes=[
            pltpu.VMEM(x.shape, x.dtype),
            pltpu.VMEM(taps.shape, taps.dtype),
            pltpu.VMEM(w_qkv.shape, w_qkv.dtype),
            pltpu.VMEM(cotangent.shape, cotangent.dtype),
            pltpu.VMEM(w_out.shape, w_out.dtype),
            pltpu.VMEM((rows + 16, width), F32),
            pltpu.VMEM((rows, 3 * width), F32),
            pltpu.VMEM((rows, width), F32),
            pltpu.SemaphoreType.DMA((3 + 2 * FRONT_STEPS,)),
        ],
        compiler_params=params(VMEM_ALL),
        cost_estimate=pl.CostEstimate(
            flops=8 * rows * width * width, bytes_accessed=8 * width * width, transcendentals=0
        ),
        name="front",
    )(lengths, before, after, x, taps, w_qkv, cotangent, w_out)


def attention_kernel(
    pre, place, lengths_ref, kv_mine, kv_other, qd_ref,
    cq_ref, dkv_mine, edge_mine, send_ref,
    visit_q, visit_k, keys_ref, marked_ref, turned_ref, query_ref, qd_cat_ref, d_turned_ref, e_ref,
    total_ref, context_ref, row_ref, d_query_ref, acc_ref, cq_full,
):
    slots = qd_ref.shape[0]
    key_slots, rows, _ = kv_mine.shape
    tile = 2 * rows
    tiles, groups = key_slots // 2, slots // 2
    me = device_index()
    window = 2 * slots
    base, parity = me // window * (window * rows), me % 2
    origin = base - pre * tile
    unit = HD**-0.5
    to_exp2 = unit * math.log2(math.e)

    def row_at(slot, side):
        return slot * tile + side * rows + lax.broadcasted_iota(jnp.int32, (rows, 1), 0)

    lane = lax.broadcasted_iota(jnp.int32, (1, LANES), 1)
    starts = jnp.zeros((1, LANES), jnp.int32)
    stops = jnp.zeros((1, LANES), jnp.int32)
    end = jnp.int32(0)
    for i in range(lengths_ref.shape[0]):
        starts = jnp.where(lane == HD + i, end, starts)
        end = end + lengths_ref[i]
        stops = jnp.where(lane == HD + i, end, stops)

    count = jnp.int32(groups)
    for u in range(groups):
        visit_q[u] = u
        visit_k[u] = u + pre // 2
        first = base + u * (2 * tile) + parity * rows
        begin, end = jnp.int32(0), jnp.int32(0)
        for i in range(lengths_ref.shape[0]):
            end = end + lengths_ref[i]
            begin = jnp.where(end <= first, end, begin)
        t_first = jnp.maximum(begin - origin, 0) // (2 * tile)

        def note(t, count, u=u):
            visit_q[count] = u
            visit_k[count] = t
            return count + 1

        count = lax.fori_loop(t_first, u + pre // 2, note, count)

    low = low_lanes((rows, LANES))
    for t in range(tiles):
        for half, source in enumerate((kv_mine, kv_other)):
            side = parity if half == 0 else 1 - parity
            for i in range(2):
                block = source[place(2 * t + i, pre)]
                at = pl.ds(half * tile + i * rows, rows)
                keys_ref[t, at] = block
                turned_ref[t, :, at] = block.T
                pos = origin + row_at(2 * t + i, side)
                mark = jnp.where((pos >= starts) & (pos < stops), 0.0, FAR)
                marked_ref[t, at] = jnp.where(low, block.astype(F32), mark).astype(BF16)
    for ref in (acc_ref, total_ref, context_ref, d_query_ref):
        ref[...] = jnp.zeros_like(ref)
    for u in range(groups):
        for i in range(2):
            qd = qd_ref[place(2 * u + i, 0), pl.ds(rows, rows)]
            at = pl.ds(i * rows, rows)
            d_turned_ref[u, :, at] = qd.T[HD:].astype(F32)
            qd = qd.astype(F32)
            pos = base + row_at(2 * u + i, parity)
            mark = jnp.where((pos >= starts) & (pos < stops), 1.0, 0.0)
            query_ref[u, at] = jnp.where(low, qd, mark).astype(BF16)
            qd_cat_ref[u, at] = jnp.where(low, qd, 0.0).astype(BF16)
            qd_cat_ref[u, pl.ds(tile + i * rows, rows)] = jnp.where(low, 0.0, qd).astype(BF16)

    nt = (((1,), (1,)), ((), ()))
    wide = (2 * tile, tile)
    q_lane = lax.broadcasted_iota(jnp.int32, wide, 1)
    q_row = q_lane // rows * tile + q_lane % rows + parity * rows
    k_sub = lax.broadcasted_iota(jnp.int32, wide, 0)
    side = jnp.where(k_sub < tile, parity, 1 - parity)
    causal = k_sub // rows % 2 * tile + k_sub % rows + side * rows <= q_row

    def forward(i, diagonal):
        u, t = visit_q[i], visit_k[i]
        scores = lax.dot_general(marked_ref[t], query_ref[u], nt, preferred_element_type=F32)
        e = jnp.exp2(scores * to_exp2)
        if diagonal:
            e = jnp.where(causal, e, 0.0)
        e_ref[i] = e
        context = jnp.dot(turned_ref[t, HD:], e.astype(BF16), preferred_element_type=F32)
        return u, jnp.sum(e.reshape(2 * tile // 8, 8, tile), axis=0), context

    def forward_some(diagonal, first, per):
        def run(j, carry):
            for u, total, context in [
                forward(first + per * j + i, diagonal) for i in range(per)
            ]:
                total_ref[u] += total
                context_ref[u] += context
            return carry

        return run

    def run_all(make, first, last):
        steps = (last - first) // PER_STEP
        lax.fori_loop(0, steps, make(first, PER_STEP), 0)
        rest = first + steps * PER_STEP
        lax.fori_loop(0, last - rest, make(rest, 1), 0)

    lax.fori_loop(0, groups // PER_STEP, forward_some(True, 0, PER_STEP), 0)
    run_all(functools.partial(forward_some, False), groups, count)
    for u in range(groups):
        inverse = 1.0 / jnp.sum(total_ref[u], axis=0, keepdims=True)
        context = (context_ref[u] * inverse).astype(BF16).astype(F32)
        context_ref[u] = context
        row_ref[u, pl.ds(0, 1)] = inverse
        row_ref[u, pl.ds(1, 1)] = jnp.sum(d_turned_ref[u] * context, axis=0, keepdims=True)

    def backward(i):
        u, t = visit_q[i], visit_k[i]
        row = row_ref[u]
        probs = e_ref[i] * row[0:1]
        d_probs = lax.dot_general(
            keys_ref[t], qd_cat_ref[u, pl.ds(tile, tile)], nt, preferred_element_type=F32
        )
        d_scores = (probs * (d_probs - row[1:2])).astype(BF16)
        both = jnp.concatenate([d_scores, probs.astype(BF16)], axis=1)
        d_keys = jnp.dot(both, qd_cat_ref[u], preferred_element_type=F32)
        d_queries = jnp.dot(turned_ref[t, :HD], d_scores, preferred_element_type=F32)
        return u, t, d_keys, d_queries

    def backward_some(first, per):
        def run(j, carry):
            for u, t, d_keys, d_queries in [
                backward(first + per * j + i) for i in range(per)
            ]:
                acc_ref[t] += d_keys
                d_query_ref[u] += d_queries
            return carry

        return run

    run_all(backward_some, 0, count)
    for u in range(groups):
        packed = jnp.concatenate([context_ref[u], d_query_ref[u] * unit], axis=0).T
        for i in range(2):
            part = packed[i * rows : (i + 1) * rows]
            cq_full[2 * u + i] = part
            cq_ref[2 * u + i] = part.astype(BF16)
    scale = jnp.where(low_lanes((1, LANES)), unit, 1.0)
    head = lax.broadcasted_iota(jnp.int32, (8, LANES), 0) < 4

    def end_rows(half, slot, first):
        slot = pre + jnp.clip(slot, 0, slots - 1)
        at = half * tile + slot % 2 * rows + first
        return acc_ref[slot // 2, pl.ds(pl.multiple_of(at, 8), 8)] * scale

    for s in range(key_slots):
        part = pl.ds(s % 2 * rows, rows)
        dkv_mine[s] = acc_ref[s // 2, part] * scale
        part = pl.ds(tile + s % 2 * rows, rows)
        send_ref[s, pl.ds(0, rows)] = (acc_ref[s // 2, part] * scale).astype(BF16)
        if s < pre:
            send_ref[s, pl.ds(rows, 16)] = jnp.zeros((16, LANES), BF16)
    for s in range(slots):
        edge_mine[s] = jnp.where(
            head, end_rows(1, s + parity, 0), end_rows(1, s - 1 + parity, rows - 8)
        )
        past, later = s - parity, s + 1 - parity
        d_edge = jnp.where(head, end_rows(0, later, 0), end_rows(0, past, rows - 8))
        q_edge = jnp.where(
            head,
            cq_full[jnp.clip(later, 0, slots - 1), pl.ds(0, 8)],
            cq_full[jnp.clip(past, 0, slots - 1), pl.ds(rows - 8, 8)],
        )
        send_ref[pre + s, pl.ds(rows, 16)] = jnp.concatenate([d_edge, q_edge]).astype(BF16)


def attention_call(lengths, kv_mine, kv_other, qd, pre):
    slots = qd.shape[0]
    key_slots, rows, _ = kv_mine.shape
    tile = 2 * rows
    tiles, groups = key_slots // 2, slots // 2
    reach = MAXLEN // (2 * tile) + 1
    place = lambda s, ordered: s if ordered else bit_reversed(s, slots)
    visits = sum(min(u + pre // 2 + 1, reach) for u in range(groups))
    smem = pl.BlockSpec(memory_space=pltpu.SMEM)
    vmem = pl.BlockSpec(memory_space=pltpu.VMEM)
    return pl.pallas_call(
        functools.partial(attention_kernel, pre, place),
        in_specs=[smem, vmem, vmem, vmem],
        out_specs=[vmem, vmem, vmem, vmem],
        out_shape=[
            jax.ShapeDtypeStruct((slots, rows, LANES), BF16),
            jax.ShapeDtypeStruct((key_slots, rows, LANES), F32),
            jax.ShapeDtypeStruct((slots, 8, LANES), F32),
            jax.ShapeDtypeStruct((key_slots, rows + 16, LANES), BF16),
        ],
        scratch_shapes=[
            pltpu.SMEM((visits,), jnp.int32),
            pltpu.SMEM((visits,), jnp.int32),
            pltpu.VMEM((tiles, 2 * tile, LANES), BF16),
            pltpu.VMEM((tiles, 2 * tile, LANES), BF16),
            pltpu.VMEM((tiles, LANES, 2 * tile), BF16),
            pltpu.VMEM((groups, tile, LANES), BF16),
            pltpu.VMEM((groups, 2 * tile, LANES), BF16),
            pltpu.VMEM((groups, HD, tile), F32),
            pltpu.VMEM((visits, 2 * tile, tile), F32),
            pltpu.VMEM((groups, 8, tile), F32),
            pltpu.VMEM((groups, HD, tile), F32),
            pltpu.VMEM((groups, 8, tile), F32),
            pltpu.VMEM((groups, HD, tile), F32),
            pltpu.VMEM((tiles, 2 * tile, LANES), F32),
            pltpu.VMEM((slots, rows, LANES), F32),
        ],
        compiler_params=params(VMEM_MOST),
        cost_estimate=pl.CostEstimate(
            flops=10 * slots * rows * MAXLEN * LANES,
            bytes_accessed=20 * slots * rows * LANES,
            transcendentals=slots * rows * MAXLEN,
        ),
        name="attention",
    )(lengths, kv_mine, kv_other, qd)


def combine_kernel(cq_ref, mine_ref, edge_ref, got_ref, out_ref):
    slots, rows, _ = cq_ref.shape
    for s in range(slots):
        at = bit_reversed(s, slots)
        out_ref[at, pl.ds(0, rows)] = cq_ref[s]
        got = got_ref[s].astype(F32)
        out_ref[at, pl.ds(rows, rows)] = (mine_ref[s] + got[:rows]).astype(BF16)
        edges = [edge_ref[s] + got[rows : rows + 8], got[rows + 8 :]]
        out_ref[at, pl.ds(2 * rows, 16)] = jnp.concatenate(edges).astype(BF16)


def combine_call(cq, mine, edge, got):
    slots, rows, _ = cq.shape
    vmem = pl.BlockSpec(memory_space=pltpu.VMEM)
    return pl.pallas_call(
        combine_kernel,
        in_specs=[vmem] * 4,
        out_specs=vmem,
        out_shape=jax.ShapeDtypeStruct((slots, 2 * rows + 16, LANES), BF16),
        compiler_params=params(VMEM_SOME),
        name="combine",
    )(cq, mine, edge, got)


def combine_windows(cq, mine, got, pre, side, window, devices):
    slots, rows, _ = cq.shape
    dkv = mine + got[:, :rows].astype(F32)
    back = [(i + window, i) for i in range(devices - window)]
    earlier = lax.ppermute(dkv[:pre].astype(BF16), AXES, back).astype(F32)
    dkv = dkv[pre:].at[slots - pre :].add(earlier).astype(BF16)
    both = jnp.concatenate([cq, dkv], axis=2)
    tails, heads = both[:, rows - 8 :], both[:, :8]
    swapped = [(i, i ^ 1) for i in range(devices)]
    tails_other = lax.ppermute(tails, AXES, swapped)
    heads_other = lax.ppermute(heads, AXES, swapped)
    last = [(i, i + window - 1) for i in range(1, devices - window, 2)]
    tail_past = lax.ppermute(tails[-1:], AXES, last)
    head_next = lax.ppermute(heads[:1], AXES, [(j, i) for i, j in last])
    before = jnp.where(
        side == 0, jnp.concatenate([tail_past, tails_other[:-1]]), tails_other
    )
    after = jnp.where(side == 0, heads_other, jnp.concatenate([heads_other[1:], head_next]))
    edge = jnp.where(jnp.arange(8)[None, :, None] < 4, after, before)
    grads = jnp.concatenate([cq, dkv, edge[..., LANES:], edge[..., :LANES]], axis=1)
    return jnp.stack([grads[bit_reversed(s, slots)] for s in range(slots)])


def back_kernel(
    lengths_ref, r_ref, taps_ref, w_ref, wo_ref, attended_ref, grad_ref, context, grads, padded
):
    heads = r_ref.shape[0]
    rows, width = context.shape
    blk = width // BACK_STEPS
    main, dkv = slice(0, rows), slice(rows, 2 * rows)
    edge_dkv, edge_cq = slice(2 * rows, 2 * rows + 8), slice(2 * rows + 8, 2 * rows + 16)
    pad = jnp.zeros((8, LANES), F32)
    for pair in range(heads // 2):
        lanes = pl.ds(pair * LANES, LANES)
        x, y = (r_ref[2 * pair + i].astype(F32) for i in range(2))
        context[:, lanes] = zip_low(x[main], y[main]).astype(BF16)

        def gather(mix, part, edge):
            return jnp.concatenate([mix(x[part], y[part]), mix(x[edge], y[edge]), pad]).astype(BF16)

        grads[:, lanes] = gather(zip_high, main, edge_cq)
        grads[:, pl.ds(width + pair * LANES, LANES)] = gather(zip_low, dkv, edge_dkv)
        grads[:, pl.ds(2 * width + pair * LANES, LANES)] = gather(zip_high, dkv, edge_dkv)
    first_row = device_index() * rows
    per = blk // LANES
    for step in range(BACK_STEPS):
        part = pl.ds(step * blk, blk)
        mixed = lax.dot_general(
            grads[...], w_ref[part, :], (((1,), (1,)), ((), ())), preferred_element_type=F32
        ).astype(BF16).astype(F32)
        edge = mixed[rows : rows + 8]
        padded[pl.ds(0, 8), part] = edge
        padded[pl.ds(8, rows), part] = mixed[:rows]
        padded[pl.ds(8 + rows, 8), part] = edge
        attended_ref[:, part] = jnp.dot(
            context[...], wo_ref[:, part], preferred_element_type=F32
        ).astype(BF16)
        grad_ref[:, part] = conv_rows(
            padded, range(step * per, (step + 1) * per), taps_ref, lengths_ref, first_row, rows,
            True,
        ).astype(BF16)


def back_call(lengths, r, taps, w_qkv, w_out):
    heads = r.shape[0]
    rows = (r.shape[1] - 16) // 2
    width = heads * HD
    smem = pl.BlockSpec(memory_space=pltpu.SMEM)
    vmem = pl.BlockSpec(memory_space=pltpu.VMEM)
    shape = jax.ShapeDtypeStruct((rows, width), BF16)
    return pl.pallas_call(
        back_kernel,
        in_specs=[smem, vmem, vmem, vmem, vmem],
        out_specs=[vmem, vmem],
        out_shape=[shape, shape],
        scratch_shapes=[
            pltpu.VMEM((rows, width), BF16),
            pltpu.VMEM((rows + 16, 3 * width), BF16),
            pltpu.VMEM((rows + 16, width), F32),
        ],
        compiler_params=params(VMEM_SOME),
        cost_estimate=pl.CostEstimate(
            flops=8 * rows * width * width, bytes_accessed=8 * width * width, transcendentals=0
        ),
        name="back",
    )(lengths, r, taps, w_qkv, w_out)


def bit_reversed(i, count):
    bits = count.bit_length() - 1
    if count != 1 << bits:
        return i
    return sum((i >> b & 1) << (bits - 1 - b) for b in range(bits))


def on_device(tokens, conv_kernel, w_qkv, w_out, lengths, cotangent):
    rows, width = tokens.shape
    heads = width // HD
    devices = lax.axis_size(AXES)
    window = 2 * heads
    windows = devices // window
    pre = MAXLEN // (2 * rows) if windows > 1 else 0
    me = lax.axis_index(AXES)
    same_side = [
        [w * window + 2 * bit_reversed(c, heads) + side for c in range(heads)]
        for w in range(windows)
        for side in range(2)
    ]
    swapped = [(i, i ^ 1) for i in range(devices)]
    up = [(i, i + 1) for i in range(devices - 1)]
    down = [(i + 1, i) for i in range(devices - 1)]

    def exchange(x):
        return lax.all_to_all(
            x, AXES, split_axis=0, concat_axis=0, axis_index_groups=same_side, tiled=True
        )

    before = lax.ppermute(tokens[rows - EDGE :], AXES, up)
    after = lax.ppermute(tokens[:EDGE], AXES, down)
    sent = front_call(lengths, before, tokens, after, conv_kernel, w_qkv, cotangent, w_out)
    qd = exchange(sent)
    kv_mine = qd[:, :rows]
    if pre:
        shift = [(i, i + window) for i in range(devices - window)]
        kv_mine = jnp.stack([kv_mine[bit_reversed(s, heads)] for s in range(heads)])
        kv_mine = jnp.concatenate([lax.ppermute(kv_mine[heads - pre :], AXES, shift), kv_mine])
    kv_other = lax.ppermute(kv_mine, AXES, swapped)
    cq, mine, edge, send = attention_call(lengths, kv_mine, kv_other, qd, pre)
    got = lax.ppermute(send, AXES, swapped)
    if pre:
        grads = combine_windows(cq, mine, got, pre, me % 2, window, devices)
    else:
        grads = combine_call(cq, mine, edge, got)
    return back_call(lengths, exchange(grads), conv_kernel, w_qkv, w_out)


def solution(mesh):
    placed = (P(AXES, None), P(), P(), P(), P(), P(AXES, None))
    return jax.shard_map(
        on_device,
        mesh=mesh,
        in_specs=placed,
        out_specs=(P(AXES, None), P(AXES, None)),
        check_vma=False,
    )
```

```python
import functools
import math

import jax
import jax.numpy as jnp
from jax import lax
from jax.experimental import pallas as pl
from jax.experimental.pallas import tpu as pltpu
from jax.sharding import PartitionSpec as P

HD = 64
KS = 7
HALF = KS // 2
MAXLEN = 2048
AXES = ("ctx", "head")
LANES = 128
EDGE = 16
PER_STEP = 4
FAR = -1e30
FRONT_STEPS = 4
BACK_STEPS = 4
VMEM_ALL = 60 * 1024 * 1024
VMEM_MOST = 44 * 1024 * 1024
VMEM_SOME = 24 * 1024 * 1024
F32 = jnp.float32
BF16 = jnp.bfloat16


def params(limit):
    return pltpu.CompilerParams(vmem_limit_bytes=limit)


def record_span(positions, lengths_ref):
    start = jnp.zeros_like(positions)
    stop = jnp.full_like(positions, jnp.iinfo(jnp.int32).max)
    end = jnp.int32(0)
    for i in range(lengths_ref.shape[0]):
        end = end + lengths_ref[i]
        past = end <= positions
        start = jnp.where(past, end, start)
        stop = jnp.where(past, stop, jnp.minimum(stop, end))
    return start, stop


def device_index():
    return lax.axis_index("ctx") * lax.axis_size("head") + lax.axis_index("head")


def low_lanes(shape):
    return lax.broadcasted_iota(jnp.int32, shape, len(shape) - 1) % LANES < HD


def swap_halves(x):
    return pltpu.roll(x, HD, x.ndim - 1)


def zip_low(x, y):
    return jnp.where(low_lanes(x.shape), x, swap_halves(y))


def zip_high(x, y):
    return jnp.where(low_lanes(x.shape), swap_halves(x), y)


def conv_masks(lengths_ref, first_row, rows):
    pos = first_row + lax.broadcasted_iota(jnp.int32, (rows, LANES), 0)
    start, stop = record_span(pos, lengths_ref)
    return [(pos + (t - HALF) >= start) & (pos + (t - HALF) < stop) for t in range(KS)]


def conv_rows(padded_ref, first_lane, count, kernel_ref, masks, rows, flip):
    pieces = []
    for c in range(count):
        lanes = pl.ds(pl.multiple_of(first_lane + c * LANES, LANES), LANES)
        total = padded_ref[pl.ds(8, rows), lanes]
        for t in range(KS):
            tap = kernel_ref[KS - 1 - t if flip else t, lanes]
            shifted = padded_ref[pl.ds(8 - HALF + t, rows), lanes]
            total = total + jnp.where(masks[t], shifted, 0.0) * tap[None, :]
        pieces.append(total)
    return jnp.concatenate(pieces, axis=1)


def front_kernel(
    lengths_ref, before_ref, after_ref, x_hbm, taps_hbm, w_hbm, cot_hbm, wo_hbm,
    out_ref, x_ref, taps_ref, w_ref, cot_ref, wo_ref, padded, projected, d_rows, sems,
):
    rows, width = x_ref.shape
    blk = width // FRONT_STEPS

    def copy(source, target, i):
        return pltpu.make_async_copy(source, target, sems.at[i])

    whole = [
        copy(source, target, i)
        for i, (source, target) in enumerate(
            ((x_hbm, x_ref), (taps_hbm, taps_ref), (cot_hbm, cot_ref))
        )
    ]

    def weight_copies(step):
        part = pl.ds(pl.multiple_of(step * blk, blk), blk)
        return (
            copy(w_hbm.at[part], w_ref.at[part], 3 + 2 * step),
            copy(wo_hbm.at[part], wo_ref.at[part], 4 + 2 * step),
        )

    for c in whole:
        c.start()
    for step in range(FRONT_STEPS):
        for c in weight_copies(step):
            c.start(priority=step % 2)
    padded[pl.ds(0, 8), :] = before_ref[...].astype(F32)[EDGE - 8 :]
    padded[pl.ds(8 + rows, 8), :] = after_ref[...].astype(F32)[:8]
    for c in whole:
        c.wait()
    padded[pl.ds(8, rows), :] = x_ref[...].astype(F32)
    projected[...] = jnp.zeros_like(projected)
    first_row = device_index() * rows

    def project(step, carry):
        part = pl.ds(pl.multiple_of(step * blk, blk), blk)
        masks = conv_masks(lengths_ref, first_row, rows)
        mixed = conv_rows(
            padded, step * blk, blk // LANES, taps_ref, masks, rows, False
        ).astype(BF16)
        for c in weight_copies(step):
            c.wait()
        projected[...] += jnp.dot(mixed, w_ref[part, :], preferred_element_type=F32)
        d_rows[:, part] = lax.dot_general(
            cot_ref[...], wo_ref[part, :], (((1,), (1,)), ((), ())), preferred_element_type=F32
        )
        return carry

    lax.fori_loop(0, FRONT_STEPS, project, 0)

    def pack(pair, carry):
        at = pl.multiple_of(pair * LANES, LANES)
        q, k, v = (projected[:, pl.ds(i * width + at, LANES)] for i in range(3))
        d = d_rows[:, pl.ds(at, LANES)]
        out_ref[2 * pair] = jnp.concatenate([zip_low(k, v), zip_low(q, d)]).astype(BF16)
        out_ref[2 * pair + 1] = jnp.concatenate([zip_high(k, v), zip_high(q, d)]).astype(BF16)
        return carry

    lax.fori_loop(0, width // LANES, pack, 0)


def front_call(lengths, before, x, after, taps, w_qkv, cotangent, w_out):
    rows, width = x.shape
    heads = width // HD
    smem = pl.BlockSpec(memory_space=pltpu.SMEM)
    vmem = pl.BlockSpec(memory_space=pltpu.VMEM)
    anywhere = pl.BlockSpec(memory_space=pl.ANY)
    return pl.pallas_call(
        front_kernel,
        in_specs=[smem, vmem, vmem] + [anywhere] * 5,
        out_specs=vmem,
        out_shape=jax.ShapeDtypeStruct((heads, 2 * rows, LANES), BF16),
        scratch_shapes=[
            pltpu.VMEM(x.shape, x.dtype),
            pltpu.VMEM(taps.shape, taps.dtype),
            pltpu.VMEM(w_qkv.shape, w_qkv.dtype),
            pltpu.VMEM(cotangent.shape, cotangent.dtype),
            pltpu.VMEM(w_out.shape, w_out.dtype),
            pltpu.VMEM((rows + 16, width), F32),
            pltpu.VMEM((rows, 3 * width), F32),
            pltpu.VMEM((rows, width), F32),
            pltpu.SemaphoreType.DMA((3 + 2 * FRONT_STEPS,)),
        ],
        compiler_params=params(VMEM_ALL),
        cost_estimate=pl.CostEstimate(
            flops=8 * rows * width * width, bytes_accessed=8 * width * width, transcendentals=0
        ),
        name="front",
    )(lengths, before, after, x, taps, w_qkv, cotangent, w_out)


def attention_kernel(
    pre, place, lengths_ref, kv_mine, kv_other, qd_ref,
    cq_ref, dkv_mine, edge_mine, send_ref,
    visit_q, visit_k, keys_ref, marked_ref, turned_ref, query_ref, qd_cat_ref, d_turned_ref, e_ref,
    total_ref, context_ref, row_ref, d_query_ref, acc_ref, cq_full,
):
    slots = qd_ref.shape[0]
    key_slots, rows, _ = kv_mine.shape
    tile = 2 * rows
    tiles, groups = key_slots // 2, slots // 2
    me = device_index()
    window = 2 * slots
    base, parity = me // window * (window * rows), me % 2
    origin = base - pre * tile
    unit = HD**-0.5
    to_exp2 = unit * math.log2(math.e)

    def row_at(slot, side):
        return slot * tile + side * rows + lax.broadcasted_iota(jnp.int32, (rows, 1), 0)

    lane = lax.broadcasted_iota(jnp.int32, (1, LANES), 1)
    starts = jnp.zeros((1, LANES), jnp.int32)
    stops = jnp.zeros((1, LANES), jnp.int32)
    end = jnp.int32(0)
    for i in range(lengths_ref.shape[0]):
        starts = jnp.where(lane == HD + i, end, starts)
        end = end + lengths_ref[i]
        stops = jnp.where(lane == HD + i, end, stops)

    count = jnp.int32(groups)
    for u in range(groups):
        visit_q[u] = u
        visit_k[u] = u + pre // 2
        first = base + u * (2 * tile) + parity * rows
        begin, end = jnp.int32(0), jnp.int32(0)
        for i in range(lengths_ref.shape[0]):
            end = end + lengths_ref[i]
            begin = jnp.where(end <= first, end, begin)
        t_first = jnp.maximum(begin - origin, 0) // (2 * tile)

        def note(t, count, u=u):
            visit_q[count] = u
            visit_k[count] = t
            return count + 1

        count = lax.fori_loop(t_first, u + pre // 2, note, count)

    low = low_lanes((rows, LANES))
    for t in range(tiles):
        for half, source in enumerate((kv_mine, kv_other)):
            side = parity if half == 0 else 1 - parity
            for i in range(2):
                block = source[place(2 * t + i, pre)]
                at = pl.ds(half * tile + i * rows, rows)
                keys_ref[t, at] = block
                turned_ref[t, :, at] = block.T
                pos = origin + row_at(2 * t + i, side)
                mark = jnp.where((pos >= starts) & (pos < stops), 0.0, FAR)
                marked_ref[t, at] = jnp.where(low, block.astype(F32), mark).astype(BF16)
    for ref in (acc_ref, total_ref, context_ref, d_query_ref):
        ref[...] = jnp.zeros_like(ref)
    for u in range(groups):
        for i in range(2):
            qd = qd_ref[place(2 * u + i, 0), pl.ds(rows, rows)]
            at = pl.ds(i * rows, rows)
            d_turned_ref[u, :, at] = qd.T[HD:].astype(F32)
            qd = qd.astype(F32)
            pos = base + row_at(2 * u + i, parity)
            mark = jnp.where((pos >= starts) & (pos < stops), 1.0, 0.0)
            query_ref[u, at] = jnp.where(low, qd, mark).astype(BF16)
            qd_cat_ref[u, at] = jnp.where(low, qd, 0.0).astype(BF16)
            qd_cat_ref[u, pl.ds(tile + i * rows, rows)] = jnp.where(low, 0.0, qd).astype(BF16)

    nt = (((1,), (1,)), ((), ()))
    wide = (2 * tile, tile)
    q_lane = lax.broadcasted_iota(jnp.int32, wide, 1)
    q_row = q_lane // rows * tile + q_lane % rows + parity * rows
    k_sub = lax.broadcasted_iota(jnp.int32, wide, 0)
    side = jnp.where(k_sub < tile, parity, 1 - parity)
    causal = k_sub // rows % 2 * tile + k_sub % rows + side * rows <= q_row

    def forward(i, diagonal):
        u, t = visit_q[i], visit_k[i]
        scores = lax.dot_general(marked_ref[t], query_ref[u], nt, preferred_element_type=F32)
        e = jnp.exp2(scores * to_exp2)
        if diagonal:
            e = jnp.where(causal, e, 0.0)
        e_ref[i] = e
        context = jnp.dot(turned_ref[t, HD:], e.astype(BF16), preferred_element_type=F32)
        return u, jnp.sum(e.reshape(2 * tile // 8, 8, tile), axis=0), context

    def forward_some(diagonal, first, per):
        def run(j, carry):
            for u, total, context in [
                forward(first + per * j + i, diagonal) for i in range(per)
            ]:
                total_ref[u] += total
                context_ref[u] += context
            return carry

        return run

    def run_all(make, first, last):
        steps = (last - first) // PER_STEP
        lax.fori_loop(0, steps, make(first, PER_STEP), 0)
        rest = first + steps * PER_STEP
        lax.fori_loop(0, last - rest, make(rest, 1), 0)

    lax.fori_loop(0, groups // PER_STEP, forward_some(True, 0, PER_STEP), 0)
    run_all(functools.partial(forward_some, False), groups, count)
    for u in range(groups):
        inverse = 1.0 / jnp.sum(total_ref[u], axis=0, keepdims=True)
        context = (context_ref[u] * inverse).astype(BF16).astype(F32)
        context_ref[u] = context
        row_ref[u, pl.ds(0, 1)] = inverse
        row_ref[u, pl.ds(1, 1)] = jnp.sum(d_turned_ref[u] * context, axis=0, keepdims=True)

    def backward(i):
        u, t = visit_q[i], visit_k[i]
        row = row_ref[u]
        probs = e_ref[i] * row[0:1]
        d_probs = lax.dot_general(
            keys_ref[t], qd_cat_ref[u, pl.ds(tile, tile)], nt, preferred_element_type=F32
        )
        d_scores = (probs * (d_probs - row[1:2])).astype(BF16)
        both = jnp.concatenate([d_scores, probs.astype(BF16)], axis=1)
        d_keys = jnp.dot(both, qd_cat_ref[u], preferred_element_type=F32)
        d_queries = jnp.dot(turned_ref[t, :HD], d_scores, preferred_element_type=F32)
        return u, t, d_keys, d_queries

    def backward_some(first, per):
        def run(j, carry):
            for u, t, d_keys, d_queries in [
                backward(first + per * j + i) for i in range(per)
            ]:
                acc_ref[t] += d_keys
                d_query_ref[u] += d_queries
            return carry

        return run

    run_all(backward_some, 0, count)
    for u in range(groups):
        packed = jnp.concatenate([context_ref[u], d_query_ref[u] * unit], axis=0).T
        for i in range(2):
            part = packed[i * rows : (i + 1) * rows]
            cq_full[2 * u + i] = part
            cq_ref[2 * u + i] = part.astype(BF16)
    scale = jnp.where(low_lanes((1, LANES)), unit, 1.0)
    head = lax.broadcasted_iota(jnp.int32, (8, LANES), 0) < 4

    def end_rows(half, slot, first):
        slot = pre + jnp.clip(slot, 0, slots - 1)
        at = half * tile + slot % 2 * rows + first
        return acc_ref[slot // 2, pl.ds(pl.multiple_of(at, 8), 8)] * scale

    for s in range(key_slots):
        part = pl.ds(s % 2 * rows, rows)
        dkv_mine[s] = acc_ref[s // 2, part] * scale
        part = pl.ds(tile + s % 2 * rows, rows)
        send_ref[s, pl.ds(0, rows)] = (acc_ref[s // 2, part] * scale).astype(BF16)
        if s < pre:
            send_ref[s, pl.ds(rows, 16)] = jnp.zeros((16, LANES), BF16)
    for s in range(slots):
        edge_mine[s] = jnp.where(
            head, end_rows(1, s + parity, 0), end_rows(1, s - 1 + parity, rows - 8)
        )
        past, later = s - parity, s + 1 - parity
        d_edge = jnp.where(head, end_rows(0, later, 0), end_rows(0, past, rows - 8))
        q_edge = jnp.where(
            head,
            cq_full[jnp.clip(later, 0, slots - 1), pl.ds(0, 8)],
            cq_full[jnp.clip(past, 0, slots - 1), pl.ds(rows - 8, 8)],
        )
        send_ref[pre + s, pl.ds(rows, 16)] = jnp.concatenate([d_edge, q_edge]).astype(BF16)


def attention_call(lengths, kv_mine, kv_other, qd, pre):
    slots = qd.shape[0]
    key_slots, rows, _ = kv_mine.shape
    tile = 2 * rows
    tiles, groups = key_slots // 2, slots // 2
    reach = MAXLEN // (2 * tile) + 1
    place = lambda s, ordered: s if ordered else bit_reversed(s, slots)
    visits = sum(min(u + pre // 2 + 1, reach) for u in range(groups))
    smem = pl.BlockSpec(memory_space=pltpu.SMEM)
    vmem = pl.BlockSpec(memory_space=pltpu.VMEM)
    return pl.pallas_call(
        functools.partial(attention_kernel, pre, place),
        in_specs=[smem, vmem, vmem, vmem],
        out_specs=[vmem, vmem, vmem, vmem],
        out_shape=[
            jax.ShapeDtypeStruct((slots, rows, LANES), BF16),
            jax.ShapeDtypeStruct((key_slots, rows, LANES), F32),
            jax.ShapeDtypeStruct((slots, 8, LANES), F32),
            jax.ShapeDtypeStruct((key_slots, rows + 16, LANES), BF16),
        ],
        scratch_shapes=[
            pltpu.SMEM((visits,), jnp.int32),
            pltpu.SMEM((visits,), jnp.int32),
            pltpu.VMEM((tiles, 2 * tile, LANES), BF16),
            pltpu.VMEM((tiles, 2 * tile, LANES), BF16),
            pltpu.VMEM((tiles, LANES, 2 * tile), BF16),
            pltpu.VMEM((groups, tile, LANES), BF16),
            pltpu.VMEM((groups, 2 * tile, LANES), BF16),
            pltpu.VMEM((groups, HD, tile), F32),
            pltpu.VMEM((visits, 2 * tile, tile), F32),
            pltpu.VMEM((groups, 8, tile), F32),
            pltpu.VMEM((groups, HD, tile), F32),
            pltpu.VMEM((groups, 8, tile), F32),
            pltpu.VMEM((groups, HD, tile), F32),
            pltpu.VMEM((tiles, 2 * tile, LANES), F32),
            pltpu.VMEM((slots, rows, LANES), F32),
        ],
        compiler_params=params(VMEM_MOST),
        cost_estimate=pl.CostEstimate(
            flops=10 * slots * rows * MAXLEN * LANES,
            bytes_accessed=20 * slots * rows * LANES,
            transcendentals=slots * rows * MAXLEN,
        ),
        name="attention",
    )(lengths, kv_mine, kv_other, qd)


def combine_kernel(cq_ref, mine_ref, edge_ref, got_ref, out_ref):
    slots, rows, _ = cq_ref.shape
    for s in range(slots):
        at = bit_reversed(s, slots)
        out_ref[at, pl.ds(0, rows)] = cq_ref[s]
        got = got_ref[s].astype(F32)
        out_ref[at, pl.ds(rows, rows)] = (mine_ref[s] + got[:rows]).astype(BF16)
        edges = [edge_ref[s] + got[rows : rows + 8], got[rows + 8 :]]
        out_ref[at, pl.ds(2 * rows, 16)] = jnp.concatenate(edges).astype(BF16)


def combine_call(cq, mine, edge, got):
    slots, rows, _ = cq.shape
    vmem = pl.BlockSpec(memory_space=pltpu.VMEM)
    return pl.pallas_call(
        combine_kernel,
        in_specs=[vmem] * 4,
        out_specs=vmem,
        out_shape=jax.ShapeDtypeStruct((slots, 2 * rows + 16, LANES), BF16),
        compiler_params=params(VMEM_SOME),
        name="combine",
    )(cq, mine, edge, got)


def combine_windows(cq, mine, got, pre, side, window, devices):
    slots, rows, _ = cq.shape
    dkv = mine + got[:, :rows].astype(F32)
    back = [(i + window, i) for i in range(devices - window)]
    earlier = lax.ppermute(dkv[:pre].astype(BF16), AXES, back).astype(F32)
    dkv = dkv[pre:].at[slots - pre :].add(earlier).astype(BF16)
    both = jnp.concatenate([cq, dkv], axis=2)
    tails, heads = both[:, rows - 8 :], both[:, :8]
    swapped = [(i, i ^ 1) for i in range(devices)]
    tails_other = lax.ppermute(tails, AXES, swapped)
    heads_other = lax.ppermute(heads, AXES, swapped)
    last = [(i, i + window - 1) for i in range(1, devices - window, 2)]
    tail_past = lax.ppermute(tails[-1:], AXES, last)
    head_next = lax.ppermute(heads[:1], AXES, [(j, i) for i, j in last])
    before = jnp.where(
        side == 0, jnp.concatenate([tail_past, tails_other[:-1]]), tails_other
    )
    after = jnp.where(side == 0, heads_other, jnp.concatenate([heads_other[1:], head_next]))
    edge = jnp.where(jnp.arange(8)[None, :, None] < 4, after, before)
    grads = jnp.concatenate([cq, dkv, edge[..., LANES:], edge[..., :LANES]], axis=1)
    return jnp.stack([grads[bit_reversed(s, slots)] for s in range(slots)])


def back_kernel(
    lengths_ref, r_ref, taps_ref, w_ref, wo_ref, attended_ref, grad_ref, context, grads, padded
):
    heads = r_ref.shape[0]
    rows, width = context.shape
    blk = width // BACK_STEPS
    main, dkv = slice(0, rows), slice(rows, 2 * rows)
    edge_dkv, edge_cq = slice(2 * rows, 2 * rows + 8), slice(2 * rows + 8, 2 * rows + 16)
    pad = jnp.zeros((8, LANES), F32)

    def unpack(pair, carry):
        at = pl.multiple_of(pair * LANES, LANES)
        x, y = (r_ref[2 * pair + i].astype(F32) for i in range(2))
        context[:, pl.ds(at, LANES)] = zip_low(x[main], y[main]).astype(BF16)

        def gather(mix, part, edge):
            return jnp.concatenate([mix(x[part], y[part]), mix(x[edge], y[edge]), pad]).astype(BF16)

        grads[:, pl.ds(at, LANES)] = gather(zip_high, main, edge_cq)
        grads[:, pl.ds(width + at, LANES)] = gather(zip_low, dkv, edge_dkv)
        grads[:, pl.ds(2 * width + at, LANES)] = gather(zip_high, dkv, edge_dkv)
        return carry

    lax.fori_loop(0, heads // 2, unpack, 0)
    first_row = device_index() * rows

    def project(step, carry):
        part = pl.ds(pl.multiple_of(step * blk, blk), blk)
        mixed = lax.dot_general(
            grads[...], w_ref[part, :], (((1,), (1,)), ((), ())), preferred_element_type=F32
        ).astype(BF16).astype(F32)
        edge = mixed[rows : rows + 8]
        padded[pl.ds(0, 8), part] = edge
        padded[pl.ds(8, rows), part] = mixed[:rows]
        padded[pl.ds(8 + rows, 8), part] = edge
        attended_ref[:, part] = jnp.dot(
            context[...], wo_ref[:, part], preferred_element_type=F32
        ).astype(BF16)
        masks = conv_masks(lengths_ref, first_row, rows)
        grad_ref[:, part] = conv_rows(
            padded, step * blk, blk // LANES, taps_ref, masks, rows, True
        ).astype(BF16)
        return carry

    lax.fori_loop(0, BACK_STEPS, project, 0)


def back_call(lengths, r, taps, w_qkv, w_out):
    heads = r.shape[0]
    rows = (r.shape[1] - 16) // 2
    width = heads * HD
    smem = pl.BlockSpec(memory_space=pltpu.SMEM)
    vmem = pl.BlockSpec(memory_space=pltpu.VMEM)
    shape = jax.ShapeDtypeStruct((rows, width), BF16)
    return pl.pallas_call(
        back_kernel,
        in_specs=[smem, vmem, vmem, vmem, vmem],
        out_specs=[vmem, vmem],
        out_shape=[shape, shape],
        scratch_shapes=[
            pltpu.VMEM((rows, width), BF16),
            pltpu.VMEM((rows + 16, 3 * width), BF16),
            pltpu.VMEM((rows + 16, width), F32),
        ],
        compiler_params=params(VMEM_SOME),
        cost_estimate=pl.CostEstimate(
            flops=8 * rows * width * width, bytes_accessed=8 * width * width, transcendentals=0
        ),
        name="back",
    )(lengths, r, taps, w_qkv, w_out)


def bit_reversed(i, count):
    bits = count.bit_length() - 1
    if count != 1 << bits:
        return i
    return sum((i >> b & 1) << (bits - 1 - b) for b in range(bits))


def on_device(tokens, conv_kernel, w_qkv, w_out, lengths, cotangent):
    rows, width = tokens.shape
    heads = width // HD
    devices = lax.axis_size(AXES)
    window = 2 * heads
    windows = devices // window
    pre = MAXLEN // (2 * rows) if windows > 1 else 0
    me = lax.axis_index(AXES)
    same_side = [
        [w * window + 2 * bit_reversed(c, heads) + side for c in range(heads)]
        for w in range(windows)
        for side in range(2)
    ]
    swapped = [(i, i ^ 1) for i in range(devices)]
    up = [(i, i + 1) for i in range(devices - 1)]
    down = [(i + 1, i) for i in range(devices - 1)]

    def exchange(x):
        return lax.all_to_all(
            x, AXES, split_axis=0, concat_axis=0, axis_index_groups=same_side, tiled=True
        )

    before = lax.ppermute(tokens[rows - EDGE :], AXES, up)
    after = lax.ppermute(tokens[:EDGE], AXES, down)
    sent = front_call(lengths, before, tokens, after, conv_kernel, w_qkv, cotangent, w_out)
    qd = exchange(sent)
    kv_mine = qd[:, :rows]
    if pre:
        shift = [(i, i + window) for i in range(devices - window)]
        kv_mine = jnp.stack([kv_mine[bit_reversed(s, heads)] for s in range(heads)])
        kv_mine = jnp.concatenate([lax.ppermute(kv_mine[heads - pre :], AXES, shift), kv_mine])
    kv_other = lax.ppermute(kv_mine, AXES, swapped)
    cq, mine, edge, send = attention_call(lengths, kv_mine, kv_other, qd, pre)
    got = lax.ppermute(send, AXES, swapped)
    if pre:
        grads = combine_windows(cq, mine, got, pre, me % 2, window, devices)
    else:
        grads = combine_call(cq, mine, edge, got)
    return back_call(lengths, exchange(grads), conv_kernel, w_qkv, w_out)


def solution(mesh):
    placed = (P(AXES, None), P(), P(), P(), P(), P(AXES, None))
    return jax.shard_map(
        on_device,
        mesh=mesh,
        in_specs=placed,
        out_specs=(P(AXES, None), P(AXES, None)),
        check_vma=False,
    )
```

```python
import functools
import math

import jax
import jax.numpy as jnp
from jax import lax
from jax.experimental import pallas as pl
from jax.experimental.pallas import tpu as pltpu
from jax.sharding import PartitionSpec as P

HD = 64
KS = 7
HALF = KS // 2
MAXLEN = 2048
AXES = ("ctx", "head")
LANES = 128
EDGE = 16
PER_STEP = 4
FAR = -1e30
FRONT_STEPS = 4
BACK_STEPS = 4
VMEM_ALL = 60 * 1024 * 1024
VMEM_MOST = 44 * 1024 * 1024
VMEM_SOME = 24 * 1024 * 1024
F32 = jnp.float32
BF16 = jnp.bfloat16


def params(limit):
    return pltpu.CompilerParams(vmem_limit_bytes=limit)


def record_span(positions, lengths_ref):
    start = jnp.zeros_like(positions)
    stop = jnp.full_like(positions, jnp.iinfo(jnp.int32).max)
    end = jnp.int32(0)
    for i in range(lengths_ref.shape[0]):
        end = end + lengths_ref[i]
        past = end <= positions
        start = jnp.where(past, end, start)
        stop = jnp.where(past, stop, jnp.minimum(stop, end))
    return start, stop


def device_index():
    return lax.axis_index("ctx") * lax.axis_size("head") + lax.axis_index("head")


def low_lanes(shape):
    return lax.broadcasted_iota(jnp.int32, shape, len(shape) - 1) % LANES < HD


def swap_halves(x):
    return pltpu.roll(x, HD, x.ndim - 1)


def zip_low(x, y):
    return jnp.where(low_lanes(x.shape), x, swap_halves(y))


def zip_high(x, y):
    return jnp.where(low_lanes(x.shape), swap_halves(x), y)


def conv_rows(padded_ref, cols, kernel_ref, lengths_ref, first_row, rows, flip):
    pos = first_row + lax.broadcasted_iota(jnp.int32, (rows, LANES), 0)
    start, stop = record_span(pos, lengths_ref)
    masks = []
    for t in range(KS):
        at = pos + (t - HALF)
        masks.append((at >= start) & (at < stop))
    pieces = []
    for c in cols:
        lanes = pl.ds(c * LANES, LANES)
        total = padded_ref[pl.ds(8, rows), lanes]
        for t in range(KS):
            tap = kernel_ref[KS - 1 - t if flip else t, lanes]
            shifted = padded_ref[pl.ds(8 - HALF + t, rows), lanes]
            total = total + jnp.where(masks[t], shifted, 0.0) * tap[None, :]
        pieces.append(total)
    return jnp.concatenate(pieces, axis=1)


def front_kernel(
    lengths_ref, before_ref, after_ref, x_hbm, taps_hbm, w_hbm, cot_hbm, wo_hbm,
    out_ref, x_ref, taps_ref, w_ref, cot_ref, wo_ref, padded, projected, d_rows, sems,
):
    rows, width = x_ref.shape
    blk = width // FRONT_STEPS

    def copy(source, target, i):
        return pltpu.make_async_copy(source, target, sems.at[i])

    whole = [
        copy(source, target, i)
        for i, (source, target) in enumerate(
            ((x_hbm, x_ref), (taps_hbm, taps_ref), (cot_hbm, cot_ref))
        )
    ]
    parts = []
    for step in range(FRONT_STEPS):
        part = pl.ds(step * blk, blk)
        at = 3 + 2 * step
        parts.append(
            (
                copy(w_hbm.at[part], w_ref.at[part], at),
                copy(wo_hbm.at[part], wo_ref.at[part], at + 1),
            )
        )
    for c in whole:
        c.start()
    for pair in parts:
        for c in pair:
            c.start()
    padded[pl.ds(0, 8), :] = before_ref[...].astype(F32)[EDGE - 8 :]
    padded[pl.ds(8 + rows, 8), :] = after_ref[...].astype(F32)[:8]
    for c in whole:
        c.wait()
    padded[pl.ds(8, rows), :] = x_ref[...].astype(F32)
    first_row = device_index() * rows
    per = blk // LANES
    for step in range(FRONT_STEPS):
        mixed = conv_rows(
            padded, range(step * per, (step + 1) * per), taps_ref, lengths_ref, first_row, rows,
            False,
        ).astype(BF16)
        parts[step][0].wait()
        part = jnp.dot(mixed, w_ref[pl.ds(step * blk, blk), :], preferred_element_type=F32)
        if step == 0:
            projected[...] = part
        else:
            projected[...] += part
        parts[step][1].wait()
        d_rows[:, pl.ds(step * blk, blk)] = lax.dot_general(
            wo_ref[pl.ds(step * blk, blk), :], cot_ref[...], (((1,), (1,)), ((), ())),
            preferred_element_type=F32,
        ).T
    for pair in range(width // LANES):
        lanes = pl.ds(pair * LANES, LANES)
        q, k, v = (projected[:, pl.ds(i * width + pair * LANES, LANES)] for i in range(3))
        d = d_rows[:, lanes]
        out_ref[2 * pair] = jnp.concatenate([zip_low(k, v), zip_low(q, d)]).astype(BF16)
        out_ref[2 * pair + 1] = jnp.concatenate([zip_high(k, v), zip_high(q, d)]).astype(BF16)


def front_call(lengths, before, x, after, taps, w_qkv, cotangent, w_out):
    rows, width = x.shape
    heads = width // HD
    smem = pl.BlockSpec(memory_space=pltpu.SMEM)
    vmem = pl.BlockSpec(memory_space=pltpu.VMEM)
    anywhere = pl.BlockSpec(memory_space=pl.ANY)
    return pl.pallas_call(
        front_kernel,
        in_specs=[smem, vmem, vmem] + [anywhere] * 5,
        out_specs=vmem,
        out_shape=jax.ShapeDtypeStruct((heads, 2 * rows, LANES), BF16),
        scratch_shapes=[
            pltpu.VMEM(x.shape, x.dtype),
            pltpu.VMEM(taps.shape, taps.dtype),
            pltpu.VMEM(w_qkv.shape, w_qkv.dtype),
            pltpu.VMEM(cotangent.shape, cotangent.dtype),
            pltpu.VMEM(w_out.shape, w_out.dtype),
            pltpu.VMEM((rows + 16, width), F32),
            pltpu.VMEM((rows, 3 * width), F32),
            pltpu.VMEM((rows, width), F32),
            pltpu.SemaphoreType.DMA((3 + 2 * FRONT_STEPS,)),
        ],
        compiler_params=params(VMEM_ALL),
        cost_estimate=pl.CostEstimate(
            flops=8 * rows * width * width, bytes_accessed=8 * width * width, transcendentals=0
        ),
        name="front",
    )(lengths, before, after, x, taps, w_qkv, cotangent, w_out)


def attention_kernel(
    pre, place, lengths_ref, kv_mine, kv_other, qd_ref,
    cq_ref, dkv_mine, edge_mine, send_ref,
    visit_q, visit_k, keys_ref, marked_ref, turned_ref, query_ref, qd_cat_ref, d_turned_ref, e_ref,
    total_ref, context_ref, row_ref, d_query_ref, acc_ref, cq_full,
):
    slots = qd_ref.shape[0]
    key_slots, rows, _ = kv_mine.shape
    tile = 2 * rows
    tiles, groups = key_slots // 2, slots // 2
    me = device_index()
    window = 2 * slots
    base, parity = me // window * (window * rows), me % 2
    origin = base - pre * tile
    unit = HD**-0.5
    to_exp2 = unit * math.log2(math.e)

    def row_at(slot, side):
        return slot * tile + side * rows + lax.broadcasted_iota(jnp.int32, (rows, 1), 0)

    lane = lax.broadcasted_iota(jnp.int32, (1, LANES), 1)
    starts = jnp.zeros((1, LANES), jnp.int32)
    stops = jnp.zeros((1, LANES), jnp.int32)
    end = jnp.int32(0)
    for i in range(lengths_ref.shape[0]):
        starts = jnp.where(lane == HD + i, end, starts)
        end = end + lengths_ref[i]
        stops = jnp.where(lane == HD + i, end, stops)

    count = jnp.int32(groups)
    for u in range(groups):
        visit_q[u] = u
        visit_k[u] = u + pre // 2
        first = base + u * (2 * tile) + parity * rows
        begin, end = jnp.int32(0), jnp.int32(0)
        for i in range(lengths_ref.shape[0]):
            end = end + lengths_ref[i]
            begin = jnp.where(end <= first, end, begin)
        t_first = jnp.maximum(begin - origin, 0) // (2 * tile)

        def note(t, count, u=u):
            visit_q[count] = u
            visit_k[count] = t
            return count + 1

        count = lax.fori_loop(t_first, u + pre // 2, note, count)

    low = low_lanes((rows, LANES))
    for t in range(tiles):
        for half, source in enumerate((kv_mine, kv_other)):
            side = parity if half == 0 else 1 - parity
            for i in range(2):
                block = source[place(2 * t + i, pre)]
                at = pl.ds(half * tile + i * rows, rows)
                keys_ref[t, at] = block
                turned_ref[t, :, at] = block.T
                pos = origin + row_at(2 * t + i, side)
                mark = jnp.where((pos >= starts) & (pos < stops), 0.0, FAR)
                marked_ref[t, at] = jnp.where(low, block.astype(F32), mark).astype(BF16)
    for ref in (acc_ref, total_ref, context_ref, d_query_ref):
        ref[...] = jnp.zeros_like(ref)
    for u in range(groups):
        for i in range(2):
            qd = qd_ref[place(2 * u + i, 0), pl.ds(rows, rows)]
            at = pl.ds(i * rows, rows)
            d_turned_ref[u, :, at] = qd.T[HD:].astype(F32)
            qd = qd.astype(F32)
            pos = base + row_at(2 * u + i, parity)
            mark = jnp.where((pos >= starts) & (pos < stops), 1.0, 0.0)
            query_ref[u, at] = jnp.where(low, qd, mark).astype(BF16)
            qd_cat_ref[u, at] = jnp.where(low, qd, 0.0).astype(BF16)
            qd_cat_ref[u, pl.ds(tile + i * rows, rows)] = jnp.where(low, 0.0, qd).astype(BF16)

    nt = (((1,), (1,)), ((), ()))
    wide = (2 * tile, tile)
    q_lane = lax.broadcasted_iota(jnp.int32, wide, 1)
    q_row = q_lane // rows * tile + q_lane % rows + parity * rows
    k_sub = lax.broadcasted_iota(jnp.int32, wide, 0)
    side = jnp.where(k_sub < tile, parity, 1 - parity)
    causal = k_sub // rows % 2 * tile + k_sub % rows + side * rows <= q_row

    def forward(i, diagonal):
        u, t = visit_q[i], visit_k[i]
        scores = lax.dot_general(marked_ref[t], query_ref[u], nt, preferred_element_type=F32)
        e = jnp.exp2(scores * to_exp2)
        if diagonal:
            e = jnp.where(causal, e, 0.0)
        e_ref[i] = e
        context = jnp.dot(turned_ref[t, HD:], e.astype(BF16), preferred_element_type=F32)
        return u, jnp.sum(e.reshape(2 * tile // 8, 8, tile), axis=0), context

    def forward_some(diagonal, first, per):
        def run(j, carry):
            for u, total, context in [
                forward(first + per * j + i, diagonal) for i in range(per)
            ]:
                total_ref[u] += total
                context_ref[u] += context
            return carry

        return run

    def run_all(make, first, last):
        steps = (last - first) // PER_STEP
        lax.fori_loop(0, steps, make(first, PER_STEP), 0)
        rest = first + steps * PER_STEP
        lax.fori_loop(0, last - rest, make(rest, 1), 0)

    lax.fori_loop(0, groups // PER_STEP, forward_some(True, 0, PER_STEP), 0)
    run_all(functools.partial(forward_some, False), groups, count)
    for u in range(groups):
        inverse = 1.0 / jnp.sum(total_ref[u], axis=0, keepdims=True)
        context = (context_ref[u] * inverse).astype(BF16).astype(F32)
        context_ref[u] = context
        row_ref[u, pl.ds(0, 1)] = inverse
        row_ref[u, pl.ds(1, 1)] = jnp.sum(d_turned_ref[u] * context, axis=0, keepdims=True)

    def backward(i):
        u, t = visit_q[i], visit_k[i]
        row = row_ref[u]
        probs = e_ref[i] * row[0:1]
        d_probs = lax.dot_general(
            keys_ref[t], qd_cat_ref[u, pl.ds(tile, tile)], nt, preferred_element_type=F32
        )
        d_scores = (probs * (d_probs - row[1:2])).astype(BF16)
        both = jnp.concatenate([d_scores, probs.astype(BF16)], axis=1)
        d_keys = jnp.dot(both, qd_cat_ref[u], preferred_element_type=F32)
        d_queries = jnp.dot(turned_ref[t, :HD], d_scores, preferred_element_type=F32)
        return u, t, d_keys, d_queries

    def backward_some(first, per):
        def run(j, carry):
            for u, t, d_keys, d_queries in [
                backward(first + per * j + i) for i in range(per)
            ]:
                acc_ref[t] += d_keys
                d_query_ref[u] += d_queries
            return carry

        return run

    run_all(backward_some, 0, count)
    for u in range(groups):
        packed = jnp.concatenate([context_ref[u], d_query_ref[u] * unit], axis=0).T
        for i in range(2):
            part = packed[i * rows : (i + 1) * rows]
            cq_full[2 * u + i] = part
            cq_ref[2 * u + i] = part.astype(BF16)
    scale = jnp.where(low_lanes((1, LANES)), unit, 1.0)
    head = lax.broadcasted_iota(jnp.int32, (8, LANES), 0) < 4

    def end_rows(half, slot, first):
        slot = pre + jnp.clip(slot, 0, slots - 1)
        at = half * tile + slot % 2 * rows + first
        return acc_ref[slot // 2, pl.ds(pl.multiple_of(at, 8), 8)] * scale

    for s in range(key_slots):
        part = pl.ds(s % 2 * rows, rows)
        dkv_mine[s] = acc_ref[s // 2, part] * scale
        part = pl.ds(tile + s % 2 * rows, rows)
        send_ref[s, pl.ds(0, rows)] = (acc_ref[s // 2, part] * scale).astype(BF16)
        if s < pre:
            send_ref[s, pl.ds(rows, 16)] = jnp.zeros((16, LANES), BF16)
    for s in range(slots):
        edge_mine[s] = jnp.where(
            head, end_rows(1, s + parity, 0), end_rows(1, s - 1 + parity, rows - 8)
        )
        past, later = s - parity, s + 1 - parity
        d_edge = jnp.where(head, end_rows(0, later, 0), end_rows(0, past, rows - 8))
        q_edge = jnp.where(
            head,
            cq_full[jnp.clip(later, 0, slots - 1), pl.ds(0, 8)],
            cq_full[jnp.clip(past, 0, slots - 1), pl.ds(rows - 8, 8)],
        )
        send_ref[pre + s, pl.ds(rows, 16)] = jnp.concatenate([d_edge, q_edge]).astype(BF16)


def attention_call(lengths, kv_mine, kv_other, qd, pre):
    slots = qd.shape[0]
    key_slots, rows, _ = kv_mine.shape
    tile = 2 * rows
    tiles, groups = key_slots // 2, slots // 2
    reach = MAXLEN // (2 * tile) + 1
    place = lambda s, ordered: s if ordered else bit_reversed(s, slots)
    visits = sum(min(u + pre // 2 + 1, reach) for u in range(groups))
    smem = pl.BlockSpec(memory_space=pltpu.SMEM)
    vmem = pl.BlockSpec(memory_space=pltpu.VMEM)
    return pl.pallas_call(
        functools.partial(attention_kernel, pre, place),
        in_specs=[smem, vmem, vmem, vmem],
        out_specs=[vmem, vmem, vmem, vmem],
        out_shape=[
            jax.ShapeDtypeStruct((slots, rows, LANES), BF16),
            jax.ShapeDtypeStruct((key_slots, rows, LANES), F32),
            jax.ShapeDtypeStruct((slots, 8, LANES), F32),
            jax.ShapeDtypeStruct((key_slots, rows + 16, LANES), BF16),
        ],
        scratch_shapes=[
            pltpu.SMEM((visits,), jnp.int32),
            pltpu.SMEM((visits,), jnp.int32),
            pltpu.VMEM((tiles, 2 * tile, LANES), BF16),
            pltpu.VMEM((tiles, 2 * tile, LANES), BF16),
            pltpu.VMEM((tiles, LANES, 2 * tile), BF16),
            pltpu.VMEM((groups, tile, LANES), BF16),
            pltpu.VMEM((groups, 2 * tile, LANES), BF16),
            pltpu.VMEM((groups, HD, tile), F32),
            pltpu.VMEM((visits, 2 * tile, tile), F32),
            pltpu.VMEM((groups, 8, tile), F32),
            pltpu.VMEM((groups, HD, tile), F32),
            pltpu.VMEM((groups, 8, tile), F32),
            pltpu.VMEM((groups, HD, tile), F32),
            pltpu.VMEM((tiles, 2 * tile, LANES), F32),
            pltpu.VMEM((slots, rows, LANES), F32),
        ],
        compiler_params=params(VMEM_MOST),
        cost_estimate=pl.CostEstimate(
            flops=10 * slots * rows * MAXLEN * LANES,
            bytes_accessed=20 * slots * rows * LANES,
            transcendentals=slots * rows * MAXLEN,
        ),
        name="attention",
    )(lengths, kv_mine, kv_other, qd)


def combine_kernel(cq_ref, mine_ref, edge_ref, got_ref, out_ref):
    slots, rows, _ = cq_ref.shape
    for s in range(slots):
        at = bit_reversed(s, slots)
        out_ref[at, pl.ds(0, rows)] = cq_ref[s]
        got = got_ref[s].astype(F32)
        out_ref[at, pl.ds(rows, rows)] = (mine_ref[s] + got[:rows]).astype(BF16)
        edges = [edge_ref[s] + got[rows : rows + 8], got[rows + 8 :]]
        out_ref[at, pl.ds(2 * rows, 16)] = jnp.concatenate(edges).astype(BF16)


def combine_call(cq, mine, edge, got):
    slots, rows, _ = cq.shape
    vmem = pl.BlockSpec(memory_space=pltpu.VMEM)
    return pl.pallas_call(
        combine_kernel,
        in_specs=[vmem] * 4,
        out_specs=vmem,
        out_shape=jax.ShapeDtypeStruct((slots, 2 * rows + 16, LANES), BF16),
        compiler_params=params(VMEM_SOME),
        name="combine",
    )(cq, mine, edge, got)


def combine_windows(cq, mine, got, pre, side, window, devices):
    slots, rows, _ = cq.shape
    dkv = mine + got[:, :rows].astype(F32)
    back = [(i + window, i) for i in range(devices - window)]
    earlier = lax.ppermute(dkv[:pre].astype(BF16), AXES, back).astype(F32)
    dkv = dkv[pre:].at[slots - pre :].add(earlier).astype(BF16)
    both = jnp.concatenate([cq, dkv], axis=2)
    tails, heads = both[:, rows - 8 :], both[:, :8]
    swapped = [(i, i ^ 1) for i in range(devices)]
    tails_other = lax.ppermute(tails, AXES, swapped)
    heads_other = lax.ppermute(heads, AXES, swapped)
    last = [(i, i + window - 1) for i in range(1, devices - window, 2)]
    tail_past = lax.ppermute(tails[-1:], AXES, last)
    head_next = lax.ppermute(heads[:1], AXES, [(j, i) for i, j in last])
    before = jnp.where(
        side == 0, jnp.concatenate([tail_past, tails_other[:-1]]), tails_other
    )
    after = jnp.where(side == 0, heads_other, jnp.concatenate([heads_other[1:], head_next]))
    edge = jnp.where(jnp.arange(8)[None, :, None] < 4, after, before)
    grads = jnp.concatenate([cq, dkv, edge[..., LANES:], edge[..., :LANES]], axis=1)
    return jnp.stack([grads[bit_reversed(s, slots)] for s in range(slots)])


def back_kernel(
    lengths_ref, r_ref, taps_ref, w_ref, wo_ref, attended_ref, grad_ref, context, grads, padded
):
    heads = r_ref.shape[0]
    rows, width = context.shape
    blk = width // BACK_STEPS
    main, dkv = slice(0, rows), slice(rows, 2 * rows)
    edge_dkv, edge_cq = slice(2 * rows, 2 * rows + 8), slice(2 * rows + 8, 2 * rows + 16)
    pad = jnp.zeros((8, LANES), F32)
    for pair in range(heads // 2):
        lanes = pl.ds(pair * LANES, LANES)
        x, y = (r_ref[2 * pair + i].astype(F32) for i in range(2))
        context[:, lanes] = zip_low(x[main], y[main]).astype(BF16)

        def gather(mix, part, edge):
            return jnp.concatenate([mix(x[part], y[part]), mix(x[edge], y[edge]), pad]).astype(BF16)

        grads[:, lanes] = gather(zip_high, main, edge_cq)
        grads[:, pl.ds(width + pair * LANES, LANES)] = gather(zip_low, dkv, edge_dkv)
        grads[:, pl.ds(2 * width + pair * LANES, LANES)] = gather(zip_high, dkv, edge_dkv)
    first_row = device_index() * rows
    per = blk // LANES
    for step in range(BACK_STEPS):
        part = pl.ds(step * blk, blk)
        mixed = lax.dot_general(
            w_ref[part, :], grads[...], (((1,), (1,)), ((), ())), preferred_element_type=F32
        ).T.astype(BF16).astype(F32)
        edge = mixed[rows : rows + 8]
        padded[pl.ds(0, 8), part] = edge
        padded[pl.ds(8, rows), part] = mixed[:rows]
        padded[pl.ds(8 + rows, 8), part] = edge
        attended_ref[:, part] = jnp.dot(
            context[...], wo_ref[:, part], preferred_element_type=F32
        ).astype(BF16)
        grad_ref[:, part] = conv_rows(
            padded, range(step * per, (step + 1) * per), taps_ref, lengths_ref, first_row, rows,
            True,
        ).astype(BF16)


def back_call(lengths, r, taps, w_qkv, w_out):
    heads = r.shape[0]
    rows = (r.shape[1] - 16) // 2
    width = heads * HD
    smem = pl.BlockSpec(memory_space=pltpu.SMEM)
    vmem = pl.BlockSpec(memory_space=pltpu.VMEM)
    shape = jax.ShapeDtypeStruct((rows, width), BF16)
    return pl.pallas_call(
        back_kernel,
        in_specs=[smem, vmem, vmem, vmem, vmem],
        out_specs=[vmem, vmem],
        out_shape=[shape, shape],
        scratch_shapes=[
            pltpu.VMEM((rows, width), BF16),
            pltpu.VMEM((rows + 16, 3 * width), BF16),
            pltpu.VMEM((rows + 16, width), F32),
        ],
        compiler_params=params(VMEM_SOME),
        cost_estimate=pl.CostEstimate(
            flops=8 * rows * width * width, bytes_accessed=8 * width * width, transcendentals=0
        ),
        name="back",
    )(lengths, r, taps, w_qkv, w_out)


def bit_reversed(i, count):
    bits = count.bit_length() - 1
    if count != 1 << bits:
        return i
    return sum((i >> b & 1) << (bits - 1 - b) for b in range(bits))


def on_device(tokens, conv_kernel, w_qkv, w_out, lengths, cotangent):
    rows, width = tokens.shape
    heads = width // HD
    devices = lax.axis_size(AXES)
    window = 2 * heads
    windows = devices // window
    pre = MAXLEN // (2 * rows) if windows > 1 else 0
    me = lax.axis_index(AXES)
    same_side = [
        [w * window + 2 * bit_reversed(c, heads) + side for c in range(heads)]
        for w in range(windows)
        for side in range(2)
    ]
    swapped = [(i, i ^ 1) for i in range(devices)]
    up = [(i, i + 1) for i in range(devices - 1)]
    down = [(i + 1, i) for i in range(devices - 1)]

    def exchange(x):
        return lax.all_to_all(
            x, AXES, split_axis=0, concat_axis=0, axis_index_groups=same_side, tiled=True
        )

    before = lax.ppermute(tokens[rows - EDGE :], AXES, up)
    after = lax.ppermute(tokens[:EDGE], AXES, down)
    sent = front_call(lengths, before, tokens, after, conv_kernel, w_qkv, cotangent, w_out)
    qd = exchange(sent)
    kv_mine = qd[:, :rows]
    if pre:
        shift = [(i, i + window) for i in range(devices - window)]
        kv_mine = jnp.stack([kv_mine[bit_reversed(s, heads)] for s in range(heads)])
        kv_mine = jnp.concatenate([lax.ppermute(kv_mine[heads - pre :], AXES, shift), kv_mine])
    kv_other = lax.ppermute(kv_mine, AXES, swapped)
    cq, mine, edge, send = attention_call(lengths, kv_mine, kv_other, qd, pre)
    got = lax.ppermute(send, AXES, swapped)
    if pre:
        grads = combine_windows(cq, mine, got, pre, me % 2, window, devices)
    else:
        grads = combine_call(cq, mine, edge, got)
    return back_call(lengths, exchange(grads), conv_kernel, w_qkv, w_out)


def solution(mesh):
    placed = (P(AXES, None), P(), P(), P(), P(), P(AXES, None))
    return jax.shard_map(
        on_device,
        mesh=mesh,
        in_specs=placed,
        out_specs=(P(AXES, None), P(AXES, None)),
        check_vma=False,
    )
```

```python
import functools
import math

import jax
import jax.numpy as jnp
from jax import lax
from jax.experimental import pallas as pl
from jax.experimental.pallas import tpu as pltpu
from jax.sharding import PartitionSpec as P

HD = 64
KS = 7
HALF = KS // 2
MAXLEN = 2048
AXES = ("ctx", "head")
LANES = 128
EDGE = 16
PER_STEP = 4
FAR = -1e30
FRONT_STEPS = 4
BACK_STEPS = 4
VMEM_ALL = 57_500_000
VMEM_MOST = 44 * 1024 * 1024
VMEM_SOME = 24 * 1024 * 1024
F32 = jnp.float32
BF16 = jnp.bfloat16


def params(limit):
    return pltpu.CompilerParams(vmem_limit_bytes=limit)


def record_span(positions, lengths_ref):
    start = jnp.zeros_like(positions)
    stop = jnp.full_like(positions, jnp.iinfo(jnp.int32).max)
    end = jnp.int32(0)
    for i in range(lengths_ref.shape[0]):
        end = end + lengths_ref[i]
        past = end <= positions
        start = jnp.where(past, end, start)
        stop = jnp.where(past, stop, jnp.minimum(stop, end))
    return start, stop


def device_index():
    return lax.axis_index("ctx") * lax.axis_size("head") + lax.axis_index("head")


def low_lanes(shape):
    return lax.broadcasted_iota(jnp.int32, shape, len(shape) - 1) % LANES < HD


def swap_halves(x):
    return pltpu.roll(x, HD, x.ndim - 1)


def zip_low(x, y):
    return jnp.where(low_lanes(x.shape), x, swap_halves(y))


def zip_high(x, y):
    return jnp.where(low_lanes(x.shape), swap_halves(x), y)


def conv_rows(padded_ref, cols, kernel_ref, lengths_ref, first_row, rows, flip):
    pos = first_row + lax.broadcasted_iota(jnp.int32, (rows, LANES), 0)
    start, stop = record_span(pos, lengths_ref)
    masks = []
    for t in range(KS):
        at = pos + (t - HALF)
        masks.append((at >= start) & (at < stop))
    pieces = []
    for c in cols:
        lanes = pl.ds(c * LANES, LANES)
        total = padded_ref[pl.ds(8, rows), lanes]
        for t in range(KS):
            tap = kernel_ref[KS - 1 - t if flip else t, lanes]
            shifted = padded_ref[pl.ds(8 - HALF + t, rows), lanes]
            total = total + jnp.where(masks[t], shifted, 0.0) * tap[None, :]
        pieces.append(total)
    return jnp.concatenate(pieces, axis=1)


def front_kernel(
    lengths_ref, inner_ref, outer_ref, x_hbm, taps_hbm, w_hbm, cot_hbm, wo_hbm,
    out_ref, x_ref, taps_ref, w_ref, cot_ref, wo_ref, padded, projected, d_rows, sems,
):
    rows, width = x_ref.shape
    blk = width // FRONT_STEPS

    def copy(source, target, i):
        return pltpu.make_async_copy(source, target, sems.at[i])

    whole = [
        copy(source, target, i)
        for i, (source, target) in enumerate(
            ((x_hbm, x_ref), (taps_hbm, taps_ref), (cot_hbm, cot_ref))
        )
    ]
    parts = []
    for step in range(FRONT_STEPS):
        part = pl.ds(step * blk, blk)
        at = 3 + 2 * step
        parts.append(
            (
                copy(w_hbm.at[part], w_ref.at[part], at),
                copy(wo_hbm.at[part], wo_ref.at[part], at + 1),
            )
        )
    for c in whole:
        c.start()
    for pair in parts:
        for c in pair:
            c.start()
    even = device_index() % 2 == 0
    inner, outer = inner_ref[...].astype(F32), outer_ref[...].astype(F32)
    padded[pl.ds(0, 8), :] = jnp.where(even, outer[EDGE - 8 :], inner[EDGE - 8 :])
    padded[pl.ds(8 + rows, 8), :] = jnp.where(even, inner[:8], outer[:8])
    for c in whole:
        c.wait()
    padded[pl.ds(8, rows), :] = x_ref[...].astype(F32)
    first_row = device_index() * rows
    per = blk // LANES
    for step in range(FRONT_STEPS):
        mixed = conv_rows(
            padded, range(step * per, (step + 1) * per), taps_ref, lengths_ref, first_row, rows,
            False,
        ).astype(BF16)
        parts[step][0].wait()
        part = jnp.dot(mixed, w_ref[pl.ds(step * blk, blk), :], preferred_element_type=F32)
        if step == 0:
            projected[...] = part
        else:
            projected[...] += part
        parts[step][1].wait()
        d_rows[:, pl.ds(step * blk, blk)] = lax.dot_general(
            cot_ref[...], wo_ref[pl.ds(step * blk, blk), :], (((1,), (1,)), ((), ())),
            preferred_element_type=F32,
        )
    for pair in range(width // LANES):
        lanes = pl.ds(pair * LANES, LANES)
        q, k, v = (projected[:, pl.ds(i * width + pair * LANES, LANES)] for i in range(3))
        d = d_rows[:, lanes]
        out_ref[2 * pair] = jnp.concatenate([zip_low(k, v), zip_low(q, d)]).astype(BF16)
        out_ref[2 * pair + 1] = jnp.concatenate([zip_high(k, v), zip_high(q, d)]).astype(BF16)


def front_call(lengths, inner, outer, x, taps, w_qkv, cotangent, w_out):
    rows, width = x.shape
    heads = width // HD
    smem = pl.BlockSpec(memory_space=pltpu.SMEM)
    vmem = pl.BlockSpec(memory_space=pltpu.VMEM)
    anywhere = pl.BlockSpec(memory_space=pl.ANY)
    return pl.pallas_call(
        front_kernel,
        in_specs=[smem, vmem, vmem] + [anywhere] * 5,
        out_specs=vmem,
        out_shape=jax.ShapeDtypeStruct((heads, 2 * rows, LANES), BF16),
        scratch_shapes=[
            pltpu.VMEM(x.shape, x.dtype),
            pltpu.VMEM(taps.shape, taps.dtype),
            pltpu.VMEM(w_qkv.shape, w_qkv.dtype),
            pltpu.VMEM(cotangent.shape, cotangent.dtype),
            pltpu.VMEM(w_out.shape, w_out.dtype),
            pltpu.VMEM((rows + 16, width), F32),
            pltpu.VMEM((rows, 3 * width), F32),
            pltpu.VMEM((rows, width), F32),
            pltpu.SemaphoreType.DMA((3 + 2 * FRONT_STEPS,)),
        ],
        compiler_params=params(VMEM_ALL),
        cost_estimate=pl.CostEstimate(
            flops=8 * rows * width * width, bytes_accessed=8 * width * width, transcendentals=0
        ),
        name="front",
    )(lengths, inner, outer, x, taps, w_qkv, cotangent, w_out)


def attention_kernel(
    pre, place, lengths_ref, kv_mine, kv_other, qd_ref,
    cq_ref, dkv_mine, edge_mine, send_ref,
    visit_q, visit_k, keys_ref, marked_ref, turned_ref, query_ref, qd_cat_ref, d_turned_ref, e_ref,
    total_ref, context_ref, row_ref, d_query_ref, acc_ref, cq_full,
):
    slots = qd_ref.shape[0]
    key_slots, rows, _ = kv_mine.shape
    tile = 2 * rows
    tiles, groups = key_slots // 2, slots // 2
    me = device_index()
    window = 2 * slots
    base, parity = me // window * (window * rows), me % 2
    origin = base - pre * tile
    unit = HD**-0.5
    to_exp2 = unit * math.log2(math.e)

    def row_at(slot, side):
        return slot * tile + side * rows + lax.broadcasted_iota(jnp.int32, (rows, 1), 0)

    lane = lax.broadcasted_iota(jnp.int32, (1, LANES), 1)
    starts = jnp.zeros((1, LANES), jnp.int32)
    stops = jnp.zeros((1, LANES), jnp.int32)
    end = jnp.int32(0)
    for i in range(lengths_ref.shape[0]):
        starts = jnp.where(lane == HD + i, end, starts)
        end = end + lengths_ref[i]
        stops = jnp.where(lane == HD + i, end, stops)

    count = jnp.int32(groups)
    for u in range(groups):
        visit_q[u] = u
        visit_k[u] = u + pre // 2
        first = base + u * (2 * tile) + parity * rows
        begin, end = jnp.int32(0), jnp.int32(0)
        for i in range(lengths_ref.shape[0]):
            end = end + lengths_ref[i]
            begin = jnp.where(end <= first, end, begin)
        t_first = jnp.maximum(begin - origin, 0) // (2 * tile)

        def note(t, count, u=u):
            visit_q[count] = u
            visit_k[count] = t
            return count + 1

        count = lax.fori_loop(t_first, u + pre // 2, note, count)

    low = low_lanes((rows, LANES))
    for t in range(tiles):
        for half, source in enumerate((kv_mine, kv_other)):
            side = parity if half == 0 else 1 - parity
            for i in range(2):
                block = source[place(2 * t + i, pre)]
                at = pl.ds(half * tile + i * rows, rows)
                keys_ref[t, at] = block
                turned_ref[t, :, at] = block.T
                pos = origin + row_at(2 * t + i, side)
                mark = jnp.where((pos >= starts) & (pos < stops), 0.0, FAR)
                marked_ref[t, at] = jnp.where(low, block.astype(F32), mark).astype(BF16)
    for ref in (acc_ref, total_ref, context_ref, d_query_ref):
        ref[...] = jnp.zeros_like(ref)
    for u in range(groups):
        for i in range(2):
            qd = qd_ref[place(2 * u + i, 0), pl.ds(rows, rows)]
            at = pl.ds(i * rows, rows)
            d_turned_ref[u, :, at] = qd.T[HD:].astype(F32)
            qd = qd.astype(F32)
            pos = base + row_at(2 * u + i, parity)
            mark = jnp.where((pos >= starts) & (pos < stops), 1.0, 0.0)
            query_ref[u, at] = jnp.where(low, qd, mark).astype(BF16)
            qd_cat_ref[u, at] = jnp.where(low, qd, 0.0).astype(BF16)
            qd_cat_ref[u, pl.ds(tile + i * rows, rows)] = jnp.where(low, 0.0, qd).astype(BF16)

    nt = (((1,), (1,)), ((), ()))
    wide = (2 * tile, tile)
    q_lane = lax.broadcasted_iota(jnp.int32, wide, 1)
    q_row = q_lane // rows * tile + q_lane % rows + parity * rows
    k_sub = lax.broadcasted_iota(jnp.int32, wide, 0)
    side = jnp.where(k_sub < tile, parity, 1 - parity)
    causal = k_sub // rows % 2 * tile + k_sub % rows + side * rows <= q_row

    def forward(i, diagonal):
        u, t = visit_q[i], visit_k[i]
        scores = lax.dot_general(marked_ref[t], query_ref[u], nt, preferred_element_type=F32)
        e = jnp.exp2(scores * to_exp2)
        if diagonal:
            e = jnp.where(causal, e, 0.0)
        e_ref[i] = e
        context = jnp.dot(turned_ref[t, HD:], e.astype(BF16), preferred_element_type=F32)
        return u, jnp.sum(e.reshape(2 * tile // 8, 8, tile), axis=0), context

    def forward_some(diagonal, first, per):
        def run(j, carry):
            for u, total, context in [
                forward(first + per * j + i, diagonal) for i in range(per)
            ]:
                total_ref[u] += total
                context_ref[u] += context
            return carry

        return run

    def run_all(make, first, last):
        steps = (last - first) // PER_STEP
        lax.fori_loop(0, steps, make(first, PER_STEP), 0)
        rest = first + steps * PER_STEP
        lax.fori_loop(0, last - rest, make(rest, 1), 0)

    lax.fori_loop(0, groups // PER_STEP, forward_some(True, 0, PER_STEP), 0)
    run_all(functools.partial(forward_some, False), groups, count)
    for u in range(groups):
        inverse = 1.0 / jnp.sum(total_ref[u], axis=0, keepdims=True)
        context = (context_ref[u] * inverse).astype(BF16).astype(F32)
        context_ref[u] = context
        row_ref[u, pl.ds(0, 1)] = inverse
        row_ref[u, pl.ds(1, 1)] = jnp.sum(d_turned_ref[u] * context, axis=0, keepdims=True)

    def backward(i):
        u, t = visit_q[i], visit_k[i]
        row = row_ref[u]
        probs = e_ref[i] * row[0:1]
        d_probs = lax.dot_general(
            keys_ref[t], qd_cat_ref[u, pl.ds(tile, tile)], nt, preferred_element_type=F32
        )
        d_scores = (probs * (d_probs - row[1:2])).astype(BF16)
        both = jnp.concatenate([d_scores, probs.astype(BF16)], axis=1)
        d_keys = jnp.dot(both, qd_cat_ref[u], preferred_element_type=F32)
        d_queries = jnp.dot(turned_ref[t, :HD], d_scores, preferred_element_type=F32)
        return u, t, d_keys, d_queries

    def backward_some(first, per):
        def run(j, carry):
            for u, t, d_keys, d_queries in [
                backward(first + per * j + i) for i in range(per)
            ]:
                acc_ref[t] += d_keys
                d_query_ref[u] += d_queries
            return carry

        return run

    run_all(backward_some, 0, count)
    for u in range(groups):
        packed = jnp.concatenate([context_ref[u], d_query_ref[u] * unit], axis=0).T
        for i in range(2):
            part = packed[i * rows : (i + 1) * rows]
            cq_full[2 * u + i] = part
            cq_ref[2 * u + i] = part.astype(BF16)
    scale = jnp.where(low_lanes((1, LANES)), unit, 1.0)
    head = lax.broadcasted_iota(jnp.int32, (8, LANES), 0) < 4

    def end_rows(half, slot, first):
        slot = pre + jnp.clip(slot, 0, slots - 1)
        at = half * tile + slot % 2 * rows + first
        return acc_ref[slot // 2, pl.ds(pl.multiple_of(at, 8), 8)] * scale

    for s in range(key_slots):
        part = pl.ds(s % 2 * rows, rows)
        dkv_mine[s] = acc_ref[s // 2, part] * scale
        part = pl.ds(tile + s % 2 * rows, rows)
        send_ref[s, pl.ds(0, rows)] = (acc_ref[s // 2, part] * scale).astype(BF16)
        if s < pre:
            send_ref[s, pl.ds(rows, 16)] = jnp.zeros((16, LANES), BF16)
    for s in range(slots):
        edge_mine[s] = jnp.where(
            head, end_rows(1, s + parity, 0), end_rows(1, s - 1 + parity, rows - 8)
        )
        past, later = s - parity, s + 1 - parity
        d_edge = jnp.where(head, end_rows(0, later, 0), end_rows(0, past, rows - 8))
        q_edge = jnp.where(
            head,
            cq_full[jnp.clip(later, 0, slots - 1), pl.ds(0, 8)],
            cq_full[jnp.clip(past, 0, slots - 1), pl.ds(rows - 8, 8)],
        )
        send_ref[pre + s, pl.ds(rows, 16)] = jnp.concatenate([d_edge, q_edge]).astype(BF16)


def attention_call(lengths, kv_mine, kv_other, qd, pre):
    slots = qd.shape[0]
    key_slots, rows, _ = kv_mine.shape
    tile = 2 * rows
    tiles, groups = key_slots // 2, slots // 2
    reach = MAXLEN // (2 * tile) + 1
    place = lambda s, ordered: s if ordered else bit_reversed(s, slots)
    visits = sum(min(u + pre // 2 + 1, reach) for u in range(groups))
    smem = pl.BlockSpec(memory_space=pltpu.SMEM)
    vmem = pl.BlockSpec(memory_space=pltpu.VMEM)
    return pl.pallas_call(
        functools.partial(attention_kernel, pre, place),
        in_specs=[smem, vmem, vmem, vmem],
        out_specs=[vmem, vmem, vmem, vmem],
        out_shape=[
            jax.ShapeDtypeStruct((slots, rows, LANES), BF16),
            jax.ShapeDtypeStruct((key_slots, rows, LANES), F32),
            jax.ShapeDtypeStruct((slots, 8, LANES), F32),
            jax.ShapeDtypeStruct((key_slots, rows + 16, LANES), BF16),
        ],
        scratch_shapes=[
            pltpu.SMEM((visits,), jnp.int32),
            pltpu.SMEM((visits,), jnp.int32),
            pltpu.VMEM((tiles, 2 * tile, LANES), BF16),
            pltpu.VMEM((tiles, 2 * tile, LANES), BF16),
            pltpu.VMEM((tiles, LANES, 2 * tile), BF16),
            pltpu.VMEM((groups, tile, LANES), BF16),
            pltpu.VMEM((groups, 2 * tile, LANES), BF16),
            pltpu.VMEM((groups, HD, tile), F32),
            pltpu.VMEM((visits, 2 * tile, tile), F32),
            pltpu.VMEM((groups, 8, tile), F32),
            pltpu.VMEM((groups, HD, tile), F32),
            pltpu.VMEM((groups, 8, tile), F32),
            pltpu.VMEM((groups, HD, tile), F32),
            pltpu.VMEM((tiles, 2 * tile, LANES), F32),
            pltpu.VMEM((slots, rows, LANES), F32),
        ],
        compiler_params=params(VMEM_MOST),
        cost_estimate=pl.CostEstimate(
            flops=10 * slots * rows * MAXLEN * LANES,
            bytes_accessed=20 * slots * rows * LANES,
            transcendentals=slots * rows * MAXLEN,
        ),
        name="attention",
    )(lengths, kv_mine, kv_other, qd)


def combine_kernel(cq_ref, mine_ref, edge_ref, got_ref, out_ref):
    slots, rows, _ = cq_ref.shape
    for s in range(slots):
        at = bit_reversed(s, slots)
        out_ref[at, pl.ds(0, rows)] = cq_ref[s]
        got = got_ref[s].astype(F32)
        out_ref[at, pl.ds(rows, rows)] = (mine_ref[s] + got[:rows]).astype(BF16)
        edges = [edge_ref[s] + got[rows : rows + 8], got[rows + 8 :]]
        out_ref[at, pl.ds(2 * rows, 16)] = jnp.concatenate(edges).astype(BF16)


def combine_call(cq, mine, edge, got):
    slots, rows, _ = cq.shape
    vmem = pl.BlockSpec(memory_space=pltpu.VMEM)
    return pl.pallas_call(
        combine_kernel,
        in_specs=[vmem] * 4,
        out_specs=vmem,
        out_shape=jax.ShapeDtypeStruct((slots, 2 * rows + 16, LANES), BF16),
        compiler_params=params(VMEM_SOME),
        name="combine",
    )(cq, mine, edge, got)


def combine_windows(cq, mine, got, pre, side, window, devices):
    slots, rows, _ = cq.shape
    dkv = mine + got[:, :rows].astype(F32)
    back = [(i + window, i) for i in range(devices - window)]
    earlier = lax.ppermute(dkv[:pre].astype(BF16), AXES, back).astype(F32)
    dkv = dkv[pre:].at[slots - pre :].add(earlier).astype(BF16)
    both = jnp.concatenate([cq, dkv], axis=2)
    tails, heads = both[:, rows - 8 :], both[:, :8]
    swapped = [(i, i ^ 1) for i in range(devices)]
    tails_other = lax.ppermute(tails, AXES, swapped)
    heads_other = lax.ppermute(heads, AXES, swapped)
    last = [(i, i + window - 1) for i in range(1, devices - window, 2)]
    tail_past = lax.ppermute(tails[-1:], AXES, last)
    head_next = lax.ppermute(heads[:1], AXES, [(j, i) for i, j in last])
    before = jnp.where(
        side == 0, jnp.concatenate([tail_past, tails_other[:-1]]), tails_other
    )
    after = jnp.where(side == 0, heads_other, jnp.concatenate([heads_other[1:], head_next]))
    edge = jnp.where(jnp.arange(8)[None, :, None] < 4, after, before)
    grads = jnp.concatenate([cq, dkv, edge[..., LANES:], edge[..., :LANES]], axis=1)
    return jnp.stack([grads[bit_reversed(s, slots)] for s in range(slots)])


def back_kernel(
    lengths_ref, r_ref, taps_ref, w_ref, wo_ref, attended_ref, grad_ref, context, grads, padded
):
    heads = r_ref.shape[0]
    rows, width = context.shape
    blk = width // BACK_STEPS
    main, dkv = slice(0, rows), slice(rows, 2 * rows)
    edge_dkv, edge_cq = slice(2 * rows, 2 * rows + 8), slice(2 * rows + 8, 2 * rows + 16)
    pad = jnp.zeros((8, LANES), F32)
    for pair in range(heads // 2):
        lanes = pl.ds(pair * LANES, LANES)
        x, y = (r_ref[2 * pair + i].astype(F32) for i in range(2))
        context[:, lanes] = zip_low(x[main], y[main]).astype(BF16)

        def gather(mix, part, edge):
            return jnp.concatenate([mix(x[part], y[part]), mix(x[edge], y[edge]), pad]).astype(BF16)

        grads[:, lanes] = gather(zip_high, main, edge_cq)
        grads[:, pl.ds(width + pair * LANES, LANES)] = gather(zip_low, dkv, edge_dkv)
        grads[:, pl.ds(2 * width + pair * LANES, LANES)] = gather(zip_high, dkv, edge_dkv)
    first_row = device_index() * rows
    per = blk // LANES
    for step in range(BACK_STEPS):
        part = pl.ds(step * blk, blk)
        mixed = lax.dot_general(
            grads[...], w_ref[part, :], (((1,), (1,)), ((), ())), preferred_element_type=F32
        ).astype(BF16).astype(F32)
        edge = mixed[rows : rows + 8]
        padded[pl.ds(0, 8), part] = edge
        padded[pl.ds(8, rows), part] = mixed[:rows]
        padded[pl.ds(8 + rows, 8), part] = edge
        attended_ref[:, part] = jnp.dot(
            context[...], wo_ref[:, part], preferred_element_type=F32
        ).astype(BF16)
        grad_ref[:, part] = conv_rows(
            padded, range(step * per, (step + 1) * per), taps_ref, lengths_ref, first_row, rows,
            True,
        ).astype(BF16)


def back_call(lengths, r, taps, w_qkv, w_out):
    heads = r.shape[0]
    rows = (r.shape[1] - 16) // 2
    width = heads * HD
    smem = pl.BlockSpec(memory_space=pltpu.SMEM)
    vmem = pl.BlockSpec(memory_space=pltpu.VMEM)
    shape = jax.ShapeDtypeStruct((rows, width), BF16)
    return pl.pallas_call(
        back_kernel,
        in_specs=[smem, vmem, vmem, vmem, vmem],
        out_specs=[vmem, vmem],
        out_shape=[shape, shape],
        scratch_shapes=[
            pltpu.VMEM((rows, width), BF16),
            pltpu.VMEM((rows + 16, 3 * width), BF16),
            pltpu.VMEM((rows + 16, width), F32),
        ],
        compiler_params=params(VMEM_SOME),
        cost_estimate=pl.CostEstimate(
            flops=8 * rows * width * width, bytes_accessed=8 * width * width, transcendentals=0
        ),
        name="back",
    )(lengths, r, taps, w_qkv, w_out)


def bit_reversed(i, count):
    bits = count.bit_length() - 1
    if count != 1 << bits:
        return i
    return sum((i >> b & 1) << (bits - 1 - b) for b in range(bits))


def on_device(tokens, conv_kernel, w_qkv, w_out, lengths, cotangent):
    rows, width = tokens.shape
    heads = width // HD
    devices = lax.axis_size(AXES)
    window = 2 * heads
    windows = devices // window
    pre = MAXLEN // (2 * rows) if windows > 1 else 0
    me = lax.axis_index(AXES)
    same_side = [
        [w * window + 2 * bit_reversed(c, heads) + side for c in range(heads)]
        for w in range(windows)
        for side in range(2)
    ]
    swapped = [(i, i ^ 1) for i in range(devices)]
    across = [(i, i + (1 if i % 2 else -1)) for i in range(1, devices - 1)]

    def exchange(x):
        return lax.all_to_all(
            x, AXES, split_axis=0, concat_axis=0, axis_index_groups=same_side, tiled=True
        )

    first, last = tokens[:EDGE], tokens[rows - EDGE :]
    even = me % 2 == 0
    inner = lax.ppermute(jnp.where(even, last, first), AXES, swapped)
    outer = lax.ppermute(jnp.where(even, first, last), AXES, across)
    sent = front_call(lengths, inner, outer, tokens, conv_kernel, w_qkv, cotangent, w_out)
    qd = exchange(sent)
    kv_mine = qd[:, :rows]
    if pre:
        shift = [(i, i + window) for i in range(devices - window)]
        kv_mine = jnp.stack([kv_mine[bit_reversed(s, heads)] for s in range(heads)])
        kv_mine = jnp.concatenate([lax.ppermute(kv_mine[heads - pre :], AXES, shift), kv_mine])
    kv_other = lax.ppermute(kv_mine, AXES, swapped)
    cq, mine, edge, send = attention_call(lengths, kv_mine, kv_other, qd, pre)
    got = lax.ppermute(send, AXES, swapped)
    if pre:
        grads = combine_windows(cq, mine, got, pre, me % 2, window, devices)
    else:
        grads = combine_call(cq, mine, edge, got)
    return back_call(lengths, exchange(grads), conv_kernel, w_qkv, w_out)


def solution(mesh):
    placed = (P(AXES, None), P(), P(), P(), P(), P(AXES, None))
    return jax.shard_map(
        on_device,
        mesh=mesh,
        in_specs=placed,
        out_specs=(P(AXES, None), P(AXES, None)),
        check_vma=False,
    )
```

```python
import functools
import math

import jax
import jax.numpy as jnp
from jax import lax
from jax.experimental import pallas as pl
from jax.experimental.pallas import tpu as pltpu
from jax.sharding import PartitionSpec as P

HD = 64
KS = 7
HALF = KS // 2
MAXLEN = 2048
AXES = ("ctx", "head")
LANES = 128
EDGE = 16
PER_STEP = 4
FAR = -1e30
FRONT_STEPS = 4
BACK_STEPS = 4
VMEM_ALL = 57_500_000
VMEM_MOST = 44 * 1024 * 1024
VMEM_SOME = 24 * 1024 * 1024
F32 = jnp.float32
BF16 = jnp.bfloat16


def params(limit):
    return pltpu.CompilerParams(vmem_limit_bytes=limit)


def record_span(positions, lengths_ref):
    start = jnp.zeros_like(positions)
    stop = jnp.full_like(positions, jnp.iinfo(jnp.int32).max)
    end = jnp.int32(0)
    for i in range(lengths_ref.shape[0]):
        end = end + lengths_ref[i]
        past = end <= positions
        start = jnp.where(past, end, start)
        stop = jnp.where(past, stop, jnp.minimum(stop, end))
    return start, stop


def device_index():
    return lax.axis_index("ctx") * lax.axis_size("head") + lax.axis_index("head")


def low_lanes(shape):
    return lax.broadcasted_iota(jnp.int32, shape, len(shape) - 1) % LANES < HD


def swap_halves(x):
    return pltpu.roll(x, HD, x.ndim - 1)


def zip_low(x, y):
    return jnp.where(low_lanes(x.shape), x, swap_halves(y))


def zip_high(x, y):
    return jnp.where(low_lanes(x.shape), swap_halves(x), y)


def conv_rows(padded_ref, cols, kernel_ref, lengths_ref, first_row, rows, flip):
    pos = first_row + lax.broadcasted_iota(jnp.int32, (rows, LANES), 0)
    start, stop = record_span(pos, lengths_ref)
    masks = []
    for t in range(KS):
        at = pos + (t - HALF)
        masks.append((at >= start) & (at < stop))
    pieces = []
    for c in cols:
        lanes = pl.ds(c * LANES, LANES)
        total = padded_ref[pl.ds(8, rows), lanes]
        for t in range(KS):
            tap = kernel_ref[KS - 1 - t if flip else t, lanes]
            shifted = padded_ref[pl.ds(8 - HALF + t, rows), lanes]
            total = total + jnp.where(masks[t], shifted, 0.0) * tap[None, :]
        pieces.append(total)
    return jnp.concatenate(pieces, axis=1)


def front_kernel(
    lengths_ref, inner_ref, outer_ref, x_hbm, taps_hbm, w_hbm, cot_hbm, wo_hbm,
    out_ref, x_ref, taps_ref, w_ref, cot_ref, wo_ref, padded, projected, d_rows, sems,
):
    rows, width = x_ref.shape
    blk = width // FRONT_STEPS

    def copy(source, target, i):
        return pltpu.make_async_copy(source, target, sems.at[i])

    whole = [
        copy(source, target, i)
        for i, (source, target) in enumerate(
            ((x_hbm, x_ref), (taps_hbm, taps_ref), (cot_hbm, cot_ref))
        )
    ]
    parts = []
    for step in range(FRONT_STEPS):
        part = pl.ds(step * blk, blk)
        at = 3 + 2 * step
        parts.append(
            (
                copy(w_hbm.at[part], w_ref.at[part], at),
                copy(wo_hbm.at[part], wo_ref.at[part], at + 1),
            )
        )
    for c in whole:
        c.start()
    for pair in parts:
        for c in pair:
            c.start()
    even = device_index() % 2 == 0
    inner, outer = inner_ref[...].astype(F32), outer_ref[...].astype(F32)
    padded[pl.ds(0, 8), :] = jnp.where(even, outer[EDGE - 8 :], inner[EDGE - 8 :])
    padded[pl.ds(8 + rows, 8), :] = jnp.where(even, inner[:8], outer[:8])
    for c in whole:
        c.wait()
    padded[pl.ds(8, rows), :] = x_ref[...].astype(F32)
    first_row = device_index() * rows
    per = blk // LANES
    for step in range(FRONT_STEPS):
        mixed = conv_rows(
            padded, range(step * per, (step + 1) * per), taps_ref, lengths_ref, first_row, rows,
            False,
        ).astype(BF16)
        parts[step][0].wait()
        part = jnp.dot(mixed, w_ref[pl.ds(step * blk, blk), :], preferred_element_type=F32)
        if step == 0:
            projected[...] = part
        else:
            projected[...] += part
        parts[step][1].wait()
        d_rows[:, pl.ds(step * blk, blk)] = lax.dot_general(
            cot_ref[...], wo_ref[pl.ds(step * blk, blk), :], (((1,), (1,)), ((), ())),
            preferred_element_type=F32,
        )
    for pair in range(width // LANES):
        lanes = pl.ds(pair * LANES, LANES)
        q, k, v = (projected[:, pl.ds(i * width + pair * LANES, LANES)] for i in range(3))
        d = d_rows[:, lanes]
        out_ref[2 * pair] = jnp.concatenate([zip_low(k, v), zip_low(q, d)]).astype(BF16)
        out_ref[2 * pair + 1] = jnp.concatenate([zip_high(k, v), zip_high(q, d)]).astype(BF16)


def front_call(lengths, inner, outer, x, taps, w_qkv, cotangent, w_out):
    rows, width = x.shape
    heads = width // HD
    smem = pl.BlockSpec(memory_space=pltpu.SMEM)
    vmem = pl.BlockSpec(memory_space=pltpu.VMEM)
    anywhere = pl.BlockSpec(memory_space=pl.ANY)
    return pl.pallas_call(
        front_kernel,
        in_specs=[smem, vmem, vmem] + [anywhere] * 5,
        out_specs=vmem,
        out_shape=jax.ShapeDtypeStruct((heads, 2 * rows, LANES), BF16),
        scratch_shapes=[
            pltpu.VMEM(x.shape, x.dtype),
            pltpu.VMEM(taps.shape, taps.dtype),
            pltpu.VMEM(w_qkv.shape, w_qkv.dtype),
            pltpu.VMEM(cotangent.shape, cotangent.dtype),
            pltpu.VMEM(w_out.shape, w_out.dtype),
            pltpu.VMEM((rows + 16, width), F32),
            pltpu.VMEM((rows, 3 * width), F32),
            pltpu.VMEM((rows, width), F32),
            pltpu.SemaphoreType.DMA((3 + 2 * FRONT_STEPS,)),
        ],
        compiler_params=params(VMEM_ALL),
        cost_estimate=pl.CostEstimate(
            flops=8 * rows * width * width, bytes_accessed=8 * width * width, transcendentals=0
        ),
        name="front",
    )(lengths, inner, outer, x, taps, w_qkv, cotangent, w_out)


def attention_kernel(
    pre, place, lengths_ref, kv_mine, kv_other, qd_ref,
    cq_ref, dkv_mine, edge_mine, send_ref,
    visit_q, visit_k, keys_ref, marked_ref, turned_ref, query_ref, qd_cat_ref, d_turned_ref, e_ref,
    total_ref, context_ref, row_ref, d_query_ref, acc_ref, cq_full,
):
    slots = qd_ref.shape[0]
    key_slots, rows, _ = kv_mine.shape
    tile = 2 * rows
    tiles, groups = key_slots // 2, slots // 2
    me = device_index()
    window = 2 * slots
    base, parity = me // window * (window * rows), me % 2
    origin = base - pre * tile
    unit = HD**-0.5
    to_exp2 = unit * math.log2(math.e)

    def row_at(slot, side):
        return slot * tile + side * rows + lax.broadcasted_iota(jnp.int32, (rows, 1), 0)

    lane = lax.broadcasted_iota(jnp.int32, (1, LANES), 1)
    starts = jnp.zeros((1, LANES), jnp.int32)
    stops = jnp.zeros((1, LANES), jnp.int32)
    end = jnp.int32(0)
    for i in range(lengths_ref.shape[0]):
        starts = jnp.where(lane == HD + i, end, starts)
        end = end + lengths_ref[i]
        stops = jnp.where(lane == HD + i, end, stops)

    count = jnp.int32(groups)
    for u in range(groups):
        first = base + u * (2 * tile) + parity * rows
        begin, end = jnp.int32(0), jnp.int32(0)
        for i in range(lengths_ref.shape[0]):
            end = end + lengths_ref[i]
            begin = jnp.where(end <= first, end, begin)
        t_first = jnp.maximum(begin - origin, 0) // (2 * tile)

        def note(t, count, u=u):
            visit_q[count] = u
            visit_k[count] = t
            return count + 1

        count = lax.fori_loop(t_first, u + pre // 2, note, count)

    low = low_lanes((rows, LANES))
    for t in range(tiles):
        for half, source in enumerate((kv_mine, kv_other)):
            side = parity if half == 0 else 1 - parity
            for i in range(2):
                block = source[place(2 * t + i, pre)]
                at = pl.ds(half * tile + i * rows, rows)
                keys_ref[t, at] = block
                turned_ref[t, :, at] = block.T
                pos = origin + row_at(2 * t + i, side)
                mark = jnp.where((pos >= starts) & (pos < stops), 0.0, FAR)
                marked_ref[t, at] = jnp.where(low, block.astype(F32), mark).astype(BF16)
    for t in range(pre // 2):
        acc_ref[t] = jnp.zeros_like(acc_ref[t])
    for u in range(groups):
        for i in range(2):
            qd = qd_ref[place(2 * u + i, 0), pl.ds(rows, rows)]
            at = pl.ds(i * rows, rows)
            d_turned_ref[u, :, at] = qd.T[HD:].astype(F32)
            qd = qd.astype(F32)
            pos = base + row_at(2 * u + i, parity)
            mark = jnp.where((pos >= starts) & (pos < stops), 1.0, 0.0)
            query_ref[u, at] = jnp.where(low, qd, mark).astype(BF16)
            qd_cat_ref[u, at] = jnp.where(low, qd, 0.0).astype(BF16)
            qd_cat_ref[u, pl.ds(tile + i * rows, rows)] = jnp.where(low, 0.0, qd).astype(BF16)

    nt = (((1,), (1,)), ((), ()))
    wide = (2 * tile, tile)
    q_lane = lax.broadcasted_iota(jnp.int32, wide, 1)
    q_row = q_lane // rows * tile + q_lane % rows + parity * rows
    k_sub = lax.broadcasted_iota(jnp.int32, wide, 0)
    side = jnp.where(k_sub < tile, parity, 1 - parity)
    causal = k_sub // rows % 2 * tile + k_sub % rows + side * rows <= q_row

    def forward(i, u, t, diagonal):
        scores = lax.dot_general(marked_ref[t], query_ref[u], nt, preferred_element_type=F32)
        e = jnp.exp2(scores * to_exp2)
        if diagonal:
            e = jnp.where(causal, e, 0.0)
        e_ref[i] = e
        context = jnp.dot(turned_ref[t, HD:], e.astype(BF16), preferred_element_type=F32)
        return jnp.sum(e.reshape(2 * tile // 8, 8, tile), axis=0), context

    def forward_some(first, per):
        def run(j, carry):
            at = [first + per * j + i for i in range(per)]
            groups_at = [visit_q[i] for i in at]
            parts = [forward(i, u, visit_k[i], False) for i, u in zip(at, groups_at)]
            for u, (total, context) in zip(groups_at, parts):
                total_ref[u] += total
                context_ref[u] += context
            return carry

        return run

    def run_rest(make):
        first = groups
        for per in (PER_STEP, 2, 1):
            steps = (count - first) // per
            lax.fori_loop(0, steps, make(first, per), 0)
            first = first + steps * per

    for u in range(groups):
        total_ref[u], context_ref[u] = forward(u, u, u + pre // 2, True)
    run_rest(forward_some)
    for u in range(groups):
        inverse = 1.0 / jnp.sum(total_ref[u], axis=0, keepdims=True)
        context = (context_ref[u] * inverse).astype(BF16).astype(F32)
        context_ref[u] = context
        row_ref[u, pl.ds(0, 1)] = inverse
        row_ref[u, pl.ds(1, 1)] = jnp.sum(d_turned_ref[u] * context, axis=0, keepdims=True)

    def backward(i, u, t):
        row = row_ref[u]
        probs = e_ref[i] * row[0:1]
        d_probs = lax.dot_general(
            keys_ref[t], qd_cat_ref[u, pl.ds(tile, tile)], nt, preferred_element_type=F32
        )
        d_scores = (probs * (d_probs - row[1:2])).astype(BF16)
        both = jnp.concatenate([d_scores, probs.astype(BF16)], axis=1)
        d_keys = jnp.dot(both, qd_cat_ref[u], preferred_element_type=F32)
        d_queries = jnp.dot(turned_ref[t, :HD], d_scores, preferred_element_type=F32)
        return d_keys, d_queries

    def backward_some(first, per):
        def run(j, carry):
            at = [(i, visit_q[i], visit_k[i]) for i in (first + per * j + i for i in range(per))]
            parts = [backward(i, u, t) for i, u, t in at]
            for (_, u, t), (d_keys, d_queries) in zip(at, parts):
                acc_ref[t] += d_keys
                d_query_ref[u] += d_queries
            return carry

        return run

    for u in range(groups):
        acc_ref[u + pre // 2], d_query_ref[u] = backward(u, u, u + pre // 2)
    run_rest(backward_some)
    for u in range(groups):
        packed = jnp.concatenate([context_ref[u], d_query_ref[u] * unit], axis=0).T
        for i in range(2):
            part = packed[i * rows : (i + 1) * rows]
            cq_full[2 * u + i] = part
            cq_ref[2 * u + i] = part.astype(BF16)
    scale = jnp.where(low_lanes((1, LANES)), unit, 1.0)
    head = lax.broadcasted_iota(jnp.int32, (8, LANES), 0) < 4

    def end_rows(half, slot, first):
        slot = pre + jnp.clip(slot, 0, slots - 1)
        at = half * tile + slot % 2 * rows + first
        return acc_ref[slot // 2, pl.ds(pl.multiple_of(at, 8), 8)] * scale

    for s in range(key_slots):
        part = pl.ds(s % 2 * rows, rows)
        dkv_mine[s] = acc_ref[s // 2, part] * scale
        part = pl.ds(tile + s % 2 * rows, rows)
        send_ref[s, pl.ds(0, rows)] = (acc_ref[s // 2, part] * scale).astype(BF16)
        if s < pre:
            send_ref[s, pl.ds(rows, 16)] = jnp.zeros((16, LANES), BF16)
    for s in range(slots):
        edge_mine[s] = jnp.where(
            head, end_rows(1, s + parity, 0), end_rows(1, s - 1 + parity, rows - 8)
        )
        past, later = s - parity, s + 1 - parity
        d_edge = jnp.where(head, end_rows(0, later, 0), end_rows(0, past, rows - 8))
        q_edge = jnp.where(
            head,
            cq_full[jnp.clip(later, 0, slots - 1), pl.ds(0, 8)],
            cq_full[jnp.clip(past, 0, slots - 1), pl.ds(rows - 8, 8)],
        )
        send_ref[pre + s, pl.ds(rows, 16)] = jnp.concatenate([d_edge, q_edge]).astype(BF16)


def attention_call(lengths, kv_mine, kv_other, qd, pre):
    slots = qd.shape[0]
    key_slots, rows, _ = kv_mine.shape
    tile = 2 * rows
    tiles, groups = key_slots // 2, slots // 2
    reach = MAXLEN // (2 * tile) + 1
    place = lambda s, ordered: s if ordered else bit_reversed(s, slots)
    visits = sum(min(u + pre // 2 + 1, reach) for u in range(groups))
    smem = pl.BlockSpec(memory_space=pltpu.SMEM)
    vmem = pl.BlockSpec(memory_space=pltpu.VMEM)
    return pl.pallas_call(
        functools.partial(attention_kernel, pre, place),
        in_specs=[smem, vmem, vmem, vmem],
        out_specs=[vmem, vmem, vmem, vmem],
        out_shape=[
            jax.ShapeDtypeStruct((slots, rows, LANES), BF16),
            jax.ShapeDtypeStruct((key_slots, rows, LANES), F32),
            jax.ShapeDtypeStruct((slots, 8, LANES), F32),
            jax.ShapeDtypeStruct((key_slots, rows + 16, LANES), BF16),
        ],
        scratch_shapes=[
            pltpu.SMEM((visits,), jnp.int32),
            pltpu.SMEM((visits,), jnp.int32),
            pltpu.VMEM((tiles, 2 * tile, LANES), BF16),
            pltpu.VMEM((tiles, 2 * tile, LANES), BF16),
            pltpu.VMEM((tiles, LANES, 2 * tile), BF16),
            pltpu.VMEM((groups, tile, LANES), BF16),
            pltpu.VMEM((groups, 2 * tile, LANES), BF16),
            pltpu.VMEM((groups, HD, tile), F32),
            pltpu.VMEM((visits, 2 * tile, tile), F32),
            pltpu.VMEM((groups, 8, tile), F32),
            pltpu.VMEM((groups, HD, tile), F32),
            pltpu.VMEM((groups, 8, tile), F32),
            pltpu.VMEM((groups, HD, tile), F32),
            pltpu.VMEM((tiles, 2 * tile, LANES), F32),
            pltpu.VMEM((slots, rows, LANES), F32),
        ],
        compiler_params=params(VMEM_MOST),
        cost_estimate=pl.CostEstimate(
            flops=10 * slots * rows * MAXLEN * LANES,
            bytes_accessed=20 * slots * rows * LANES,
            transcendentals=slots * rows * MAXLEN,
        ),
        name="attention",
    )(lengths, kv_mine, kv_other, qd)


def combine_kernel(cq_ref, mine_ref, edge_ref, got_ref, out_ref):
    slots, rows, _ = cq_ref.shape
    for s in range(slots):
        at = bit_reversed(s, slots)
        out_ref[at, pl.ds(0, rows)] = cq_ref[s]
        got = got_ref[s].astype(F32)
        out_ref[at, pl.ds(rows, rows)] = (mine_ref[s] + got[:rows]).astype(BF16)
        edges = [edge_ref[s] + got[rows : rows + 8], got[rows + 8 :]]
        out_ref[at, pl.ds(2 * rows, 16)] = jnp.concatenate(edges).astype(BF16)


def combine_call(cq, mine, edge, got):
    slots, rows, _ = cq.shape
    vmem = pl.BlockSpec(memory_space=pltpu.VMEM)
    return pl.pallas_call(
        combine_kernel,
        in_specs=[vmem] * 4,
        out_specs=vmem,
        out_shape=jax.ShapeDtypeStruct((slots, 2 * rows + 16, LANES), BF16),
        compiler_params=params(VMEM_SOME),
        name="combine",
    )(cq, mine, edge, got)


def combine_windows(cq, mine, got, pre, side, window, devices):
    slots, rows, _ = cq.shape
    dkv = mine + got[:, :rows].astype(F32)
    back = [(i + window, i) for i in range(devices - window)]
    earlier = lax.ppermute(dkv[:pre].astype(BF16), AXES, back).astype(F32)
    dkv = dkv[pre:].at[slots - pre :].add(earlier).astype(BF16)
    both = jnp.concatenate([cq, dkv], axis=2)
    tails, heads = both[:, rows - 8 :], both[:, :8]
    swapped = [(i, i ^ 1) for i in range(devices)]
    tails_other = lax.ppermute(tails, AXES, swapped)
    heads_other = lax.ppermute(heads, AXES, swapped)
    last = [(i, i + window - 1) for i in range(1, devices - window, 2)]
    tail_past = lax.ppermute(tails[-1:], AXES, last)
    head_next = lax.ppermute(heads[:1], AXES, [(j, i) for i, j in last])
    before = jnp.where(
        side == 0, jnp.concatenate([tail_past, tails_other[:-1]]), tails_other
    )
    after = jnp.where(side == 0, heads_other, jnp.concatenate([heads_other[1:], head_next]))
    edge = jnp.where(jnp.arange(8)[None, :, None] < 4, after, before)
    grads = jnp.concatenate([cq, dkv, edge[..., LANES:], edge[..., :LANES]], axis=1)
    return jnp.stack([grads[bit_reversed(s, slots)] for s in range(slots)])


def back_kernel(
    lengths_ref, r_ref, taps_ref, w_ref, wo_ref, attended_ref, grad_ref, context, grads, padded
):
    heads = r_ref.shape[0]
    rows, width = context.shape
    blk = width // BACK_STEPS
    main, dkv = slice(0, rows), slice(rows, 2 * rows)
    edge_dkv, edge_cq = slice(2 * rows, 2 * rows + 8), slice(2 * rows + 8, 2 * rows + 16)
    pad = jnp.zeros((8, LANES), F32)
    for pair in range(heads // 2):
        lanes = pl.ds(pair * LANES, LANES)
        x, y = (r_ref[2 * pair + i].astype(F32) for i in range(2))
        context[:, lanes] = zip_low(x[main], y[main]).astype(BF16)

        def gather(mix, part, edge):
            return jnp.concatenate([mix(x[part], y[part]), mix(x[edge], y[edge]), pad]).astype(BF16)

        grads[:, lanes] = gather(zip_high, main, edge_cq)
        grads[:, pl.ds(width + pair * LANES, LANES)] = gather(zip_low, dkv, edge_dkv)
        grads[:, pl.ds(2 * width + pair * LANES, LANES)] = gather(zip_high, dkv, edge_dkv)
    first_row = device_index() * rows
    per = blk // LANES
    for step in range(BACK_STEPS):
        part = pl.ds(step * blk, blk)
        mixed = lax.dot_general(
            grads[...], w_ref[part, :], (((1,), (1,)), ((), ())), preferred_element_type=F32
        ).astype(BF16).astype(F32)
        edge = mixed[rows : rows + 8]
        padded[pl.ds(0, 8), part] = edge
        padded[pl.ds(8, rows), part] = mixed[:rows]
        padded[pl.ds(8 + rows, 8), part] = edge
        attended_ref[:, part] = jnp.dot(
            context[...], wo_ref[:, part], preferred_element_type=F32
        ).astype(BF16)
        grad_ref[:, part] = conv_rows(
            padded, range(step * per, (step + 1) * per), taps_ref, lengths_ref, first_row, rows,
            True,
        ).astype(BF16)


def back_call(lengths, r, taps, w_qkv, w_out):
    heads = r.shape[0]
    rows = (r.shape[1] - 16) // 2
    width = heads * HD
    smem = pl.BlockSpec(memory_space=pltpu.SMEM)
    vmem = pl.BlockSpec(memory_space=pltpu.VMEM)
    shape = jax.ShapeDtypeStruct((rows, width), BF16)
    return pl.pallas_call(
        back_kernel,
        in_specs=[smem, vmem, vmem, vmem, vmem],
        out_specs=[vmem, vmem],
        out_shape=[shape, shape],
        scratch_shapes=[
            pltpu.VMEM((rows, width), BF16),
            pltpu.VMEM((rows + 16, 3 * width), BF16),
            pltpu.VMEM((rows + 16, width), F32),
        ],
        compiler_params=params(VMEM_SOME),
        cost_estimate=pl.CostEstimate(
            flops=8 * rows * width * width, bytes_accessed=8 * width * width, transcendentals=0
        ),
        name="back",
    )(lengths, r, taps, w_qkv, w_out)


def bit_reversed(i, count):
    bits = count.bit_length() - 1
    if count != 1 << bits:
        return i
    return sum((i >> b & 1) << (bits - 1 - b) for b in range(bits))


def on_device(tokens, conv_kernel, w_qkv, w_out, lengths, cotangent):
    rows, width = tokens.shape
    heads = width // HD
    devices = lax.axis_size(AXES)
    window = 2 * heads
    windows = devices // window
    pre = MAXLEN // (2 * rows) if windows > 1 else 0
    me = lax.axis_index(AXES)
    same_side = [
        [w * window + 2 * bit_reversed(c, heads) + side for c in range(heads)]
        for w in range(windows)
        for side in range(2)
    ]
    swapped = [(i, i ^ 1) for i in range(devices)]
    across = [(i, i + (1 if i % 2 else -1)) for i in range(1, devices - 1)]

    def exchange(x):
        return lax.all_to_all(
            x, AXES, split_axis=0, concat_axis=0, axis_index_groups=same_side, tiled=True
        )

    first, last = tokens[:EDGE], tokens[rows - EDGE :]
    even = me % 2 == 0
    inner = lax.ppermute(jnp.where(even, last, first), AXES, swapped)
    outer = lax.ppermute(jnp.where(even, first, last), AXES, across)
    sent = front_call(lengths, inner, outer, tokens, conv_kernel, w_qkv, cotangent, w_out)
    qd = exchange(sent)
    kv_mine = qd[:, :rows]
    if pre:
        shift = [(i, i + window) for i in range(devices - window)]
        kv_mine = jnp.stack([kv_mine[bit_reversed(s, heads)] for s in range(heads)])
        kv_mine = jnp.concatenate([lax.ppermute(kv_mine[heads - pre :], AXES, shift), kv_mine])
    kv_other = lax.ppermute(kv_mine, AXES, swapped)
    cq, mine, edge, send = attention_call(lengths, kv_mine, kv_other, qd, pre)
    got = lax.ppermute(send, AXES, swapped)
    if pre:
        grads = combine_windows(cq, mine, got, pre, me % 2, window, devices)
    else:
        grads = combine_call(cq, mine, edge, got)
    return back_call(lengths, exchange(grads), conv_kernel, w_qkv, w_out)


def solution(mesh):
    placed = (P(AXES, None), P(), P(), P(), P(), P(AXES, None))
    return jax.shard_map(
        on_device,
        mesh=mesh,
        in_specs=placed,
        out_specs=(P(AXES, None), P(AXES, None)),
        check_vma=False,
    )
```

```python
import functools
import math

import jax
import jax.numpy as jnp
from jax import lax
from jax.experimental import pallas as pl
from jax.experimental.pallas import tpu as pltpu
from jax.sharding import PartitionSpec as P

HD = 64
KS = 7
HALF = KS // 2
MAXLEN = 2048
AXES = ("ctx", "head")
LANES = 128
EDGE = 16
PER_STEP = 4
FAR = -1e30
FRONT_STEPS = 4
BACK_STEPS = 4
VMEM_ALL = 57_500_000
VMEM_MOST = 44 * 1024 * 1024
VMEM_SOME = 24 * 1024 * 1024
F32 = jnp.float32
BF16 = jnp.bfloat16


def params(limit):
    return pltpu.CompilerParams(vmem_limit_bytes=limit)


def record_span(positions, lengths_ref):
    start = jnp.zeros_like(positions)
    stop = jnp.full_like(positions, jnp.iinfo(jnp.int32).max)
    end = jnp.int32(0)
    for i in range(lengths_ref.shape[0]):
        end = end + lengths_ref[i]
        past = end <= positions
        start = jnp.where(past, end, start)
        stop = jnp.where(past, stop, jnp.minimum(stop, end))
    return start, stop


def device_index():
    return lax.axis_index("ctx") * lax.axis_size("head") + lax.axis_index("head")


def low_lanes(shape):
    return lax.broadcasted_iota(jnp.int32, shape, len(shape) - 1) % LANES < HD


def swap_halves(x):
    return pltpu.roll(x, HD, x.ndim - 1)


def zip_low(x, y):
    return jnp.where(low_lanes(x.shape), x, swap_halves(y))


def zip_high(x, y):
    return jnp.where(low_lanes(x.shape), swap_halves(x), y)


def conv_rows(padded_ref, cols, kernel_ref, lengths_ref, first_row, rows, flip):
    pos = first_row + lax.broadcasted_iota(jnp.int32, (rows, LANES), 0)
    start, stop = record_span(pos, lengths_ref)
    masks = []
    for t in range(KS):
        at = pos + (t - HALF)
        masks.append((at >= start) & (at < stop))
    pieces = []
    for c in cols:
        lanes = pl.ds(c * LANES, LANES)
        total = padded_ref[pl.ds(8, rows), lanes]
        for t in range(KS):
            tap = kernel_ref[KS - 1 - t if flip else t, lanes]
            shifted = padded_ref[pl.ds(8 - HALF + t, rows), lanes]
            total = total + jnp.where(masks[t], shifted, 0.0) * tap[None, :]
        pieces.append(total)
    return jnp.concatenate(pieces, axis=1)


def front_kernel(
    lengths_ref, inner_ref, outer_ref, x_hbm, taps_hbm, w_hbm, cot_hbm, wo_hbm,
    out_ref, d_ref, x_ref, taps_ref, w_ref, cot_ref, wo_ref, padded, projected, d_rows, sems,
):
    rows, width = x_ref.shape
    blk = width // FRONT_STEPS

    def copy(source, target, i):
        return pltpu.make_async_copy(source, target, sems.at[i])

    whole = [
        copy(source, target, i)
        for i, (source, target) in enumerate(
            ((x_hbm, x_ref), (taps_hbm, taps_ref), (cot_hbm, cot_ref))
        )
    ]
    parts = []
    for step in range(FRONT_STEPS):
        part = pl.ds(step * blk, blk)
        at = 3 + 2 * step
        parts.append(
            (
                copy(w_hbm.at[part], w_ref.at[part], at),
                copy(wo_hbm.at[part], wo_ref.at[part], at + 1),
            )
        )
    for c in whole:
        c.start()
    for pair in parts:
        for c in pair:
            c.start()
    even = device_index() % 2 == 0
    inner, outer = inner_ref[...].astype(F32), outer_ref[...].astype(F32)
    padded[pl.ds(0, 8), :] = jnp.where(even, outer[EDGE - 8 :], inner[EDGE - 8 :])
    padded[pl.ds(8 + rows, 8), :] = jnp.where(even, inner[:8], outer[:8])
    for c in whole:
        c.wait()
    padded[pl.ds(8, rows), :] = x_ref[...].astype(F32)
    first_row = device_index() * rows
    per = blk // LANES
    for step in range(FRONT_STEPS):
        mixed = conv_rows(
            padded, range(step * per, (step + 1) * per), taps_ref, lengths_ref, first_row, rows,
            False,
        ).astype(BF16)
        parts[step][0].wait()
        part = jnp.dot(mixed, w_ref[pl.ds(step * blk, blk), :], preferred_element_type=F32)
        if step == 0:
            projected[...] = part
        else:
            projected[...] += part
        parts[step][1].wait()
        d_rows[:, pl.ds(step * blk, blk)] = lax.dot_general(
            cot_ref[...], wo_ref[pl.ds(step * blk, blk), :], (((1,), (1,)), ((), ())),
            preferred_element_type=F32,
        )
    for pair in range(width // LANES):
        lanes = pl.ds(pair * LANES, LANES)
        q, k, v = (projected[:, pl.ds(i * width + pair * LANES, LANES)] for i in range(3))
        d = d_rows[:, lanes]
        for i, mix in enumerate((zip_low, zip_high)):
            folded = mix(q[: rows // 2], q[rows // 2 :])
            out_ref[2 * pair + i] = jnp.concatenate([mix(k, v), folded]).astype(BF16)
            d_ref[2 * pair + i] = mix(d[: rows // 2], d[rows // 2 :]).astype(BF16)


def front_call(lengths, inner, outer, x, taps, w_qkv, cotangent, w_out):
    rows, width = x.shape
    heads = width // HD
    smem = pl.BlockSpec(memory_space=pltpu.SMEM)
    vmem = pl.BlockSpec(memory_space=pltpu.VMEM)
    anywhere = pl.BlockSpec(memory_space=pl.ANY)
    return pl.pallas_call(
        front_kernel,
        in_specs=[smem, vmem, vmem] + [anywhere] * 5,
        out_specs=[vmem, vmem],
        out_shape=[
            jax.ShapeDtypeStruct((heads, rows + rows // 2, LANES), BF16),
            jax.ShapeDtypeStruct((heads, rows // 2, LANES), BF16),
        ],
        scratch_shapes=[
            pltpu.VMEM(x.shape, x.dtype),
            pltpu.VMEM(taps.shape, taps.dtype),
            pltpu.VMEM(w_qkv.shape, w_qkv.dtype),
            pltpu.VMEM(cotangent.shape, cotangent.dtype),
            pltpu.VMEM(w_out.shape, w_out.dtype),
            pltpu.VMEM((rows + 16, width), F32),
            pltpu.VMEM((rows, 3 * width), F32),
            pltpu.VMEM((rows, width), F32),
            pltpu.SemaphoreType.DMA((3 + 2 * FRONT_STEPS,)),
        ],
        compiler_params=params(VMEM_ALL),
        cost_estimate=pl.CostEstimate(
            flops=8 * rows * width * width, bytes_accessed=8 * width * width, transcendentals=0
        ),
        name="front",
    )(lengths, inner, outer, x, taps, w_qkv, cotangent, w_out)


def list_visits(pre, groups, rows, lengths_ref, visit_q, visit_k):
    tile = 2 * rows
    me = device_index()
    window = 4 * groups
    base, parity = me // window * (window * rows), me % 2
    origin = base - pre * tile
    count = jnp.int32(groups)
    for u in range(groups):
        first = base + u * (2 * tile) + parity * rows
        begin, end = jnp.int32(0), jnp.int32(0)
        for i in range(lengths_ref.shape[0]):
            end = end + lengths_ref[i]
            begin = jnp.where(end <= first, end, begin)
        t_first = jnp.maximum(begin - origin, 0) // (2 * tile)

        def note(t, count, u=u):
            visit_q[count] = u
            visit_k[count] = t
            return count + 1

        count = lax.fori_loop(t_first, u + pre // 2, note, count)
    return base, parity, origin, count


def run_rest(make, first, count):
    for per in (PER_STEP, 2, 1):
        steps = (count - first) // per
        lax.fori_loop(0, steps, make(first, per), 0)
        first = first + steps * per


def forward_kernel(
    pre, place, lengths_ref, kv_mine, kv_other, kvq_ref,
    context_out, e_ref, inverse_ref, turned_context, keys_ref, turned_ref, q_ref,
    visit_q, visit_k, marked_ref, query_ref, total_ref, context_ref,
):
    slots = kvq_ref.shape[0]
    key_slots, rows, _ = kv_mine.shape
    tile, half_rows = 2 * rows, rows // 2
    tiles, groups = key_slots // 2, slots // 2
    base, parity, origin, count = list_visits(pre, groups, rows, lengths_ref, visit_q, visit_k)
    to_exp2 = HD**-0.5 * math.log2(math.e)

    def row_at(slot, side):
        return slot * tile + side * rows + lax.broadcasted_iota(jnp.int32, (rows, 1), 0)

    lane = lax.broadcasted_iota(jnp.int32, (1, LANES), 1)
    starts = jnp.zeros((1, LANES), jnp.int32)
    stops = jnp.zeros((1, LANES), jnp.int32)
    end = jnp.int32(0)
    for i in range(lengths_ref.shape[0]):
        starts = jnp.where(lane == HD + i, end, starts)
        end = end + lengths_ref[i]
        stops = jnp.where(lane == HD + i, end, stops)

    low = low_lanes((rows, LANES))
    for t in range(tiles):
        for half, source in enumerate((kv_mine, kv_other)):
            side = parity if half == 0 else 1 - parity
            for i in range(2):
                block = source[place(2 * t + i, pre)]
                at = pl.ds(half * tile + i * rows, rows)
                keys_ref[t, at] = block
                turned_ref[t, :, at] = block.T
                pos = origin + row_at(2 * t + i, side)
                mark = jnp.where((pos >= starts) & (pos < stops), 0.0, FAR)
                marked_ref[t, at] = jnp.where(low, block.astype(F32), mark).astype(BF16)
    for u in range(groups):
        for i in range(2):
            folded = kvq_ref[place(2 * u + i, 0), pl.ds(rows, half_rows)].astype(F32)
            q = jnp.concatenate([folded, swap_halves(folded)])
            at = pl.ds(i * rows, rows)
            pos = base + row_at(2 * u + i, parity)
            mark = jnp.where((pos >= starts) & (pos < stops), 1.0, 0.0)
            query_ref[u, at] = jnp.where(low, q, mark).astype(BF16)
            q_ref[u, at] = jnp.where(low, q, 0.0).astype(BF16)

    nt = (((1,), (1,)), ((), ()))
    wide = (2 * tile, tile)
    q_lane = lax.broadcasted_iota(jnp.int32, wide, 1)
    q_row = q_lane // rows * tile + q_lane % rows + parity * rows
    k_sub = lax.broadcasted_iota(jnp.int32, wide, 0)
    side = jnp.where(k_sub < tile, parity, 1 - parity)
    causal = k_sub // rows % 2 * tile + k_sub % rows + side * rows <= q_row

    def forward(i, u, t, diagonal):
        scores = lax.dot_general(marked_ref[t], query_ref[u], nt, preferred_element_type=F32)
        e = jnp.exp2(scores * to_exp2)
        if diagonal:
            e = jnp.where(causal, e, 0.0)
        e_ref[i] = e
        context = jnp.dot(turned_ref[t, HD:], e.astype(BF16), preferred_element_type=F32)
        return jnp.sum(e.reshape(2 * tile // 8, 8, tile), axis=0), context

    def forward_some(first, per):
        def run(j, carry):
            at = [first + per * j + i for i in range(per)]
            groups_at = [visit_q[i] for i in at]
            parts = [forward(i, u, visit_k[i], False) for i, u in zip(at, groups_at)]
            for u, (total, context) in zip(groups_at, parts):
                total_ref[u] += total
                context_ref[u] += context
            return carry

        return run

    for u in range(groups):
        total_ref[u], context_ref[u] = forward(u, u, u + pre // 2, True)
    run_rest(forward_some, groups, count)
    for u in range(groups):
        inverse = 1.0 / jnp.sum(total_ref[u], axis=0, keepdims=True)
        context = (context_ref[u] * inverse).astype(BF16).astype(F32)
        turned_context[u] = context
        inverse_ref[u] = jnp.broadcast_to(inverse, (8, tile))
        wide_context = jnp.concatenate([context, jnp.zeros_like(context)]).T
        for i in range(2):
            x = wide_context[i * rows : (i + 1) * rows]
            context_out[place(2 * u + i, 0)] = zip_low(x[:half_rows], x[half_rows:]).astype(BF16)


def backward_kernel(
    pre, place, lengths_ref, folded_ref, e_ref, inverse_ref, turned_context, keys_ref, turned_ref,
    q_ref, dq_ref, dkv_mine, edge_mine, send_ref,
    visit_q, visit_k, d_ref, row_ref, d_query_ref, acc_ref, dq_full,
):
    groups, tile, _ = q_ref.shape
    slots, rows, half_rows = 2 * groups, tile // 2, tile // 4
    tiles = keys_ref.shape[0]
    key_slots = 2 * tiles
    base, parity, origin, count = list_visits(pre, groups, rows, lengths_ref, visit_q, visit_k)
    unit = HD**-0.5
    nt = (((1,), (1,)), ((), ()))
    low = low_lanes((rows, LANES))
    for t in range(pre // 2):
        acc_ref[t] = jnp.zeros_like(acc_ref[t])
    for u in range(groups):
        turned = []
        for i in range(2):
            folded = folded_ref[place(2 * u + i, 0)].astype(F32)
            d = jnp.where(low, 0.0, jnp.concatenate([swap_halves(folded), folded])).astype(BF16)
            d_ref[u, pl.ds(i * rows, rows)] = d
            turned.append(d.T[HD:].astype(F32))
        products = jnp.concatenate(turned, axis=1) * turned_context[u]
        row_ref[u, pl.ds(0, 1)] = inverse_ref[u, pl.ds(0, 1)]
        row_ref[u, pl.ds(1, 1)] = jnp.sum(products, axis=0, keepdims=True)

    def backward(i, u, t):
        row = row_ref[u]
        probs = e_ref[i] * row[0:1]
        d_probs = lax.dot_general(
            keys_ref[t], d_ref[u], nt, preferred_element_type=F32
        )
        d_scores = (probs * (d_probs - row[1:2])).astype(BF16)
        both = jnp.concatenate([d_scores, probs.astype(BF16)], axis=1)
        pairs = jnp.concatenate([q_ref[u], d_ref[u]])
        d_keys = jnp.dot(both, pairs, preferred_element_type=F32)
        d_queries = jnp.dot(turned_ref[t, :HD], d_scores, preferred_element_type=F32)
        return d_keys, d_queries

    def backward_some(first, per):
        def run(j, carry):
            at = [(i, visit_q[i], visit_k[i]) for i in (first + per * j + i for i in range(per))]
            parts = [backward(i, u, t) for i, u, t in at]
            for (_, u, t), (d_keys, d_queries) in zip(at, parts):
                acc_ref[t] += d_keys
                d_query_ref[u] += d_queries
            return carry

        return run

    for u in range(groups):
        acc_ref[u + pre // 2], d_query_ref[u] = backward(u, u, u + pre // 2)
    run_rest(backward_some, groups, count)
    for u in range(groups):
        d_query = d_query_ref[u] * unit
        wide = jnp.concatenate([jnp.zeros_like(d_query), d_query]).T
        for i in range(2):
            part = wide[i * rows : (i + 1) * rows]
            dq_full[2 * u + i] = part
            dq_ref[2 * u + i] = part.astype(BF16)
    scale = jnp.where(low_lanes((1, LANES)), unit, 1.0)
    head = lax.broadcasted_iota(jnp.int32, (8, LANES), 0) < 4

    def end_rows(half, slot, first):
        slot = pre + jnp.clip(slot, 0, slots - 1)
        at = half * tile + slot % 2 * rows + first
        return acc_ref[slot // 2, pl.ds(pl.multiple_of(at, 8), 8)] * scale

    for s in range(key_slots):
        part = pl.ds(s % 2 * rows, rows)
        dkv_mine[s] = acc_ref[s // 2, part] * scale
        part = pl.ds(tile + s % 2 * rows, rows)
        send_ref[s, pl.ds(0, rows)] = (acc_ref[s // 2, part] * scale).astype(BF16)
        if s < pre:
            send_ref[s, pl.ds(rows, 16)] = jnp.zeros((16, LANES), BF16)
    for s in range(slots):
        edge_mine[s] = jnp.where(
            head, end_rows(1, s + parity, 0), end_rows(1, s - 1 + parity, rows - 8)
        )
        past, later = s - parity, s + 1 - parity
        d_edge = jnp.where(head, end_rows(0, later, 0), end_rows(0, past, rows - 8))
        q_edge = jnp.where(
            head,
            dq_full[jnp.clip(later, 0, slots - 1), pl.ds(0, 8)],
            dq_full[jnp.clip(past, 0, slots - 1), pl.ds(rows - 8, 8)],
        )
        send_ref[pre + s, pl.ds(rows, 16)] = jnp.concatenate([d_edge, q_edge]).astype(BF16)


def forward_call(lengths, kv_mine, kv_other, kvq, pre, place):
    slots = kvq.shape[0]
    key_slots, rows, _ = kv_mine.shape
    tile = 2 * rows
    tiles, groups = key_slots // 2, slots // 2
    reach = MAXLEN // (2 * tile) + 1
    visits = sum(min(u + pre // 2 + 1, reach) for u in range(groups))
    smem = pl.BlockSpec(memory_space=pltpu.SMEM)
    vmem = pl.BlockSpec(memory_space=pltpu.VMEM)
    return pl.pallas_call(
        functools.partial(forward_kernel, pre, place),
        in_specs=[smem, vmem, vmem, vmem],
        out_specs=[vmem] * 7,
        out_shape=[
            jax.ShapeDtypeStruct((slots, rows // 2, LANES), BF16),
            jax.ShapeDtypeStruct((visits, 2 * tile, tile), F32),
            jax.ShapeDtypeStruct((groups, 8, tile), F32),
            jax.ShapeDtypeStruct((groups, HD, tile), F32),
            jax.ShapeDtypeStruct((tiles, 2 * tile, LANES), BF16),
            jax.ShapeDtypeStruct((tiles, LANES, 2 * tile), BF16),
            jax.ShapeDtypeStruct((groups, tile, LANES), BF16),
        ],
        scratch_shapes=[
            pltpu.SMEM((visits,), jnp.int32),
            pltpu.SMEM((visits,), jnp.int32),
            pltpu.VMEM((tiles, 2 * tile, LANES), BF16),
            pltpu.VMEM((groups, tile, LANES), BF16),
            pltpu.VMEM((groups, 8, tile), F32),
            pltpu.VMEM((groups, HD, tile), F32),
        ],
        compiler_params=params(VMEM_SOME),
        cost_estimate=pl.CostEstimate(
            flops=4 * slots * rows * MAXLEN * LANES,
            bytes_accessed=20 * slots * rows * LANES,
            transcendentals=slots * rows * MAXLEN,
        ),
        name="attention_forward",
    )(lengths, kv_mine, kv_other, kvq)


def backward_call(lengths, folded, e, inverse, context, keys, turned, q, pre, place):
    groups, tile, _ = q.shape
    tiles = keys.shape[0]
    visits = e.shape[0]
    slots, key_slots, rows = 2 * groups, 2 * tiles, tile // 2
    smem = pl.BlockSpec(memory_space=pltpu.SMEM)
    vmem = pl.BlockSpec(memory_space=pltpu.VMEM)
    return pl.pallas_call(
        functools.partial(backward_kernel, pre, place),
        in_specs=[smem] + [vmem] * 7,
        out_specs=[vmem] * 4,
        out_shape=[
            jax.ShapeDtypeStruct((slots, rows, LANES), BF16),
            jax.ShapeDtypeStruct((key_slots, rows, LANES), F32),
            jax.ShapeDtypeStruct((slots, 8, LANES), F32),
            jax.ShapeDtypeStruct((key_slots, rows + 16, LANES), BF16),
        ],
        scratch_shapes=[
            pltpu.SMEM((visits,), jnp.int32),
            pltpu.SMEM((visits,), jnp.int32),
            pltpu.VMEM((groups, tile, LANES), BF16),
            pltpu.VMEM((groups, 8, tile), F32),
            pltpu.VMEM((groups, HD, tile), F32),
            pltpu.VMEM((tiles, 2 * tile, LANES), F32),
            pltpu.VMEM((slots, rows, LANES), F32),
        ],
        compiler_params=params(VMEM_SOME),
        cost_estimate=pl.CostEstimate(
            flops=6 * slots * rows * MAXLEN * LANES,
            bytes_accessed=20 * slots * rows * LANES,
            transcendentals=0,
        ),
        name="attention_backward",
    )(lengths, folded, e, inverse, context, keys, turned, q)


def combine_kernel(dq_ref, mine_ref, edge_ref, got_ref, out_ref):
    slots, rows, _ = dq_ref.shape
    for s in range(slots):
        at = bit_reversed(s, slots)
        got = got_ref[s].astype(F32)
        dq = dq_ref[s].astype(F32)
        folded = zip_high(dq[: rows // 2], dq[rows // 2 :])
        out_ref[at, pl.ds(0, rows)] = (mine_ref[s] + got[:rows]).astype(BF16)
        out_ref[at, pl.ds(rows, rows // 2)] = folded.astype(BF16)
        edges = [edge_ref[s] + got[rows : rows + 8], got[rows + 8 :]]
        out_ref[at, pl.ds(rows + rows // 2, 16)] = jnp.concatenate(edges).astype(BF16)


def combine_call(dq, mine, edge, got):
    slots, rows, _ = dq.shape
    vmem = pl.BlockSpec(memory_space=pltpu.VMEM)
    return pl.pallas_call(
        combine_kernel,
        in_specs=[vmem] * 4,
        out_specs=vmem,
        out_shape=jax.ShapeDtypeStruct((slots, rows + rows // 2 + 16, LANES), BF16),
        compiler_params=params(VMEM_SOME),
        name="combine",
    )(dq, mine, edge, got)


def combine_windows(dq, mine, got, pre, side, window, devices):
    slots, rows, _ = dq.shape
    dkv = mine + got[:, :rows].astype(F32)
    back = [(i + window, i) for i in range(devices - window)]
    earlier = lax.ppermute(dkv[:pre].astype(BF16), AXES, back).astype(F32)
    dkv = dkv[pre:].at[slots - pre :].add(earlier).astype(BF16)
    both = jnp.concatenate([dq, dkv], axis=2)
    tails, heads = both[:, rows - 8 :], both[:, :8]
    swapped = [(i, i ^ 1) for i in range(devices)]
    tails_other = lax.ppermute(tails, AXES, swapped)
    heads_other = lax.ppermute(heads, AXES, swapped)
    last = [(i, i + window - 1) for i in range(1, devices - window, 2)]
    tail_past = lax.ppermute(tails[-1:], AXES, last)
    head_next = lax.ppermute(heads[:1], AXES, [(j, i) for i, j in last])
    before = jnp.where(
        side == 0, jnp.concatenate([tail_past, tails_other[:-1]]), tails_other
    )
    after = jnp.where(side == 0, heads_other, jnp.concatenate([heads_other[1:], head_next]))
    edge = jnp.where(jnp.arange(8)[None, :, None] < 4, after, before)
    folded = jnp.concatenate([dq[:, : rows // 2, HD:], dq[:, rows // 2 :, HD:]], axis=2)
    grads = jnp.concatenate([dkv, folded, edge[..., LANES:], edge[..., :LANES]], axis=1)
    return jnp.stack([grads[bit_reversed(s, slots)] for s in range(slots)])


def back_kernel(
    lengths_ref, context_ref, r_ref, taps_ref, w_ref, wo_ref,
    attended_ref, grad_ref, context, grads, padded,
):
    heads = r_ref.shape[0]
    rows, width = context.shape
    blk = width // BACK_STEPS
    half_rows = rows // 2
    dkv, dq = slice(0, rows), slice(rows, rows + half_rows)
    edge_dkv = slice(dq.stop, dq.stop + 8)
    edge_dq = slice(dq.stop + 8, dq.stop + 16)
    pad = jnp.zeros((8, LANES), F32)

    def unfold(x, y):
        return jnp.concatenate([zip_low(x, y), zip_high(x, y)])

    for pair in range(heads // 2):
        lanes = pl.ds(pair * LANES, LANES)
        x, y = (context_ref[2 * pair + i].astype(F32) for i in range(2))
        context[:, lanes] = unfold(x, y).astype(BF16)
        x, y = (r_ref[2 * pair + i].astype(F32) for i in range(2))
        edge = zip_high(x[edge_dq], y[edge_dq])
        grads[:, lanes] = jnp.concatenate([unfold(x[dq], y[dq]), edge, pad]).astype(BF16)
        for i, mix in enumerate((zip_low, zip_high)):
            grads[:, pl.ds((i + 1) * width + pair * LANES, LANES)] = jnp.concatenate(
                [mix(x[dkv], y[dkv]), mix(x[edge_dkv], y[edge_dkv]), pad]
            ).astype(BF16)
    first_row = device_index() * rows
    per = blk // LANES
    for step in range(BACK_STEPS):
        part = pl.ds(step * blk, blk)
        mixed = lax.dot_general(
            grads[...], w_ref[part, :], (((1,), (1,)), ((), ())), preferred_element_type=F32
        ).astype(BF16).astype(F32)
        edge = mixed[rows : rows + 8]
        padded[pl.ds(0, 8), part] = edge
        padded[pl.ds(8, rows), part] = mixed[:rows]
        padded[pl.ds(8 + rows, 8), part] = edge
        attended_ref[:, part] = jnp.dot(
            context[...], wo_ref[:, part], preferred_element_type=F32
        ).astype(BF16)
        grad_ref[:, part] = conv_rows(
            padded, range(step * per, (step + 1) * per), taps_ref, lengths_ref, first_row, rows,
            True,
        ).astype(BF16)


def back_call(lengths, context, r, taps, w_qkv, w_out):
    heads = r.shape[0]
    rows = 2 * context.shape[1]
    width = heads * HD
    smem = pl.BlockSpec(memory_space=pltpu.SMEM)
    vmem = pl.BlockSpec(memory_space=pltpu.VMEM)
    shape = jax.ShapeDtypeStruct((rows, width), BF16)
    return pl.pallas_call(
        back_kernel,
        in_specs=[smem] + [vmem] * 5,
        out_specs=[vmem, vmem],
        out_shape=[shape, shape],
        scratch_shapes=[
            pltpu.VMEM((rows, width), BF16),
            pltpu.VMEM((rows + 16, 3 * width), BF16),
            pltpu.VMEM((rows + 16, width), F32),
        ],
        compiler_params=params(VMEM_SOME),
        cost_estimate=pl.CostEstimate(
            flops=8 * rows * width * width, bytes_accessed=8 * width * width, transcendentals=0
        ),
        name="back",
    )(lengths, context, r, taps, w_qkv, w_out)


def bit_reversed(i, count):
    bits = count.bit_length() - 1
    if count != 1 << bits:
        return i
    return sum((i >> b & 1) << (bits - 1 - b) for b in range(bits))


def on_device(tokens, conv_kernel, w_qkv, w_out, lengths, cotangent):
    rows, width = tokens.shape
    heads = width // HD
    devices = lax.axis_size(AXES)
    window = 2 * heads
    windows = devices // window
    pre = MAXLEN // (2 * rows) if windows > 1 else 0
    me = lax.axis_index(AXES)
    same_side = [
        [w * window + 2 * bit_reversed(c, heads) + side for c in range(heads)]
        for w in range(windows)
        for side in range(2)
    ]
    swapped = [(i, i ^ 1) for i in range(devices)]
    across = [(i, i + (1 if i % 2 else -1)) for i in range(1, devices - 1)]

    def exchange(x):
        return lax.all_to_all(
            x, AXES, split_axis=0, concat_axis=0, axis_index_groups=same_side, tiled=True
        )

    first, last = tokens[:EDGE], tokens[rows - EDGE :]
    even = me % 2 == 0
    inner = lax.ppermute(jnp.where(even, last, first), AXES, swapped)
    outer = lax.ppermute(jnp.where(even, first, last), AXES, across)
    kvq, folded = front_call(lengths, inner, outer, tokens, conv_kernel, w_qkv, cotangent, w_out)
    kvq = exchange(kvq)
    kvq, folded = lax.optimization_barrier((kvq, folded))
    folded = exchange(folded)
    kv_mine = kvq[:, :rows]
    if pre:
        shift = [(i, i + window) for i in range(devices - window)]
        kv_mine = jnp.stack([kv_mine[bit_reversed(s, heads)] for s in range(heads)])
        kv_mine = jnp.concatenate([lax.ppermute(kv_mine[heads - pre :], AXES, shift), kv_mine])
    kv_other = lax.ppermute(kv_mine, AXES, swapped)
    place = lambda s, ordered: s if ordered else bit_reversed(s, heads)
    context, *kept = forward_call(lengths, kv_mine, kv_other, kvq, pre, place)
    context = exchange(context)
    dq, mine, edge, send = backward_call(lengths, folded, *kept, pre, place)
    got = lax.ppermute(send, AXES, swapped)
    if pre:
        grads = combine_windows(dq, mine, got, pre, me % 2, window, devices)
    else:
        grads = combine_call(dq, mine, edge, got)
    return back_call(lengths, context, exchange(grads), conv_kernel, w_qkv, w_out)


def solution(mesh):
    placed = (P(AXES, None), P(), P(), P(), P(), P(AXES, None))
    return jax.shard_map(
        on_device,
        mesh=mesh,
        in_specs=placed,
        out_specs=(P(AXES, None), P(AXES, None)),
        check_vma=False,
    )
```

```python
import functools
import math

import jax
import jax.numpy as jnp
from jax import lax
from jax.experimental import pallas as pl
from jax.experimental.pallas import tpu as pltpu
from jax.sharding import PartitionSpec as P

HD = 64
KS = 7
HALF = KS // 2
MAXLEN = 2048
AXES = ("ctx", "head")
LANES = 128
EDGE = 16
PER_STEP = (8, 4, 2, 1)
FAR = -1e30
FRONT_STEPS = 4
BACK_STEPS = 4
VMEM_ALL = 57_500_000
VMEM_MOST = 44 * 1024 * 1024
VMEM_SOME = 24 * 1024 * 1024
F32 = jnp.float32
BF16 = jnp.bfloat16


def params(limit):
    return pltpu.CompilerParams(vmem_limit_bytes=limit)


def record_span(positions, lengths_ref):
    start = jnp.zeros_like(positions)
    stop = jnp.full_like(positions, jnp.iinfo(jnp.int32).max)
    end = jnp.int32(0)
    for i in range(lengths_ref.shape[0]):
        end = end + lengths_ref[i]
        past = end <= positions
        start = jnp.where(past, end, start)
        stop = jnp.where(past, stop, jnp.minimum(stop, end))
    return start, stop


def device_index():
    return lax.axis_index("ctx") * lax.axis_size("head") + lax.axis_index("head")


def low_lanes(shape):
    return lax.broadcasted_iota(jnp.int32, shape, len(shape) - 1) % LANES < HD


def swap_halves(x):
    return pltpu.roll(x, HD, x.ndim - 1)


def zip_low(x, y):
    return jnp.where(low_lanes(x.shape), x, swap_halves(y))


def zip_high(x, y):
    return jnp.where(low_lanes(x.shape), swap_halves(x), y)


def conv_masks(lengths_ref, first_row, rows):
    pos = first_row + lax.broadcasted_iota(jnp.int32, (rows, LANES), 0)
    start, stop = record_span(pos, lengths_ref)
    return [(pos + (t - HALF) >= start) & (pos + (t - HALF) < stop) for t in range(KS)]


def conv_rows(padded_ref, cols, kernel_ref, masks, rows, flip):
    pieces = []
    for c in cols:
        lanes = pl.ds(c * LANES, LANES)
        total = padded_ref[pl.ds(8, rows), lanes]
        for t in range(KS):
            tap = kernel_ref[KS - 1 - t if flip else t, lanes]
            shifted = padded_ref[pl.ds(8 - HALF + t, rows), lanes]
            total = total + jnp.where(masks[t], shifted, 0.0) * tap[None, :]
        pieces.append(total)
    return jnp.concatenate(pieces, axis=1)


def front_kernel(
    lengths_ref, inner_ref, outer_ref, x_hbm, taps_hbm, w_hbm, cot_hbm, wo_hbm,
    out_ref, x_ref, taps_ref, w_ref, cot_ref, wo_ref, padded, projected, d_rows, sems,
):
    rows, width = x_ref.shape
    blk = width // FRONT_STEPS

    def copy(source, target, i):
        return pltpu.make_async_copy(source, target, sems.at[i])

    whole = [
        copy(source, target, i)
        for i, (source, target) in enumerate(
            ((x_hbm, x_ref), (taps_hbm, taps_ref), (cot_hbm, cot_ref))
        )
    ]
    parts = []
    for step in range(FRONT_STEPS):
        part = pl.ds(step * blk, blk)
        at = 3 + 2 * step
        parts.append(
            (
                copy(w_hbm.at[part], w_ref.at[part], at),
                copy(wo_hbm.at[part], wo_ref.at[part], at + 1),
            )
        )
    for c in whole:
        c.start()
    for pair in parts:
        for c in pair:
            c.start()
    even = device_index() % 2 == 0
    inner, outer = inner_ref[...].astype(F32), outer_ref[...].astype(F32)
    padded[pl.ds(0, 8), :] = jnp.where(even, outer[EDGE - 8 :], inner[EDGE - 8 :])
    padded[pl.ds(8 + rows, 8), :] = jnp.where(even, inner[:8], outer[:8])
    for c in whole:
        c.wait()
    padded[pl.ds(8, rows), :] = x_ref[...].astype(F32)
    masks = conv_masks(lengths_ref, device_index() * rows, rows)
    per = blk // LANES
    for step in range(FRONT_STEPS):
        mixed = conv_rows(
            padded, range(step * per, (step + 1) * per), taps_ref, masks, rows, False
        ).astype(BF16)
        parts[step][0].wait()
        part = jnp.dot(mixed, w_ref[pl.ds(step * blk, blk), :], preferred_element_type=F32)
        if step == 0:
            projected[...] = part
        else:
            projected[...] += part
        parts[step][1].wait()
        d_rows[:, pl.ds(step * blk, blk)] = lax.dot_general(
            cot_ref[...], wo_ref[pl.ds(step * blk, blk), :], (((1,), (1,)), ((), ())),
            preferred_element_type=F32,
        )
    for pair in range(width // LANES):
        lanes = pl.ds(pair * LANES, LANES)
        q, k, v = (projected[:, pl.ds(i * width + pair * LANES, LANES)] for i in range(3))
        d = d_rows[:, lanes]
        out_ref[2 * pair] = jnp.concatenate([zip_low(k, v), zip_low(q, d)]).astype(BF16)
        out_ref[2 * pair + 1] = jnp.concatenate([zip_high(k, v), zip_high(q, d)]).astype(BF16)


def front_call(lengths, inner, outer, x, taps, w_qkv, cotangent, w_out):
    rows, width = x.shape
    heads = width // HD
    smem = pl.BlockSpec(memory_space=pltpu.SMEM)
    vmem = pl.BlockSpec(memory_space=pltpu.VMEM)
    anywhere = pl.BlockSpec(memory_space=pl.ANY)
    return pl.pallas_call(
        front_kernel,
        in_specs=[smem, vmem, vmem] + [anywhere] * 5,
        out_specs=vmem,
        out_shape=jax.ShapeDtypeStruct((heads, 2 * rows, LANES), BF16),
        scratch_shapes=[
            pltpu.VMEM(x.shape, x.dtype),
            pltpu.VMEM(taps.shape, taps.dtype),
            pltpu.VMEM(w_qkv.shape, w_qkv.dtype),
            pltpu.VMEM(cotangent.shape, cotangent.dtype),
            pltpu.VMEM(w_out.shape, w_out.dtype),
            pltpu.VMEM((rows + 16, width), F32),
            pltpu.VMEM((rows, 3 * width), F32),
            pltpu.VMEM((rows, width), F32),
            pltpu.SemaphoreType.DMA((3 + 2 * FRONT_STEPS,)),
        ],
        compiler_params=params(VMEM_ALL),
        cost_estimate=pl.CostEstimate(
            flops=8 * rows * width * width, bytes_accessed=8 * width * width, transcendentals=0
        ),
        name="front",
    )(lengths, inner, outer, x, taps, w_qkv, cotangent, w_out)


def attention_kernel(
    pre, place, lengths_ref, kv_mine, kv_other, qd_ref,
    cq_ref, dkv_mine, edge_mine, send_ref,
    visit_q, visit_k, keys_ref, marked_ref, turned_ref, query_ref, qd_cat_ref, d_turned_ref, e_ref,
    total_ref, context_ref, row_ref, d_query_ref, acc_ref, cq_full,
):
    slots = qd_ref.shape[0]
    key_slots, rows, _ = kv_mine.shape
    tile = 2 * rows
    tiles, groups = key_slots // 2, slots // 2
    me = device_index()
    window = 2 * slots
    base, parity = me // window * (window * rows), me % 2
    origin = base - pre * tile
    unit = HD**-0.5
    to_exp2 = unit * math.log2(math.e)

    def row_at(slot, side):
        return slot * tile + side * rows + lax.broadcasted_iota(jnp.int32, (rows, 1), 0)

    lane = lax.broadcasted_iota(jnp.int32, (1, LANES), 1)
    starts = jnp.zeros((1, LANES), jnp.int32)
    stops = jnp.zeros((1, LANES), jnp.int32)
    end = jnp.int32(0)
    for i in range(lengths_ref.shape[0]):
        starts = jnp.where(lane == HD + i, end, starts)
        end = end + lengths_ref[i]
        stops = jnp.where(lane == HD + i, end, stops)

    count = jnp.int32(groups)
    for u in range(groups):
        first = base + u * (2 * tile) + parity * rows
        begin, end = jnp.int32(0), jnp.int32(0)
        for i in range(lengths_ref.shape[0]):
            end = end + lengths_ref[i]
            begin = jnp.where(end <= first, end, begin)
        t_first = jnp.maximum(begin - origin, 0) // (2 * tile)

        def note(t, count, u=u):
            visit_q[count] = u
            visit_k[count] = t
            return count + 1

        count = lax.fori_loop(t_first, u + pre // 2, note, count)

    low = low_lanes((rows, LANES))
    for t in range(tiles):
        for half, source in enumerate((kv_mine, kv_other)):
            side = parity if half == 0 else 1 - parity
            for i in range(2):
                block = source[place(2 * t + i, pre)]
                at = pl.ds(half * tile + i * rows, rows)
                keys_ref[t, at] = block
                turned_ref[t, :, at] = block.T
                pos = origin + row_at(2 * t + i, side)
                mark = jnp.where((pos >= starts) & (pos < stops), 0.0, FAR)
                marked_ref[t, at] = jnp.where(low, block.astype(F32), mark).astype(BF16)
    for t in range(pre // 2):
        acc_ref[t] = jnp.zeros_like(acc_ref[t])
    for u in range(groups):
        for i in range(2):
            qd = qd_ref[place(2 * u + i, 0), pl.ds(rows, rows)]
            at = pl.ds(i * rows, rows)
            d_turned_ref[u, :, at] = qd.T[HD:].astype(F32)
            qd = qd.astype(F32)
            pos = base + row_at(2 * u + i, parity)
            mark = jnp.where((pos >= starts) & (pos < stops), 1.0, 0.0)
            query_ref[u, at] = jnp.where(low, qd, mark).astype(BF16)
            qd_cat_ref[u, at] = jnp.where(low, qd, 0.0).astype(BF16)
            qd_cat_ref[u, pl.ds(tile + i * rows, rows)] = jnp.where(low, 0.0, qd).astype(BF16)

    nt = (((1,), (1,)), ((), ()))
    wide = (2 * tile, tile)
    q_lane = lax.broadcasted_iota(jnp.int32, wide, 1)
    q_row = q_lane // rows * tile + q_lane % rows + parity * rows
    k_sub = lax.broadcasted_iota(jnp.int32, wide, 0)
    side = jnp.where(k_sub < tile, parity, 1 - parity)
    causal = k_sub // rows % 2 * tile + k_sub % rows + side * rows <= q_row

    def forward(i, u, t, diagonal):
        scores = lax.dot_general(marked_ref[t], query_ref[u], nt, preferred_element_type=F32)
        e = jnp.exp2(scores * to_exp2)
        if diagonal:
            e = jnp.where(causal, e, 0.0)
        e_ref[i] = e
        context = jnp.dot(turned_ref[t, HD:], e.astype(BF16), preferred_element_type=F32)
        return jnp.sum(e.reshape(2 * tile // 8, 8, tile), axis=0), context

    def forward_some(first, per):
        def run(j, carry):
            at = [first + per * j + i for i in range(per)]
            groups_at = [visit_q[i] for i in at]
            parts = [forward(i, u, visit_k[i], False) for i, u in zip(at, groups_at)]
            for u, (total, context) in zip(groups_at, parts):
                total_ref[u] += total
                context_ref[u] += context
            return carry

        return run

    def run_rest(make):
        first = groups
        for per in PER_STEP:
            steps = (count - first) // per
            lax.fori_loop(0, steps, make(first, per), 0)
            first = first + steps * per

    for u in range(groups):
        total_ref[u], context_ref[u] = forward(u, u, u + pre // 2, True)
    run_rest(forward_some)
    for u in range(groups):
        inverse = 1.0 / jnp.sum(total_ref[u], axis=0, keepdims=True)
        context = (context_ref[u] * inverse).astype(BF16).astype(F32)
        context_ref[u] = context
        row_ref[u, pl.ds(0, 1)] = inverse
        row_ref[u, pl.ds(1, 1)] = jnp.sum(d_turned_ref[u] * context, axis=0, keepdims=True)

    def backward(i, u, t):
        row = row_ref[u]
        probs = e_ref[i] * row[0:1]
        d_probs = lax.dot_general(
            keys_ref[t], qd_cat_ref[u, pl.ds(tile, tile)], nt, preferred_element_type=F32
        )
        d_scores = (probs * (d_probs - row[1:2])).astype(BF16)
        both = jnp.concatenate([d_scores, probs.astype(BF16)], axis=1)
        d_keys = jnp.dot(both, qd_cat_ref[u], preferred_element_type=F32)
        d_queries = jnp.dot(turned_ref[t, :HD], d_scores, preferred_element_type=F32)
        return d_keys, d_queries

    def backward_some(first, per):
        def run(j, carry):
            at = [(i, visit_q[i], visit_k[i]) for i in (first + per * j + i for i in range(per))]
            parts = [backward(i, u, t) for i, u, t in at]
            for (_, u, t), (d_keys, d_queries) in zip(at, parts):
                acc_ref[t] += d_keys
                d_query_ref[u] += d_queries
            return carry

        return run

    for u in range(groups):
        acc_ref[u + pre // 2], d_query_ref[u] = backward(u, u, u + pre // 2)
    run_rest(backward_some)
    for u in range(groups):
        packed = jnp.concatenate([context_ref[u], d_query_ref[u] * unit], axis=0).T
        for i in range(2):
            part = packed[i * rows : (i + 1) * rows]
            cq_full[2 * u + i] = part
            cq_ref[2 * u + i] = part.astype(BF16)
    scale = jnp.where(low_lanes((1, LANES)), unit, 1.0)
    head = lax.broadcasted_iota(jnp.int32, (8, LANES), 0) < 4

    def end_rows(half, slot, first):
        slot = pre + jnp.clip(slot, 0, slots - 1)
        at = half * tile + slot % 2 * rows + first
        return acc_ref[slot // 2, pl.ds(pl.multiple_of(at, 8), 8)] * scale

    for s in range(key_slots):
        part = pl.ds(s % 2 * rows, rows)
        dkv_mine[s] = acc_ref[s // 2, part] * scale
        part = pl.ds(tile + s % 2 * rows, rows)
        send_ref[s, pl.ds(0, rows)] = (acc_ref[s // 2, part] * scale).astype(BF16)
        if s < pre:
            send_ref[s, pl.ds(rows, 16)] = jnp.zeros((16, LANES), BF16)
    for s in range(slots):
        edge_mine[s] = jnp.where(
            head, end_rows(1, s + parity, 0), end_rows(1, s - 1 + parity, rows - 8)
        )
        past, later = s - parity, s + 1 - parity
        d_edge = jnp.where(head, end_rows(0, later, 0), end_rows(0, past, rows - 8))
        q_edge = jnp.where(
            head,
            cq_full[jnp.clip(later, 0, slots - 1), pl.ds(0, 8)],
            cq_full[jnp.clip(past, 0, slots - 1), pl.ds(rows - 8, 8)],
        )
        send_ref[pre + s, pl.ds(rows, 16)] = jnp.concatenate([d_edge, q_edge]).astype(BF16)


def attention_call(lengths, kv_mine, kv_other, qd, pre):
    slots = qd.shape[0]
    key_slots, rows, _ = kv_mine.shape
    tile = 2 * rows
    tiles, groups = key_slots // 2, slots // 2
    reach = MAXLEN // (2 * tile) + 1
    place = lambda s, ordered: s if ordered else bit_reversed(s, slots)
    visits = sum(min(u + pre // 2 + 1, reach) for u in range(groups))
    smem = pl.BlockSpec(memory_space=pltpu.SMEM)
    vmem = pl.BlockSpec(memory_space=pltpu.VMEM)
    return pl.pallas_call(
        functools.partial(attention_kernel, pre, place),
        in_specs=[smem, vmem, vmem, vmem],
        out_specs=[vmem, vmem, vmem, vmem],
        out_shape=[
            jax.ShapeDtypeStruct((slots, rows, LANES), BF16),
            jax.ShapeDtypeStruct((key_slots, rows, LANES), F32),
            jax.ShapeDtypeStruct((slots, 8, LANES), F32),
            jax.ShapeDtypeStruct((key_slots, rows + 16, LANES), BF16),
        ],
        scratch_shapes=[
            pltpu.SMEM((visits,), jnp.int32),
            pltpu.SMEM((visits,), jnp.int32),
            pltpu.VMEM((tiles, 2 * tile, LANES), BF16),
            pltpu.VMEM((tiles, 2 * tile, LANES), BF16),
            pltpu.VMEM((tiles, LANES, 2 * tile), BF16),
            pltpu.VMEM((groups, tile, LANES), BF16),
            pltpu.VMEM((groups, 2 * tile, LANES), BF16),
            pltpu.VMEM((groups, HD, tile), F32),
            pltpu.VMEM((visits, 2 * tile, tile), F32),
            pltpu.VMEM((groups, 8, tile), F32),
            pltpu.VMEM((groups, HD, tile), F32),
            pltpu.VMEM((groups, 8, tile), F32),
            pltpu.VMEM((groups, HD, tile), F32),
            pltpu.VMEM((tiles, 2 * tile, LANES), F32),
            pltpu.VMEM((slots, rows, LANES), F32),
        ],
        compiler_params=params(VMEM_MOST),
        cost_estimate=pl.CostEstimate(
            flops=10 * slots * rows * MAXLEN * LANES,
            bytes_accessed=20 * slots * rows * LANES,
            transcendentals=slots * rows * MAXLEN,
        ),
        name="attention",
    )(lengths, kv_mine, kv_other, qd)


def combine_kernel(cq_ref, mine_ref, edge_ref, got_ref, out_ref):
    slots, rows, _ = cq_ref.shape
    for s in range(slots):
        at = bit_reversed(s, slots)
        out_ref[at, pl.ds(0, rows)] = cq_ref[s]
        got = got_ref[s].astype(F32)
        out_ref[at, pl.ds(rows, rows)] = (mine_ref[s] + got[:rows]).astype(BF16)
        edges = [edge_ref[s] + got[rows : rows + 8], got[rows + 8 :]]
        out_ref[at, pl.ds(2 * rows, 16)] = jnp.concatenate(edges).astype(BF16)


def combine_call(cq, mine, edge, got):
    slots, rows, _ = cq.shape
    vmem = pl.BlockSpec(memory_space=pltpu.VMEM)
    return pl.pallas_call(
        combine_kernel,
        in_specs=[vmem] * 4,
        out_specs=vmem,
        out_shape=jax.ShapeDtypeStruct((slots, 2 * rows + 16, LANES), BF16),
        compiler_params=params(VMEM_SOME),
        name="combine",
    )(cq, mine, edge, got)


def combine_windows(cq, mine, got, pre, side, window, devices):
    slots, rows, _ = cq.shape
    dkv = mine + got[:, :rows].astype(F32)
    back = [(i + window, i) for i in range(devices - window)]
    earlier = lax.ppermute(dkv[:pre].astype(BF16), AXES, back).astype(F32)
    dkv = dkv[pre:].at[slots - pre :].add(earlier).astype(BF16)
    both = jnp.concatenate([cq, dkv], axis=2)
    tails, heads = both[:, rows - 8 :], both[:, :8]
    swapped = [(i, i ^ 1) for i in range(devices)]
    tails_other = lax.ppermute(tails, AXES, swapped)
    heads_other = lax.ppermute(heads, AXES, swapped)
    last = [(i, i + window - 1) for i in range(1, devices - window, 2)]
    tail_past = lax.ppermute(tails[-1:], AXES, last)
    head_next = lax.ppermute(heads[:1], AXES, [(j, i) for i, j in last])
    before = jnp.where(
        side == 0, jnp.concatenate([tail_past, tails_other[:-1]]), tails_other
    )
    after = jnp.where(side == 0, heads_other, jnp.concatenate([heads_other[1:], head_next]))
    edge = jnp.where(jnp.arange(8)[None, :, None] < 4, after, before)
    grads = jnp.concatenate([cq, dkv, edge[..., LANES:], edge[..., :LANES]], axis=1)
    return jnp.stack([grads[bit_reversed(s, slots)] for s in range(slots)])


def back_kernel(
    lengths_ref, r_ref, taps_ref, w_ref, wo_ref, attended_ref, grad_ref, context, grads, padded
):
    heads = r_ref.shape[0]
    rows, width = context.shape
    blk = width // BACK_STEPS
    main, dkv = slice(0, rows), slice(rows, 2 * rows)
    edge_dkv, edge_cq = slice(2 * rows, 2 * rows + 8), slice(2 * rows + 8, 2 * rows + 16)
    pad = jnp.zeros((8, LANES), F32)
    for pair in range(heads // 2):
        x, y = (r_ref[2 * pair + i, pl.ds(0, rows)].astype(F32) for i in range(2))
        context[:, pl.ds(pair * LANES, LANES)] = zip_low(x, y).astype(BF16)
    for step in range(BACK_STEPS):
        part = pl.ds(step * blk, blk)
        attended_ref[:, part] = jnp.dot(
            context[...], wo_ref[:, part], preferred_element_type=F32
        ).astype(BF16)
    for pair in range(heads // 2):
        x, y = (r_ref[2 * pair + i].astype(F32) for i in range(2))

        def gather(mix, part, edge):
            return jnp.concatenate([mix(x[part], y[part]), mix(x[edge], y[edge]), pad]).astype(BF16)

        lanes = pl.ds(pair * LANES, LANES)
        grads[:, lanes] = gather(zip_high, main, edge_cq)
        grads[:, pl.ds(width + pair * LANES, LANES)] = gather(zip_low, dkv, edge_dkv)
        grads[:, pl.ds(2 * width + pair * LANES, LANES)] = gather(zip_high, dkv, edge_dkv)
    masks = conv_masks(lengths_ref, device_index() * rows, rows)
    per = blk // LANES
    for step in range(BACK_STEPS):
        part = pl.ds(step * blk, blk)
        mixed = lax.dot_general(
            grads[...], w_ref[part, :], (((1,), (1,)), ((), ())), preferred_element_type=F32
        ).astype(BF16).astype(F32)
        edge = mixed[rows : rows + 8]
        padded[pl.ds(0, 8), part] = edge
        padded[pl.ds(8, rows), part] = mixed[:rows]
        padded[pl.ds(8 + rows, 8), part] = edge
        grad_ref[:, part] = conv_rows(
            padded, range(step * per, (step + 1) * per), taps_ref, masks, rows, True
        ).astype(BF16)


def back_call(lengths, r, taps, w_qkv, w_out):
    heads = r.shape[0]
    rows = (r.shape[1] - 16) // 2
    width = heads * HD
    smem = pl.BlockSpec(memory_space=pltpu.SMEM)
    vmem = pl.BlockSpec(memory_space=pltpu.VMEM)
    shape = jax.ShapeDtypeStruct((rows, width), BF16)
    return pl.pallas_call(
        back_kernel,
        in_specs=[smem, vmem, vmem, vmem, vmem],
        out_specs=[vmem, vmem],
        out_shape=[shape, shape],
        scratch_shapes=[
            pltpu.VMEM((rows, width), BF16),
            pltpu.VMEM((rows + 16, 3 * width), BF16),
            pltpu.VMEM((rows + 16, width), F32),
        ],
        compiler_params=params(VMEM_SOME),
        cost_estimate=pl.CostEstimate(
            flops=8 * rows * width * width, bytes_accessed=8 * width * width, transcendentals=0
        ),
        name="back",
    )(lengths, r, taps, w_qkv, w_out)


def bit_reversed(i, count):
    bits = count.bit_length() - 1
    if count != 1 << bits:
        return i
    return sum((i >> b & 1) << (bits - 1 - b) for b in range(bits))


def on_device(tokens, conv_kernel, w_qkv, w_out, lengths, cotangent):
    rows, width = tokens.shape
    heads = width // HD
    devices = lax.axis_size(AXES)
    window = 2 * heads
    windows = devices // window
    pre = MAXLEN // (2 * rows) if windows > 1 else 0
    me = lax.axis_index(AXES)
    same_side = [
        [w * window + 2 * bit_reversed(c, heads) + side for c in range(heads)]
        for w in range(windows)
        for side in range(2)
    ]
    swapped = [(i, i ^ 1) for i in range(devices)]
    across = [(i, i + (1 if i % 2 else -1)) for i in range(1, devices - 1)]

    def exchange(x):
        return lax.all_to_all(
            x, AXES, split_axis=0, concat_axis=0, axis_index_groups=same_side, tiled=True
        )

    first, last = tokens[:EDGE], tokens[rows - EDGE :]
    even = me % 2 == 0
    inner = lax.ppermute(jnp.where(even, last, first), AXES, swapped)
    outer = lax.ppermute(jnp.where(even, first, last), AXES, across)
    sent = front_call(lengths, inner, outer, tokens, conv_kernel, w_qkv, cotangent, w_out)
    qd = exchange(sent)
    kv_mine = qd[:, :rows]
    if pre:
        shift = [(i, i + window) for i in range(devices - window)]
        kv_mine = jnp.stack([kv_mine[bit_reversed(s, heads)] for s in range(heads)])
        kv_mine = jnp.concatenate([lax.ppermute(kv_mine[heads - pre :], AXES, shift), kv_mine])
    kv_other = lax.ppermute(kv_mine, AXES, swapped)
    cq, mine, edge, send = attention_call(lengths, kv_mine, kv_other, qd, pre)
    got = lax.ppermute(send, AXES, swapped)
    if pre:
        grads = combine_windows(cq, mine, got, pre, me % 2, window, devices)
    else:
        grads = combine_call(cq, mine, edge, got)
    return back_call(lengths, exchange(grads), conv_kernel, w_qkv, w_out)


def solution(mesh):
    placed = (P(AXES, None), P(), P(), P(), P(), P(AXES, None))
    return jax.shard_map(
        on_device,
        mesh=mesh,
        in_specs=placed,
        out_specs=(P(AXES, None), P(AXES, None)),
        check_vma=False,
    )
```

```python
import functools
import math

import jax
import jax.numpy as jnp
from jax import lax
from jax.experimental import pallas as pl
from jax.experimental.pallas import tpu as pltpu
from jax.sharding import PartitionSpec as P

HD = 64
KS = 7
HALF = KS // 2
MAXLEN = 2048
AXES = ("ctx", "head")
LANES = 128
EDGE = 16
PER_STEP = (8, 4, 2, 1)
FAR = -1e30
FRONT_STEPS = 4
BACK_STEPS = 4
VMEM_ALL = 55_000_000
VMEM_MOST = 44 * 1024 * 1024
VMEM_SOME = 24 * 1024 * 1024
F32 = jnp.float32
BF16 = jnp.bfloat16


def params(limit):
    return pltpu.CompilerParams(vmem_limit_bytes=limit)


def record_span(positions, lengths_ref):
    start = jnp.zeros_like(positions)
    stop = jnp.full_like(positions, jnp.iinfo(jnp.int32).max)
    end = jnp.int32(0)
    for i in range(lengths_ref.shape[0]):
        end = end + lengths_ref[i]
        past = end <= positions
        start = jnp.where(past, end, start)
        stop = jnp.where(past, stop, jnp.minimum(stop, end))
    return start, stop


def device_index():
    return lax.axis_index("ctx") * lax.axis_size("head") + lax.axis_index("head")


def low_lanes(shape):
    return lax.broadcasted_iota(jnp.int32, shape, len(shape) - 1) % LANES < HD


def swap_halves(x):
    return pltpu.roll(x, HD, x.ndim - 1)


def zip_low(x, y):
    return jnp.where(low_lanes(x.shape), x, swap_halves(y))


def zip_high(x, y):
    return jnp.where(low_lanes(x.shape), swap_halves(x), y)


def conv_masks(lengths_ref, first_row, rows):
    pos = first_row + lax.broadcasted_iota(jnp.int32, (rows, LANES), 0)
    start, stop = record_span(pos, lengths_ref)
    return [(pos + (t - HALF) >= start) & (pos + (t - HALF) < stop) for t in range(KS)]


def conv_rows(padded_ref, cols, kernel_ref, masks, rows, flip):
    pieces = []
    for c in cols:
        lanes = pl.ds(c * LANES, LANES)
        total = padded_ref[pl.ds(8, rows), lanes]
        for t in range(KS):
            tap = kernel_ref[KS - 1 - t if flip else t, lanes]
            shifted = padded_ref[pl.ds(8 - HALF + t, rows), lanes]
            total = total + jnp.where(masks[t], shifted, 0.0) * tap[None, :]
        pieces.append(total)
    return jnp.concatenate(pieces, axis=1)


def front_kernel(
    lengths_ref, inner_ref, outer_ref, x_hbm, taps_hbm, w_hbm, cot_hbm, wo_hbm,
    out_ref, x_ref, taps_ref, w_ref, cot_ref, wo_ref, padded, projected, d_rows, sems,
):
    rows, width = x_ref.shape
    blk = width // FRONT_STEPS

    def copy(source, target, i):
        return pltpu.make_async_copy(source, target, sems.at[i])

    whole = [
        copy(source, target, i)
        for i, (source, target) in enumerate(
            ((x_hbm, x_ref), (taps_hbm, taps_ref), (cot_hbm, cot_ref))
        )
    ]
    parts = []
    for step in range(FRONT_STEPS):
        part = pl.ds(step * blk, blk)
        at = 3 + 2 * step
        parts.append(
            (
                copy(w_hbm.at[part], w_ref.at[part], at),
                copy(wo_hbm.at[part], wo_ref.at[part], at + 1),
            )
        )
    for c in whole:
        c.start()
    for pair in parts:
        for c in pair:
            c.start()
    even = device_index() % 2 == 0
    inner, outer = inner_ref[...].astype(F32), outer_ref[...].astype(F32)
    padded[pl.ds(0, 8), :] = jnp.where(even, outer[EDGE - 8 :], inner[EDGE - 8 :])
    padded[pl.ds(8 + rows, 8), :] = jnp.where(even, inner[:8], outer[:8])
    for c in whole:
        c.wait()
    padded[pl.ds(8, rows), :] = x_ref[...].astype(F32)
    masks = conv_masks(lengths_ref, device_index() * rows, rows)
    per = blk // LANES
    for step in range(FRONT_STEPS):
        mixed = conv_rows(
            padded, range(step * per, (step + 1) * per), taps_ref, masks, rows, False
        ).astype(BF16)
        parts[step][0].wait()
        part = jnp.dot(mixed, w_ref[pl.ds(step * blk, blk), :], preferred_element_type=F32)
        if step == 0:
            projected[...] = part
        else:
            projected[...] += part
        parts[step][1].wait()
        d_rows[:, pl.ds(step * blk, blk)] = lax.dot_general(
            cot_ref[...], wo_ref[pl.ds(step * blk, blk), :], (((1,), (1,)), ((), ())),
            preferred_element_type=F32,
        )
    for pair in range(width // LANES):
        lanes = pl.ds(pair * LANES, LANES)
        q, k, v = (projected[:, pl.ds(i * width + pair * LANES, LANES)] for i in range(3))
        d = d_rows[:, lanes]
        out_ref[2 * pair] = jnp.concatenate([zip_low(k, v), zip_low(q, d)]).astype(BF16)
        out_ref[2 * pair + 1] = jnp.concatenate([zip_high(k, v), zip_high(q, d)]).astype(BF16)


def front_call(lengths, inner, outer, x, taps, w_qkv, cotangent, w_out):
    rows, width = x.shape
    heads = width // HD
    smem = pl.BlockSpec(memory_space=pltpu.SMEM)
    vmem = pl.BlockSpec(memory_space=pltpu.VMEM)
    anywhere = pl.BlockSpec(memory_space=pl.ANY)
    return pl.pallas_call(
        front_kernel,
        in_specs=[smem, vmem, vmem] + [anywhere] * 5,
        out_specs=vmem,
        out_shape=jax.ShapeDtypeStruct((heads, 2 * rows, LANES), BF16),
        scratch_shapes=[
            pltpu.VMEM(x.shape, x.dtype),
            pltpu.VMEM(taps.shape, taps.dtype),
            pltpu.VMEM(w_qkv.shape, w_qkv.dtype),
            pltpu.VMEM(cotangent.shape, cotangent.dtype),
            pltpu.VMEM(w_out.shape, w_out.dtype),
            pltpu.VMEM((rows + 16, width), F32),
            pltpu.VMEM((rows, 3 * width), F32),
            pltpu.VMEM((rows, width), F32),
            pltpu.SemaphoreType.DMA((3 + 2 * FRONT_STEPS,)),
        ],
        compiler_params=params(VMEM_ALL),
        cost_estimate=pl.CostEstimate(
            flops=8 * rows * width * width, bytes_accessed=8 * width * width, transcendentals=0
        ),
        name="front",
    )(lengths, inner, outer, x, taps, w_qkv, cotangent, w_out)


def attention_kernel(
    pre, place, lengths_ref, kv_mine, kv_other, qd_ref,
    cq_ref, dkv_mine, edge_mine, send_ref,
    visit_q, visit_k, keys_ref, marked_ref, turned_ref, query_ref, qd_cat_ref, d_turned_ref, e_ref,
    total_ref, context_ref, row_ref, d_query_ref, acc_ref, cq_full,
):
    slots = qd_ref.shape[0]
    key_slots, rows, _ = kv_mine.shape
    tile = 2 * rows
    tiles, groups = key_slots // 2, slots // 2
    me = device_index()
    window = 2 * slots
    base, parity = me // window * (window * rows), me % 2
    origin = base - pre * tile
    unit = HD**-0.5
    to_exp2 = unit * math.log2(math.e)

    row_in_block = lax.broadcasted_iota(jnp.int32, (rows, LANES), 0)

    def recorded(slot, side, first):
        at = first + slot * tile + side * rows
        return (row_in_block >= starts - at) & (row_in_block < stops - at)

    lane = lax.broadcasted_iota(jnp.int32, (1, LANES), 1)
    starts = jnp.zeros((1, LANES), jnp.int32)
    stops = jnp.zeros((1, LANES), jnp.int32)
    end = jnp.int32(0)
    for i in range(lengths_ref.shape[0]):
        starts = jnp.where(lane == HD + i, end, starts)
        end = end + lengths_ref[i]
        stops = jnp.where(lane == HD + i, end, stops)

    count = jnp.int32(groups)
    for u in range(groups):
        first = base + u * (2 * tile) + parity * rows
        begin, end = jnp.int32(0), jnp.int32(0)
        for i in range(lengths_ref.shape[0]):
            end = end + lengths_ref[i]
            begin = jnp.where(end <= first, end, begin)
        t_first = jnp.maximum(begin - origin, 0) // (2 * tile)

        def note(t, count, u=u):
            visit_q[count] = u
            visit_k[count] = t
            return count + 1

        count = lax.fori_loop(t_first, u + pre // 2, note, count)

    low = low_lanes((rows, LANES))
    for t in range(tiles):
        for half, source in enumerate((kv_mine, kv_other)):
            side = parity if half == 0 else 1 - parity
            for i in range(2):
                block = source[place(2 * t + i, pre)]
                at = pl.ds(half * tile + i * rows, rows)
                keys_ref[t, at] = block
                turned_ref[t, :, at] = block.T
                mark = jnp.where(recorded(2 * t + i, side, origin), 0.0, FAR)
                marked_ref[t, at] = jnp.where(low, block.astype(F32), mark).astype(BF16)
    for t in range(pre // 2):
        acc_ref[t] = jnp.zeros_like(acc_ref[t])
    for u in range(groups):
        for i in range(2):
            qd = qd_ref[place(2 * u + i, 0), pl.ds(rows, rows)]
            at = pl.ds(i * rows, rows)
            d_turned_ref[u, :, at] = qd.T[HD:].astype(F32)
            qd = qd.astype(F32)
            mark = jnp.where(recorded(2 * u + i, parity, base), 1.0, 0.0)
            query_ref[u, at] = jnp.where(low, qd, mark).astype(BF16)
            qd_cat_ref[u, at] = jnp.where(low, qd, 0.0).astype(BF16)
            qd_cat_ref[u, pl.ds(tile + i * rows, rows)] = jnp.where(low, 0.0, qd).astype(BF16)

    nt = (((1,), (1,)), ((), ()))
    wide = (2 * tile, tile)
    q_lane = lax.broadcasted_iota(jnp.int32, wide, 1)
    q_row = q_lane // rows * tile + q_lane % rows + parity * rows
    k_sub = lax.broadcasted_iota(jnp.int32, wide, 0)
    side = jnp.where(k_sub < tile, parity, 1 - parity)
    causal = k_sub // rows % 2 * tile + k_sub % rows + side * rows <= q_row

    def forward(i, u, t, diagonal):
        scores = lax.dot_general(marked_ref[t], query_ref[u], nt, preferred_element_type=F32)
        e = jnp.exp2(scores * to_exp2)
        if diagonal:
            e = jnp.where(causal, e, 0.0)
        e_ref[i] = e
        context = jnp.dot(turned_ref[t, HD:], e.astype(BF16), preferred_element_type=F32)
        return jnp.sum(e.reshape(2 * tile // 8, 8, tile), axis=0), context

    def forward_some(first, per):
        def run(j, carry):
            at = [first + per * j + i for i in range(per)]
            groups_at = [visit_q[i] for i in at]
            parts = [forward(i, u, visit_k[i], False) for i, u in zip(at, groups_at)]
            for u, (total, context) in zip(groups_at, parts):
                total_ref[u] += total
                context_ref[u] += context
            return carry

        return run

    def run_rest(make):
        first = groups
        for per in PER_STEP:
            steps = (count - first) // per
            lax.fori_loop(0, steps, make(first, per), 0)
            first = first + steps * per

    for u in range(groups):
        total_ref[u], context_ref[u] = forward(u, u, u + pre // 2, True)
    run_rest(forward_some)
    for u in range(groups):
        inverse = 1.0 / jnp.sum(total_ref[u], axis=0, keepdims=True)
        context = (context_ref[u] * inverse).astype(BF16).astype(F32)
        context_ref[u] = context
        row_ref[u, pl.ds(0, 1)] = inverse
        row_ref[u, pl.ds(1, 1)] = jnp.sum(d_turned_ref[u] * context, axis=0, keepdims=True)

    def backward(i, u, t):
        row = row_ref[u]
        probs = e_ref[i] * row[0:1]
        d_probs = lax.dot_general(
            keys_ref[t], qd_cat_ref[u, pl.ds(tile, tile)], nt, preferred_element_type=F32
        )
        d_scores = (probs * (d_probs - row[1:2])).astype(BF16)
        both = jnp.concatenate([d_scores, probs.astype(BF16)], axis=1)
        d_keys = jnp.dot(both, qd_cat_ref[u], preferred_element_type=F32)
        d_queries = jnp.dot(turned_ref[t, :HD], d_scores, preferred_element_type=F32)
        return d_keys, d_queries

    def backward_some(first, per):
        def run(j, carry):
            at = [(i, visit_q[i], visit_k[i]) for i in (first + per * j + i for i in range(per))]
            parts = [backward(i, u, t) for i, u, t in at]
            for (_, u, t), (d_keys, d_queries) in zip(at, parts):
                acc_ref[t] += d_keys
                d_query_ref[u] += d_queries
            return carry

        return run

    for u in range(groups):
        acc_ref[u + pre // 2], d_query_ref[u] = backward(u, u, u + pre // 2)
    run_rest(backward_some)
    for u in range(groups):
        packed = jnp.concatenate([context_ref[u], d_query_ref[u] * unit], axis=0).T
        for i in range(2):
            part = packed[i * rows : (i + 1) * rows]
            cq_full[2 * u + i] = part
            cq_ref[2 * u + i] = part.astype(BF16)
    scale = jnp.where(low_lanes((1, LANES)), unit, 1.0)
    head = lax.broadcasted_iota(jnp.int32, (8, LANES), 0) < 4

    def end_rows(half, slot, first):
        slot = pre + jnp.clip(slot, 0, slots - 1)
        at = half * tile + slot % 2 * rows + first
        return acc_ref[slot // 2, pl.ds(pl.multiple_of(at, 8), 8)] * scale

    for s in range(key_slots):
        part = pl.ds(s % 2 * rows, rows)
        dkv_mine[s] = acc_ref[s // 2, part] * scale
        part = pl.ds(tile + s % 2 * rows, rows)
        send_ref[s, pl.ds(0, rows)] = (acc_ref[s // 2, part] * scale).astype(BF16)
        if s < pre:
            send_ref[s, pl.ds(rows, 16)] = jnp.zeros((16, LANES), BF16)
    for s in range(slots):
        edge_mine[s] = jnp.where(
            head, end_rows(1, s + parity, 0), end_rows(1, s - 1 + parity, rows - 8)
        )
        past, later = s - parity, s + 1 - parity
        d_edge = jnp.where(head, end_rows(0, later, 0), end_rows(0, past, rows - 8))
        q_edge = jnp.where(
            head,
            cq_full[jnp.clip(later, 0, slots - 1), pl.ds(0, 8)],
            cq_full[jnp.clip(past, 0, slots - 1), pl.ds(rows - 8, 8)],
        )
        send_ref[pre + s, pl.ds(rows, 16)] = jnp.concatenate([d_edge, q_edge]).astype(BF16)


def attention_call(lengths, kv_mine, kv_other, qd, pre):
    slots = qd.shape[0]
    key_slots, rows, _ = kv_mine.shape
    tile = 2 * rows
    tiles, groups = key_slots // 2, slots // 2
    reach = MAXLEN // (2 * tile) + 1
    place = lambda s, ordered: s if ordered else bit_reversed(s, slots)
    visits = sum(min(u + pre // 2 + 1, reach) for u in range(groups))
    smem = pl.BlockSpec(memory_space=pltpu.SMEM)
    vmem = pl.BlockSpec(memory_space=pltpu.VMEM)
    return pl.pallas_call(
        functools.partial(attention_kernel, pre, place),
        in_specs=[smem, vmem, vmem, vmem],
        out_specs=[vmem, vmem, vmem, vmem],
        out_shape=[
            jax.ShapeDtypeStruct((slots, rows, LANES), BF16),
            jax.ShapeDtypeStruct((key_slots, rows, LANES), F32),
            jax.ShapeDtypeStruct((slots, 8, LANES), F32),
            jax.ShapeDtypeStruct((key_slots, rows + 16, LANES), BF16),
        ],
        scratch_shapes=[
            pltpu.SMEM((visits,), jnp.int32),
            pltpu.SMEM((visits,), jnp.int32),
            pltpu.VMEM((tiles, 2 * tile, LANES), BF16),
            pltpu.VMEM((tiles, 2 * tile, LANES), BF16),
            pltpu.VMEM((tiles, LANES, 2 * tile), BF16),
            pltpu.VMEM((groups, tile, LANES), BF16),
            pltpu.VMEM((groups, 2 * tile, LANES), BF16),
            pltpu.VMEM((groups, HD, tile), F32),
            pltpu.VMEM((visits, 2 * tile, tile), F32),
            pltpu.VMEM((groups, 8, tile), F32),
            pltpu.VMEM((groups, HD, tile), F32),
            pltpu.VMEM((groups, 8, tile), F32),
            pltpu.VMEM((groups, HD, tile), F32),
            pltpu.VMEM((tiles, 2 * tile, LANES), F32),
            pltpu.VMEM((slots, rows, LANES), F32),
        ],
        compiler_params=params(VMEM_MOST),
        cost_estimate=pl.CostEstimate(
            flops=10 * slots * rows * MAXLEN * LANES,
            bytes_accessed=20 * slots * rows * LANES,
            transcendentals=slots * rows * MAXLEN,
        ),
        name="attention",
    )(lengths, kv_mine, kv_other, qd)


def combine_kernel(cq_ref, mine_ref, edge_ref, got_ref, out_ref):
    slots, rows, _ = cq_ref.shape
    for s in range(slots):
        at = bit_reversed(s, slots)
        out_ref[at, pl.ds(0, rows)] = cq_ref[s]
        got = got_ref[s].astype(F32)
        out_ref[at, pl.ds(rows, rows)] = (mine_ref[s] + got[:rows]).astype(BF16)
        edges = [edge_ref[s] + got[rows : rows + 8], got[rows + 8 :]]
        out_ref[at, pl.ds(2 * rows, 16)] = jnp.concatenate(edges).astype(BF16)


def combine_call(cq, mine, edge, got):
    slots, rows, _ = cq.shape
    vmem = pl.BlockSpec(memory_space=pltpu.VMEM)
    return pl.pallas_call(
        combine_kernel,
        in_specs=[vmem] * 4,
        out_specs=vmem,
        out_shape=jax.ShapeDtypeStruct((slots, 2 * rows + 16, LANES), BF16),
        compiler_params=params(VMEM_SOME),
        name="combine",
    )(cq, mine, edge, got)


def combine_windows(cq, mine, got, pre, side, window, devices):
    slots, rows, _ = cq.shape
    dkv = mine + got[:, :rows].astype(F32)
    back = [(i + window, i) for i in range(devices - window)]
    earlier = lax.ppermute(dkv[:pre].astype(BF16), AXES, back).astype(F32)
    dkv = dkv[pre:].at[slots - pre :].add(earlier).astype(BF16)
    both = jnp.concatenate([cq, dkv], axis=2)
    tails, heads = both[:, rows - 8 :], both[:, :8]
    swapped = [(i, i ^ 1) for i in range(devices)]
    tails_other = lax.ppermute(tails, AXES, swapped)
    heads_other = lax.ppermute(heads, AXES, swapped)
    last = [(i, i + window - 1) for i in range(1, devices - window, 2)]
    tail_past = lax.ppermute(tails[-1:], AXES, last)
    head_next = lax.ppermute(heads[:1], AXES, [(j, i) for i, j in last])
    before = jnp.where(
        side == 0, jnp.concatenate([tail_past, tails_other[:-1]]), tails_other
    )
    after = jnp.where(side == 0, heads_other, jnp.concatenate([heads_other[1:], head_next]))
    edge = jnp.where(jnp.arange(8)[None, :, None] < 4, after, before)
    grads = jnp.concatenate([cq, dkv, edge[..., LANES:], edge[..., :LANES]], axis=1)
    return jnp.stack([grads[bit_reversed(s, slots)] for s in range(slots)])


def back_kernel(
    lengths_ref, r_ref, taps_ref, w_ref, wo_ref, attended_ref, grad_ref, context, grads, padded
):
    heads = r_ref.shape[0]
    rows, width = context.shape
    blk = width // BACK_STEPS
    main, dkv = slice(0, rows), slice(rows, 2 * rows)
    edge_dkv, edge_cq = slice(2 * rows, 2 * rows + 8), slice(2 * rows + 8, 2 * rows + 16)
    pad = jnp.zeros((8, LANES), F32)
    for pair in range(heads // 2):
        x, y = (r_ref[2 * pair + i, pl.ds(0, rows)].astype(F32) for i in range(2))
        context[:, pl.ds(pair * LANES, LANES)] = zip_low(x, y).astype(BF16)
    for step in range(BACK_STEPS):
        part = pl.ds(step * blk, blk)
        attended_ref[:, part] = jnp.dot(
            context[...], wo_ref[:, part], preferred_element_type=F32
        ).astype(BF16)
    for pair in range(heads // 2):
        x, y = (r_ref[2 * pair + i].astype(F32) for i in range(2))

        def gather(mix, part, edge):
            return jnp.concatenate([mix(x[part], y[part]), mix(x[edge], y[edge]), pad]).astype(BF16)

        lanes = pl.ds(pair * LANES, LANES)
        grads[:, lanes] = gather(zip_high, main, edge_cq)
        grads[:, pl.ds(width + pair * LANES, LANES)] = gather(zip_low, dkv, edge_dkv)
        grads[:, pl.ds(2 * width + pair * LANES, LANES)] = gather(zip_high, dkv, edge_dkv)
    masks = conv_masks(lengths_ref, device_index() * rows, rows)
    per = blk // LANES
    for step in range(BACK_STEPS):
        part = pl.ds(step * blk, blk)
        mixed = lax.dot_general(
            grads[...], w_ref[part, :], (((1,), (1,)), ((), ())), preferred_element_type=F32
        ).astype(BF16).astype(F32)
        edge = mixed[rows : rows + 8]
        padded[pl.ds(0, 8), part] = edge
        padded[pl.ds(8, rows), part] = mixed[:rows]
        padded[pl.ds(8 + rows, 8), part] = edge
        grad_ref[:, part] = conv_rows(
            padded, range(step * per, (step + 1) * per), taps_ref, masks, rows, True
        ).astype(BF16)


def back_call(lengths, r, taps, w_qkv, w_out):
    heads = r.shape[0]
    rows = (r.shape[1] - 16) // 2
    width = heads * HD
    smem = pl.BlockSpec(memory_space=pltpu.SMEM)
    vmem = pl.BlockSpec(memory_space=pltpu.VMEM)
    shape = jax.ShapeDtypeStruct((rows, width), BF16)
    return pl.pallas_call(
        back_kernel,
        in_specs=[smem, vmem, vmem, vmem, vmem],
        out_specs=[vmem, vmem],
        out_shape=[shape, shape],
        scratch_shapes=[
            pltpu.VMEM((rows, width), BF16),
            pltpu.VMEM((rows + 16, 3 * width), BF16),
            pltpu.VMEM((rows + 16, width), F32),
        ],
        compiler_params=params(VMEM_SOME),
        cost_estimate=pl.CostEstimate(
            flops=8 * rows * width * width, bytes_accessed=8 * width * width, transcendentals=0
        ),
        name="back",
    )(lengths, r, taps, w_qkv, w_out)


def bit_reversed(i, count):
    bits = count.bit_length() - 1
    if count != 1 << bits:
        return i
    return sum((i >> b & 1) << (bits - 1 - b) for b in range(bits))


def on_device(tokens, conv_kernel, w_qkv, w_out, lengths, cotangent):
    rows, width = tokens.shape
    heads = width // HD
    devices = lax.axis_size(AXES)
    window = 2 * heads
    windows = devices // window
    pre = MAXLEN // (2 * rows) if windows > 1 else 0
    me = lax.axis_index(AXES)
    same_side = [
        [w * window + 2 * bit_reversed(c, heads) + side for c in range(heads)]
        for w in range(windows)
        for side in range(2)
    ]
    swapped = [(i, i ^ 1) for i in range(devices)]
    across = [(i, i + (1 if i % 2 else -1)) for i in range(1, devices - 1)]

    def exchange(x):
        return lax.all_to_all(
            x, AXES, split_axis=0, concat_axis=0, axis_index_groups=same_side, tiled=True
        )

    first, last = tokens[:EDGE], tokens[rows - EDGE :]
    even = me % 2 == 0
    inner = lax.ppermute(jnp.where(even, last, first), AXES, swapped)
    outer = lax.ppermute(jnp.where(even, first, last), AXES, across)
    sent = front_call(lengths, inner, outer, tokens, conv_kernel, w_qkv, cotangent, w_out)
    qd = exchange(sent)
    kv_mine = qd[:, :rows]
    if pre:
        shift = [(i, i + window) for i in range(devices - window)]
        kv_mine = jnp.stack([kv_mine[bit_reversed(s, heads)] for s in range(heads)])
        kv_mine = jnp.concatenate([lax.ppermute(kv_mine[heads - pre :], AXES, shift), kv_mine])
    kv_other = lax.ppermute(kv_mine, AXES, swapped)
    cq, mine, edge, send = attention_call(lengths, kv_mine, kv_other, qd, pre)
    got = lax.ppermute(send, AXES, swapped)
    if pre:
        grads = combine_windows(cq, mine, got, pre, me % 2, window, devices)
    else:
        grads = combine_call(cq, mine, edge, got)
    return back_call(lengths, exchange(grads), conv_kernel, w_qkv, w_out)


def solution(mesh):
    placed = (P(AXES, None), P(), P(), P(), P(), P(AXES, None))
    return jax.shard_map(
        on_device,
        mesh=mesh,
        in_specs=placed,
        out_specs=(P(AXES, None), P(AXES, None)),
        check_vma=False,
    )
```

```python
import functools
import math

import jax
import jax.numpy as jnp
from jax import lax
from jax.experimental import pallas as pl
from jax.experimental.pallas import tpu as pltpu
from jax.sharding import PartitionSpec as P

HD = 64
KS = 7
HALF = KS // 2
MAXLEN = 2048
AXES = ("ctx", "head")
LANES = 128
EDGE = 16
PER_STEP = (8, 4, 2, 1)
FAR = -1e30
FRONT_STEPS = 4
BACK_STEPS = 4
VMEM_ALL = 57_500_000
VMEM_MOST = 44 * 1024 * 1024
VMEM_SOME = 24 * 1024 * 1024
F32 = jnp.float32
BF16 = jnp.bfloat16


def params(limit):
    return pltpu.CompilerParams(vmem_limit_bytes=limit)


def record_span(positions, lengths_ref):
    start = jnp.zeros_like(positions)
    stop = jnp.full_like(positions, jnp.iinfo(jnp.int32).max)
    end = jnp.int32(0)
    for i in range(lengths_ref.shape[0]):
        end = end + lengths_ref[i]
        past = end <= positions
        start = jnp.where(past, end, start)
        stop = jnp.where(past, stop, jnp.minimum(stop, end))
    return start, stop


def device_index():
    return lax.axis_index("ctx") * lax.axis_size("head") + lax.axis_index("head")


def low_lanes(shape):
    return lax.broadcasted_iota(jnp.int32, shape, len(shape) - 1) % LANES < HD


def swap_halves(x):
    return pltpu.roll(x, HD, x.ndim - 1)


def zip_low(x, y):
    return jnp.where(low_lanes(x.shape), x, swap_halves(y))


def zip_high(x, y):
    return jnp.where(low_lanes(x.shape), swap_halves(x), y)


def conv_masks(lengths_ref, first_row, rows):
    pos = first_row + lax.broadcasted_iota(jnp.int32, (rows, LANES), 0)
    start, stop = record_span(pos, lengths_ref)
    return [(pos + (t - HALF) >= start) & (pos + (t - HALF) < stop) for t in range(KS)]


def conv_rows(padded_ref, cols, kernel_ref, masks, rows, flip):
    pieces = []
    for c in cols:
        lanes = pl.ds(c * LANES, LANES)
        total = padded_ref[pl.ds(8, rows), lanes]
        for t in range(KS):
            tap = kernel_ref[KS - 1 - t if flip else t, lanes]
            shifted = padded_ref[pl.ds(8 - HALF + t, rows), lanes]
            total = total + jnp.where(masks[t], shifted, 0.0) * tap[None, :]
        pieces.append(total)
    return jnp.concatenate(pieces, axis=1)


def front_kernel(
    lengths_ref, inner_ref, outer_ref, x_hbm, taps_hbm, w_hbm, cot_hbm, wo_hbm,
    out_ref, x_ref, taps_ref, w_ref, cot_ref, wo_ref, padded, projected, d_rows, sems,
):
    rows, width = x_ref.shape
    blk = width // FRONT_STEPS

    def copy(source, target, i):
        return pltpu.make_async_copy(source, target, sems.at[i])

    whole = [
        copy(source, target, i)
        for i, (source, target) in enumerate(
            ((x_hbm, x_ref), (taps_hbm, taps_ref), (cot_hbm, cot_ref))
        )
    ]
    parts = []
    for step in range(FRONT_STEPS):
        part = pl.ds(step * blk, blk)
        at = 3 + 2 * step
        parts.append(
            (
                copy(w_hbm.at[part], w_ref.at[part], at),
                copy(wo_hbm.at[part], wo_ref.at[part], at + 1),
            )
        )
    for c in whole:
        c.start()
    for pair in parts:
        for c in pair:
            c.start()
    even = device_index() % 2 == 0
    inner, outer = inner_ref[...].astype(F32), outer_ref[...].astype(F32)
    padded[pl.ds(0, 8), :] = jnp.where(even, outer[EDGE - 8 :], inner[EDGE - 8 :])
    padded[pl.ds(8 + rows, 8), :] = jnp.where(even, inner[:8], outer[:8])
    for c in whole[:2]:
        c.wait()
    padded[pl.ds(8, rows), :] = x_ref[...].astype(F32)
    masks = conv_masks(lengths_ref, device_index() * rows, rows)
    per = blk // LANES
    for step in range(FRONT_STEPS):
        mixed = conv_rows(
            padded, range(step * per, (step + 1) * per), taps_ref, masks, rows, False
        ).astype(BF16)
        parts[step][0].wait()
        part = jnp.dot(mixed, w_ref[pl.ds(step * blk, blk), :], preferred_element_type=F32)
        if step == 0:
            projected[...] = part
        else:
            projected[...] += part
        if step == 0:
            whole[2].wait()
        parts[step][1].wait()
        d_rows[:, pl.ds(step * blk, blk)] = lax.dot_general(
            cot_ref[...], wo_ref[pl.ds(step * blk, blk), :], (((1,), (1,)), ((), ())),
            preferred_element_type=F32,
        )
    for pair in range(width // LANES):
        lanes = pl.ds(pair * LANES, LANES)
        q, k, v = (projected[:, pl.ds(i * width + pair * LANES, LANES)] for i in range(3))
        d = d_rows[:, lanes]
        out_ref[2 * pair] = jnp.concatenate([zip_low(k, v), zip_low(q, d)]).astype(BF16)
        out_ref[2 * pair + 1] = jnp.concatenate([zip_high(k, v), zip_high(q, d)]).astype(BF16)


def front_call(lengths, inner, outer, x, taps, w_qkv, cotangent, w_out):
    rows, width = x.shape
    heads = width // HD
    smem = pl.BlockSpec(memory_space=pltpu.SMEM)
    vmem = pl.BlockSpec(memory_space=pltpu.VMEM)
    anywhere = pl.BlockSpec(memory_space=pl.ANY)
    return pl.pallas_call(
        front_kernel,
        in_specs=[smem, vmem, vmem] + [anywhere] * 5,
        out_specs=vmem,
        out_shape=jax.ShapeDtypeStruct((heads, 2 * rows, LANES), BF16),
        scratch_shapes=[
            pltpu.VMEM(x.shape, x.dtype),
            pltpu.VMEM(taps.shape, taps.dtype),
            pltpu.VMEM(w_qkv.shape, w_qkv.dtype),
            pltpu.VMEM(cotangent.shape, cotangent.dtype),
            pltpu.VMEM(w_out.shape, w_out.dtype),
            pltpu.VMEM((rows + 16, width), F32),
            pltpu.VMEM((rows, 3 * width), F32),
            pltpu.VMEM((rows, width), F32),
            pltpu.SemaphoreType.DMA((3 + 2 * FRONT_STEPS,)),
        ],
        compiler_params=params(VMEM_ALL),
        cost_estimate=pl.CostEstimate(
            flops=8 * rows * width * width, bytes_accessed=8 * width * width, transcendentals=0
        ),
        name="front",
    )(lengths, inner, outer, x, taps, w_qkv, cotangent, w_out)


def attention_kernel(
    pre, place, lengths_ref, kv_mine, kv_other, qd_ref,
    cq_ref, dkv_mine, edge_mine, send_ref,
    visit_q, visit_k, keys_ref, marked_ref, turned_ref, query_ref, qd_cat_ref, d_turned_ref, e_ref,
    total_ref, context_ref, row_ref, d_query_ref, acc_ref, cq_full,
):
    slots = qd_ref.shape[0]
    key_slots, rows, _ = kv_mine.shape
    tile = 2 * rows
    tiles, groups = key_slots // 2, slots // 2
    me = device_index()
    window = 2 * slots
    base, parity = me // window * (window * rows), me % 2
    origin = base - pre * tile
    unit = HD**-0.5
    to_exp2 = unit * math.log2(math.e)

    row_in_block = lax.broadcasted_iota(jnp.int32, (rows, LANES), 0)

    def recorded(slot, side, first):
        at = first + slot * tile + side * rows
        return (row_in_block >= starts - at) & (row_in_block < stops - at)

    lane = lax.broadcasted_iota(jnp.int32, (1, LANES), 1)
    starts = jnp.zeros((1, LANES), jnp.int32)
    stops = jnp.zeros((1, LANES), jnp.int32)
    end = jnp.int32(0)
    for i in range(lengths_ref.shape[0]):
        starts = jnp.where(lane == HD + i, end, starts)
        end = end + lengths_ref[i]
        stops = jnp.where(lane == HD + i, end, stops)

    count = jnp.int32(groups)
    for u in range(groups):
        first = base + u * (2 * tile) + parity * rows
        begin, end = jnp.int32(0), jnp.int32(0)
        for i in range(lengths_ref.shape[0]):
            end = end + lengths_ref[i]
            begin = jnp.where(end <= first, end, begin)
        t_first = jnp.maximum(begin - origin, 0) // (2 * tile)

        def note(t, count, u=u):
            visit_q[count] = u
            visit_k[count] = t
            return count + 1

        count = lax.fori_loop(t_first, u + pre // 2, note, count)

    low = low_lanes((rows, LANES))
    for t in range(tiles):
        for half, source in enumerate((kv_mine, kv_other)):
            side = parity if half == 0 else 1 - parity
            for i in range(2):
                block = source[place(2 * t + i, pre)]
                at = pl.ds(half * tile + i * rows, rows)
                keys_ref[t, at] = block
                turned_ref[t, :, at] = block.T
                mark = jnp.where(recorded(2 * t + i, side, origin), 0.0, FAR)
                marked_ref[t, at] = jnp.where(low, block.astype(F32), mark).astype(BF16)
    for t in range(pre // 2):
        acc_ref[t] = jnp.zeros_like(acc_ref[t])
    for u in range(groups):
        for i in range(2):
            qd = qd_ref[place(2 * u + i, 0), pl.ds(rows, rows)]
            at = pl.ds(i * rows, rows)
            d_turned_ref[u, :, at] = qd.T[HD:].astype(F32)
            qd = qd.astype(F32)
            mark = jnp.where(recorded(2 * u + i, parity, base), 1.0, 0.0)
            query_ref[u, at] = jnp.where(low, qd, mark).astype(BF16)
            qd_cat_ref[u, at] = jnp.where(low, qd, 0.0).astype(BF16)
            qd_cat_ref[u, pl.ds(tile + i * rows, rows)] = jnp.where(low, 0.0, qd).astype(BF16)

    nt = (((1,), (1,)), ((), ()))
    wide = (2 * tile, tile)
    q_lane = lax.broadcasted_iota(jnp.int32, wide, 1)
    q_row = q_lane // rows * tile + q_lane % rows + parity * rows
    k_sub = lax.broadcasted_iota(jnp.int32, wide, 0)
    side = jnp.where(k_sub < tile, parity, 1 - parity)
    causal = k_sub // rows % 2 * tile + k_sub % rows + side * rows <= q_row

    def forward(i, u, t, diagonal):
        scores = lax.dot_general(marked_ref[t], query_ref[u], nt, preferred_element_type=F32)
        e = jnp.exp2(scores * to_exp2)
        if diagonal:
            e = jnp.where(causal, e, 0.0)
        e_ref[i] = e
        context = jnp.dot(turned_ref[t, HD:], e.astype(BF16), preferred_element_type=F32)
        return jnp.sum(e.reshape(2 * tile // 8, 8, tile), axis=0), context

    def forward_some(first, per):
        def run(j, carry):
            at = [first + per * j + i for i in range(per)]
            groups_at = [visit_q[i] for i in at]
            parts = [forward(i, u, visit_k[i], False) for i, u in zip(at, groups_at)]
            for u, (total, context) in zip(groups_at, parts):
                total_ref[u] += total
                context_ref[u] += context
            return carry

        return run

    def run_rest(make):
        first = groups
        for per in PER_STEP:
            steps = (count - first) // per
            lax.fori_loop(0, steps, make(first, per), 0)
            first = first + steps * per

    for u in range(groups):
        total_ref[u], context_ref[u] = forward(u, u, u + pre // 2, True)
    run_rest(forward_some)
    for u in range(groups):
        inverse = 1.0 / jnp.sum(total_ref[u], axis=0, keepdims=True)
        context = (context_ref[u] * inverse).astype(BF16).astype(F32)
        context_ref[u] = context
        row_ref[u, pl.ds(0, 1)] = inverse
        row_ref[u, pl.ds(1, 1)] = jnp.sum(d_turned_ref[u] * context, axis=0, keepdims=True)

    def backward(i, u, t):
        row = row_ref[u]
        probs = e_ref[i] * row[0:1]
        d_probs = lax.dot_general(
            keys_ref[t], qd_cat_ref[u, pl.ds(tile, tile)], nt, preferred_element_type=F32
        )
        d_scores = (probs * (d_probs - row[1:2])).astype(BF16)
        both = jnp.concatenate([d_scores, probs.astype(BF16)], axis=1)
        d_keys = jnp.dot(both, qd_cat_ref[u], preferred_element_type=F32)
        d_queries = jnp.dot(turned_ref[t, :HD], d_scores, preferred_element_type=F32)
        return d_keys, d_queries

    def backward_some(first, per):
        def run(j, carry):
            at = [(i, visit_q[i], visit_k[i]) for i in (first + per * j + i for i in range(per))]
            parts = [backward(i, u, t) for i, u, t in at]
            for (_, u, t), (d_keys, d_queries) in zip(at, parts):
                acc_ref[t] += d_keys
                d_query_ref[u] += d_queries
            return carry

        return run

    for u in range(groups):
        acc_ref[u + pre // 2], d_query_ref[u] = backward(u, u, u + pre // 2)
    run_rest(backward_some)
    for u in range(groups):
        packed = jnp.concatenate([context_ref[u], d_query_ref[u] * unit], axis=0).T
        for i in range(2):
            part = packed[i * rows : (i + 1) * rows]
            cq_full[2 * u + i] = part
            cq_ref[2 * u + i] = part.astype(BF16)
    scale = jnp.where(low_lanes((1, LANES)), unit, 1.0)
    head = lax.broadcasted_iota(jnp.int32, (8, LANES), 0) < 4

    def end_rows(half, slot, first):
        slot = pre + jnp.clip(slot, 0, slots - 1)
        at = half * tile + slot % 2 * rows + first
        return acc_ref[slot // 2, pl.ds(pl.multiple_of(at, 8), 8)] * scale

    for s in range(key_slots):
        part = pl.ds(s % 2 * rows, rows)
        dkv_mine[s] = acc_ref[s // 2, part] * scale
        part = pl.ds(tile + s % 2 * rows, rows)
        send_ref[s, pl.ds(0, rows)] = (acc_ref[s // 2, part] * scale).astype(BF16)
        if s < pre:
            send_ref[s, pl.ds(rows, 16)] = jnp.zeros((16, LANES), BF16)
    for s in range(slots):
        edge_mine[s] = jnp.where(
            head, end_rows(1, s + parity, 0), end_rows(1, s - 1 + parity, rows - 8)
        )
        past, later = s - parity, s + 1 - parity
        d_edge = jnp.where(head, end_rows(0, later, 0), end_rows(0, past, rows - 8))
        q_edge = jnp.where(
            head,
            cq_full[jnp.clip(later, 0, slots - 1), pl.ds(0, 8)],
            cq_full[jnp.clip(past, 0, slots - 1), pl.ds(rows - 8, 8)],
        )
        send_ref[pre + s, pl.ds(rows, 16)] = jnp.concatenate([d_edge, q_edge]).astype(BF16)


def attention_call(lengths, kv_mine, kv_other, qd, pre):
    slots = qd.shape[0]
    key_slots, rows, _ = kv_mine.shape
    tile = 2 * rows
    tiles, groups = key_slots // 2, slots // 2
    reach = MAXLEN // (2 * tile) + 1
    place = lambda s, ordered: s if ordered else bit_reversed(s, slots)
    visits = sum(min(u + pre // 2 + 1, reach) for u in range(groups))
    smem = pl.BlockSpec(memory_space=pltpu.SMEM)
    vmem = pl.BlockSpec(memory_space=pltpu.VMEM)
    return pl.pallas_call(
        functools.partial(attention_kernel, pre, place),
        in_specs=[smem, vmem, vmem, vmem],
        out_specs=[vmem, vmem, vmem, vmem],
        out_shape=[
            jax.ShapeDtypeStruct((slots, rows, LANES), BF16),
            jax.ShapeDtypeStruct((key_slots, rows, LANES), F32),
            jax.ShapeDtypeStruct((slots, 8, LANES), F32),
            jax.ShapeDtypeStruct((key_slots, rows + 16, LANES), BF16),
        ],
        scratch_shapes=[
            pltpu.SMEM((visits,), jnp.int32),
            pltpu.SMEM((visits,), jnp.int32),
            pltpu.VMEM((tiles, 2 * tile, LANES), BF16),
            pltpu.VMEM((tiles, 2 * tile, LANES), BF16),
            pltpu.VMEM((tiles, LANES, 2 * tile), BF16),
            pltpu.VMEM((groups, tile, LANES), BF16),
            pltpu.VMEM((groups, 2 * tile, LANES), BF16),
            pltpu.VMEM((groups, HD, tile), F32),
            pltpu.VMEM((visits, 2 * tile, tile), F32),
            pltpu.VMEM((groups, 8, tile), F32),
            pltpu.VMEM((groups, HD, tile), F32),
            pltpu.VMEM((groups, 8, tile), F32),
            pltpu.VMEM((groups, HD, tile), F32),
            pltpu.VMEM((tiles, 2 * tile, LANES), F32),
            pltpu.VMEM((slots, rows, LANES), F32),
        ],
        compiler_params=params(VMEM_MOST),
        cost_estimate=pl.CostEstimate(
            flops=10 * slots * rows * MAXLEN * LANES,
            bytes_accessed=20 * slots * rows * LANES,
            transcendentals=slots * rows * MAXLEN,
        ),
        name="attention",
    )(lengths, kv_mine, kv_other, qd)


def combine_kernel(cq_ref, mine_ref, edge_ref, got_ref, out_ref):
    slots, rows, _ = cq_ref.shape
    for s in range(slots):
        at = bit_reversed(s, slots)
        out_ref[at, pl.ds(0, rows)] = cq_ref[s]
        got = got_ref[s].astype(F32)
        out_ref[at, pl.ds(rows, rows)] = (mine_ref[s] + got[:rows]).astype(BF16)
        edges = [edge_ref[s] + got[rows : rows + 8], got[rows + 8 :]]
        out_ref[at, pl.ds(2 * rows, 16)] = jnp.concatenate(edges).astype(BF16)


def combine_call(cq, mine, edge, got):
    slots, rows, _ = cq.shape
    vmem = pl.BlockSpec(memory_space=pltpu.VMEM)
    return pl.pallas_call(
        combine_kernel,
        in_specs=[vmem] * 4,
        out_specs=vmem,
        out_shape=jax.ShapeDtypeStruct((slots, 2 * rows + 16, LANES), BF16),
        compiler_params=params(VMEM_SOME),
        name="combine",
    )(cq, mine, edge, got)


def combine_windows(cq, mine, got, pre, side, window, devices):
    slots, rows, _ = cq.shape
    dkv = mine + got[:, :rows].astype(F32)
    back = [(i + window, i) for i in range(devices - window)]
    earlier = lax.ppermute(dkv[:pre].astype(BF16), AXES, back).astype(F32)
    dkv = dkv[pre:].at[slots - pre :].add(earlier).astype(BF16)
    both = jnp.concatenate([cq, dkv], axis=2)
    tails, heads = both[:, rows - 8 :], both[:, :8]
    swapped = [(i, i ^ 1) for i in range(devices)]
    tails_other = lax.ppermute(tails, AXES, swapped)
    heads_other = lax.ppermute(heads, AXES, swapped)
    last = [(i, i + window - 1) for i in range(1, devices - window, 2)]
    tail_past = lax.ppermute(tails[-1:], AXES, last)
    head_next = lax.ppermute(heads[:1], AXES, [(j, i) for i, j in last])
    before = jnp.where(
        side == 0, jnp.concatenate([tail_past, tails_other[:-1]]), tails_other
    )
    after = jnp.where(side == 0, heads_other, jnp.concatenate([heads_other[1:], head_next]))
    edge = jnp.where(jnp.arange(8)[None, :, None] < 4, after, before)
    grads = jnp.concatenate([cq, dkv, edge[..., LANES:], edge[..., :LANES]], axis=1)
    return jnp.stack([grads[bit_reversed(s, slots)] for s in range(slots)])


def back_kernel(
    lengths_ref, r_ref, taps_ref, w_ref, wo_ref, attended_ref, grad_ref, context, grads, padded
):
    heads = r_ref.shape[0]
    rows, width = context.shape
    blk = width // BACK_STEPS
    main, dkv = slice(0, rows), slice(rows, 2 * rows)
    edge_dkv, edge_cq = slice(2 * rows, 2 * rows + 8), slice(2 * rows + 8, 2 * rows + 16)
    pad = jnp.zeros((8, LANES), F32)
    for pair in range(heads // 2):
        x, y = (r_ref[2 * pair + i, pl.ds(0, rows)].astype(F32) for i in range(2))
        context[:, pl.ds(pair * LANES, LANES)] = zip_low(x, y).astype(BF16)
    for step in range(BACK_STEPS):
        part = pl.ds(step * blk, blk)
        attended_ref[:, part] = jnp.dot(
            context[...], wo_ref[:, part], preferred_element_type=F32
        ).astype(BF16)
    for pair in range(heads // 2):
        x, y = (r_ref[2 * pair + i].astype(F32) for i in range(2))

        def gather(mix, part, edge):
            return jnp.concatenate([mix(x[part], y[part]), mix(x[edge], y[edge]), pad]).astype(BF16)

        lanes = pl.ds(pair * LANES, LANES)
        grads[:, lanes] = gather(zip_high, main, edge_cq)
        grads[:, pl.ds(width + pair * LANES, LANES)] = gather(zip_low, dkv, edge_dkv)
        grads[:, pl.ds(2 * width + pair * LANES, LANES)] = gather(zip_high, dkv, edge_dkv)
    masks = conv_masks(lengths_ref, device_index() * rows, rows)
    per = blk // LANES
    for step in range(BACK_STEPS):
        part = pl.ds(step * blk, blk)
        mixed = lax.dot_general(
            grads[...], w_ref[part, :], (((1,), (1,)), ((), ())), preferred_element_type=F32
        ).astype(BF16).astype(F32)
        edge = mixed[rows : rows + 8]
        padded[pl.ds(0, 8), part] = edge
        padded[pl.ds(8, rows), part] = mixed[:rows]
        padded[pl.ds(8 + rows, 8), part] = edge
        grad_ref[:, part] = conv_rows(
            padded, range(step * per, (step + 1) * per), taps_ref, masks, rows, True
        ).astype(BF16)


def back_call(lengths, r, taps, w_qkv, w_out):
    heads = r.shape[0]
    rows = (r.shape[1] - 16) // 2
    width = heads * HD
    smem = pl.BlockSpec(memory_space=pltpu.SMEM)
    vmem = pl.BlockSpec(memory_space=pltpu.VMEM)
    shape = jax.ShapeDtypeStruct((rows, width), BF16)
    return pl.pallas_call(
        back_kernel,
        in_specs=[smem, vmem, vmem, vmem, vmem],
        out_specs=[vmem, vmem],
        out_shape=[shape, shape],
        scratch_shapes=[
            pltpu.VMEM((rows, width), BF16),
            pltpu.VMEM((rows + 16, 3 * width), BF16),
            pltpu.VMEM((rows + 16, width), F32),
        ],
        compiler_params=params(VMEM_SOME),
        cost_estimate=pl.CostEstimate(
            flops=8 * rows * width * width, bytes_accessed=8 * width * width, transcendentals=0
        ),
        name="back",
    )(lengths, r, taps, w_qkv, w_out)


def bit_reversed(i, count):
    bits = count.bit_length() - 1
    if count != 1 << bits:
        return i
    return sum((i >> b & 1) << (bits - 1 - b) for b in range(bits))


def on_device(tokens, conv_kernel, w_qkv, w_out, lengths, cotangent):
    rows, width = tokens.shape
    heads = width // HD
    devices = lax.axis_size(AXES)
    window = 2 * heads
    windows = devices // window
    pre = MAXLEN // (2 * rows) if windows > 1 else 0
    me = lax.axis_index(AXES)
    same_side = [
        [w * window + 2 * bit_reversed(c, heads) + side for c in range(heads)]
        for w in range(windows)
        for side in range(2)
    ]
    swapped = [(i, i ^ 1) for i in range(devices)]
    across = [(i, i + (1 if i % 2 else -1)) for i in range(1, devices - 1)]

    def exchange(x):
        return lax.all_to_all(
            x, AXES, split_axis=0, concat_axis=0, axis_index_groups=same_side, tiled=True
        )

    first, last = tokens[:EDGE], tokens[rows - EDGE :]
    even = me % 2 == 0
    inner = lax.ppermute(jnp.where(even, last, first), AXES, swapped)
    outer = lax.ppermute(jnp.where(even, first, last), AXES, across)
    sent = front_call(lengths, inner, outer, tokens, conv_kernel, w_qkv, cotangent, w_out)
    qd = exchange(sent)
    kv_mine = qd[:, :rows]
    if pre:
        shift = [(i, i + window) for i in range(devices - window)]
        kv_mine = jnp.stack([kv_mine[bit_reversed(s, heads)] for s in range(heads)])
        kv_mine = jnp.concatenate([lax.ppermute(kv_mine[heads - pre :], AXES, shift), kv_mine])
    kv_other = lax.ppermute(kv_mine, AXES, swapped)
    cq, mine, edge, send = attention_call(lengths, kv_mine, kv_other, qd, pre)
    got = lax.ppermute(send, AXES, swapped)
    if pre:
        grads = combine_windows(cq, mine, got, pre, me % 2, window, devices)
    else:
        grads = combine_call(cq, mine, edge, got)
    return back_call(lengths, exchange(grads), conv_kernel, w_qkv, w_out)


def solution(mesh):
    placed = (P(AXES, None), P(), P(), P(), P(), P(AXES, None))
    return jax.shard_map(
        on_device,
        mesh=mesh,
        in_specs=placed,
        out_specs=(P(AXES, None), P(AXES, None)),
        check_vma=False,
    )
```

```python
import functools
import math

import jax
import jax.numpy as jnp
from jax import lax
from jax.experimental import pallas as pl
from jax.experimental.pallas import tpu as pltpu
from jax.sharding import PartitionSpec as P

HD = 64
KS = 7
HALF = KS // 2
MAXLEN = 2048
AXES = ("ctx", "head")
LANES = 128
EDGE = 16
PER_STEP = (8, 4, 2, 1)
FAR = -1e30
FRONT_STEPS = 4
BACK_STEPS = 4
VMEM_ALL = 57_500_000
VMEM_MOST = 44 * 1024 * 1024
VMEM_SOME = 24 * 1024 * 1024
F32 = jnp.float32
BF16 = jnp.bfloat16


def params(limit):
    return pltpu.CompilerParams(vmem_limit_bytes=limit)


def record_span(positions, lengths_ref):
    start = jnp.zeros_like(positions)
    stop = jnp.full_like(positions, jnp.iinfo(jnp.int32).max)
    end = jnp.int32(0)
    for i in range(lengths_ref.shape[0]):
        end = end + lengths_ref[i]
        past = end <= positions
        start = jnp.where(past, end, start)
        stop = jnp.where(past, stop, jnp.minimum(stop, end))
    return start, stop


def device_index():
    return lax.axis_index("ctx") * lax.axis_size("head") + lax.axis_index("head")


def low_lanes(shape):
    return lax.broadcasted_iota(jnp.int32, shape, len(shape) - 1) % LANES < HD


def swap_halves(x):
    return pltpu.roll(x, HD, x.ndim - 1)


def zip_low(x, y):
    return jnp.where(low_lanes(x.shape), x, swap_halves(y))


def zip_high(x, y):
    return jnp.where(low_lanes(x.shape), swap_halves(x), y)


def conv_masks(lengths_ref, first_row, rows):
    pos = first_row + lax.broadcasted_iota(jnp.int32, (rows, LANES), 0)
    start, stop = record_span(pos, lengths_ref)
    return [(pos + (t - HALF) >= start) & (pos + (t - HALF) < stop) for t in range(KS)]


def conv_rows(padded_ref, cols, kernel_ref, masks, rows, flip):
    pieces = []
    for c in cols:
        lanes = pl.ds(c * LANES, LANES)
        total = padded_ref[pl.ds(8, rows), lanes]
        for t in range(KS):
            tap = kernel_ref[KS - 1 - t if flip else t, lanes]
            shifted = padded_ref[pl.ds(8 - HALF + t, rows), lanes]
            total = total + jnp.where(masks[t], shifted, 0.0) * tap[None, :]
        pieces.append(total)
    return jnp.concatenate(pieces, axis=1)


def front_kernel(
    lengths_ref, inner_ref, outer_ref, x_hbm, taps_hbm, w_hbm, cot_hbm, wo_hbm,
    out_ref, x_ref, taps_ref, w_ref, cot_ref, wo_ref, padded, projected, d_rows, sems,
):
    rows, width = x_ref.shape
    blk = width // FRONT_STEPS

    def copy(source, target, i):
        return pltpu.make_async_copy(source, target, sems.at[i])

    whole = [
        copy(source, target, i)
        for i, (source, target) in enumerate(
            ((x_hbm, x_ref), (taps_hbm, taps_ref), (cot_hbm, cot_ref))
        )
    ]
    parts = []
    for step in range(FRONT_STEPS):
        part = pl.ds(step * blk, blk)
        at = 3 + 2 * step
        parts.append(
            (
                copy(w_hbm.at[part], w_ref.at[part], at),
                copy(wo_hbm.at[part], wo_ref.at[part], at + 1),
            )
        )
    for c in whole:
        c.start()
    for pair in parts:
        for c in reversed(pair):
            c.start()
    even = device_index() % 2 == 0
    inner, outer = inner_ref[...].astype(F32), outer_ref[...].astype(F32)
    padded[pl.ds(0, 8), :] = jnp.where(even, outer[EDGE - 8 :], inner[EDGE - 8 :])
    padded[pl.ds(8 + rows, 8), :] = jnp.where(even, inner[:8], outer[:8])
    for c in whole[:2]:
        c.wait()
    padded[pl.ds(8, rows), :] = x_ref[...].astype(F32)
    masks = conv_masks(lengths_ref, device_index() * rows, rows)
    per = blk // LANES
    for step in range(FRONT_STEPS):
        mixed = conv_rows(
            padded, range(step * per, (step + 1) * per), taps_ref, masks, rows, False
        ).astype(BF16)
        if step == 0:
            whole[2].wait()
        parts[step][1].wait()
        d_rows[:, pl.ds(step * blk, blk)] = lax.dot_general(
            cot_ref[...], wo_ref[pl.ds(step * blk, blk), :], (((1,), (1,)), ((), ())),
            preferred_element_type=F32,
        )
        parts[step][0].wait()
        part = jnp.dot(mixed, w_ref[pl.ds(step * blk, blk), :], preferred_element_type=F32)
        if step == 0:
            projected[...] = part
        else:
            projected[...] += part
    for pair in range(width // LANES):
        lanes = pl.ds(pair * LANES, LANES)
        q, k, v = (projected[:, pl.ds(i * width + pair * LANES, LANES)] for i in range(3))
        d = d_rows[:, lanes]
        out_ref[2 * pair] = jnp.concatenate([zip_low(k, v), zip_low(q, d)]).astype(BF16)
        out_ref[2 * pair + 1] = jnp.concatenate([zip_high(k, v), zip_high(q, d)]).astype(BF16)


def front_call(lengths, inner, outer, x, taps, w_qkv, cotangent, w_out):
    rows, width = x.shape
    heads = width // HD
    smem = pl.BlockSpec(memory_space=pltpu.SMEM)
    vmem = pl.BlockSpec(memory_space=pltpu.VMEM)
    anywhere = pl.BlockSpec(memory_space=pl.ANY)
    return pl.pallas_call(
        front_kernel,
        in_specs=[smem, vmem, vmem] + [anywhere] * 5,
        out_specs=vmem,
        out_shape=jax.ShapeDtypeStruct((heads, 2 * rows, LANES), BF16),
        scratch_shapes=[
            pltpu.VMEM(x.shape, x.dtype),
            pltpu.VMEM(taps.shape, taps.dtype),
            pltpu.VMEM(w_qkv.shape, w_qkv.dtype),
            pltpu.VMEM(cotangent.shape, cotangent.dtype),
            pltpu.VMEM(w_out.shape, w_out.dtype),
            pltpu.VMEM((rows + 16, width), F32),
            pltpu.VMEM((rows, 3 * width), F32),
            pltpu.VMEM((rows, width), F32),
            pltpu.SemaphoreType.DMA((3 + 2 * FRONT_STEPS,)),
        ],
        compiler_params=params(VMEM_ALL),
        cost_estimate=pl.CostEstimate(
            flops=8 * rows * width * width, bytes_accessed=8 * width * width, transcendentals=0
        ),
        name="front",
    )(lengths, inner, outer, x, taps, w_qkv, cotangent, w_out)


def attention_kernel(
    pre, place, lengths_ref, kv_mine, kv_other, qd_ref,
    cq_ref, dkv_mine, edge_mine, send_ref,
    visit_q, visit_k, keys_ref, marked_ref, turned_ref, query_ref, qd_cat_ref, d_turned_ref, e_ref,
    total_ref, context_ref, row_ref, d_query_ref, acc_ref, cq_full,
):
    slots = qd_ref.shape[0]
    key_slots, rows, _ = kv_mine.shape
    tile = 2 * rows
    tiles, groups = key_slots // 2, slots // 2
    me = device_index()
    window = 2 * slots
    base, parity = me // window * (window * rows), me % 2
    origin = base - pre * tile
    unit = HD**-0.5
    to_exp2 = unit * math.log2(math.e)

    row_in_block = lax.broadcasted_iota(jnp.int32, (rows, LANES), 0)

    def recorded(slot, side, first):
        at = first + slot * tile + side * rows
        return (row_in_block >= starts - at) & (row_in_block < stops - at)

    lane = lax.broadcasted_iota(jnp.int32, (1, LANES), 1)
    starts = jnp.zeros((1, LANES), jnp.int32)
    stops = jnp.zeros((1, LANES), jnp.int32)
    end = jnp.int32(0)
    for i in range(lengths_ref.shape[0]):
        starts = jnp.where(lane == HD + i, end, starts)
        end = end + lengths_ref[i]
        stops = jnp.where(lane == HD + i, end, stops)

    count = jnp.int32(groups)
    for u in range(groups):
        first = base + u * (2 * tile) + parity * rows
        begin, end = jnp.int32(0), jnp.int32(0)
        for i in range(lengths_ref.shape[0]):
            end = end + lengths_ref[i]
            begin = jnp.where(end <= first, end, begin)
        t_first = jnp.maximum(begin - origin, 0) // (2 * tile)

        def note(t, count, u=u):
            visit_q[count] = u
            visit_k[count] = t
            return count + 1

        count = lax.fori_loop(t_first, u + pre // 2, note, count)

    low = low_lanes((rows, LANES))
    for t in range(tiles):
        for half, source in enumerate((kv_mine, kv_other)):
            side = parity if half == 0 else 1 - parity
            for i in range(2):
                block = source[place(2 * t + i, pre)]
                at = pl.ds(half * tile + i * rows, rows)
                keys_ref[t, at] = block
                turned_ref[t, :, at] = block.T
                mark = jnp.where(recorded(2 * t + i, side, origin), 0.0, FAR)
                marked_ref[t, at] = jnp.where(low, block.astype(F32), mark).astype(BF16)
    for t in range(pre // 2):
        acc_ref[t] = jnp.zeros_like(acc_ref[t])
    for u in range(groups):
        for i in range(2):
            qd = qd_ref[place(2 * u + i, 0), pl.ds(rows, rows)]
            at = pl.ds(i * rows, rows)
            d_turned_ref[u, :, at] = qd.T[HD:].astype(F32)
            qd = qd.astype(F32)
            mark = jnp.where(recorded(2 * u + i, parity, base), 1.0, 0.0)
            query_ref[u, at] = jnp.where(low, qd, mark).astype(BF16)
            qd_cat_ref[u, at] = jnp.where(low, qd, 0.0).astype(BF16)
            qd_cat_ref[u, pl.ds(tile + i * rows, rows)] = jnp.where(low, 0.0, qd).astype(BF16)

    nt = (((1,), (1,)), ((), ()))
    wide = (2 * tile, tile)
    q_lane = lax.broadcasted_iota(jnp.int32, wide, 1)
    q_row = q_lane // rows * tile + q_lane % rows + parity * rows
    k_sub = lax.broadcasted_iota(jnp.int32, wide, 0)
    side = jnp.where(k_sub < tile, parity, 1 - parity)
    causal = k_sub // rows % 2 * tile + k_sub % rows + side * rows <= q_row

    def forward(i, u, t, diagonal):
        scores = lax.dot_general(marked_ref[t], query_ref[u], nt, preferred_element_type=F32)
        e = jnp.exp2(scores * to_exp2)
        if diagonal:
            e = jnp.where(causal, e, 0.0)
        e_ref[i] = e
        context = jnp.dot(turned_ref[t, HD:], e.astype(BF16), preferred_element_type=F32)
        return jnp.sum(e.reshape(2 * tile // 8, 8, tile), axis=0), context

    def forward_some(first, per):
        def run(j, carry):
            at = [first + per * j + i for i in range(per)]
            groups_at = [visit_q[i] for i in at]
            parts = [forward(i, u, visit_k[i], False) for i, u in zip(at, groups_at)]
            for u, (total, context) in zip(groups_at, parts):
                total_ref[u] += total
                context_ref[u] += context
            return carry

        return run

    def run_rest(make):
        first = groups
        for per in PER_STEP:
            steps = (count - first) // per
            lax.fori_loop(0, steps, make(first, per), 0)
            first = first + steps * per

    for u in range(groups):
        total_ref[u], context_ref[u] = forward(u, u, u + pre // 2, True)
    run_rest(forward_some)
    for u in range(groups):
        inverse = 1.0 / jnp.sum(total_ref[u], axis=0, keepdims=True)
        context = (context_ref[u] * inverse).astype(BF16).astype(F32)
        context_ref[u] = context
        row_ref[u, pl.ds(0, 1)] = inverse
        row_ref[u, pl.ds(1, 1)] = jnp.sum(d_turned_ref[u] * context, axis=0, keepdims=True)

    def backward(i, u, t):
        row = row_ref[u]
        probs = e_ref[i] * row[0:1]
        d_probs = lax.dot_general(
            keys_ref[t], qd_cat_ref[u, pl.ds(tile, tile)], nt, preferred_element_type=F32
        )
        d_scores = (probs * (d_probs - row[1:2])).astype(BF16)
        both = jnp.concatenate([d_scores, probs.astype(BF16)], axis=1)
        d_keys = jnp.dot(both, qd_cat_ref[u], preferred_element_type=F32)
        d_queries = jnp.dot(turned_ref[t, :HD], d_scores, preferred_element_type=F32)
        return d_keys, d_queries

    def backward_some(first, per):
        def run(j, carry):
            at = [(i, visit_q[i], visit_k[i]) for i in (first + per * j + i for i in range(per))]
            parts = [backward(i, u, t) for i, u, t in at]
            for (_, u, t), (d_keys, d_queries) in zip(at, parts):
                acc_ref[t] += d_keys
                d_query_ref[u] += d_queries
            return carry

        return run

    for u in range(groups):
        acc_ref[u + pre // 2], d_query_ref[u] = backward(u, u, u + pre // 2)
    run_rest(backward_some)
    for u in range(groups):
        packed = jnp.concatenate([context_ref[u], d_query_ref[u] * unit], axis=0).T
        for i in range(2):
            part = packed[i * rows : (i + 1) * rows]
            cq_full[2 * u + i] = part
            cq_ref[2 * u + i] = part.astype(BF16)
    scale = jnp.where(low_lanes((1, LANES)), unit, 1.0)
    head = lax.broadcasted_iota(jnp.int32, (8, LANES), 0) < 4

    def end_rows(half, slot, first):
        slot = pre + jnp.clip(slot, 0, slots - 1)
        at = half * tile + slot % 2 * rows + first
        return acc_ref[slot // 2, pl.ds(pl.multiple_of(at, 8), 8)] * scale

    for s in range(key_slots):
        part = pl.ds(s % 2 * rows, rows)
        dkv_mine[s] = acc_ref[s // 2, part] * scale
        part = pl.ds(tile + s % 2 * rows, rows)
        send_ref[s, pl.ds(0, rows)] = (acc_ref[s // 2, part] * scale).astype(BF16)
        if s < pre:
            send_ref[s, pl.ds(rows, 16)] = jnp.zeros((16, LANES), BF16)
    for s in range(slots):
        edge_mine[s] = jnp.where(
            head, end_rows(1, s + parity, 0), end_rows(1, s - 1 + parity, rows - 8)
        )
        past, later = s - parity, s + 1 - parity
        d_edge = jnp.where(head, end_rows(0, later, 0), end_rows(0, past, rows - 8))
        q_edge = jnp.where(
            head,
            cq_full[jnp.clip(later, 0, slots - 1), pl.ds(0, 8)],
            cq_full[jnp.clip(past, 0, slots - 1), pl.ds(rows - 8, 8)],
        )
        send_ref[pre + s, pl.ds(rows, 16)] = jnp.concatenate([d_edge, q_edge]).astype(BF16)


def attention_call(lengths, kv_mine, kv_other, qd, pre):
    slots = qd.shape[0]
    key_slots, rows, _ = kv_mine.shape
    tile = 2 * rows
    tiles, groups = key_slots // 2, slots // 2
    reach = MAXLEN // (2 * tile) + 1
    place = lambda s, ordered: s if ordered else bit_reversed(s, slots)
    visits = sum(min(u + pre // 2 + 1, reach) for u in range(groups))
    smem = pl.BlockSpec(memory_space=pltpu.SMEM)
    vmem = pl.BlockSpec(memory_space=pltpu.VMEM)
    return pl.pallas_call(
        functools.partial(attention_kernel, pre, place),
        in_specs=[smem, vmem, vmem, vmem],
        out_specs=[vmem, vmem, vmem, vmem],
        out_shape=[
            jax.ShapeDtypeStruct((slots, rows, LANES), BF16),
            jax.ShapeDtypeStruct((key_slots, rows, LANES), F32),
            jax.ShapeDtypeStruct((slots, 8, LANES), F32),
            jax.ShapeDtypeStruct((key_slots, rows + 16, LANES), BF16),
        ],
        scratch_shapes=[
            pltpu.SMEM((visits,), jnp.int32),
            pltpu.SMEM((visits,), jnp.int32),
            pltpu.VMEM((tiles, 2 * tile, LANES), BF16),
            pltpu.VMEM((tiles, 2 * tile, LANES), BF16),
            pltpu.VMEM((tiles, LANES, 2 * tile), BF16),
            pltpu.VMEM((groups, tile, LANES), BF16),
            pltpu.VMEM((groups, 2 * tile, LANES), BF16),
            pltpu.VMEM((groups, HD, tile), F32),
            pltpu.VMEM((visits, 2 * tile, tile), F32),
            pltpu.VMEM((groups, 8, tile), F32),
            pltpu.VMEM((groups, HD, tile), F32),
            pltpu.VMEM((groups, 8, tile), F32),
            pltpu.VMEM((groups, HD, tile), F32),
            pltpu.VMEM((tiles, 2 * tile, LANES), F32),
            pltpu.VMEM((slots, rows, LANES), F32),
        ],
        compiler_params=params(VMEM_MOST),
        cost_estimate=pl.CostEstimate(
            flops=10 * slots * rows * MAXLEN * LANES,
            bytes_accessed=20 * slots * rows * LANES,
            transcendentals=slots * rows * MAXLEN,
        ),
        name="attention",
    )(lengths, kv_mine, kv_other, qd)


def combine_kernel(cq_ref, mine_ref, edge_ref, got_ref, out_ref):
    slots, rows, _ = cq_ref.shape
    for s in range(slots):
        at = bit_reversed(s, slots)
        out_ref[at, pl.ds(0, rows)] = cq_ref[s]
        got = got_ref[s].astype(F32)
        out_ref[at, pl.ds(rows, rows)] = (mine_ref[s] + got[:rows]).astype(BF16)
        edges = [edge_ref[s] + got[rows : rows + 8], got[rows + 8 :]]
        out_ref[at, pl.ds(2 * rows, 16)] = jnp.concatenate(edges).astype(BF16)


def combine_call(cq, mine, edge, got):
    slots, rows, _ = cq.shape
    vmem = pl.BlockSpec(memory_space=pltpu.VMEM)
    return pl.pallas_call(
        combine_kernel,
        in_specs=[vmem] * 4,
        out_specs=vmem,
        out_shape=jax.ShapeDtypeStruct((slots, 2 * rows + 16, LANES), BF16),
        compiler_params=params(VMEM_SOME),
        name="combine",
    )(cq, mine, edge, got)


def combine_windows(cq, mine, got, pre, side, window, devices):
    slots, rows, _ = cq.shape
    dkv = mine + got[:, :rows].astype(F32)
    back = [(i + window, i) for i in range(devices - window)]
    earlier = lax.ppermute(dkv[:pre].astype(BF16), AXES, back).astype(F32)
    dkv = dkv[pre:].at[slots - pre :].add(earlier).astype(BF16)
    both = jnp.concatenate([cq, dkv], axis=2)
    tails, heads = both[:, rows - 8 :], both[:, :8]
    swapped = [(i, i ^ 1) for i in range(devices)]
    tails_other = lax.ppermute(tails, AXES, swapped)
    heads_other = lax.ppermute(heads, AXES, swapped)
    last = [(i, i + window - 1) for i in range(1, devices - window, 2)]
    tail_past = lax.ppermute(tails[-1:], AXES, last)
    head_next = lax.ppermute(heads[:1], AXES, [(j, i) for i, j in last])
    before = jnp.where(
        side == 0, jnp.concatenate([tail_past, tails_other[:-1]]), tails_other
    )
    after = jnp.where(side == 0, heads_other, jnp.concatenate([heads_other[1:], head_next]))
    edge = jnp.where(jnp.arange(8)[None, :, None] < 4, after, before)
    grads = jnp.concatenate([cq, dkv, edge[..., LANES:], edge[..., :LANES]], axis=1)
    return jnp.stack([grads[bit_reversed(s, slots)] for s in range(slots)])


def back_kernel(
    lengths_ref, r_ref, taps_ref, w_ref, wo_ref, attended_ref, grad_ref, context, grads, padded
):
    heads = r_ref.shape[0]
    rows, width = context.shape
    blk = width // BACK_STEPS
    main, dkv = slice(0, rows), slice(rows, 2 * rows)
    edge_dkv, edge_cq = slice(2 * rows, 2 * rows + 8), slice(2 * rows + 8, 2 * rows + 16)
    pad = jnp.zeros((8, LANES), F32)
    for pair in range(heads // 2):
        x, y = (r_ref[2 * pair + i, pl.ds(0, rows)].astype(F32) for i in range(2))
        context[:, pl.ds(pair * LANES, LANES)] = zip_low(x, y).astype(BF16)
    for step in range(BACK_STEPS):
        part = pl.ds(step * blk, blk)
        attended_ref[:, part] = jnp.dot(
            context[...], wo_ref[:, part], preferred_element_type=F32
        ).astype(BF16)
    for pair in range(heads // 2):
        x, y = (r_ref[2 * pair + i].astype(F32) for i in range(2))

        def gather(mix, part, edge):
            return jnp.concatenate([mix(x[part], y[part]), mix(x[edge], y[edge]), pad]).astype(BF16)

        lanes = pl.ds(pair * LANES, LANES)
        grads[:, lanes] = gather(zip_high, main, edge_cq)
        grads[:, pl.ds(width + pair * LANES, LANES)] = gather(zip_low, dkv, edge_dkv)
        grads[:, pl.ds(2 * width + pair * LANES, LANES)] = gather(zip_high, dkv, edge_dkv)
    masks = conv_masks(lengths_ref, device_index() * rows, rows)
    per = blk // LANES
    for step in range(BACK_STEPS):
        part = pl.ds(step * blk, blk)
        mixed = lax.dot_general(
            grads[...], w_ref[part, :], (((1,), (1,)), ((), ())), preferred_element_type=F32
        ).astype(BF16).astype(F32)
        edge = mixed[rows : rows + 8]
        padded[pl.ds(0, 8), part] = edge
        padded[pl.ds(8, rows), part] = mixed[:rows]
        padded[pl.ds(8 + rows, 8), part] = edge
        grad_ref[:, part] = conv_rows(
            padded, range(step * per, (step + 1) * per), taps_ref, masks, rows, True
        ).astype(BF16)


def back_call(lengths, r, taps, w_qkv, w_out):
    heads = r.shape[0]
    rows = (r.shape[1] - 16) // 2
    width = heads * HD
    smem = pl.BlockSpec(memory_space=pltpu.SMEM)
    vmem = pl.BlockSpec(memory_space=pltpu.VMEM)
    shape = jax.ShapeDtypeStruct((rows, width), BF16)
    return pl.pallas_call(
        back_kernel,
        in_specs=[smem, vmem, vmem, vmem, vmem],
        out_specs=[vmem, vmem],
        out_shape=[shape, shape],
        scratch_shapes=[
            pltpu.VMEM((rows, width), BF16),
            pltpu.VMEM((rows + 16, 3 * width), BF16),
            pltpu.VMEM((rows + 16, width), F32),
        ],
        compiler_params=params(VMEM_SOME),
        cost_estimate=pl.CostEstimate(
            flops=8 * rows * width * width, bytes_accessed=8 * width * width, transcendentals=0
        ),
        name="back",
    )(lengths, r, taps, w_qkv, w_out)


def bit_reversed(i, count):
    bits = count.bit_length() - 1
    if count != 1 << bits:
        return i
    return sum((i >> b & 1) << (bits - 1 - b) for b in range(bits))


def on_device(tokens, conv_kernel, w_qkv, w_out, lengths, cotangent):
    rows, width = tokens.shape
    heads = width // HD
    devices = lax.axis_size(AXES)
    window = 2 * heads
    windows = devices // window
    pre = MAXLEN // (2 * rows) if windows > 1 else 0
    me = lax.axis_index(AXES)
    same_side = [
        [w * window + 2 * bit_reversed(c, heads) + side for c in range(heads)]
        for w in range(windows)
        for side in range(2)
    ]
    swapped = [(i, i ^ 1) for i in range(devices)]
    across = [(i, i + (1 if i % 2 else -1)) for i in range(1, devices - 1)]

    def exchange(x):
        return lax.all_to_all(
            x, AXES, split_axis=0, concat_axis=0, axis_index_groups=same_side, tiled=True
        )

    first, last = tokens[:EDGE], tokens[rows - EDGE :]
    even = me % 2 == 0
    inner = lax.ppermute(jnp.where(even, last, first), AXES, swapped)
    outer = lax.ppermute(jnp.where(even, first, last), AXES, across)
    sent = front_call(lengths, inner, outer, tokens, conv_kernel, w_qkv, cotangent, w_out)
    qd = exchange(sent)
    kv_mine = qd[:, :rows]
    if pre:
        shift = [(i, i + window) for i in range(devices - window)]
        kv_mine = jnp.stack([kv_mine[bit_reversed(s, heads)] for s in range(heads)])
        kv_mine = jnp.concatenate([lax.ppermute(kv_mine[heads - pre :], AXES, shift), kv_mine])
    kv_other = lax.ppermute(kv_mine, AXES, swapped)
    cq, mine, edge, send = attention_call(lengths, kv_mine, kv_other, qd, pre)
    got = lax.ppermute(send, AXES, swapped)
    if pre:
        grads = combine_windows(cq, mine, got, pre, me % 2, window, devices)
    else:
        grads = combine_call(cq, mine, edge, got)
    return back_call(lengths, exchange(grads), conv_kernel, w_qkv, w_out)


def solution(mesh):
    placed = (P(AXES, None), P(), P(), P(), P(), P(AXES, None))
    return jax.shard_map(
        on_device,
        mesh=mesh,
        in_specs=placed,
        out_specs=(P(AXES, None), P(AXES, None)),
        check_vma=False,
    )
```
